32 devices in a mesh: inp: 4 (over y, x), chan: 8 (over z, core).
Axes of the slice: x: 2, y: 2, z: 4, core: 2. Of those that a mesh axis runs over, the one named last changes fastest.
Arguments:
- voltages: bfloat16 [128, 128, 8192], P('inp', 'chan'), may hold values from -6 to 6
- history: bfloat16 [128, 7, 8192], P('inp'), may hold values from -6 to 6
- taper: float32 [8, 8192], replicated, may hold values from -2 to 2
Outputs:
- visibility: bfloat16 [2, 2048, 128, 128], P(None, ('inp', 'chan'))
The draws below stay inside these ranges and needn't reach their ends.
All inputs are finite; a program needn't handle non-finite values.
Results may differ from the reference program's by a relative error of at most 0.005.
Values may be sent and summed in bfloat16 or wider, within the bound.
No kernel may reach another device: no remote copies, remote signals or barrier semaphores. Data moves between devices by JAX's collectives and lax.ppermute only.
A program may use at most 192 MiB of HBM per device.

```python
import math
import jax
import jax.numpy as jnp
from jax import lax

TAPS = 8
BAND = 2048
FRAME = 8192
LOW = 1024
NIN = 128
SPECTRA = 128


def block_scale(key, shape, cuts, least, top_value):
    def one(dim, parts):
        heights = jax.random.uniform(jax.random.fold_in(jax.random.fold_in(key, 6), dim), (parts,), jnp.float32, least / len(cuts), top_value / len(cuts))
        return jnp.repeat(jnp.exp(heights), shape[dim] // parts).reshape((-1,) + (1,) * (len(shape) - dim - 1))

    level = one(*cuts[0])
    for cut in cuts[1:]:
        level = level * one(*cut)
    return level


def noise(rng, extent, deviation, reach, pieces=(), kind=jnp.bfloat16):
    values = deviation * jax.random.normal(rng, extent, jnp.float32)
    if pieces:
        values = values * block_scale(rng, extent, pieces, -0.22, 0.18)
    return jnp.clip(values, -reach, reach).astype(kind)


def setup_inputs(seed: int = 0) -> dict:
    key_of = jax.random.split(jax.random.key(seed), 4)
    voltages = noise(key_of[0], (NIN, SPECTRA, FRAME), 1.0, 6.0, ((0, 4), (1, 8)))
    history = noise(key_of[1], (NIN, TAPS - 1, FRAME), 1.0, 6.0, ((0, 4),))
    taper = noise(key_of[2], (TAPS, FRAME), 0.35, 2.0, (), jnp.float32)
    return {"voltages": voltages, "history": history, "taper": taper}


def reference(voltages, history, taper):
    scale_factor = 1.0 / math.sqrt(FRAME)

    def one_input(pair_rows):
        earlier, current = pair_rows
        extended = jnp.concatenate([earlier, current], axis=0).astype(jnp.float32)
        filtered = jnp.zeros((SPECTRA, FRAME), jnp.float32)
        for offset in range(TAPS):
            filtered = filtered + taper[offset][None, :] * extended[offset:offset + SPECTRA]
        transformed = jnp.fft.rfft(filtered, axis=-1)[:, LOW:LOW + BAND]
        real_part = jnp.real(transformed) * scale_factor
        imag_part = jnp.imag(transformed) * scale_factor
        return jnp.stack([real_part, imag_part]).astype(jnp.bfloat16)
    spectra = lax.map(one_input, (history, voltages))
    width = 128
    count = BAND // width

    def one_block(block_index):
        start = (block_index * width).astype(jnp.int32)
        piece = lax.dynamic_slice_in_dim(spectra, start, width, axis=3).astype(jnp.float32)
        real_part = piece[:, 0]
        imag_part = piece[:, 1]
        vis_real = jnp.einsum('isk,jsk->kij', real_part, real_part) + jnp.einsum('isk,jsk->kij', imag_part, imag_part)
        vis_imag = jnp.einsum('isk,jsk->kij', imag_part, real_part) - jnp.einsum('isk,jsk->kij', real_part, imag_part)
        return (jnp.stack([vis_real, vis_imag]) / SPECTRA).astype(jnp.bfloat16)
    blocks = lax.map(one_block, jnp.arange(count, dtype=jnp.int32))
    return jnp.transpose(blocks, (1, 0, 2, 3, 4)).reshape(2, BAND, NIN, NIN)
```

```python
import math

import jax
import jax.numpy as jnp
import ml_dtypes
import numpy as np
from jax import lax
from jax.experimental import pallas as pl
from jax.experimental.pallas import tpu as pltpu
from jax.sharding import PartitionSpec as P

BAND = 2048
LOW = 1024
LANES = 128
RADIX = 64
HALF = 16
CLASSES = RADIX // 2
ROOT = math.sqrt(0.5)
F32 = jnp.float32
BF16 = jnp.bfloat16
VMEM = 56 * 1024 * 1024


def stage_table(frame):
    high = BAND // RADIX
    lane = np.arange(LANES)
    table = np.zeros((CLASSES, 2, high, 2, 2, LANES))
    for q in range(CLASSES):
        for half in range(2):
            low = q if half == 0 else (RADIX - q if q else RADIX // 2)
            k = low + RADIX * (LOW // RADIX + np.arange(high))
            angle = 2.0 * np.pi * (np.outer(k, lane) % frame) / frame
            cos, sin = np.cos(angle), np.sin(angle)
            if q == 0:
                table[q, half, :, 0, half] = cos
                table[q, half, :, 1, half] = -sin
            elif half == 0:
                table[q, half, :, 0, 0] = cos
                table[q, half, :, 0, 1] = sin
                table[q, half, :, 1, 0] = -sin
                table[q, half, :, 1, 1] = cos
            else:
                table[q, half, :, 0, 0] = cos
                table[q, half, :, 0, 1] = -sin
                table[q, half, :, 1, 0] = -sin
                table[q, half, :, 1, 1] = -cos
    table = table / math.sqrt(frame)
    return table.reshape(CLASSES, 2 * high * 2, 2 * LANES)


def lane_order(n_inp, times):
    size = n_inp * 2 * times * HALF
    source = np.arange(size).reshape(n_inp * 2, times, HALF).transpose(1, 0, 2).reshape(-1)
    matrix = np.zeros((size, size))
    matrix[source, np.arange(size)] = 1.0
    return matrix


def real_dft8(x):
    s = [x[j] + x[j + 4] for j in range(4)]
    d = [x[j] - x[j + 4] for j in range(4)]
    e0, e1 = s[0] + s[2], s[0] - s[2]
    o0, o1 = s[1] + s[3], s[3] - s[1]
    u, v = (d[1] - d[3]) * ROOT, (d[1] + d[3]) * ROOT
    return [
        (e0 + o0, None),
        (d[0] + u, -(d[2] + v)),
        (e1, o1),
        (d[0] - u, d[2] - v),
        (e0 - o0, None),
    ]


def complex_dft8(x):
    def add(a, b):
        return (a[0] + b[0], a[1] + b[1])

    def sub(a, b):
        return (a[0] - b[0], a[1] - b[1])

    def add_i(a, b):
        return (a[0] - b[1], a[1] + b[0])

    def sub_i(a, b):
        return (a[0] + b[1], a[1] - b[0])

    s = [add(x[j], x[j + 4]) for j in range(4)]
    d = [sub(x[j], x[j + 4]) for j in range(4)]
    e0, e1 = add(s[0], s[2]), sub(s[0], s[2])
    o0, o1 = add(s[1], s[3]), sub(s[1], s[3])
    p, m = sub(d[1], d[3]), add(d[1], d[3])
    b = ((p[0] + m[1]) * ROOT, (p[1] - m[0]) * ROOT)
    c = ((m[1] - p[0]) * ROOT, (-p[1] - m[0]) * ROOT)
    f, g = sub_i(d[0], d[2]), add_i(d[0], d[2])
    return [
        add(e0, o0),
        add(f, b),
        sub_i(e1, o1),
        add(g, c),
        sub(e0, o0),
        sub(f, b),
        add_i(e1, o1),
        sub(g, c),
    ]


def turned(value, step):
    angle = 2.0 * math.pi * (step % RADIX) / RADIX
    cos, sin = math.cos(angle), math.sin(angle)
    real, imag = value
    if imag is None:
        return (real * cos, real * -sin)
    if step % RADIX == 0:
        return value
    return (real * cos + imag * sin, imag * cos - real * sin)


def transform_rows(fir, mid, zed, count):
    def one(s, carry):
        for low in range(8):
            parts = real_dft8([fir[8 * high + low, s] for high in range(8)])
            mid[0, low] = parts[0][0]
            mid[7, low] = parts[4][0]
            for k in (1, 2, 3):
                value = turned(parts[k], low * k)
                mid[2 * k - 1, low] = value[0]
                mid[2 * k, low] = value[1]
        rows = pl.ds(pl.multiple_of(s * HALF, HALF), HALF)

        def put(q, half, value):
            zed[q, rows, half * LANES : (half + 1) * LANES] = value.astype(BF16)

        parts = real_dft8([mid[0, low] for low in range(8)])
        put(0, 0, parts[0][0])
        put(0, 1, parts[4][0])
        for m in (1, 2, 3):
            put(8 * m, 0, parts[m][0])
            put(8 * m, 1, parts[m][1])
        for k in (1, 2, 3):
            parts = complex_dft8([(mid[2 * k - 1, low], mid[2 * k, low]) for low in range(8)])
            for m in range(8):
                index = k + 8 * m
                if index < CLASSES:
                    put(index, 0, parts[m][0])
                    put(index, 1, parts[m][1])
                else:
                    put(RADIX - index, 0, parts[m][0])
                    put(RADIX - index, 1, -parts[m][1])
        parts = complex_dft8([turned((mid[7, low], None), 4 * low) for low in range(8)])
        for m in range(4):
            put(4 + 8 * m, 0, parts[m][0])
            put(4 + 8 * m, 1, parts[m][1])
        return carry

    lax.fori_loop(0, count, one, 0)


def filter_rows(volt, taper, fir, turn, first, count, hist=None, keep=None):
    taps = taper.shape[0]
    s_dev = volt.shape[1]
    wanted = [f for f in range(first - taps + 1, first + count) if f < s_dev]

    def one(a, carry):
        lanes = pl.ds(pl.multiple_of(a * LANES, LANES), LANES)
        turn[...] = volt[:, :, lanes].astype(F32).reshape(HALF * s_dev, LANES)
        frames = {}
        for f in wanted:
            if f >= 0:
                frames[f] = turn[pl.ds(f, HALF, stride=s_dev), :]
            elif hist is not None:
                frames[f] = hist[taps - 1 + f, :, lanes].astype(F32) * keep
        weights = [taper[t : t + 1, lanes] for t in range(taps)]
        for j in range(count):
            total = None
            for t in range(taps):
                f = first + j + t - taps + 1
                if f in frames:
                    term = weights[t] * frames[f]
                    total = term if total is None else total + term
            fir[a, j] = total
        return carry

    lax.fori_loop(0, RADIX, one, 0)


def tail_kernel(volt, taper, table, out, turn, fir, mid, zed):
    s_dev = volt.shape[1]
    count = taper.shape[0] - 1
    filter_rows(volt, taper, fir, turn, s_dev, count)
    transform_rows(fir, mid, zed, count)

    def one(q, carry):
        out[q, 0] = lax.dot_general(
            zed[q], table[q], (((1,), (1,)), ((), ())), preferred_element_type=F32
        ).astype(BF16)
        return carry

    lax.fori_loop(0, CLASSES, one, 0)


def spectra_kernel(first, boundary, *refs):
    if boundary:
        keep, volt, hist, carried, unit, taper, table, out, turn, fir, mid, zed, wide = refs
        filter_rows(volt, taper, fir, turn, first, fir.shape[1], hist, keep[0])
    else:
        volt, taper, table, out, turn, fir, mid, zed, wide = refs
        filter_rows(volt, taper, fir, turn, first, fir.shape[1])
    transform_rows(fir, mid, zed, fir.shape[1])
    contract = (((1,), (1,)), ((), ()))
    step = RADIX

    def one(q, carry):
        value = lax.dot_general(table[q], zed[q], contract, preferred_element_type=F32)
        if boundary:
            value = value + lax.dot_general(
                unit[...], carried[q, 0], contract, preferred_element_type=F32
            )
        wide[pl.ds(pl.multiple_of(q * step, step), step), :] = value[:step]
        other = jnp.where(q == 0, CLASSES, RADIX - q)
        wide[pl.ds(pl.multiple_of(other * step, step), step), :] = value[step:]
        return carry

    lax.fori_loop(0, CLASSES, one, 0)
    channels = out.shape[2] // 2
    split = RADIX // channels
    high = out.shape[0] // split

    def two(g, carry):
        for part in range(2):
            rows = wide[pl.ds(g * 2 + part, RADIX, stride=step), :].astype(BF16)
            for u in range(split):
                out[g * split + u, 0, part * channels : (part + 1) * channels, :] = rows[
                    u * channels : (u + 1) * channels
                ]
        return carry

    lax.fori_loop(0, high, two, 0)


def order_kernel(got, order, out, turn):
    n_inp, pair, _, rows, _ = got.shape
    tiles = out.shape[2] // LANES
    times = order.shape[1] // out.shape[2]
    for c in range(pair):
        wide = jnp.concatenate([got[a, c, h] for a in range(n_inp) for h in range(2)], axis=1)
        value = jnp.dot(wide, order[...], preferred_element_type=F32)
        for s in range(times):
            for tile in range(tiles):
                start = (s * tiles + tile) * LANES
                turn[tile, pl.ds((c * times + s) * rows, rows), :] = value[:, start : start + LANES]

    def one(r, carry):
        for tile in range(tiles):
            out[r, :, tile * LANES : (tile + 1) * LANES] = turn[
                tile, pl.ds(r, pair * times, stride=rows), :
            ].astype(BF16)
        return carry

    lax.fori_loop(0, rows, one, 0)


def gram_kernel(scale, one_ref, two_ref, out):
    width = out.shape[-1]
    for k in range(out.shape[1]):
        real = jnp.concatenate([one_ref[0, k], two_ref[0, k]], axis=0)
        imag = jnp.concatenate([one_ref[1, k], two_ref[1, k]], axis=0)
        left = jnp.concatenate([real, imag], axis=0)
        right = jnp.concatenate([-imag, real], axis=0)
        value = lax.dot_general(
            left,
            jnp.concatenate([left, right], axis=1),
            (((0,), (0,)), ((), ())),
            preferred_element_type=F32,
        )
        value = value * scale
        out[0, k] = value[:, :width].astype(BF16)
        out[1, k] = value[:, width:].astype(BF16)


def params():
    return pltpu.CompilerParams(vmem_limit_bytes=VMEM)


def cost(flops, moved):
    return pl.CostEstimate(flops=int(flops), bytes_accessed=int(moved), transcendentals=0)


def on_device(voltages, history, taper):
    in_dev, s_dev, frame = voltages.shape
    taps = taper.shape[0]
    n_inp = lax.axis_size("inp")
    n_chan = lax.axis_size("chan")
    groups = n_inp * n_chan
    channels = BAND // groups
    total = n_inp * in_dev
    halves = in_dev // HALF
    times = s_dev // 2
    early = taps - 1
    rows = times * HALF
    assert frame == RADIX * LANES and halves == 2 and rows == LANES
    assert early == times - 1 and RADIX % channels == 0 and total % LANES == 0

    outputs = 2 * BAND // CLASSES
    table = jnp.asarray(stage_table(frame).astype(np.float32).astype(ml_dtypes.bfloat16))
    unit = jnp.asarray(np.eye(outputs).astype(ml_dtypes.bfloat16))
    order = jnp.asarray(lane_order(n_inp, times).astype(ml_dtypes.bfloat16))
    assert table.shape == (CLASSES, outputs, 2 * LANES) and outputs == LANES

    volt_spec = pl.BlockSpec((HALF, s_dev, frame), lambda h: (h, 0, 0))
    taper_spec = pl.BlockSpec((taps, frame), lambda h: (0, 0))
    table_spec = pl.BlockSpec(table.shape, lambda h: (0, 0, 0))

    def scratch(count):
        return [
            pltpu.VMEM((HALF * s_dev, LANES), F32),
            pltpu.VMEM((RADIX, count, HALF, LANES), F32),
            pltpu.VMEM((8, 8, HALF, LANES), F32),
            pltpu.VMEM((CLASSES, count * HALF, 2 * LANES), BF16),
        ]

    wide = [pltpu.VMEM((RADIX * RADIX, LANES), F32)]
    carried = pl.pallas_call(
        tail_kernel,
        grid=(halves,),
        in_specs=[volt_spec, taper_spec, table_spec],
        out_specs=pl.BlockSpec((CLASSES, 1, early * HALF, outputs), lambda h: (0, h, 0, 0)),
        out_shape=jax.ShapeDtypeStruct((CLASSES, halves, early * HALF, outputs), BF16),
        scratch_shapes=scratch(early),
        compiler_params=params(),
        cost_estimate=cost(4e9, 2e7),
        name="carried",
    )(voltages, taper, table)
    carried = lax.ppermute(carried, "chan", [(i, i + 1) for i in range(n_chan - 1)])

    send_spec = pl.BlockSpec((groups, 1, 2 * channels, LANES), lambda h: (0, h, 0, 0))
    send_shape = jax.ShapeDtypeStruct((groups, halves, 2 * channels, LANES), BF16)
    late_send = pl.pallas_call(
        lambda *refs: spectra_kernel(times, False, *refs),
        grid=(halves,),
        in_specs=[volt_spec, taper_spec, table_spec],
        out_specs=send_spec,
        out_shape=send_shape,
        scratch_shapes=scratch(times) + wide,
        compiler_params=params(),
        cost_estimate=cost(8e9, 4e7),
        name="late",
    )(voltages, taper, table)

    def exchange(value):
        value = lax.all_to_all(value, ("inp", "chan"), split_axis=0, concat_axis=0, tiled=True)
        return value.reshape(n_inp, n_chan, halves, 2 * channels, LANES)

    late_got = exchange(late_send)

    keep = (lax.axis_index("chan") == 0).astype(F32).reshape(1)
    carried = jnp.pad(carried, ((0, 0), (0, 0), (0, HALF), (0, 0)))
    early_send = pl.pallas_call(
        lambda *refs: spectra_kernel(0, True, *refs),
        grid=(halves,),
        in_specs=[
            pl.BlockSpec(memory_space=pltpu.SMEM),
            volt_spec,
            pl.BlockSpec((early, HALF, frame), lambda h: (0, h, 0)),
            pl.BlockSpec((CLASSES, 1, rows, outputs), lambda h: (0, h, 0, 0)),
            pl.BlockSpec(unit.shape, lambda h: (0, 0)),
            taper_spec,
            table_spec,
        ],
        out_specs=send_spec,
        out_shape=send_shape,
        scratch_shapes=scratch(times) + wide,
        compiler_params=params(),
        cost_estimate=cost(8e9, 4e7),
        name="early",
    )(keep, voltages, jnp.transpose(history, (1, 0, 2)), carried, unit, taper, table)
    early_got = exchange(early_send)

    def ordered(got, name):
        pair = 16 // times
        steps = n_chan // pair
        return pl.pallas_call(
            order_kernel,
            grid=(steps,),
            in_specs=[
                pl.BlockSpec(
                    (n_inp, pair, halves, 2 * channels, LANES), lambda c: (0, c, 0, 0, 0)
                ),
                pl.BlockSpec(order.shape, lambda c: (0, 0)),
            ],
            out_specs=pl.BlockSpec((2 * channels, pair * times, total), lambda c: (0, c, 0)),
            out_shape=jax.ShapeDtypeStruct((2 * channels, n_chan * times, total), BF16),
            scratch_shapes=[
                pltpu.VMEM((total // LANES, pair * times * 2 * channels, LANES), F32)
            ],
            compiler_params=params(),
            cost_estimate=cost(2e9, 1e7),
            name=name,
        )(got, order).reshape(2, channels, n_chan * times, total)

    late_rows = ordered(late_got, "late_order")
    early_rows = ordered(early_got, "early_order")
    block = 8
    side_spec = pl.BlockSpec((2, block, n_chan * times, total), lambda k: (0, k, 0, 0))
    return pl.pallas_call(
        lambda *refs: gram_kernel(1.0 / (n_chan * s_dev), *refs),
        grid=(channels // block,),
        in_specs=[side_spec, side_spec],
        out_specs=pl.BlockSpec((2, block, total, total), lambda k: (0, k, 0, 0)),
        out_shape=jax.ShapeDtypeStruct((2, channels, total, total), BF16),
        compiler_params=params(),
        cost_estimate=cost(4e9, 1e7),
        name="gram",
    )(late_rows, early_rows)


def solution(mesh):
    in_specs = (P("inp", "chan", None), P("inp", None, None), P())
    out_specs = P(None, ("inp", "chan"), None, None)
    return jax.shard_map(
        on_device, mesh=mesh, in_specs=in_specs, out_specs=out_specs, check_vma=False
    )
```

```python
import math

import jax
import jax.numpy as jnp
import ml_dtypes
import numpy as np
from jax import lax
from jax.experimental import pallas as pl
from jax.experimental.pallas import tpu as pltpu
from jax.sharding import PartitionSpec as P

BAND = 2048
LOW = 1024
LANES = 128
RADIX = 64
HALF = 16
CLASSES = RADIX // 2
ROOT = math.sqrt(0.5)
F32 = jnp.float32
BF16 = jnp.bfloat16
VMEM = 56 * 1024 * 1024


def stage_table(frame):
    high = BAND // RADIX
    lane = np.arange(LANES)
    table = np.zeros((CLASSES, 2, high, 2, 2, LANES))
    for q in range(CLASSES):
        for half in range(2):
            low = q if half == 0 else (RADIX - q if q else RADIX // 2)
            k = low + RADIX * (LOW // RADIX + np.arange(high))
            angle = 2.0 * np.pi * (np.outer(k, lane) % frame) / frame
            cos, sin = np.cos(angle), np.sin(angle)
            if q == 0:
                table[q, half, :, 0, half] = cos
                table[q, half, :, 1, half] = -sin
            elif half == 0:
                table[q, half, :, 0, 0] = cos
                table[q, half, :, 0, 1] = sin
                table[q, half, :, 1, 0] = -sin
                table[q, half, :, 1, 1] = cos
            else:
                table[q, half, :, 0, 0] = cos
                table[q, half, :, 0, 1] = -sin
                table[q, half, :, 1, 0] = -sin
                table[q, half, :, 1, 1] = -cos
    table = table / math.sqrt(frame)
    return table.reshape(CLASSES, 2 * high * 2, 2 * LANES)


def lane_order(n_inp, times):
    size = n_inp * 2 * times * HALF
    source = np.arange(size).reshape(n_inp * 2, times, HALF).transpose(1, 0, 2).reshape(-1)
    matrix = np.zeros((size, size))
    matrix[source, np.arange(size)] = 1.0
    return matrix


def real_dft8(x):
    s = [x[j] + x[j + 4] for j in range(4)]
    d = [x[j] - x[j + 4] for j in range(4)]
    e0, e1 = s[0] + s[2], s[0] - s[2]
    o0, o1 = s[1] + s[3], s[3] - s[1]
    u, v = (d[1] - d[3]) * ROOT, (d[1] + d[3]) * ROOT
    return [
        (e0 + o0, None),
        (d[0] + u, -(d[2] + v)),
        (e1, o1),
        (d[0] - u, d[2] - v),
        (e0 - o0, None),
    ]


def complex_dft8(x):
    def add(a, b):
        return (a[0] + b[0], a[1] + b[1])

    def sub(a, b):
        return (a[0] - b[0], a[1] - b[1])

    def add_i(a, b):
        return (a[0] - b[1], a[1] + b[0])

    def sub_i(a, b):
        return (a[0] + b[1], a[1] - b[0])

    s = [add(x[j], x[j + 4]) for j in range(4)]
    d = [sub(x[j], x[j + 4]) for j in range(4)]
    e0, e1 = add(s[0], s[2]), sub(s[0], s[2])
    o0, o1 = add(s[1], s[3]), sub(s[1], s[3])
    p, m = sub(d[1], d[3]), add(d[1], d[3])
    b = ((p[0] + m[1]) * ROOT, (p[1] - m[0]) * ROOT)
    c = ((m[1] - p[0]) * ROOT, (-p[1] - m[0]) * ROOT)
    f, g = sub_i(d[0], d[2]), add_i(d[0], d[2])
    return [
        add(e0, o0),
        add(f, b),
        sub_i(e1, o1),
        add(g, c),
        sub(e0, o0),
        sub(f, b),
        add_i(e1, o1),
        sub(g, c),
    ]


def turned(value, step):
    angle = 2.0 * math.pi * (step % RADIX) / RADIX
    cos, sin = math.cos(angle), math.sin(angle)
    real, imag = value
    if imag is None:
        return (real * cos, real * -sin)
    if step % RADIX == 0:
        return value
    return (real * cos + imag * sin, imag * cos - real * sin)


def unrolled(count, copies, body):
    def step(i, carry):
        for copy in range(copies):
            body(i * copies + copy, copy)
        return carry

    lax.fori_loop(0, count // copies, step, 0)


def transform_rows(fir, mid, zed, count):
    def one(s, carry):
        for low in range(8):
            parts = real_dft8([fir[8 * high + low, s] for high in range(8)])
            mid[0, low] = parts[0][0]
            mid[7, low] = parts[4][0]
            for k in (1, 2, 3):
                value = turned(parts[k], low * k)
                mid[2 * k - 1, low] = value[0]
                mid[2 * k, low] = value[1]
        rows = pl.ds(pl.multiple_of(s * HALF, HALF), HALF)

        def put(q, half, value):
            zed[q, rows, half * LANES : (half + 1) * LANES] = value.astype(BF16)

        parts = real_dft8([mid[0, low] for low in range(8)])
        put(0, 0, parts[0][0])
        put(0, 1, parts[4][0])
        for m in (1, 2, 3):
            put(8 * m, 0, parts[m][0])
            put(8 * m, 1, parts[m][1])
        for k in (1, 2, 3):
            parts = complex_dft8([(mid[2 * k - 1, low], mid[2 * k, low]) for low in range(8)])
            for m in range(8):
                index = k + 8 * m
                if index < CLASSES:
                    put(index, 0, parts[m][0])
                    put(index, 1, parts[m][1])
                else:
                    put(RADIX - index, 0, parts[m][0])
                    put(RADIX - index, 1, -parts[m][1])
        parts = complex_dft8([turned((mid[7, low], None), 4 * low) for low in range(8)])
        for m in range(4):
            put(4 + 8 * m, 0, parts[m][0])
            put(4 + 8 * m, 1, parts[m][1])
        return carry

    lax.fori_loop(0, count, one, 0)


def filter_rows(volt, taper, fir, turn, first, count, hist=None, keep=None):
    taps = taper.shape[0]
    s_dev = volt.shape[1]
    wanted = [f for f in range(first - taps + 1, first + count) if f < s_dev]

    def one(a, slot):
        lanes = pl.ds(pl.multiple_of(a * LANES, LANES), LANES)
        turn[slot] = volt[:, :, lanes].astype(F32).reshape(HALF * s_dev, LANES)
        frames = {}
        for f in wanted:
            if f >= 0:
                frames[f] = turn[slot, pl.ds(f, HALF, stride=s_dev), :]
            elif hist is not None:
                frames[f] = hist[taps - 1 + f, :, lanes].astype(F32) * keep
        weights = [taper[t : t + 1, lanes] for t in range(taps)]
        for j in range(count):
            total = None
            for t in range(taps):
                f = first + j + t - taps + 1
                if f in frames:
                    term = weights[t] * frames[f]
                    total = term if total is None else total + term
            fir[a, j] = total

    unrolled(RADIX, turn.shape[0], one)


def tail_kernel(volt, taper, table, out, turn, fir, mid, zed):
    s_dev = volt.shape[1]
    count = taper.shape[0] - 1
    filter_rows(volt, taper, fir, turn, s_dev, count)
    transform_rows(fir, mid, zed, count)

    def one(q, copy):
        out[q, 0] = lax.dot_general(
            zed[q], table[q], (((1,), (1,)), ((), ())), preferred_element_type=F32
        ).astype(BF16)

    unrolled(CLASSES, 8, one)


def spectra_kernel(first, boundary, *refs):
    if boundary:
        keep, volt, hist, carried, unit, taper, table, out, turn, fir, mid, zed, wide = refs
        filter_rows(volt, taper, fir, turn, first, fir.shape[1], hist, keep[0])
    else:
        volt, taper, table, out, turn, fir, mid, zed, wide = refs
        filter_rows(volt, taper, fir, turn, first, fir.shape[1])
    transform_rows(fir, mid, zed, fir.shape[1])
    contract = (((1,), (1,)), ((), ()))
    step = RADIX

    def one(q, copy):
        value = lax.dot_general(table[q], zed[q], contract, preferred_element_type=F32)
        if boundary:
            value = value + lax.dot_general(
                unit[...], carried[q, 0], contract, preferred_element_type=F32
            )
        wide[pl.ds(pl.multiple_of(q * step, step), step), :] = value[:step]
        other = jnp.where(q == 0, CLASSES, RADIX - q)
        wide[pl.ds(pl.multiple_of(other * step, step), step), :] = value[step:]

    unrolled(CLASSES, 8, one)
    channels = out.shape[2] // 2
    split = RADIX // channels
    high = out.shape[0] // split

    def two(g, copy):
        for part in range(2):
            rows = wide[pl.ds(g * 2 + part, RADIX, stride=step), :].astype(BF16)
            for u in range(split):
                out[g * split + u, 0, part * channels : (part + 1) * channels, :] = rows[
                    u * channels : (u + 1) * channels
                ]

    unrolled(high, 4, two)


def order_kernel(got, order, out, turn):
    n_inp, pair, _, rows, _ = got.shape
    tiles = out.shape[2] // LANES
    times = order.shape[1] // out.shape[2]
    width = tiles * LANES
    wide = jnp.concatenate(
        [
            jnp.concatenate([got[a, c, h] for a in range(n_inp) for h in range(2)], axis=1)
            for c in range(pair)
        ],
        axis=0,
    )
    for s in range(times):
        value = jnp.dot(
            wide, order[:, s * width : (s + 1) * width], preferred_element_type=F32
        )
        for c in range(pair):
            for tile in range(tiles):
                turn[tile, pl.ds((c * times + s) * rows, rows), :] = value[
                    c * rows : (c + 1) * rows, tile * LANES : (tile + 1) * LANES
                ]

    def one(r, copy):
        for tile in range(tiles):
            out[r, :, tile * LANES : (tile + 1) * LANES] = turn[
                tile, pl.ds(r, pair * times, stride=rows), :
            ].astype(BF16)

    unrolled(rows, 8, one)


def gram_kernel(scale, one_ref, two_ref, out):
    width = out.shape[-1]
    for k in range(out.shape[1]):
        real = jnp.concatenate([one_ref[0, k], two_ref[0, k]], axis=0)
        imag = jnp.concatenate([one_ref[1, k], two_ref[1, k]], axis=0)
        left = jnp.concatenate([real, imag], axis=0)
        right = jnp.concatenate([-imag, real], axis=0)
        value = lax.dot_general(
            left,
            jnp.concatenate([left, right], axis=1),
            (((0,), (0,)), ((), ())),
            preferred_element_type=F32,
        )
        value = value * scale
        out[0, k] = value[:, :width].astype(BF16)
        out[1, k] = value[:, width:].astype(BF16)


def params():
    return pltpu.CompilerParams(vmem_limit_bytes=VMEM)


def cost(flops, moved):
    return pl.CostEstimate(flops=int(flops), bytes_accessed=int(moved), transcendentals=0)


def on_device(voltages, history, taper):
    in_dev, s_dev, frame = voltages.shape
    taps = taper.shape[0]
    n_inp = lax.axis_size("inp")
    n_chan = lax.axis_size("chan")
    groups = n_inp * n_chan
    channels = BAND // groups
    total = n_inp * in_dev
    halves = in_dev // HALF
    times = s_dev // 2
    early = taps - 1
    rows = times * HALF
    assert frame == RADIX * LANES and halves == 2 and rows == LANES
    assert early == times - 1 and RADIX % channels == 0 and total % LANES == 0

    outputs = 2 * BAND // CLASSES
    table = jnp.asarray(stage_table(frame).astype(np.float32).astype(ml_dtypes.bfloat16))
    unit = jnp.asarray(np.eye(outputs).astype(ml_dtypes.bfloat16))
    order = jnp.asarray(lane_order(n_inp, times).astype(ml_dtypes.bfloat16))
    assert table.shape == (CLASSES, outputs, 2 * LANES) and outputs == LANES

    volt_spec = pl.BlockSpec((HALF, s_dev, frame), lambda h: (h, 0, 0))
    taper_spec = pl.BlockSpec((taps, frame), lambda h: (0, 0))
    table_spec = pl.BlockSpec(table.shape, lambda h: (0, 0, 0))

    def scratch(count):
        return [
            pltpu.VMEM((4, HALF * s_dev, LANES), F32),
            pltpu.VMEM((RADIX, count, HALF, LANES), F32),
            pltpu.VMEM((8, 8, HALF, LANES), F32),
            pltpu.VMEM((CLASSES, count * HALF, 2 * LANES), BF16),
        ]

    wide = [pltpu.VMEM((RADIX * RADIX, LANES), F32)]
    carried = pl.pallas_call(
        tail_kernel,
        grid=(halves,),
        in_specs=[volt_spec, taper_spec, table_spec],
        out_specs=pl.BlockSpec((CLASSES, 1, early * HALF, outputs), lambda h: (0, h, 0, 0)),
        out_shape=jax.ShapeDtypeStruct((CLASSES, halves, early * HALF, outputs), BF16),
        scratch_shapes=scratch(early),
        compiler_params=params(),
        cost_estimate=cost(4e9, 2e7),
        name="carried",
    )(voltages, taper, table)
    carried, later_taper = lax.optimization_barrier((carried, taper))
    carried = lax.ppermute(carried, "chan", [(i, i + 1) for i in range(n_chan - 1)])

    send_spec = pl.BlockSpec((groups, 1, 2 * channels, LANES), lambda h: (0, h, 0, 0))
    send_shape = jax.ShapeDtypeStruct((groups, halves, 2 * channels, LANES), BF16)
    late_send = pl.pallas_call(
        lambda *refs: spectra_kernel(times, False, *refs),
        grid=(halves,),
        in_specs=[volt_spec, taper_spec, table_spec],
        out_specs=send_spec,
        out_shape=send_shape,
        scratch_shapes=scratch(times) + wide,
        compiler_params=params(),
        cost_estimate=cost(8e9, 4e7),
        name="late",
    )(voltages, later_taper, table)

    def exchange(value):
        value = lax.all_to_all(value, ("inp", "chan"), split_axis=0, concat_axis=0, tiled=True)
        return value.reshape(n_inp, n_chan, halves, 2 * channels, LANES)

    late_got = exchange(late_send)

    keep = (lax.axis_index("chan") == 0).astype(F32).reshape(1)
    carried = jnp.pad(carried, ((0, 0), (0, 0), (0, HALF), (0, 0)))
    early_send = pl.pallas_call(
        lambda *refs: spectra_kernel(0, True, *refs),
        grid=(halves,),
        in_specs=[
            pl.BlockSpec(memory_space=pltpu.SMEM),
            volt_spec,
            pl.BlockSpec((early, HALF, frame), lambda h: (0, h, 0)),
            pl.BlockSpec((CLASSES, 1, rows, outputs), lambda h: (0, h, 0, 0)),
            pl.BlockSpec(unit.shape, lambda h: (0, 0)),
            taper_spec,
            table_spec,
        ],
        out_specs=send_spec,
        out_shape=send_shape,
        scratch_shapes=scratch(times) + wide,
        compiler_params=params(),
        cost_estimate=cost(8e9, 4e7),
        name="early",
    )(keep, voltages, jnp.transpose(history, (1, 0, 2)), carried, unit, taper, table)
    early_got = exchange(early_send)

    def ordered(got, name):
        pair = 16 // times
        steps = n_chan // pair
        return pl.pallas_call(
            order_kernel,
            grid=(steps,),
            in_specs=[
                pl.BlockSpec(
                    (n_inp, pair, halves, 2 * channels, LANES), lambda c: (0, c, 0, 0, 0)
                ),
                pl.BlockSpec(order.shape, lambda c: (0, 0)),
            ],
            out_specs=pl.BlockSpec((2 * channels, pair * times, total), lambda c: (0, c, 0)),
            out_shape=jax.ShapeDtypeStruct((2 * channels, n_chan * times, total), BF16),
            scratch_shapes=[
                pltpu.VMEM((total // LANES, pair * times * 2 * channels, LANES), F32)
            ],
            compiler_params=params(),
            cost_estimate=cost(2e9, 1e7),
            name=name,
        )(got, order).reshape(2, channels, n_chan * times, total)

    late_rows = ordered(late_got, "late_order")
    early_rows = ordered(early_got, "early_order")
    block = 8
    side_spec = pl.BlockSpec((2, block, n_chan * times, total), lambda k: (0, k, 0, 0))
    return pl.pallas_call(
        lambda *refs: gram_kernel(1.0 / (n_chan * s_dev), *refs),
        grid=(channels // block,),
        in_specs=[side_spec, side_spec],
        out_specs=pl.BlockSpec((2, block, total, total), lambda k: (0, k, 0, 0)),
        out_shape=jax.ShapeDtypeStruct((2, channels, total, total), BF16),
        compiler_params=params(),
        cost_estimate=cost(4e9, 1e7),
        name="gram",
    )(late_rows, early_rows)


def solution(mesh):
    in_specs = (P("inp", "chan", None), P("inp", None, None), P())
    out_specs = P(None, ("inp", "chan"), None, None)
    return jax.shard_map(
        on_device, mesh=mesh, in_specs=in_specs, out_specs=out_specs, check_vma=False
    )
```

```python
import math

import jax
import jax.numpy as jnp
import ml_dtypes
import numpy as np
from jax import lax
from jax.experimental import pallas as pl
from jax.experimental.pallas import tpu as pltpu
from jax.sharding import PartitionSpec as P

BAND = 2048
LOW = 1024
LANES = 128
RADIX = 64
HALF = 16
CLASSES = RADIX // 2
ROOT = math.sqrt(0.5)
F32 = jnp.float32
BF16 = jnp.bfloat16
VMEM = 56 * 1024 * 1024


def stage_table(frame):
    high = BAND // RADIX
    lane = np.arange(LANES)
    table = np.zeros((CLASSES, 2, high, 2, 2, LANES))
    for q in range(CLASSES):
        for half in range(2):
            low = q if half == 0 else (RADIX - q if q else RADIX // 2)
            k = low + RADIX * (LOW // RADIX + np.arange(high))
            angle = 2.0 * np.pi * (np.outer(k, lane) % frame) / frame
            cos, sin = np.cos(angle), np.sin(angle)
            if q == 0:
                table[q, half, :, 0, half] = cos
                table[q, half, :, 1, half] = -sin
            elif half == 0:
                table[q, half, :, 0, 0] = cos
                table[q, half, :, 0, 1] = sin
                table[q, half, :, 1, 0] = -sin
                table[q, half, :, 1, 1] = cos
            else:
                table[q, half, :, 0, 0] = cos
                table[q, half, :, 0, 1] = -sin
                table[q, half, :, 1, 0] = -sin
                table[q, half, :, 1, 1] = -cos
    table = table / math.sqrt(frame)
    return table.reshape(CLASSES, 2 * high * 2, 2 * LANES)


def real_dft8(x):
    s = [x[j] + x[j + 4] for j in range(4)]
    d = [x[j] - x[j + 4] for j in range(4)]
    e0, e1 = s[0] + s[2], s[0] - s[2]
    o0, o1 = s[1] + s[3], s[3] - s[1]
    u, v = (d[1] - d[3]) * ROOT, (d[1] + d[3]) * ROOT
    return [
        (e0 + o0, None),
        (d[0] + u, -(d[2] + v)),
        (e1, o1),
        (d[0] - u, d[2] - v),
        (e0 - o0, None),
    ]


def complex_dft8(x):
    def add(a, b):
        return (a[0] + b[0], a[1] + b[1])

    def sub(a, b):
        return (a[0] - b[0], a[1] - b[1])

    def add_i(a, b):
        return (a[0] - b[1], a[1] + b[0])

    def sub_i(a, b):
        return (a[0] + b[1], a[1] - b[0])

    s = [add(x[j], x[j + 4]) for j in range(4)]
    d = [sub(x[j], x[j + 4]) for j in range(4)]
    e0, e1 = add(s[0], s[2]), sub(s[0], s[2])
    o0, o1 = add(s[1], s[3]), sub(s[1], s[3])
    p, m = sub(d[1], d[3]), add(d[1], d[3])
    b = ((p[0] + m[1]) * ROOT, (p[1] - m[0]) * ROOT)
    c = ((m[1] - p[0]) * ROOT, (-p[1] - m[0]) * ROOT)
    f, g = sub_i(d[0], d[2]), add_i(d[0], d[2])
    return [
        add(e0, o0),
        add(f, b),
        sub_i(e1, o1),
        add(g, c),
        sub(e0, o0),
        sub(f, b),
        add_i(e1, o1),
        sub(g, c),
    ]


def turned(value, step):
    angle = 2.0 * math.pi * (step % RADIX) / RADIX
    cos, sin = math.cos(angle), math.sin(angle)
    real, imag = value
    if imag is None:
        return (real * cos, real * -sin)
    if step % RADIX == 0:
        return value
    return (real * cos + imag * sin, imag * cos - real * sin)


def unrolled(count, copies, body):
    def step(i, carry):
        for copy in range(copies):
            body(i * copies + copy, copy)
        return carry

    lax.fori_loop(0, count // copies, step, 0)


def transform_rows(fir, mid, zed, count):
    def one(s, carry):
        for low in range(8):
            parts = real_dft8([fir[8 * high + low, s] for high in range(8)])
            mid[0, low] = parts[0][0]
            mid[7, low] = parts[4][0]
            for k in (1, 2, 3):
                value = turned(parts[k], low * k)
                mid[2 * k - 1, low] = value[0]
                mid[2 * k, low] = value[1]
        rows = pl.ds(pl.multiple_of(s * HALF, HALF), HALF)

        def put(q, half, value):
            zed[q, rows, half * LANES : (half + 1) * LANES] = value.astype(BF16)

        parts = real_dft8([mid[0, low] for low in range(8)])
        put(0, 0, parts[0][0])
        put(0, 1, parts[4][0])
        for m in (1, 2, 3):
            put(8 * m, 0, parts[m][0])
            put(8 * m, 1, parts[m][1])
        for k in (1, 2, 3):
            parts = complex_dft8([(mid[2 * k - 1, low], mid[2 * k, low]) for low in range(8)])
            for m in range(8):
                index = k + 8 * m
                if index < CLASSES:
                    put(index, 0, parts[m][0])
                    put(index, 1, parts[m][1])
                else:
                    put(RADIX - index, 0, parts[m][0])
                    put(RADIX - index, 1, -parts[m][1])
        parts = complex_dft8([turned((mid[7, low], None), 4 * low) for low in range(8)])
        for m in range(4):
            put(4 + 8 * m, 0, parts[m][0])
            put(4 + 8 * m, 1, parts[m][1])
        return carry

    lax.fori_loop(0, count, one, 0)


def filter_rows(volt, taper, fir, turn, first, hist=None, keep=None):
    count = fir.shape[1]
    tiles = volt.shape[2] // LANES
    base = pl.program_id(1) * tiles
    taps = taper.shape[0]
    s_dev = volt.shape[1]
    wanted = [f for f in range(first - taps + 1, first + count) if f < s_dev]

    def one(a, slot):
        lanes = pl.ds(pl.multiple_of(a * LANES, LANES), LANES)
        turn[slot] = volt[:, :, lanes].astype(F32).reshape(HALF * s_dev, LANES)
        frames = {}
        for f in wanted:
            if f >= 0:
                frames[f] = turn[slot, pl.ds(f, HALF, stride=s_dev), :]
            elif hist is not None:
                frames[f] = hist[taps - 1 + f, :, lanes].astype(F32) * keep
        weights = [taper[t : t + 1, lanes] for t in range(taps)]
        for j in range(count):
            total = None
            for t in range(taps):
                f = first + j + t - taps + 1
                if f in frames:
                    term = weights[t] * frames[f]
                    total = term if total is None else total + term
            fir[base + a, j] = total

    unrolled(tiles, turn.shape[0], one)


def with_table(table, held, sem):
    copy = pltpu.make_async_copy(table, held, sem)

    @pl.when((pl.program_id(0) == 0) & (pl.program_id(1) == 0))
    def _():
        copy.start()

    @pl.when((pl.program_id(0) == 0) & (pl.program_id(1) == pl.num_programs(1) - 1))
    def _():
        copy.wait()


CONTRACT = (((1,), (1,)), ((), ()))


def carried_kernel(volt, taper, table, out, turn, fir, mid, zed, held, sem):
    with_table(table, held, sem)
    filter_rows(volt, taper, fir, turn, volt.shape[1])

    @pl.when(pl.program_id(1) == pl.num_programs(1) - 1)
    def _():
        transform_rows(fir, mid, zed, fir.shape[1])

        def one(q, copy):
            out[q, 0] = lax.dot_general(
                zed[q], held[q], CONTRACT, preferred_element_type=F32
            ).astype(BF16)

        unrolled(CLASSES, 8, one)


def spectra_kernel(first, boundary, *refs):
    if boundary:
        keep, volt, hist, carried, unit, taper, table, out, *scratch = refs
    else:
        volt, taper, table, out, *scratch = refs
    turn, fir, mid, zed, held, sem, wide = scratch
    with_table(table, held, sem)
    if boundary:
        filter_rows(volt, taper, fir, turn, first, hist, keep[0])
    else:
        filter_rows(volt, taper, fir, turn, first)

    @pl.when(pl.program_id(1) == pl.num_programs(1) - 1)
    def _():
        transform_rows(fir, mid, zed, fir.shape[1])
        step = RADIX

        def one(q, copy):
            value = lax.dot_general(held[q], zed[q], CONTRACT, preferred_element_type=F32)
            if boundary:
                part = carried[q, 0]
                short = zed.shape[1] - part.shape[0]
                part = jnp.concatenate([part, jnp.zeros((short, LANES), BF16)], axis=0)
                value = value + lax.dot_general(
                    unit[...], part, CONTRACT, preferred_element_type=F32
                )
            wide[pl.ds(pl.multiple_of(q * step, step), step), :] = value[:step]
            other = jnp.where(q == 0, CLASSES, RADIX - q)
            wide[pl.ds(pl.multiple_of(other * step, step), step), :] = value[step:]

        unrolled(CLASSES, 8, one)
        channels = out.shape[2] // 2
        split = RADIX // channels
        high = out.shape[0] // split

        def two(g, copy):
            for part in range(2):
                rows = wide[pl.ds(g * 2 + part, RADIX, stride=step), :].astype(BF16)
                for u in range(split):
                    out[g * split + u, 0, part * channels : (part + 1) * channels, :] = rows[
                        u * channels : (u + 1) * channels
                    ]

        unrolled(high, 4, two)


def reorder(got, turn, put):
    n_inp, pair, halves, rows, _ = got.shape
    blocks = LANES // HALF
    block = lax.broadcasted_iota(jnp.int32, (HALF, LANES), 1) // HALF
    masks = {d: (block & d) == 0 for d in (1, 2, 4)}

    def one(b, copy):
        here = pl.ds(pl.multiple_of(b * HALF, HALF), HALF)
        for c in range(pair):
            for tile in range(n_inp * halves // blocks):
                x = []
                for p in range(blocks):
                    a, h = divmod(tile * blocks + p, halves)
                    x.append(got[a, c, h, here, :].astype(F32))
                for d in (1, 2, 4):
                    for p in range(blocks):
                        if p & d == 0:
                            low, up = x[p], x[p | d]
                            x[p] = jnp.where(masks[d], low, pltpu.roll(up, HALF * d, 1))
                            x[p | d] = jnp.where(masks[d], pltpu.roll(low, LANES - HALF * d, 1), up)
                for s in range(blocks):
                    start = (c * blocks + s) * rows
                    turn[tile, pl.ds(pl.multiple_of(start + b * HALF, HALF), HALF), :] = x[s]

    unrolled(rows // HALF, 2, one)

    def two(r, copy):
        for tile in range(turn.shape[0]):
            put(r, tile, turn[tile, pl.ds(r, pair * blocks, stride=rows), :].astype(BF16))

    unrolled(rows, 8, two)


def order_kernel(got, out, turn):
    def put(r, tile, value):
        out[r, :, tile * LANES : (tile + 1) * LANES] = value

    reorder(got, turn, put)


def finish_kernel(scale, steps, got, late, out, turn, early):
    j = pl.program_id(0)
    pair = got.shape[1] * (LANES // HALF)
    block = out.shape[1]
    width = out.shape[-1]
    channels = early.shape[0] // 2

    @pl.when(j < steps)
    def _():
        times = pl.ds(pl.multiple_of(j * pair, pair), pair)

        def put(r, tile, value):
            early[r, times, tile * LANES : (tile + 1) * LANES] = value

        reorder(got, turn, put)

    @pl.when(j >= steps)
    def _():
        first = (j - steps) * block
        for k in range(block):
            real = jnp.concatenate([late[0, k], early[first + k]], axis=0)
            imag = jnp.concatenate([late[1, k], early[channels + first + k]], axis=0)
            left = jnp.concatenate([real, imag], axis=0)
            right = jnp.concatenate([-imag, real], axis=0)
            value = lax.dot_general(
                left,
                jnp.concatenate([left, right], axis=1),
                (((0,), (0,)), ((), ())),
                preferred_element_type=F32,
            )
            value = value * scale
            out[0, k] = value[:, :width].astype(BF16)
            out[1, k] = value[:, width:].astype(BF16)


def params():
    return pltpu.CompilerParams(vmem_limit_bytes=VMEM)


def cost(flops, moved):
    return pl.CostEstimate(flops=int(flops), bytes_accessed=int(moved), transcendentals=0)


def on_device(voltages, history, taper):
    in_dev, s_dev, frame = voltages.shape
    taps = taper.shape[0]
    n_inp = lax.axis_size("inp")
    n_chan = lax.axis_size("chan")
    groups = n_inp * n_chan
    channels = BAND // groups
    total = n_inp * in_dev
    halves = in_dev // HALF
    times = s_dev // 2
    early = taps - 1
    rows = times * HALF
    assert frame == RADIX * LANES and halves == 2 and rows == LANES
    assert early == times - 1 and RADIX % channels == 0 and total % LANES == 0

    outputs = 2 * BAND // CLASSES
    table = jnp.asarray(stage_table(frame).astype(np.float32).astype(ml_dtypes.bfloat16))
    unit = jnp.asarray(np.eye(outputs).astype(ml_dtypes.bfloat16))
    assert table.shape == (CLASSES, outputs, 2 * LANES) and outputs == LANES

    chunks = 4
    part = frame // chunks
    volt_spec = pl.BlockSpec((HALF, s_dev, part), lambda h, j: (h, 0, j))
    taper_spec = pl.BlockSpec((taps, part), lambda h, j: (0, j))
    table_spec = pl.BlockSpec(memory_space=pl.ANY)
    grid = (halves, chunks)

    def scratch(count):
        return [
            pltpu.VMEM((4, HALF * s_dev, LANES), F32),
            pltpu.VMEM((RADIX, count, HALF, LANES), F32),
            pltpu.VMEM((8, 8, HALF, LANES), F32),
            pltpu.VMEM((CLASSES, count * HALF, 2 * LANES), BF16),
            pltpu.VMEM(table.shape, BF16),
            pltpu.SemaphoreType.DMA,
        ]

    wide = [pltpu.VMEM((RADIX * RADIX, LANES), F32)]
    carried_spec = pl.BlockSpec((CLASSES, 1, early * HALF, outputs), lambda h, j: (0, h, 0, 0))
    carried = pl.pallas_call(
        carried_kernel,
        grid=grid,
        in_specs=[volt_spec, taper_spec, table_spec],
        out_specs=carried_spec,
        out_shape=jax.ShapeDtypeStruct((CLASSES, halves, early * HALF, outputs), BF16),
        scratch_shapes=scratch(early),
        compiler_params=params(),
        cost_estimate=cost(1e10, 2e7),
        name="carried",
    )(voltages, taper, table)
    carried, later_taper = lax.optimization_barrier((carried, taper))
    carried = lax.ppermute(carried, "chan", [(i, i + 1) for i in range(n_chan - 1)])

    send_spec = pl.BlockSpec((groups, 1, 2 * channels, LANES), lambda h, j: (0, h, 0, 0))
    send_shape = jax.ShapeDtypeStruct((groups, halves, 2 * channels, LANES), BF16)
    late_send = pl.pallas_call(
        lambda *refs: spectra_kernel(times, False, *refs),
        grid=grid,
        in_specs=[volt_spec, taper_spec, table_spec],
        out_specs=send_spec,
        out_shape=send_shape,
        scratch_shapes=scratch(times) + wide,
        compiler_params=params(),
        cost_estimate=cost(5e10, 4e7),
        name="late",
    )(voltages, later_taper, table)

    def exchange(value):
        value = lax.all_to_all(value, ("inp", "chan"), split_axis=0, concat_axis=0, tiled=True)
        return value.reshape(n_inp, n_chan, halves, 2 * channels, LANES)

    late_got = exchange(late_send)

    keep = (lax.axis_index("chan") == 0).astype(F32).reshape(1)
    early_send = pl.pallas_call(
        lambda *refs: spectra_kernel(0, True, *refs),
        grid=grid,
        in_specs=[
            pl.BlockSpec(memory_space=pltpu.SMEM),
            volt_spec,
            pl.BlockSpec((early, HALF, part), lambda h, j: (0, h, j)),
            carried_spec,
            pl.BlockSpec(unit.shape, lambda h, j: (0, 0)),
            taper_spec,
            table_spec,
        ],
        out_specs=send_spec,
        out_shape=send_shape,
        scratch_shapes=scratch(times) + wide,
        compiler_params=params(),
        cost_estimate=cost(2e11, 4e7),
        name="early",
    )(keep, voltages, jnp.transpose(history, (1, 0, 2)), carried, unit, taper, table)
    early_got = exchange(early_send)

    pair = 16 // times
    steps = n_chan // pair
    span = n_chan * times
    got_block = (n_inp, pair, halves, 2 * channels, LANES)
    turn = pltpu.VMEM((total // LANES, pair * times * 2 * channels, LANES), F32)
    late_rows = pl.pallas_call(
        order_kernel,
        grid=(steps,),
        in_specs=[pl.BlockSpec(got_block, lambda c: (0, c, 0, 0, 0))],
        out_specs=pl.BlockSpec((2 * channels, pair * times, total), lambda c: (0, c, 0)),
        out_shape=jax.ShapeDtypeStruct((2 * channels, span, total), BF16),
        scratch_shapes=[turn],
        compiler_params=params(),
        cost_estimate=cost(1e10, 1e7),
        name="order",
    )(late_got).reshape(2, channels, span, total)

    block = 8
    return pl.pallas_call(
        lambda *refs: finish_kernel(1.0 / (n_chan * s_dev), steps, *refs),
        grid=(steps + channels // block,),
        in_specs=[
            pl.BlockSpec(got_block, lambda j: (0, jnp.minimum(j, steps - 1), 0, 0, 0)),
            pl.BlockSpec(
                (2, block, span, total), lambda j: (0, jnp.maximum(j - steps, 0), 0, 0)
            ),
        ],
        out_specs=pl.BlockSpec(
            (2, block, total, total), lambda j: (0, jnp.maximum(j - steps, 0), 0, 0)
        ),
        out_shape=jax.ShapeDtypeStruct((2, channels, total, total), BF16),
        scratch_shapes=[turn, pltpu.VMEM((2 * channels, span, total), BF16)],
        compiler_params=params(),
        cost_estimate=cost(1e10, 1e7),
        name="finish",
    )(early_got, late_rows)


def solution(mesh):
    in_specs = (P("inp", "chan", None), P("inp", None, None), P())
    out_specs = P(None, ("inp", "chan"), None, None)
    return jax.shard_map(
        on_device, mesh=mesh, in_specs=in_specs, out_specs=out_specs, check_vma=False
    )
```

```python
import math

import jax
import jax.numpy as jnp
import ml_dtypes
import numpy as np
from jax import lax
from jax.experimental import pallas as pl
from jax.experimental.pallas import tpu as pltpu
from jax.sharding import PartitionSpec as P

BAND = 2048
LOW = 1024
LANES = 128
RADIX = 64
HALF = 16
CLASSES = RADIX // 2
ROOT = math.sqrt(0.5)
F32 = jnp.float32
BF16 = jnp.bfloat16
VMEM = 60 * 1024 * 1024


def stage_table(frame):
    high = BAND // RADIX
    lane = np.arange(LANES)
    table = np.zeros((CLASSES, 2, high, 2, 2, LANES))
    for q in range(CLASSES):
        for half in range(2):
            low = q if half == 0 else (RADIX - q if q else RADIX // 2)
            k = low + RADIX * (LOW // RADIX + np.arange(high))
            angle = 2.0 * np.pi * (np.outer(k, lane) % frame) / frame
            cos, sin = np.cos(angle), np.sin(angle)
            if q == 0:
                table[q, half, :, 0, half] = cos
                table[q, half, :, 1, half] = -sin
            elif half == 0:
                table[q, half, :, 0, 0] = cos
                table[q, half, :, 0, 1] = sin
                table[q, half, :, 1, 0] = -sin
                table[q, half, :, 1, 1] = cos
            else:
                table[q, half, :, 0, 0] = cos
                table[q, half, :, 0, 1] = -sin
                table[q, half, :, 1, 0] = -sin
                table[q, half, :, 1, 1] = -cos
    table = table / math.sqrt(frame)
    return table.reshape(CLASSES, 2 * high * 2, 2 * LANES)


def real_dft8(x):
    s = [x[j] + x[j + 4] for j in range(4)]
    d = [x[j] - x[j + 4] for j in range(4)]
    e0, e1 = s[0] + s[2], s[0] - s[2]
    o0, o1 = s[1] + s[3], s[3] - s[1]
    u, v = (d[1] - d[3]) * ROOT, (d[1] + d[3]) * ROOT
    return [
        (e0 + o0, None),
        (d[0] + u, -(d[2] + v)),
        (e1, o1),
        (d[0] - u, d[2] - v),
        (e0 - o0, None),
    ]


def complex_dft8(x):
    def add(a, b):
        return (a[0] + b[0], a[1] + b[1])

    def sub(a, b):
        return (a[0] - b[0], a[1] - b[1])

    def add_i(a, b):
        return (a[0] - b[1], a[1] + b[0])

    def sub_i(a, b):
        return (a[0] + b[1], a[1] - b[0])

    s = [add(x[j], x[j + 4]) for j in range(4)]
    d = [sub(x[j], x[j + 4]) for j in range(4)]
    e0, e1 = add(s[0], s[2]), sub(s[0], s[2])
    o0, o1 = add(s[1], s[3]), sub(s[1], s[3])
    p, m = sub(d[1], d[3]), add(d[1], d[3])
    b = ((p[0] + m[1]) * ROOT, (p[1] - m[0]) * ROOT)
    c = ((m[1] - p[0]) * ROOT, (-p[1] - m[0]) * ROOT)
    f, g = sub_i(d[0], d[2]), add_i(d[0], d[2])
    return [
        add(e0, o0),
        add(f, b),
        sub_i(e1, o1),
        add(g, c),
        sub(e0, o0),
        sub(f, b),
        add_i(e1, o1),
        sub(g, c),
    ]


def turned(value, step):
    angle = 2.0 * math.pi * (step % RADIX) / RADIX
    cos, sin = math.cos(angle), math.sin(angle)
    real, imag = value
    if imag is None:
        return (real * cos, real * -sin)
    if step % RADIX == 0:
        return value
    return (real * cos + imag * sin, imag * cos - real * sin)


def unrolled(count, copies, body):
    def step(i, carry):
        for copy in range(copies):
            body(i * copies + copy, copy)
        return carry

    lax.fori_loop(0, count // copies, step, 0)


def transform_rows(fir, mid, zed, count):
    def one(s, carry):
        for low in range(8):
            parts = real_dft8([fir[8 * high + low, s] for high in range(8)])
            mid[0, low] = parts[0][0]
            mid[7, low] = parts[4][0]
            for k in (1, 2, 3):
                value = turned(parts[k], low * k)
                mid[2 * k - 1, low] = value[0]
                mid[2 * k, low] = value[1]
        rows = pl.ds(pl.multiple_of(s * HALF, HALF), HALF)

        def put(q, half, value):
            zed[q, rows, half * LANES : (half + 1) * LANES] = value.astype(BF16)

        parts = real_dft8([mid[0, low] for low in range(8)])
        put(0, 0, parts[0][0])
        put(0, 1, parts[4][0])
        for m in (1, 2, 3):
            put(8 * m, 0, parts[m][0])
            put(8 * m, 1, parts[m][1])
        for k in (1, 2, 3):
            parts = complex_dft8([(mid[2 * k - 1, low], mid[2 * k, low]) for low in range(8)])
            for m in range(8):
                index = k + 8 * m
                if index < CLASSES:
                    put(index, 0, parts[m][0])
                    put(index, 1, parts[m][1])
                else:
                    put(RADIX - index, 0, parts[m][0])
                    put(RADIX - index, 1, -parts[m][1])
        parts = complex_dft8([turned((mid[7, low], None), 4 * low) for low in range(8)])
        for m in range(4):
            put(4 + 8 * m, 0, parts[m][0])
            put(4 + 8 * m, 1, parts[m][1])
        return carry

    lax.fori_loop(0, count, one, 0)


def swap_matrix():
    row = np.arange(HALF * HALF)
    return (row[None, :] == (row % HALF * HALF + row // HALF)[:, None]).astype(np.float32)


def filter_rows(volt, taper, swap, fir, first, hist=None, keep=None):
    taps = taper.shape[0]
    s_dev = volt.shape[1]
    count = fir.shape[1]
    tiles = volt.shape[2] // LANES
    base = pl.program_id(1) * tiles
    start = max(first - taps + 1, 0)
    stop = min(first + count, s_dev)

    def one(a, copy):
        lanes = pl.ds(pl.multiple_of(a * LANES, LANES), LANES)
        rows = volt[:, :, lanes].reshape(HALF * s_dev, LANES)
        turned_rows = jnp.dot(
            swap[start * HALF : stop * HALF, :], rows, preferred_element_type=F32
        )
        frames = {}
        for f in range(start, stop):
            frames[f] = turned_rows[(f - start) * HALF : (f - start + 1) * HALF]
        if hist is not None:
            for f in range(first - taps + 1, 0):
                frames[f] = hist[taps - 1 + f, :, lanes].astype(F32) * keep
        weights = [taper[t : t + 1, lanes] for t in range(taps)]
        for j in range(count):
            total = None
            for t in range(taps):
                f = first + j + t - taps + 1
                if f in frames:
                    term = weights[t] * frames[f]
                    total = term if total is None else total + term
            fir[base + a, j] = total

    unrolled(tiles, 4, one)


def with_table(table, held, sem):
    copy = pltpu.make_async_copy(table, held, sem)

    @pl.when((pl.program_id(0) == 0) & (pl.program_id(1) == 0))
    def _():
        copy.start()

    @pl.when((pl.program_id(0) == 0) & (pl.program_id(1) == pl.num_programs(1) - 1))
    def _():
        copy.wait()


CONTRACT = (((1,), (1,)), ((), ()))


def carried_kernel(volt, taper, swap, table, out, fir, mid, zed, held, sem):
    with_table(table, held, sem)
    filter_rows(volt, taper, swap, fir, volt.shape[1])

    @pl.when(pl.program_id(1) == pl.num_programs(1) - 1)
    def _():
        transform_rows(fir, mid, zed, fir.shape[1])

        def one(q, copy):
            out[q, 0] = lax.dot_general(
                zed[q], held[q], CONTRACT, preferred_element_type=F32
            ).astype(BF16)

        unrolled(CLASSES, 8, one)


def spectra_kernel(first, boundary, *refs):
    if boundary:
        keep, volt, hist, carried, unit, taper, swap, table, out, *scratch = refs
    else:
        volt, taper, swap, table, out, *scratch = refs
    fir, mid, zed, held, sem, wide = scratch
    with_table(table, held, sem)
    if boundary:
        filter_rows(volt, taper, swap, fir, first, hist, keep[0])
    else:
        filter_rows(volt, taper, swap, fir, first)

    @pl.when(pl.program_id(1) == pl.num_programs(1) - 1)
    def _():
        transform_rows(fir, mid, zed, fir.shape[1])
        step = RADIX

        def one(q, copy):
            value = lax.dot_general(held[q], zed[q], CONTRACT, preferred_element_type=F32)
            if boundary:
                part = carried[q, 0]
                short = zed.shape[1] - part.shape[0]
                part = jnp.concatenate([part, jnp.zeros((short, LANES), BF16)], axis=0)
                value = value + lax.dot_general(
                    unit[...], part, CONTRACT, preferred_element_type=F32
                )
            wide[q] = value[:step].astype(BF16)
            wide[jnp.where(q == 0, CLASSES, RADIX - q)] = value[step:].astype(BF16)

        unrolled(CLASSES, 8, one)
        channels = out.shape[2] // 2
        split = RADIX // channels
        high = HALF // 2

        def two(b, copy):
            here = pl.ds(pl.multiple_of(b * HALF, HALF), HALF)
            for first_k in range(0, RADIX, 2 * HALF):
                pieces = [
                    jnp.concatenate([wide[k + j, here, :] for j in range(HALF)], axis=0)
                    for k in (first_k, first_k + HALF)
                ]
                value = jnp.dot(
                    swap[...], jnp.concatenate(pieces, axis=1), preferred_element_type=F32
                )
                for side in range(2):
                    u, k = divmod(first_k + side * HALF, channels)
                    for j in range(HALF):
                        out[
                            (b * high + j // 2) * split + u,
                            0,
                            j % 2 * channels + k : j % 2 * channels + k + HALF,
                            :,
                        ] = value[
                            j * HALF : (j + 1) * HALF, side * LANES : (side + 1) * LANES
                        ].astype(BF16)

        unrolled(step // HALF, 2, two)


def reorder(got, swap, put):
    n_inp, pair, halves, rows, _ = got.shape
    blocks = LANES // HALF
    block = lax.broadcasted_iota(jnp.int32, (HALF, LANES), 1) // HALF
    masks = {d: (block & d) == 0 for d in (1, 2, 4)}

    def tiles_of(c, tile, here):
        x = []
        for p in range(blocks):
            a, h = divmod(tile * blocks + p, halves)
            x.append(got[a, c, h, here, :].astype(F32))
        for d in (1, 2, 4):
            for p in range(blocks):
                if p & d == 0:
                    low, up = x[p], x[p | d]
                    x[p] = jnp.where(masks[d], low, pltpu.roll(up, HALF * d, 1))
                    x[p | d] = jnp.where(masks[d], pltpu.roll(low, LANES - HALF * d, 1), up)
        return [value.astype(BF16) for value in x]

    def one(b, copy):
        for tile in range(n_inp * halves // blocks):
            sides = []
            for side in range(2):
                here = pl.ds(pl.multiple_of((2 * b + side) * HALF, HALF), HALF)
                pieces = [x for c in range(pair) for x in tiles_of(c, tile, here)]
                sides.append(jnp.concatenate(pieces, axis=0))
            value = jnp.dot(
                swap[...], jnp.concatenate(sides, axis=1), preferred_element_type=F32
            )
            for side in range(2):
                for j in range(HALF):
                    put(
                        (2 * b + side) * HALF + j,
                        tile,
                        value[
                            j * HALF : (j + 1) * HALF, side * LANES : (side + 1) * LANES
                        ].astype(BF16),
                    )

    unrolled(rows // HALF // 2, 1, one)


def gram_kernel(scale, steps, *refs):
    if scale is None:
        got, swap, out, held = refs
        block = out.shape[0]
    else:
        got, swap, prior, out, held = refs
        block = out.shape[1]
    j = pl.program_id(0)
    pair = got.shape[1] * (LANES // HALF)
    channels = held.shape[0] // 2
    width = held.shape[-1]

    @pl.when(j < steps)
    def _():
        times = pl.ds(pl.multiple_of(j * pair, pair), pair)

        def put(r, tile, value):
            held[r, times, tile * LANES : (tile + 1) * LANES] = value

        reorder(got, swap, put)

    @pl.when(j >= steps)
    def _():
        first = (j - steps) * block
        for k in range(block):
            real, imag = held[first + k], held[channels + first + k]
            left = jnp.concatenate([real, imag], axis=0)
            right = jnp.concatenate([-imag, real], axis=0)
            value = lax.dot_general(
                left,
                jnp.concatenate([left, right], axis=1),
                (((0,), (0,)), ((), ())),
                preferred_element_type=F32,
            )
            if scale is None:
                out[k] = value
            else:
                value = (value + prior[k]) * scale
                out[0, k] = value[:, :width].astype(BF16)
                out[1, k] = value[:, width:].astype(BF16)


def params():
    return pltpu.CompilerParams(vmem_limit_bytes=VMEM)


def cost(flops, moved):
    return pl.CostEstimate(flops=int(flops), bytes_accessed=int(moved), transcendentals=0)


def on_device(voltages, history, taper):
    in_dev, s_dev, frame = voltages.shape
    taps = taper.shape[0]
    n_inp = lax.axis_size("inp")
    n_chan = lax.axis_size("chan")
    groups = n_inp * n_chan
    channels = BAND // groups
    total = n_inp * in_dev
    halves = in_dev // HALF
    times = s_dev // 2
    early = taps - 1
    rows = times * HALF
    assert frame == RADIX * LANES and halves == 2 and rows == LANES
    assert early == times - 1 and RADIX % channels == 0 and total % LANES == 0

    outputs = 2 * BAND // CLASSES
    table = jnp.asarray(stage_table(frame).astype(np.float32).astype(ml_dtypes.bfloat16))
    unit = jnp.asarray(np.eye(outputs).astype(ml_dtypes.bfloat16))
    assert table.shape == (CLASSES, outputs, 2 * LANES) and outputs == LANES

    chunks = 4
    part = frame // chunks
    volt_spec = pl.BlockSpec((HALF, s_dev, part), lambda h, j: (h, 0, j))
    taper_spec = pl.BlockSpec((taps, part), lambda h, j: (0, j))
    table_spec = pl.BlockSpec(memory_space=pl.ANY)
    swap = jnp.asarray(swap_matrix().astype(ml_dtypes.bfloat16))
    swap_spec = pl.BlockSpec(swap.shape, lambda *_: (0, 0))
    grid = (halves, chunks)

    def scratch(count):
        return [
            pltpu.VMEM((RADIX, count, HALF, LANES), F32),
            pltpu.VMEM((8, 8, HALF, LANES), F32),
            pltpu.VMEM((CLASSES, count * HALF, 2 * LANES), BF16),
            pltpu.VMEM(table.shape, BF16),
            pltpu.SemaphoreType.DMA,
        ]

    wide = [pltpu.VMEM((RADIX, RADIX, LANES), BF16)]
    carried_spec = pl.BlockSpec((CLASSES, 1, early * HALF, outputs), lambda h, j: (0, h, 0, 0))
    carried = pl.pallas_call(
        carried_kernel,
        grid=grid,
        in_specs=[volt_spec, taper_spec, swap_spec, table_spec],
        out_specs=carried_spec,
        out_shape=jax.ShapeDtypeStruct((CLASSES, halves, early * HALF, outputs), BF16),
        scratch_shapes=scratch(early),
        compiler_params=params(),
        cost_estimate=cost(1e10, 2e7),
        name="carried",
    )(voltages, taper, swap, table)
    carried, later_taper = lax.optimization_barrier((carried, taper))
    carried = lax.ppermute(carried, "chan", [(i, i + 1) for i in range(n_chan - 1)])

    send_spec = pl.BlockSpec((groups, 1, 2 * channels, LANES), lambda h, j: (0, h, 0, 0))
    send_shape = jax.ShapeDtypeStruct((groups, halves, 2 * channels, LANES), BF16)
    late_send = pl.pallas_call(
        lambda *refs: spectra_kernel(times, False, *refs),
        grid=grid,
        in_specs=[volt_spec, taper_spec, swap_spec, table_spec],
        out_specs=send_spec,
        out_shape=send_shape,
        scratch_shapes=scratch(times) + wide,
        compiler_params=params(),
        cost_estimate=cost(5e10, 4e7),
        name="late",
    )(voltages, later_taper, swap, table)

    def exchange(value):
        value = lax.all_to_all(value, ("inp", "chan"), split_axis=0, concat_axis=0, tiled=True)
        return value.reshape(n_inp, n_chan, halves, 2 * channels, LANES)

    late_got = exchange(late_send)

    keep = (lax.axis_index("chan") == 0).astype(F32).reshape(1)
    early_send = pl.pallas_call(
        lambda *refs: spectra_kernel(0, True, *refs),
        grid=grid,
        in_specs=[
            pl.BlockSpec(memory_space=pltpu.SMEM),
            volt_spec,
            pl.BlockSpec((early, HALF, part), lambda h, j: (0, h, j)),
            carried_spec,
            pl.BlockSpec(unit.shape, lambda h, j: (0, 0)),
            taper_spec,
            swap_spec,
            table_spec,
        ],
        out_specs=send_spec,
        out_shape=send_shape,
        scratch_shapes=scratch(times) + wide,
        compiler_params=params(),
        cost_estimate=cost(2e11, 4e7),
        name="early",
    )(keep, voltages, jnp.transpose(history, (1, 0, 2)), carried, unit, taper, swap, table)
    early_got = exchange(early_send)

    pair = 16 // times
    steps = n_chan // pair
    span = n_chan * times
    got_block = (n_inp, pair, halves, 2 * channels, LANES)
    block = 8
    got_spec = pl.BlockSpec(got_block, lambda j: (0, jnp.minimum(j, steps - 1), 0, 0, 0))
    prior_spec = pl.BlockSpec(
        (block, total, 2 * total), lambda j: (jnp.maximum(j - steps, 0), 0, 0)
    )
    held = pltpu.VMEM((2 * channels, span, total), BF16)
    prior = pl.pallas_call(
        lambda *refs: gram_kernel(None, steps, *refs),
        grid=(steps + channels // block,),
        in_specs=[got_spec, swap_spec],
        out_specs=prior_spec,
        out_shape=jax.ShapeDtypeStruct((channels, total, 2 * total), F32),
        scratch_shapes=[held],
        compiler_params=params(),
        cost_estimate=cost(1e10, 1e7),
        name="late_gram",
    )(late_got, swap)
    return pl.pallas_call(
        lambda *refs: gram_kernel(1.0 / (n_chan * s_dev), steps, *refs),
        grid=(steps + channels // block,),
        in_specs=[got_spec, swap_spec, prior_spec],
        out_specs=pl.BlockSpec(
            (2, block, total, total), lambda j: (0, jnp.maximum(j - steps, 0), 0, 0)
        ),
        out_shape=jax.ShapeDtypeStruct((2, channels, total, total), BF16),
        scratch_shapes=[held],
        compiler_params=params(),
        cost_estimate=cost(1e10, 1e7),
        name="early_gram",
    )(early_got, swap, prior)


def solution(mesh):
    in_specs = (P("inp", "chan", None), P("inp", None, None), P())
    out_specs = P(None, ("inp", "chan"), None, None)
    return jax.shard_map(
        on_device, mesh=mesh, in_specs=in_specs, out_specs=out_specs, check_vma=False
    )
```

```python
import math

import jax
import jax.numpy as jnp
import ml_dtypes
import numpy as np
from jax import lax
from jax.experimental import pallas as pl
from jax.experimental.pallas import tpu as pltpu
from jax.sharding import PartitionSpec as P

BAND = 2048
LOW = 1024
LANES = 128
RADIX = 64
HALF = 16
CLASSES = RADIX // 2
ROOT = math.sqrt(0.5)
F32 = jnp.float32
BF16 = jnp.bfloat16
VMEM = 63 * 1024 * 1024


def stage_table(frame):
    high = BAND // RADIX
    lane = np.arange(LANES)
    table = np.zeros((CLASSES, 2, high, 2, 2, LANES))
    for q in range(CLASSES):
        for half in range(2):
            low = q if half == 0 else (RADIX - q if q else RADIX // 2)
            k = low + RADIX * (LOW // RADIX + np.arange(high))
            angle = 2.0 * np.pi * (np.outer(k, lane) % frame) / frame
            cos, sin = np.cos(angle), np.sin(angle)
            if q == 0:
                table[q, half, :, 0, half] = cos
                table[q, half, :, 1, half] = -sin
            elif half == 0:
                table[q, half, :, 0, 0] = cos
                table[q, half, :, 0, 1] = sin
                table[q, half, :, 1, 0] = -sin
                table[q, half, :, 1, 1] = cos
            else:
                table[q, half, :, 0, 0] = cos
                table[q, half, :, 0, 1] = -sin
                table[q, half, :, 1, 0] = -sin
                table[q, half, :, 1, 1] = -cos
    table = table / math.sqrt(frame)
    return table.reshape(CLASSES, 2 * high * 2, 2 * LANES)


def real_dft8(x):
    s = [x[j] + x[j + 4] for j in range(4)]
    d = [x[j] - x[j + 4] for j in range(4)]
    e0, e1 = s[0] + s[2], s[0] - s[2]
    o0, o1 = s[1] + s[3], s[3] - s[1]
    u, v = (d[1] - d[3]) * ROOT, (d[1] + d[3]) * ROOT
    return [
        (e0 + o0, None),
        (d[0] + u, -(d[2] + v)),
        (e1, o1),
        (d[0] - u, d[2] - v),
        (e0 - o0, None),
    ]


def complex_dft8(x):
    def add(a, b):
        return (a[0] + b[0], a[1] + b[1])

    def sub(a, b):
        return (a[0] - b[0], a[1] - b[1])

    def add_i(a, b):
        return (a[0] - b[1], a[1] + b[0])

    def sub_i(a, b):
        return (a[0] + b[1], a[1] - b[0])

    s = [add(x[j], x[j + 4]) for j in range(4)]
    d = [sub(x[j], x[j + 4]) for j in range(4)]
    e0, e1 = add(s[0], s[2]), sub(s[0], s[2])
    o0, o1 = add(s[1], s[3]), sub(s[1], s[3])
    p, m = sub(d[1], d[3]), add(d[1], d[3])
    b = ((p[0] + m[1]) * ROOT, (p[1] - m[0]) * ROOT)
    c = ((m[1] - p[0]) * ROOT, (-p[1] - m[0]) * ROOT)
    f, g = sub_i(d[0], d[2]), add_i(d[0], d[2])
    return [
        add(e0, o0),
        add(f, b),
        sub_i(e1, o1),
        add(g, c),
        sub(e0, o0),
        sub(f, b),
        add_i(e1, o1),
        sub(g, c),
    ]


def turned(value, step):
    angle = 2.0 * math.pi * (step % RADIX) / RADIX
    cos, sin = math.cos(angle), math.sin(angle)
    real, imag = value
    if imag is None:
        return (real * cos, real * -sin)
    if step % RADIX == 0:
        return value
    return (real * cos + imag * sin, imag * cos - real * sin)


def unrolled(count, copies, body):
    def step(i, carry):
        for copy in range(copies):
            body(i * copies + copy, copy)
        return carry

    lax.fori_loop(0, count // copies, step, 0)


def transform_rows(fir, mid, zed, count):
    def one(s, carry):
        for low in range(8):
            parts = real_dft8([fir[8 * high + low, s] for high in range(8)])
            mid[0, low] = parts[0][0]
            mid[7, low] = parts[4][0]
            for k in (1, 2, 3):
                value = turned(parts[k], low * k)
                mid[2 * k - 1, low] = value[0]
                mid[2 * k, low] = value[1]
        rows = pl.ds(pl.multiple_of(s * HALF, HALF), HALF)

        def put(q, half, value):
            zed[q, rows, half * LANES : (half + 1) * LANES] = value.astype(BF16)

        parts = real_dft8([mid[0, low] for low in range(8)])
        put(0, 0, parts[0][0])
        put(0, 1, parts[4][0])
        for m in (1, 2, 3):
            put(8 * m, 0, parts[m][0])
            put(8 * m, 1, parts[m][1])
        for k in (1, 2, 3):
            parts = complex_dft8([(mid[2 * k - 1, low], mid[2 * k, low]) for low in range(8)])
            for m in range(8):
                index = k + 8 * m
                if index < CLASSES:
                    put(index, 0, parts[m][0])
                    put(index, 1, parts[m][1])
                else:
                    put(RADIX - index, 0, parts[m][0])
                    put(RADIX - index, 1, -parts[m][1])
        parts = complex_dft8([turned((mid[7, low], None), 4 * low) for low in range(8)])
        for m in range(4):
            put(4 + 8 * m, 0, parts[m][0])
            put(4 + 8 * m, 1, parts[m][1])
        return carry

    lax.fori_loop(0, count, one, 0)


def filter_rows(volt, taper, fir, turn, first, hist=None, keep=None):
    count = fir.shape[1]
    tiles = volt.shape[2] // LANES
    base = pl.program_id(1) * tiles
    taps = taper.shape[0]
    s_dev = volt.shape[1]
    wanted = [f for f in range(first - taps + 1, first + count) if f < s_dev]

    def one(a, slot):
        lanes = pl.ds(pl.multiple_of(a * LANES, LANES), LANES)
        turn[slot] = volt[:, :, lanes].astype(F32).reshape(HALF * s_dev, LANES)
        frames = {}
        for f in wanted:
            if f >= 0:
                frames[f] = turn[slot, pl.ds(f, HALF, stride=s_dev), :]
            elif hist is not None:
                frames[f] = hist[taps - 1 + f, :, lanes].astype(F32) * keep
        weights = [taper[t : t + 1, lanes] for t in range(taps)]
        for j in range(count):
            total = None
            for t in range(taps):
                f = first + j + t - taps + 1
                if f in frames:
                    term = weights[t] * frames[f]
                    total = term if total is None else total + term
            fir[base + a, j] = total

    unrolled(tiles, turn.shape[0], one)


def with_table(table, held, sem):
    copy = pltpu.make_async_copy(table, held, sem)

    @pl.when((pl.program_id(0) == 0) & (pl.program_id(1) == 0))
    def _():
        copy.start()

    @pl.when((pl.program_id(0) == 0) & (pl.program_id(1) == pl.num_programs(1) - 1))
    def _():
        copy.wait()


CONTRACT = (((1,), (1,)), ((), ()))


def carried_kernel(volt, taper, table, out, turn, fir, mid, zed, held, sem):
    with_table(table, held, sem)
    filter_rows(volt, taper, fir, turn, volt.shape[1])

    @pl.when(pl.program_id(1) == pl.num_programs(1) - 1)
    def _():
        transform_rows(fir, mid, zed, fir.shape[1])

        def one(q, copy):
            out[q, 0] = jnp.dot(zed[q], held[q], preferred_element_type=F32).astype(BF16)

        unrolled(CLASSES, 8, one)


def spectra_kernel(first, boundary, *refs):
    if boundary:
        keep, volt, hist, carried, unit, taper, table, out, *scratch = refs
    else:
        volt, taper, table, out, *scratch = refs
    turn, fir, mid, zed, held, sem, wide = scratch
    with_table(table, held, sem)
    if boundary:
        filter_rows(volt, taper, fir, turn, first, hist, keep[0])
    else:
        filter_rows(volt, taper, fir, turn, first)

    @pl.when(pl.program_id(1) == pl.num_programs(1) - 1)
    def _():
        transform_rows(fir, mid, zed, fir.shape[1])
        step = RADIX

        def one(q, copy):
            value = lax.dot_general(held[q], zed[q], CONTRACT, preferred_element_type=F32)
            if boundary:
                part = carried[q, 0]
                short = zed.shape[1] - part.shape[0]
                part = jnp.concatenate([part, jnp.zeros((short, LANES), BF16)], axis=0)
                value = value + lax.dot_general(
                    unit[...], part, CONTRACT, preferred_element_type=F32
                )
            wide[pl.ds(pl.multiple_of(q * step, step), step), :] = value[:step]
            other = jnp.where(q == 0, CLASSES, RADIX - q)
            wide[pl.ds(pl.multiple_of(other * step, step), step), :] = value[step:]

        unrolled(CLASSES, 8, one)
        channels = out.shape[2] // 2
        split = RADIX // channels
        high = out.shape[0] // split

        def two(g, copy):
            for part in range(2):
                rows = wide[pl.ds(g * 2 + part, RADIX, stride=step), :].astype(BF16)
                for u in range(split):
                    out[g * split + u, 0, part * channels : (part + 1) * channels, :] = rows[
                        u * channels : (u + 1) * channels
                    ]

        unrolled(high, 4, two)


def reorder(got, turn, put):
    n_inp, pair, halves, rows, _ = got.shape
    blocks = LANES // HALF
    block = lax.broadcasted_iota(jnp.int32, (HALF, LANES), 1) // HALF
    masks = {d: (block & d) == 0 for d in (1, 2, 4)}

    def one(b, copy):
        here = pl.ds(pl.multiple_of(b * HALF, HALF), HALF)
        for c in range(pair):
            for tile in range(n_inp * halves // blocks):
                x = []
                for p in range(blocks):
                    a, h = divmod(tile * blocks + p, halves)
                    x.append(got[a, c, h, here, :].astype(F32))
                for d in (1, 2, 4):
                    for p in range(blocks):
                        if p & d == 0:
                            low, up = x[p], x[p | d]
                            x[p] = jnp.where(masks[d], low, pltpu.roll(up, HALF * d, 1))
                            x[p | d] = jnp.where(masks[d], pltpu.roll(low, LANES - HALF * d, 1), up)
                for s in range(blocks):
                    start = (c * blocks + s) * rows
                    turn[tile, pl.ds(pl.multiple_of(start + b * HALF, HALF), HALF), :] = x[s]

    unrolled(rows // HALF, 2, one)

    def two(r, copy):
        for tile in range(turn.shape[0]):
            put(r, tile, turn[tile, pl.ds(r, pair * blocks, stride=rows), :].astype(BF16))

    unrolled(rows, 8, two)


def order_kernel(got, out, turn):
    def put(r, tile, value):
        out[r, :, tile * LANES : (tile + 1) * LANES] = value

    reorder(got, turn, put)


def finish_kernel(scale, steps, got, late, out, turn, early):
    j = pl.program_id(0)
    pair = got.shape[1] * (LANES // HALF)
    block = out.shape[1]
    width = out.shape[-1]
    channels = early.shape[0] // 2

    @pl.when(j < steps)
    def _():
        times = pl.ds(pl.multiple_of(j * pair, pair), pair)

        def put(r, tile, value):
            early[r, times, tile * LANES : (tile + 1) * LANES] = value

        reorder(got, turn, put)

    @pl.when(j >= steps)
    def _():
        first = (j - steps) * block
        for k in range(block):
            real = jnp.concatenate([late[0, k], early[first + k]], axis=0)
            imag = jnp.concatenate([late[1, k], early[channels + first + k]], axis=0)
            left = jnp.concatenate([real, imag], axis=0)
            right = jnp.concatenate([-imag, real], axis=0)
            value = lax.dot_general(
                left,
                jnp.concatenate([left, right], axis=1),
                (((0,), (0,)), ((), ())),
                preferred_element_type=F32,
            )
            value = value * scale
            out[0, k] = value[:, :width].astype(BF16)
            out[1, k] = value[:, width:].astype(BF16)


def params():
    return pltpu.CompilerParams(vmem_limit_bytes=VMEM)


def cost(flops, moved):
    return pl.CostEstimate(flops=int(flops), bytes_accessed=int(moved), transcendentals=0)


def on_device(voltages, history, taper):
    in_dev, s_dev, frame = voltages.shape
    taps = taper.shape[0]
    n_inp = lax.axis_size("inp")
    n_chan = lax.axis_size("chan")
    groups = n_inp * n_chan
    channels = BAND // groups
    total = n_inp * in_dev
    halves = in_dev // HALF
    times = s_dev // 2
    early = taps - 1
    rows = times * HALF
    assert frame == RADIX * LANES and halves == 2 and rows == LANES
    assert early == times - 1 and RADIX % channels == 0 and total % LANES == 0

    outputs = 2 * BAND // CLASSES
    stage = stage_table(frame).astype(np.float32).astype(ml_dtypes.bfloat16)
    table = jnp.asarray(stage)
    upright = jnp.asarray(np.ascontiguousarray(stage.transpose(0, 2, 1)))
    unit = jnp.asarray(np.eye(outputs).astype(ml_dtypes.bfloat16))
    assert table.shape == (CLASSES, outputs, 2 * LANES) and outputs == LANES

    chunks = 4
    part = frame // chunks
    volt_spec = pl.BlockSpec((HALF, s_dev, part), lambda h, j: (h, 0, j))
    taper_spec = pl.BlockSpec((taps, part), lambda h, j: (0, j))
    table_spec = pl.BlockSpec(memory_space=pl.ANY)
    grid = (halves, chunks)

    def scratch(count, shape):
        return [
            pltpu.VMEM((4, HALF * s_dev, LANES), F32),
            pltpu.VMEM((RADIX, count, HALF, LANES), F32),
            pltpu.VMEM((8, 8, HALF, LANES), F32),
            pltpu.VMEM((CLASSES, count * HALF, 2 * LANES), BF16),
            pltpu.VMEM(shape, BF16),
            pltpu.SemaphoreType.DMA,
        ]

    wide = [pltpu.VMEM((RADIX * RADIX, LANES), F32)]
    carried_spec = pl.BlockSpec((CLASSES, 1, early * HALF, outputs), lambda h, j: (0, h, 0, 0))
    carried = pl.pallas_call(
        carried_kernel,
        grid=grid,
        in_specs=[volt_spec, taper_spec, table_spec],
        out_specs=carried_spec,
        out_shape=jax.ShapeDtypeStruct((CLASSES, halves, early * HALF, outputs), BF16),
        scratch_shapes=scratch(early, upright.shape),
        compiler_params=params(),
        cost_estimate=cost(1e10, 2e7),
        name="carried",
    )(voltages, taper, upright)
    carried, later_taper = lax.optimization_barrier((carried, taper))
    carried = lax.ppermute(carried, "chan", [(i, i + 1) for i in range(n_chan - 1)])

    send_spec = pl.BlockSpec((groups, 1, 2 * channels, LANES), lambda h, j: (0, h, 0, 0))
    send_shape = jax.ShapeDtypeStruct((groups, halves, 2 * channels, LANES), BF16)
    late_send = pl.pallas_call(
        lambda *refs: spectra_kernel(times, False, *refs),
        grid=grid,
        in_specs=[volt_spec, taper_spec, table_spec],
        out_specs=send_spec,
        out_shape=send_shape,
        scratch_shapes=scratch(times, table.shape) + wide,
        compiler_params=params(),
        cost_estimate=cost(5e10, 4e7),
        name="late",
    )(voltages, later_taper, table)

    def exchange(value):
        value = lax.all_to_all(value, ("inp", "chan"), split_axis=0, concat_axis=0, tiled=True)
        return value.reshape(n_inp, n_chan, halves, 2 * channels, LANES)

    late_got = exchange(late_send)

    keep = (lax.axis_index("chan") == 0).astype(F32).reshape(1)
    early_send = pl.pallas_call(
        lambda *refs: spectra_kernel(0, True, *refs),
        grid=grid,
        in_specs=[
            pl.BlockSpec(memory_space=pltpu.SMEM),
            volt_spec,
            pl.BlockSpec((early, HALF, part), lambda h, j: (0, h, j)),
            carried_spec,
            pl.BlockSpec(unit.shape, lambda h, j: (0, 0)),
            taper_spec,
            table_spec,
        ],
        out_specs=send_spec,
        out_shape=send_shape,
        scratch_shapes=scratch(times, table.shape) + wide,
        compiler_params=params(),
        cost_estimate=cost(2e11, 4e7),
        name="early",
    )(keep, voltages, jnp.transpose(history, (1, 0, 2)), carried, unit, taper, table)
    early_got = exchange(early_send)

    pair = 16 // times
    steps = n_chan // pair
    span = n_chan * times
    got_block = (n_inp, pair, halves, 2 * channels, LANES)
    turn = pltpu.VMEM((total // LANES, pair * times * 2 * channels, LANES), F32)
    late_rows = pl.pallas_call(
        order_kernel,
        grid=(steps,),
        in_specs=[pl.BlockSpec(got_block, lambda c: (0, c, 0, 0, 0))],
        out_specs=pl.BlockSpec((2 * channels, pair * times, total), lambda c: (0, c, 0)),
        out_shape=jax.ShapeDtypeStruct((2 * channels, span, total), BF16),
        scratch_shapes=[turn],
        compiler_params=params(),
        cost_estimate=cost(1e4, 1e4),
        name="order",
    )(late_got).reshape(2, channels, span, total)

    block = 8
    return pl.pallas_call(
        lambda *refs: finish_kernel(1.0 / (n_chan * s_dev), steps, *refs),
        grid=(steps + channels // block,),
        in_specs=[
            pl.BlockSpec(got_block, lambda j: (0, jnp.minimum(j, steps - 1), 0, 0, 0)),
            pl.BlockSpec(
                (2, block, span, total), lambda j: (0, jnp.maximum(j - steps, 0), 0, 0)
            ),
        ],
        out_specs=pl.BlockSpec(
            (2, block, total, total), lambda j: (0, jnp.maximum(j - steps, 0), 0, 0)
        ),
        out_shape=jax.ShapeDtypeStruct((2, channels, total, total), BF16),
        scratch_shapes=[turn, pltpu.VMEM((2 * channels, span, total), BF16)],
        compiler_params=params(),
        cost_estimate=cost(1e10, 1e7),
        name="finish",
    )(early_got, late_rows)


def solution(mesh):
    in_specs = (P("inp", "chan", None), P("inp", None, None), P())
    out_specs = P(None, ("inp", "chan"), None, None)
    return jax.shard_map(
        on_device, mesh=mesh, in_specs=in_specs, out_specs=out_specs, check_vma=False
    )
```

```python
import math

import jax
import jax.numpy as jnp
import ml_dtypes
import numpy as np
from jax import lax
from jax.experimental import pallas as pl
from jax.experimental.pallas import tpu as pltpu
from jax.sharding import PartitionSpec as P

BAND = 2048
LOW = 1024
LANES = 128
RADIX = 64
HALF = 16
CLASSES = RADIX // 2
ROOT = math.sqrt(0.5)
F32 = jnp.float32
BF16 = jnp.bfloat16
VMEM = 63 * 1024 * 1024


def stage_table(frame):
    high = BAND // RADIX
    lane = np.arange(LANES)
    table = np.zeros((CLASSES, 2, high, 2, 2, LANES))
    for q in range(CLASSES):
        for half in range(2):
            low = q if half == 0 else (RADIX - q if q else RADIX // 2)
            k = low + RADIX * (LOW // RADIX + np.arange(high))
            angle = 2.0 * np.pi * (np.outer(k, lane) % frame) / frame
            cos, sin = np.cos(angle), np.sin(angle)
            if q == 0:
                table[q, half, :, 0, half] = cos
                table[q, half, :, 1, half] = -sin
            elif half == 0:
                table[q, half, :, 0, 0] = cos
                table[q, half, :, 0, 1] = sin
                table[q, half, :, 1, 0] = -sin
                table[q, half, :, 1, 1] = cos
            else:
                table[q, half, :, 0, 0] = cos
                table[q, half, :, 0, 1] = -sin
                table[q, half, :, 1, 0] = -sin
                table[q, half, :, 1, 1] = -cos
    table = table / math.sqrt(frame)
    return table.reshape(CLASSES, 2 * high * 2, 2 * LANES)


def real_dft8(x):
    s = [x[j] + x[j + 4] for j in range(4)]
    d = [x[j] - x[j + 4] for j in range(4)]
    e0, e1 = s[0] + s[2], s[0] - s[2]
    o0, o1 = s[1] + s[3], s[3] - s[1]
    u, v = (d[1] - d[3]) * ROOT, (d[1] + d[3]) * ROOT
    return [
        (e0 + o0, None),
        (d[0] + u, -(d[2] + v)),
        (e1, o1),
        (d[0] - u, d[2] - v),
        (e0 - o0, None),
    ]


def complex_dft8(x):
    def add(a, b):
        return (a[0] + b[0], a[1] + b[1])

    def sub(a, b):
        return (a[0] - b[0], a[1] - b[1])

    def add_i(a, b):
        return (a[0] - b[1], a[1] + b[0])

    def sub_i(a, b):
        return (a[0] + b[1], a[1] - b[0])

    s = [add(x[j], x[j + 4]) for j in range(4)]
    d = [sub(x[j], x[j + 4]) for j in range(4)]
    e0, e1 = add(s[0], s[2]), sub(s[0], s[2])
    o0, o1 = add(s[1], s[3]), sub(s[1], s[3])
    p, m = sub(d[1], d[3]), add(d[1], d[3])
    b = ((p[0] + m[1]) * ROOT, (p[1] - m[0]) * ROOT)
    c = ((m[1] - p[0]) * ROOT, (-p[1] - m[0]) * ROOT)
    f, g = sub_i(d[0], d[2]), add_i(d[0], d[2])
    return [
        add(e0, o0),
        add(f, b),
        sub_i(e1, o1),
        add(g, c),
        sub(e0, o0),
        sub(f, b),
        add_i(e1, o1),
        sub(g, c),
    ]


def turned(value, step):
    angle = 2.0 * math.pi * (step % RADIX) / RADIX
    cos, sin = math.cos(angle), math.sin(angle)
    real, imag = value
    if imag is None:
        return (real * cos, real * -sin)
    if step % RADIX == 0:
        return value
    return (real * cos + imag * sin, imag * cos - real * sin)


def unrolled(count, copies, body):
    def step(i, carry):
        for copy in range(copies):
            body(i * copies + copy, copy)
        return carry

    lax.fori_loop(0, count // copies, step, 0)


def transform_rows(fir, mid, zed, count):
    def one(s, carry):
        for low in range(8):
            parts = real_dft8([fir[8 * high + low, s] for high in range(8)])
            mid[0, low] = parts[0][0]
            mid[7, low] = parts[4][0]
            for k in (1, 2, 3):
                value = turned(parts[k], low * k)
                mid[2 * k - 1, low] = value[0]
                mid[2 * k, low] = value[1]
        rows = pl.ds(pl.multiple_of(s * HALF, HALF), HALF)

        def put(q, half, value):
            zed[q, rows, half * LANES : (half + 1) * LANES] = value.astype(BF16)

        parts = real_dft8([mid[0, low] for low in range(8)])
        put(0, 0, parts[0][0])
        put(0, 1, parts[4][0])
        for m in (1, 2, 3):
            put(8 * m, 0, parts[m][0])
            put(8 * m, 1, parts[m][1])
        for k in (1, 2, 3):
            parts = complex_dft8([(mid[2 * k - 1, low], mid[2 * k, low]) for low in range(8)])
            for m in range(8):
                index = k + 8 * m
                if index < CLASSES:
                    put(index, 0, parts[m][0])
                    put(index, 1, parts[m][1])
                else:
                    put(RADIX - index, 0, parts[m][0])
                    put(RADIX - index, 1, -parts[m][1])
        parts = complex_dft8([turned((mid[7, low], None), 4 * low) for low in range(8)])
        for m in range(4):
            put(4 + 8 * m, 0, parts[m][0])
            put(4 + 8 * m, 1, parts[m][1])
        return carry

    lax.fori_loop(0, count, one, 0)


def filter_rows(volt, taper, fir, first, hist=None, keep=None):
    count = fir.shape[1]
    tiles = volt.shape[2] // LANES
    base = pl.program_id(1) * tiles
    taps = taper.shape[0]
    s_dev = volt.shape[1]
    wanted = [f for f in range(first - taps + 1, first + count) if f < s_dev]

    def one(a, slot):
        lanes = pl.ds(pl.multiple_of(a * LANES, LANES), LANES)
        by_time = jnp.swapaxes(volt[:, :, lanes], 0, 1)
        frames = {}
        for f in wanted:
            if f >= 0:
                frames[f] = by_time[f].astype(F32)
            elif hist is not None:
                frames[f] = hist[taps - 1 + f, :, lanes].astype(F32) * keep
        weights = [taper[t : t + 1, lanes] for t in range(taps)]
        for j in range(count):
            total = None
            for t in range(taps):
                f = first + j + t - taps + 1
                if f in frames:
                    term = weights[t] * frames[f]
                    total = term if total is None else total + term
            fir[base + a, j] = total

    unrolled(tiles, 4, one)


def with_table(table, held, sem):
    copy = pltpu.make_async_copy(table, held, sem)

    @pl.when((pl.program_id(0) == 0) & (pl.program_id(1) == 0))
    def _():
        copy.start()

    @pl.when((pl.program_id(0) == 0) & (pl.program_id(1) == pl.num_programs(1) - 1))
    def _():
        copy.wait()


CONTRACT = (((1,), (1,)), ((), ()))


def carried_kernel(volt, taper, table, out, fir, mid, zed, held, sem):
    with_table(table, held, sem)
    filter_rows(volt, taper, fir, volt.shape[1])

    @pl.when(pl.program_id(1) == pl.num_programs(1) - 1)
    def _():
        transform_rows(fir, mid, zed, fir.shape[1])

        def one(q, copy):
            out[q, 0] = jnp.dot(zed[q], held[q], preferred_element_type=F32).astype(BF16)

        unrolled(CLASSES, 8, one)


def spectra_kernel(first, boundary, *refs):
    if boundary:
        keep, volt, hist, carried, unit, taper, table, out, *scratch = refs
    else:
        volt, taper, table, out, *scratch = refs
    fir, mid, zed, held, sem, wide = scratch
    with_table(table, held, sem)
    if boundary:
        filter_rows(volt, taper, fir, first, hist, keep[0])
    else:
        filter_rows(volt, taper, fir, first)

    @pl.when(pl.program_id(1) == pl.num_programs(1) - 1)
    def _():
        transform_rows(fir, mid, zed, fir.shape[1])
        step = RADIX

        def one(q, copy):
            value = lax.dot_general(held[q], zed[q], CONTRACT, preferred_element_type=F32)
            if boundary:
                part = carried[q, 0]
                short = zed.shape[1] - part.shape[0]
                part = jnp.concatenate([part, jnp.zeros((short, LANES), BF16)], axis=0)
                value = value + lax.dot_general(
                    unit[...], part, CONTRACT, preferred_element_type=F32
                )
            wide[q] = value[:step].astype(BF16)
            wide[jnp.where(q == 0, CLASSES, RADIX - q)] = value[step:].astype(BF16)

        unrolled(CLASSES, 8, one)
        channels = out.shape[2] // 2
        split = RADIX // channels
        high = HALF // 2

        def two(b, copy):
            here = pl.ds(pl.multiple_of(b * HALF, HALF), HALF)
            for first_k in range(0, RADIX, HALF):
                value = jnp.swapaxes(wide[first_k : first_k + HALF, here, :], 0, 1)
                u, k = divmod(first_k, channels)
                for j in range(HALF):
                    start = j % 2 * channels + k
                    out[(b * high + j // 2) * split + u, 0, start : start + HALF, :] = value[j]

        unrolled(step // HALF, 2, two)


def reorder(got, put):
    n_inp, pair, halves, rows, _ = got.shape
    blocks = LANES // HALF
    block = lax.broadcasted_iota(jnp.int32, (HALF, LANES), 1) // HALF
    masks = {d: (block & d) == 0 for d in (1, 2, 4)}

    def one(b, copy):
        here = pl.ds(pl.multiple_of(b * HALF, HALF), HALF)
        for tile in range(n_inp * halves // blocks):
            pieces = []
            for c in range(pair):
                x = []
                for p in range(blocks):
                    a, h = divmod(tile * blocks + p, halves)
                    x.append(got[a, c, h, here, :])
                for d in (1, 2, 4):
                    for p in range(blocks):
                        if p & d == 0:
                            low, up = x[p], x[p | d]
                            x[p] = jnp.where(masks[d], low, pltpu.roll(up, HALF * d, 1))
                            x[p | d] = jnp.where(
                                masks[d], pltpu.roll(low, LANES - HALF * d, 1), up
                            )
                pieces += x
            value = jnp.swapaxes(jnp.stack(pieces), 0, 1)
            for j in range(HALF):
                put(b * HALF + j, tile, value[j])

    unrolled(rows // HALF, 2, one)


def order_kernel(got, out):
    def put(r, tile, value):
        out[r, :, tile * LANES : (tile + 1) * LANES] = value

    reorder(got, put)


def finish_kernel(scale, steps, got, late, out, early):
    j = pl.program_id(0)
    pair = got.shape[1] * (LANES // HALF)
    block = out.shape[1]
    width = out.shape[-1]
    channels = early.shape[0] // 2

    @pl.when(j < steps)
    def _():
        times = pl.ds(pl.multiple_of(j * pair, pair), pair)

        def put(r, tile, value):
            early[r, times, tile * LANES : (tile + 1) * LANES] = value

        reorder(got, put)

    @pl.when(j >= steps)
    def _():
        first = (j - steps) * block
        for k in range(block):
            real = jnp.concatenate([late[0, k], early[first + k]], axis=0)
            imag = jnp.concatenate([late[1, k], early[channels + first + k]], axis=0)
            left = jnp.concatenate([real, imag], axis=0)
            right = jnp.concatenate([-imag, real], axis=0)
            value = lax.dot_general(
                left,
                jnp.concatenate([left, right], axis=1),
                (((0,), (0,)), ((), ())),
                preferred_element_type=F32,
            )
            value = value * scale
            out[0, k] = value[:, :width].astype(BF16)
            out[1, k] = value[:, width:].astype(BF16)


def params():
    return pltpu.CompilerParams(vmem_limit_bytes=VMEM)


def cost(flops, moved):
    return pl.CostEstimate(flops=int(flops), bytes_accessed=int(moved), transcendentals=0)


def on_device(voltages, history, taper):
    in_dev, s_dev, frame = voltages.shape
    taps = taper.shape[0]
    n_inp = lax.axis_size("inp")
    n_chan = lax.axis_size("chan")
    groups = n_inp * n_chan
    channels = BAND // groups
    total = n_inp * in_dev
    halves = in_dev // HALF
    times = s_dev // 2
    early = taps - 1
    rows = times * HALF
    assert frame == RADIX * LANES and halves == 2 and rows == LANES
    assert early == times - 1 and RADIX % channels == 0 and total % LANES == 0

    outputs = 2 * BAND // CLASSES
    stage = stage_table(frame).astype(np.float32).astype(ml_dtypes.bfloat16)
    table = jnp.asarray(stage)
    upright = jnp.asarray(np.ascontiguousarray(stage.transpose(0, 2, 1)))
    unit = jnp.asarray(np.eye(outputs).astype(ml_dtypes.bfloat16))
    assert table.shape == (CLASSES, outputs, 2 * LANES) and outputs == LANES

    chunks = 4
    part = frame // chunks
    volt_spec = pl.BlockSpec((HALF, s_dev, part), lambda h, j: (h, 0, j))
    taper_spec = pl.BlockSpec((taps, part), lambda h, j: (0, j))
    table_spec = pl.BlockSpec(memory_space=pl.ANY)
    grid = (halves, chunks)

    def scratch(count, shape):
        return [
            pltpu.VMEM((RADIX, count, HALF, LANES), F32),
            pltpu.VMEM((8, 8, HALF, LANES), F32),
            pltpu.VMEM((CLASSES, count * HALF, 2 * LANES), BF16),
            pltpu.VMEM(shape, BF16),
            pltpu.SemaphoreType.DMA,
        ]

    wide = [pltpu.VMEM((RADIX, RADIX, LANES), BF16)]
    carried_spec = pl.BlockSpec((CLASSES, 1, early * HALF, outputs), lambda h, j: (0, h, 0, 0))
    carried = pl.pallas_call(
        carried_kernel,
        grid=grid,
        in_specs=[volt_spec, taper_spec, table_spec],
        out_specs=carried_spec,
        out_shape=jax.ShapeDtypeStruct((CLASSES, halves, early * HALF, outputs), BF16),
        scratch_shapes=scratch(early, upright.shape),
        compiler_params=params(),
        cost_estimate=cost(1e10, 2e7),
        name="carried",
    )(voltages, taper, upright)
    carried, later_taper = lax.optimization_barrier((carried, taper))
    carried = lax.ppermute(carried, "chan", [(i, i + 1) for i in range(n_chan - 1)])

    send_spec = pl.BlockSpec((groups, 1, 2 * channels, LANES), lambda h, j: (0, h, 0, 0))
    send_shape = jax.ShapeDtypeStruct((groups, halves, 2 * channels, LANES), BF16)
    late_send = pl.pallas_call(
        lambda *refs: spectra_kernel(times, False, *refs),
        grid=grid,
        in_specs=[volt_spec, taper_spec, table_spec],
        out_specs=send_spec,
        out_shape=send_shape,
        scratch_shapes=scratch(times, table.shape) + wide,
        compiler_params=params(),
        cost_estimate=cost(5e10, 4e7),
        name="late",
    )(voltages, later_taper, table)

    def exchange(value):
        value = lax.all_to_all(value, ("inp", "chan"), split_axis=0, concat_axis=0, tiled=True)
        return value.reshape(n_inp, n_chan, halves, 2 * channels, LANES)

    late_got = exchange(late_send)

    keep = (lax.axis_index("chan") == 0).astype(F32).reshape(1)
    early_send = pl.pallas_call(
        lambda *refs: spectra_kernel(0, True, *refs),
        grid=grid,
        in_specs=[
            pl.BlockSpec(memory_space=pltpu.SMEM),
            volt_spec,
            pl.BlockSpec((early, HALF, part), lambda h, j: (0, h, j)),
            carried_spec,
            pl.BlockSpec(unit.shape, lambda h, j: (0, 0)),
            taper_spec,
            table_spec,
        ],
        out_specs=send_spec,
        out_shape=send_shape,
        scratch_shapes=scratch(times, table.shape) + wide,
        compiler_params=params(),
        cost_estimate=cost(2e11, 4e7),
        name="early",
    )(keep, voltages, jnp.transpose(history, (1, 0, 2)), carried, unit, taper, table)
    early_got = exchange(early_send)

    pair = 16 // times
    steps = n_chan // pair
    span = n_chan * times
    got_block = (n_inp, pair, halves, 2 * channels, LANES)
    late_rows = pl.pallas_call(
        order_kernel,
        grid=(steps,),
        in_specs=[pl.BlockSpec(got_block, lambda c: (0, c, 0, 0, 0))],
        out_specs=pl.BlockSpec((2 * channels, pair * times, total), lambda c: (0, c, 0)),
        out_shape=jax.ShapeDtypeStruct((2 * channels, span, total), BF16),
        compiler_params=params(),
        cost_estimate=cost(1e4, 1e4),
        name="order",
    )(late_got).reshape(2, channels, span, total)

    block = 8
    return pl.pallas_call(
        lambda *refs: finish_kernel(1.0 / (n_chan * s_dev), steps, *refs),
        grid=(steps + channels // block,),
        in_specs=[
            pl.BlockSpec(got_block, lambda j: (0, jnp.minimum(j, steps - 1), 0, 0, 0)),
            pl.BlockSpec(
                (2, block, span, total), lambda j: (0, jnp.maximum(j - steps, 0), 0, 0)
            ),
        ],
        out_specs=pl.BlockSpec(
            (2, block, total, total), lambda j: (0, jnp.maximum(j - steps, 0), 0, 0)
        ),
        out_shape=jax.ShapeDtypeStruct((2, channels, total, total), BF16),
        scratch_shapes=[pltpu.VMEM((2 * channels, span, total), BF16)],
        compiler_params=params(),
        cost_estimate=cost(1e10, 1e7),
        name="finish",
    )(early_got, late_rows)


def solution(mesh):
    in_specs = (P("inp", "chan", None), P("inp", None, None), P())
    out_specs = P(None, ("inp", "chan"), None, None)
    return jax.shard_map(
        on_device, mesh=mesh, in_specs=in_specs, out_specs=out_specs, check_vma=False
    )
```

```python
import math

import jax
import jax.numpy as jnp
import ml_dtypes
import numpy as np
from jax import lax
from jax.experimental import pallas as pl
from jax.experimental.pallas import tpu as pltpu
from jax.sharding import PartitionSpec as P

BAND = 2048
LOW = 1024
LANES = 128
RADIX = 64
HALF = 16
PAIR = 2
BLOCK = 8
CLASSES = RADIX // 2
ROOT = math.sqrt(0.5)
F32 = jnp.float32
BF16 = jnp.bfloat16
VMEM = 63 * 1024 * 1024


def stage_table(frame):
    high = BAND // RADIX
    lane = np.arange(LANES)
    table = np.zeros((CLASSES, 2, high, 2, 2, LANES))
    for q in range(CLASSES):
        for half in range(2):
            low = q if half == 0 else (RADIX - q if q else RADIX // 2)
            k = low + RADIX * (LOW // RADIX + np.arange(high))
            angle = 2.0 * np.pi * (np.outer(k, lane) % frame) / frame
            cos, sin = np.cos(angle), np.sin(angle)
            if q == 0:
                table[q, half, :, 0, half] = cos
                table[q, half, :, 1, half] = -sin
            elif half == 0:
                table[q, half, :, 0, 0] = cos
                table[q, half, :, 0, 1] = sin
                table[q, half, :, 1, 0] = -sin
                table[q, half, :, 1, 1] = cos
            else:
                table[q, half, :, 0, 0] = cos
                table[q, half, :, 0, 1] = -sin
                table[q, half, :, 1, 0] = -sin
                table[q, half, :, 1, 1] = -cos
    table = table / math.sqrt(frame)
    return table.reshape(CLASSES, 2 * high * 2, 2 * LANES)


def real_dft8(x):
    s = [x[j] + x[j + 4] for j in range(4)]
    d = [x[j] - x[j + 4] for j in range(4)]
    e0, e1 = s[0] + s[2], s[0] - s[2]
    o0, o1 = s[1] + s[3], s[3] - s[1]
    u, v = (d[1] - d[3]) * ROOT, (d[1] + d[3]) * ROOT
    return [
        (e0 + o0, None),
        (d[0] + u, -(d[2] + v)),
        (e1, o1),
        (d[0] - u, d[2] - v),
        (e0 - o0, None),
    ]


def complex_dft8(x):
    def add(a, b):
        return (a[0] + b[0], a[1] + b[1])

    def sub(a, b):
        return (a[0] - b[0], a[1] - b[1])

    def add_i(a, b):
        return (a[0] - b[1], a[1] + b[0])

    def sub_i(a, b):
        return (a[0] + b[1], a[1] - b[0])

    s = [add(x[j], x[j + 4]) for j in range(4)]
    d = [sub(x[j], x[j + 4]) for j in range(4)]
    e0, e1 = add(s[0], s[2]), sub(s[0], s[2])
    o0, o1 = add(s[1], s[3]), sub(s[1], s[3])
    p, m = sub(d[1], d[3]), add(d[1], d[3])
    b = ((p[0] + m[1]) * ROOT, (p[1] - m[0]) * ROOT)
    c = ((m[1] - p[0]) * ROOT, (-p[1] - m[0]) * ROOT)
    f, g = sub_i(d[0], d[2]), add_i(d[0], d[2])
    return [
        add(e0, o0),
        add(f, b),
        sub_i(e1, o1),
        add(g, c),
        sub(e0, o0),
        sub(f, b),
        add_i(e1, o1),
        sub(g, c),
    ]


def turned(value, step):
    angle = 2.0 * math.pi * (step % RADIX) / RADIX
    cos, sin = math.cos(angle), math.sin(angle)
    real, imag = value
    if imag is None:
        return (real * cos, real * -sin)
    if step % RADIX == 0:
        return value
    return (real * cos + imag * sin, imag * cos - real * sin)


def unrolled(count, copies, body):
    def step(i, carry):
        for copy in range(copies):
            body(i * copies + copy, copy)
        return carry

    lax.fori_loop(0, count // copies, step, 0)


def transform_rows(fir, mid, zed, half):
    halves = zed.shape[1] // (fir.shape[1] * HALF)

    def one(s, carry):
        for low in range(8):
            parts = real_dft8([fir[8 * high + low, s] for high in range(8)])
            mid[0, low] = parts[0][0]
            mid[7, low] = parts[4][0]
            for k in (1, 2, 3):
                value = turned(parts[k], low * k)
                mid[2 * k - 1, low] = value[0]
                mid[2 * k, low] = value[1]
        rows = pl.ds(pl.multiple_of((s * halves + half) * HALF, HALF), HALF)

        def put(q, half, value):
            zed[q, rows, half * LANES : (half + 1) * LANES] = value.astype(BF16)

        parts = real_dft8([mid[0, low] for low in range(8)])
        put(0, 0, parts[0][0])
        put(0, 1, parts[4][0])
        for m in (1, 2, 3):
            put(8 * m, 0, parts[m][0])
            put(8 * m, 1, parts[m][1])
        for k in (1, 2, 3):
            parts = complex_dft8([(mid[2 * k - 1, low], mid[2 * k, low]) for low in range(8)])
            for m in range(8):
                index = k + 8 * m
                if index < CLASSES:
                    put(index, 0, parts[m][0])
                    put(index, 1, parts[m][1])
                else:
                    put(RADIX - index, 0, parts[m][0])
                    put(RADIX - index, 1, -parts[m][1])
        parts = complex_dft8([turned((mid[7, low], None), 4 * low) for low in range(8)])
        for m in range(4):
            put(4 + 8 * m, 0, parts[m][0])
            put(4 + 8 * m, 1, parts[m][1])
        return carry

    lax.fori_loop(0, fir.shape[1], one, 0)


CHUNKS = 4
CONTRACT = (((1,), (1,)), ((), ()))


def fill(first, hist, keep, volt_in, taper_in, table_in, volt, taper, held, fir, mid, zed, sems):
    taps = taper.shape[0]
    in_dev, s_dev, frame = volt.shape
    halves = in_dev // HALF
    count = fir.shape[1]
    part = frame // CHUNKS
    wanted = [f for f in range(first - taps + 1, first + count) if f < s_dev]

    def volt_copy(h, j):
        where = (pl.ds(h * HALF, HALF), slice(None), pl.ds(pl.multiple_of(j * part, part), part))
        return pltpu.make_async_copy(volt_in.at[where], volt.at[where], sems.at[h * CHUNKS + j])

    taper_copy = pltpu.make_async_copy(taper_in, taper, sems.at[halves * CHUNKS])
    table_copy = pltpu.make_async_copy(table_in, held, sems.at[halves * CHUNKS + 1])
    taper_copy.start()
    for h in range(halves):
        for j in range(CHUNKS):
            volt_copy(h, j).start()
    table_copy.start()
    taper_copy.wait()

    def one_half(h, carry):
        inputs = pl.ds(pl.multiple_of(h * HALF, HALF), HALF)

        def one_chunk(j, carry):
            volt_copy(h, j).wait()

            def one(i, copy):
                a = j * (part // LANES) + i
                lanes = pl.ds(pl.multiple_of(a * LANES, LANES), LANES)
                by_time = jnp.swapaxes(volt[inputs, :, lanes], 0, 1)
                frames = {}
                for f in wanted:
                    if f >= 0:
                        frames[f] = by_time[f].astype(F32)
                    elif hist is not None:
                        frames[f] = hist[taps - 1 + f, inputs, lanes].astype(F32) * keep
                weights = [taper[t : t + 1, lanes] for t in range(taps)]
                for row in range(count):
                    total = None
                    for t in range(taps):
                        f = first + row + t - taps + 1
                        if f in frames:
                            term = weights[t] * frames[f]
                            total = term if total is None else total + term
                    fir[a, row] = total

            unrolled(part // LANES, 4, one)
            return carry

        lax.fori_loop(0, CHUNKS, one_chunk, 0)
        transform_rows(fir, mid, zed, h)
        return carry

    lax.fori_loop(0, halves, one_half, 0)
    table_copy.wait()


def carried_kernel(volt_in, taper_in, table_in, out, volt, taper, held, fir, mid, zed, sems):
    fill(
        volt.shape[1], None, None,
        volt_in, taper_in, table_in, volt, taper, held, fir, mid, zed, sems,
    )

    def one(q, copy):
        out[q] = jnp.dot(zed[q], held[q], preferred_element_type=F32).astype(BF16)

    unrolled(CLASSES, 4, one)


def spectra_kernel(first, boundary, *refs):
    if boundary:
        keep, hist, carried, unit, *refs = refs
        keep = keep[0]
    else:
        keep, hist = None, None
    volt_in, taper_in, table_in, out, volt, taper, held, fir, mid, zed, sems, wide = refs
    fill(
        first, hist, keep,
        volt_in, taper_in, table_in, volt, taper, held, fir, mid, zed, sems,
    )
    step = RADIX

    def one(q, copy):
        value = lax.dot_general(held[q], zed[q], CONTRACT, preferred_element_type=F32)
        if boundary:
            part = carried[q]
            short = zed.shape[1] - part.shape[0]
            part = jnp.concatenate([part, jnp.zeros((short, LANES), BF16)], axis=0)
            value = value + lax.dot_general(
                unit[...], part, CONTRACT, preferred_element_type=F32
            )
        wide[q] = value[:step].astype(BF16)
        wide[jnp.where(q == 0, CLASSES, RADIX - q)] = value[step:].astype(BF16)

    unrolled(CLASSES, 4, one)
    channels = out.shape[2] // 2
    split = RADIX // channels
    high = HALF // 2

    def two(b, copy):
        here = pl.ds(pl.multiple_of(b * HALF, HALF), HALF)
        for tile in range(out.shape[1]):
            lanes = slice(tile * LANES, (tile + 1) * LANES)
            for first_k in range(0, RADIX, HALF):
                value = jnp.swapaxes(wide[first_k : first_k + HALF, here, lanes], 0, 1)
                u, k = divmod(first_k, channels)
                for j in range(HALF):
                    start = j % 2 * channels + k
                    out[(b * high + j // 2) * split + u, tile, start : start + HALF, :] = value[j]

    unrolled(step // HALF, 1, two)


def reorder(got, first, put):
    n_inp, _, sets, rows, _ = got.shape
    blocks = HALF // (sets * PAIR)
    width = LANES // blocks
    block = lax.broadcasted_iota(jnp.int32, (HALF, LANES), 1) // width
    masks = {d: (block & d) == 0 for d in (1, 2)}
    assert blocks == 4

    def one(b, copy):
        here = pl.ds(pl.multiple_of(b * HALF, HALF), HALF)
        for tile in range(n_inp // blocks):
            pieces = []
            for c in range(PAIR):
                for part in range(sets):
                    x = [got[tile * blocks + p, first + c, part, here, :] for p in range(blocks)]
                    for d in (1, 2):
                        for p in range(blocks):
                            if p & d == 0:
                                low, up = x[p], x[p | d]
                                x[p] = jnp.where(masks[d], low, pltpu.roll(up, width * d, 1))
                                x[p | d] = jnp.where(
                                    masks[d], pltpu.roll(low, LANES - width * d, 1), up
                                )
                    pieces += x
            value = jnp.swapaxes(jnp.stack(pieces), 0, 1)
            for j in range(HALF):
                put(b * HALF + j, tile, value[j])

    unrolled(rows // HALF, 2, one)


def order_kernel(got, out):
    def step(j, carry):
        def put(r, tile, value):
            out[r, pl.ds(pl.multiple_of(j * HALF, HALF), HALF), tile * LANES : (tile + 1) * LANES] = value

        reorder(got, j * PAIR, put)
        return carry

    lax.fori_loop(0, got.shape[1] // PAIR, step, 0)


def finish_kernel(scale, got_in, late_in, out_ref, got, late, early, out, sems):
    steps = got.shape[1] // PAIR
    channels, width = out.shape[1], out.shape[-1]
    count = channels // BLOCK

    def got_copy(j):
        where = (slice(None), pl.ds(j * PAIR, PAIR))
        return pltpu.make_async_copy(got_in.at[where], got.at[where], sems.at[j])

    def out_copy(j):
        where = (slice(None), pl.ds(j * BLOCK, BLOCK))
        return pltpu.make_async_copy(out.at[where], out_ref.at[where], sems.at[j])

    for j in range(steps):
        got_copy(j).start()
    late_copy = pltpu.make_async_copy(late_in, late, sems.at[steps])
    late_copy.start()

    def order(j, carry):
        got_copy(j).wait()

        def put(r, tile, value):
            early[r, pl.ds(pl.multiple_of(j * HALF, HALF), HALF), tile * LANES : (tile + 1) * LANES] = value

        reorder(got, j * PAIR, put)
        return carry

    lax.fori_loop(0, steps, order, 0)
    late_copy.wait()

    def gram(j, carry):
        for i in range(BLOCK):
            k = j * BLOCK + i
            real = jnp.concatenate([late[k], early[k]], axis=0)
            imag = jnp.concatenate([late[channels + k], early[channels + k]], axis=0)
            left = jnp.concatenate([real, imag], axis=0)
            right = jnp.concatenate([-imag, real], axis=0)
            value = lax.dot_general(
                left,
                jnp.concatenate([left, right], axis=1),
                (((0,), (0,)), ((), ())),
                preferred_element_type=F32,
            )
            value = value * scale
            out[0, k] = value[:, :width].astype(BF16)
            out[1, k] = value[:, width:].astype(BF16)
        out_copy(j).start()
        return carry

    lax.fori_loop(0, count, gram, 0)

    def finish(j, carry):
        out_copy(j).wait()
        return carry

    lax.fori_loop(0, count, finish, 0)


def params():
    return pltpu.CompilerParams(vmem_limit_bytes=VMEM)


def cost(flops, moved):
    return pl.CostEstimate(flops=int(flops), bytes_accessed=int(moved), transcendentals=0)


def on_device(voltages, history, taper):
    in_dev, s_dev, frame = voltages.shape
    taps = taper.shape[0]
    n_inp = lax.axis_size("inp")
    n_chan = lax.axis_size("chan")
    groups = n_inp * n_chan
    channels = BAND // groups
    total = n_inp * in_dev
    times = s_dev // 2
    early = taps - 1
    blocks = LANES // in_dev
    sets = times // blocks
    span = n_chan * times
    assert frame == RADIX * LANES and in_dev == 2 * HALF and PAIR * times == HALF
    assert early == times - 1 and RADIX % channels == 0 and n_inp % blocks == 0
    assert n_chan % PAIR == 0 and channels % BLOCK == 0

    outputs = 2 * BAND // CLASSES
    stage = stage_table(frame).astype(np.float32).astype(ml_dtypes.bfloat16)
    table = jnp.asarray(stage)
    upright = jnp.asarray(np.ascontiguousarray(stage.transpose(0, 2, 1)))
    unit = jnp.asarray(np.eye(outputs).astype(ml_dtypes.bfloat16))
    assert table.shape == (CLASSES, outputs, 2 * LANES) and outputs == LANES

    away = pl.BlockSpec(memory_space=pl.ANY)
    near = pl.BlockSpec(memory_space=pltpu.VMEM)

    def scratch(count, shape):
        return [
            pltpu.VMEM(voltages.shape, BF16),
            pltpu.VMEM(taper.shape, F32),
            pltpu.VMEM(shape, BF16),
            pltpu.VMEM((RADIX, count, HALF, LANES), F32),
            pltpu.VMEM((8, 8, HALF, LANES), F32),
            pltpu.VMEM((CLASSES, count * in_dev, 2 * LANES), BF16),
            pltpu.SemaphoreType.DMA((2 * CHUNKS + 2,)),
        ]

    wide = [pltpu.VMEM((RADIX, RADIX, times * in_dev), BF16)]
    carried = pl.pallas_call(
        carried_kernel,
        in_specs=[away] * 3,
        out_specs=near,
        out_shape=jax.ShapeDtypeStruct((CLASSES, early * in_dev, outputs), BF16),
        scratch_shapes=scratch(early, upright.shape),
        compiler_params=params(),
        cost_estimate=cost(1e10, 2e7),
        name="carried",
    )(voltages, taper, upright)
    carried, later_taper = lax.optimization_barrier((carried, taper))
    carried = lax.ppermute(carried, "chan", [(i, i + 1) for i in range(n_chan - 1)])

    send_shape = jax.ShapeDtypeStruct((groups, sets, 2 * channels, LANES), BF16)
    late_send = pl.pallas_call(
        lambda *refs: spectra_kernel(times, False, *refs),
        in_specs=[away] * 3,
        out_specs=near,
        out_shape=send_shape,
        scratch_shapes=scratch(times, table.shape) + wide,
        compiler_params=params(),
        cost_estimate=cost(5e10, 4e7),
        name="late",
    )(voltages, later_taper, table)

    def exchange(value):
        value = lax.all_to_all(value, ("inp", "chan"), split_axis=0, concat_axis=0, tiled=True)
        return value.reshape(n_inp, n_chan, sets, 2 * channels, LANES)

    late_got = exchange(late_send)

    keep = (lax.axis_index("chan") == 0).astype(F32).reshape(1)
    early_send = pl.pallas_call(
        lambda *refs: spectra_kernel(0, True, *refs),
        in_specs=[pl.BlockSpec(memory_space=pltpu.SMEM), near, near, near] + [away] * 3,
        out_specs=near,
        out_shape=send_shape,
        scratch_shapes=scratch(times, table.shape) + wide,
        compiler_params=params(),
        cost_estimate=cost(2e11, 4e7),
        name="early",
    )(keep, jnp.transpose(history, (1, 0, 2)), carried, unit, voltages, taper, table)
    early_got = exchange(early_send)

    late_rows = pl.pallas_call(
        order_kernel,
        in_specs=[near],
        out_specs=near,
        out_shape=jax.ShapeDtypeStruct((2 * channels, span, total), BF16),
        compiler_params=params(),
        cost_estimate=cost(1e4, 1e4),
        name="order",
    )(late_got)

    held = pltpu.VMEM((2 * channels, span, total), BF16)
    return pl.pallas_call(
        lambda *refs: finish_kernel(1.0 / (n_chan * s_dev), *refs),
        in_specs=[away, away],
        out_specs=away,
        out_shape=jax.ShapeDtypeStruct((2, channels, total, total), BF16),
        scratch_shapes=[
            pltpu.VMEM(early_got.shape, BF16),
            held,
            held,
            pltpu.VMEM((2, channels, total, total), BF16),
            pltpu.SemaphoreType.DMA((max(n_chan // PAIR + 1, channels // BLOCK),)),
        ],
        compiler_params=params(),
        cost_estimate=cost(1e10, 1e7),
        name="finish",
    )(early_got, late_rows)


def solution(mesh):
    in_specs = (P("inp", "chan", None), P("inp", None, None), P())
    out_specs = P(None, ("inp", "chan"), None, None)
    return jax.shard_map(
        on_device, mesh=mesh, in_specs=in_specs, out_specs=out_specs, check_vma=False
    )
```

```python
import math

import jax
import jax.numpy as jnp
import ml_dtypes
import numpy as np
from jax import lax
from jax.experimental import pallas as pl
from jax.experimental.pallas import tpu as pltpu
from jax.sharding import PartitionSpec as P

BAND = 2048
LOW = 1024
LANES = 128
RADIX = 64
HALF = 16
PAIR = 2
CLASSES = RADIX // 2
ROOT = math.sqrt(0.5)
F32 = jnp.float32
BF16 = jnp.bfloat16
VMEM = 63 * 1024 * 1024


def stage_table(frame):
    high = BAND // RADIX
    lane = np.arange(LANES)
    table = np.zeros((CLASSES, 2, high, 2, 2, LANES))
    for q in range(CLASSES):
        for half in range(2):
            low = q if half == 0 else (RADIX - q if q else RADIX // 2)
            k = low + RADIX * (LOW // RADIX + np.arange(high))
            angle = 2.0 * np.pi * (np.outer(k, lane) % frame) / frame
            cos, sin = np.cos(angle), np.sin(angle)
            if q == 0:
                table[q, half, :, 0, half] = cos
                table[q, half, :, 1, half] = -sin
            elif half == 0:
                table[q, half, :, 0, 0] = cos
                table[q, half, :, 0, 1] = sin
                table[q, half, :, 1, 0] = -sin
                table[q, half, :, 1, 1] = cos
            else:
                table[q, half, :, 0, 0] = cos
                table[q, half, :, 0, 1] = -sin
                table[q, half, :, 1, 0] = -sin
                table[q, half, :, 1, 1] = -cos
    table = table / math.sqrt(frame)
    return table.reshape(CLASSES, 2 * high * 2, 2 * LANES)


def real_dft8(x):
    s = [x[j] + x[j + 4] for j in range(4)]
    d = [x[j] - x[j + 4] for j in range(4)]
    e0, e1 = s[0] + s[2], s[0] - s[2]
    o0, o1 = s[1] + s[3], s[3] - s[1]
    u, v = (d[1] - d[3]) * ROOT, (d[1] + d[3]) * ROOT
    return [
        (e0 + o0, None),
        (d[0] + u, -(d[2] + v)),
        (e1, o1),
        (d[0] - u, d[2] - v),
        (e0 - o0, None),
    ]


def complex_dft8(x):
    def add(a, b):
        return (a[0] + b[0], a[1] + b[1])

    def sub(a, b):
        return (a[0] - b[0], a[1] - b[1])

    def add_i(a, b):
        return (a[0] - b[1], a[1] + b[0])

    def sub_i(a, b):
        return (a[0] + b[1], a[1] - b[0])

    s = [add(x[j], x[j + 4]) for j in range(4)]
    d = [sub(x[j], x[j + 4]) for j in range(4)]
    e0, e1 = add(s[0], s[2]), sub(s[0], s[2])
    o0, o1 = add(s[1], s[3]), sub(s[1], s[3])
    p, m = sub(d[1], d[3]), add(d[1], d[3])
    b = ((p[0] + m[1]) * ROOT, (p[1] - m[0]) * ROOT)
    c = ((m[1] - p[0]) * ROOT, (-p[1] - m[0]) * ROOT)
    f, g = sub_i(d[0], d[2]), add_i(d[0], d[2])
    return [
        add(e0, o0),
        add(f, b),
        sub_i(e1, o1),
        add(g, c),
        sub(e0, o0),
        sub(f, b),
        add_i(e1, o1),
        sub(g, c),
    ]


def turned(value, step):
    angle = 2.0 * math.pi * (step % RADIX) / RADIX
    cos, sin = math.cos(angle), math.sin(angle)
    real, imag = value
    if imag is None:
        return (real * cos, real * -sin)
    if step % RADIX == 0:
        return value
    return (real * cos + imag * sin, imag * cos - real * sin)


def unrolled(count, copies, body):
    def step(i, carry):
        for copy in range(copies):
            body(i * copies + copy, copy)
        return carry

    lax.fori_loop(0, count // copies, step, 0)


def transform_rows(fir, mid, zed, half):
    halves = zed.shape[1] // (fir.shape[1] * HALF)

    def one(s, carry):
        for low in range(8):
            parts = real_dft8([fir[8 * high + low, s] for high in range(8)])
            mid[0, low] = parts[0][0]
            mid[7, low] = parts[4][0]
            for k in (1, 2, 3):
                value = turned(parts[k], low * k)
                mid[2 * k - 1, low] = value[0]
                mid[2 * k, low] = value[1]
        rows = pl.ds(pl.multiple_of((s * halves + half) * HALF, HALF), HALF)

        def put(q, half, value):
            zed[q, rows, half * LANES : (half + 1) * LANES] = value.astype(BF16)

        parts = real_dft8([mid[0, low] for low in range(8)])
        put(0, 0, parts[0][0])
        put(0, 1, parts[4][0])
        for m in (1, 2, 3):
            put(8 * m, 0, parts[m][0])
            put(8 * m, 1, parts[m][1])
        for k in (1, 2, 3):
            parts = complex_dft8([(mid[2 * k - 1, low], mid[2 * k, low]) for low in range(8)])
            for m in range(8):
                index = k + 8 * m
                if index < CLASSES:
                    put(index, 0, parts[m][0])
                    put(index, 1, parts[m][1])
                else:
                    put(RADIX - index, 0, parts[m][0])
                    put(RADIX - index, 1, -parts[m][1])
        parts = complex_dft8([turned((mid[7, low], None), 4 * low) for low in range(8)])
        for m in range(4):
            put(4 + 8 * m, 0, parts[m][0])
            put(4 + 8 * m, 1, parts[m][1])
        return carry

    lax.fori_loop(0, fir.shape[1], one, 0)


CHUNKS = 4
CONTRACT = (((1,), (1,)), ((), ()))


def fill(first, hist, keep, volt_in, taper_in, table_in, volt, taper, held, fir, mid, zed, sems):
    taps = taper.shape[0]
    in_dev, s_dev, frame = volt.shape
    halves = in_dev // HALF
    count = fir.shape[1]
    part = frame // CHUNKS
    wanted = [f for f in range(first - taps + 1, first + count) if f < s_dev]

    def volt_copy(h, j):
        where = (pl.ds(h * HALF, HALF), slice(None), pl.ds(pl.multiple_of(j * part, part), part))
        return pltpu.make_async_copy(volt_in.at[where], volt.at[where], sems.at[h * CHUNKS + j])

    taper_copy = pltpu.make_async_copy(taper_in, taper, sems.at[halves * CHUNKS])
    table_copy = pltpu.make_async_copy(table_in, held, sems.at[halves * CHUNKS + 1])
    taper_copy.start()
    for h in range(halves):
        for j in range(CHUNKS):
            volt_copy(h, j).start()
    table_copy.start()
    taper_copy.wait()

    def one_half(h, carry):
        inputs = pl.ds(pl.multiple_of(h * HALF, HALF), HALF)

        def one_chunk(j, carry):
            volt_copy(h, j).wait()

            def one(i, copy):
                a = j * (part // LANES) + i
                lanes = pl.ds(pl.multiple_of(a * LANES, LANES), LANES)
                by_time = jnp.swapaxes(volt[inputs, :, lanes], 0, 1)
                frames = {}
                for f in wanted:
                    if f >= 0:
                        frames[f] = by_time[f].astype(F32)
                    elif hist is not None:
                        frames[f] = hist[taps - 1 + f, inputs, lanes].astype(F32) * keep
                weights = [taper[t : t + 1, lanes] for t in range(taps)]
                for row in range(count):
                    total = None
                    for t in range(taps):
                        f = first + row + t - taps + 1
                        if f in frames:
                            term = weights[t] * frames[f]
                            total = term if total is None else total + term
                    fir[a, row] = total

            unrolled(part // LANES, 8, one)
            return carry

        lax.fori_loop(0, CHUNKS, one_chunk, 0)
        transform_rows(fir, mid, zed, h)
        return carry

    lax.fori_loop(0, halves, one_half, 0)
    table_copy.wait()


def carried_kernel(volt_in, taper_in, table_in, out_ref, *scratch):
    *scratch, out, out_sems = scratch
    volt, taper, held, fir, mid, zed, sems = scratch
    fill(
        volt.shape[1], None, None,
        volt_in, taper_in, table_in, volt, taper, held, fir, mid, zed, sems,
    )
    block = CLASSES // CHUNKS

    def out_copy(j):
        where = pl.ds(j * block, block)
        return pltpu.make_async_copy(out.at[where], out_ref.at[where], out_sems.at[j])

    def some(j, carry):
        for i in range(block):
            q = j * block + i
            out[q] = jnp.dot(zed[q], held[q], preferred_element_type=F32).astype(BF16)
        out_copy(j).start()
        return carry

    lax.fori_loop(0, CHUNKS, some, 0)

    def finish(j, carry):
        out_copy(j).wait()
        return carry

    lax.fori_loop(0, CHUNKS, finish, 0)


def spectra_kernel(first, boundary, *refs):
    if boundary:
        keep, hist, carried, unit, *refs = refs
        keep = keep[0]
    else:
        keep, hist = None, None
    volt_in, taper_in, table_in, out, volt, taper, held, fir, mid, zed, sems, wide = refs
    fill(
        first, hist, keep,
        volt_in, taper_in, table_in, volt, taper, held, fir, mid, zed, sems,
    )
    step = RADIX

    def one(q, copy):
        value = lax.dot_general(held[q], zed[q], CONTRACT, preferred_element_type=F32)
        if boundary:
            part = carried[q]
            short = zed.shape[1] - part.shape[0]
            part = jnp.concatenate([part, jnp.zeros((short, LANES), BF16)], axis=0)
            value = value + lax.dot_general(
                unit[...], part, CONTRACT, preferred_element_type=F32
            )
        wide[q] = value[:step].astype(BF16)
        wide[jnp.where(q == 0, CLASSES, RADIX - q)] = value[step:].astype(BF16)

    unrolled(CLASSES, 4, one)
    channels = out.shape[2] // 2
    split = RADIX // channels
    high = HALF // 2

    def two(b, copy):
        here = pl.ds(pl.multiple_of(b * HALF, HALF), HALF)
        for tile in range(out.shape[1]):
            lanes = slice(tile * LANES, (tile + 1) * LANES)
            for first_k in range(0, RADIX, HALF):
                value = jnp.swapaxes(wide[first_k : first_k + HALF, here, lanes], 0, 1)
                u, k = divmod(first_k, channels)
                for j in range(HALF):
                    start = j % 2 * channels + k
                    out[(b * high + j // 2) * split + u, tile, start : start + HALF, :] = value[j]

    unrolled(step // HALF, 1, two)


def reorder(got, row, first, put):
    n_inp, _, sets, _, _ = got.shape
    blocks = HALF // (sets * PAIR)
    width = LANES // blocks
    block = lax.broadcasted_iota(jnp.int32, (HALF, LANES), 1) // width
    masks = {d: (block & d) == 0 for d in (1, 2)}
    here = pl.ds(pl.multiple_of(row, HALF), HALF)
    assert blocks == 4
    for tile in range(n_inp // blocks):
        pieces = []
        for c in range(PAIR):
            for part in range(sets):
                x = [got[tile * blocks + p, first + c, part, here, :] for p in range(blocks)]
                for d in (1, 2):
                    for p in range(blocks):
                        if p & d == 0:
                            low, up = x[p], x[p | d]
                            x[p] = jnp.where(masks[d], low, pltpu.roll(up, width * d, 1))
                            x[p | d] = jnp.where(
                                masks[d], pltpu.roll(low, LANES - width * d, 1), up
                            )
                pieces += x
        value = jnp.swapaxes(jnp.stack(pieces), 0, 1)
        for i in range(HALF):
            put(i, tile, value[i])


def reorder_unit(got, out, block, u):
    steps = got.shape[1] // PAIR
    channels = got.shape[3] // 2
    pair = lax.rem(u, steps)
    row = lax.div(u, steps) * channels + block * HALF
    times = pl.ds(pl.multiple_of(pair * HALF, HALF), HALF)

    def put(i, tile, value):
        out[row + i, times, tile * LANES : (tile + 1) * LANES] = value

    reorder(got, row, pair * PAIR, put)


def order_kernel(got, out):
    units = 2 * (got.shape[1] // PAIR)
    count = got.shape[3] // 2 // HALF * units

    def one(m, copy):
        reorder_unit(got, out, lax.div(m, units), lax.rem(m, units))

    unrolled(count, 2, one)


def finish_kernel(scale, got_in, late_in, out_ref, got, late, early, out, sems):
    steps = got.shape[1] // PAIR
    units = 2 * steps
    channels, width = out.shape[1], out.shape[-1]
    blocks = channels // HALF
    each = HALF // units

    got_copy = pltpu.make_async_copy(got_in, got, sems.at[blocks])
    late_copy = pltpu.make_async_copy(late_in, late, sems.at[blocks + 1])

    def out_copy(j):
        where = (slice(None), pl.ds(j * HALF, HALF))
        return pltpu.make_async_copy(out.at[where], out_ref.at[where], sems.at[j])

    got_copy.start()
    late_copy.start()
    got_copy.wait()

    def gram(k):
        real = jnp.concatenate([late[k], early[k]], axis=0)
        imag = jnp.concatenate([late[channels + k], early[channels + k]], axis=0)
        left = jnp.concatenate([real, imag], axis=0)
        right = jnp.concatenate([-imag, real], axis=0)
        value = lax.dot_general(
            left,
            jnp.concatenate([left, right], axis=1),
            (((0,), (0,)), ((), ())),
            preferred_element_type=F32,
        )
        value = value * scale
        out[0, k] = value[:, :width].astype(BF16)
        out[1, k] = value[:, width:].astype(BF16)

    def first(u, copy):
        reorder_unit(got, early, 0, u)

    unrolled(units, 2, first)
    late_copy.wait()

    def block_step(b, carry):
        def unit(u, copy):
            for i in range(each):
                gram((b - 1) * HALF + u * each + i)
            reorder_unit(got, early, b, u)

        unrolled(units, 2, unit)
        out_copy(b - 1).start()
        return carry

    lax.fori_loop(1, blocks, block_step, 0)

    def last(u, copy):
        for i in range(each):
            gram((blocks - 1) * HALF + u * each + i)

    unrolled(units, 2, last)
    out_copy(blocks - 1).start()

    def finish(j, carry):
        out_copy(j).wait()
        return carry

    lax.fori_loop(0, blocks, finish, 0)


def params():
    return pltpu.CompilerParams(vmem_limit_bytes=VMEM)


def cost(flops, moved):
    return pl.CostEstimate(flops=int(flops), bytes_accessed=int(moved), transcendentals=0)


def on_device(voltages, history, taper):
    in_dev, s_dev, frame = voltages.shape
    taps = taper.shape[0]
    n_inp = lax.axis_size("inp")
    n_chan = lax.axis_size("chan")
    groups = n_inp * n_chan
    channels = BAND // groups
    total = n_inp * in_dev
    times = s_dev // 2
    early = taps - 1
    blocks = LANES // in_dev
    sets = times // blocks
    span = n_chan * times
    assert frame == RADIX * LANES and in_dev == 2 * HALF and PAIR * times == HALF
    assert early == times - 1 and RADIX % channels == 0 and n_inp % blocks == 0
    assert n_chan % PAIR == 0 and channels % HALF == 0

    outputs = 2 * BAND // CLASSES
    stage = stage_table(frame).astype(np.float32).astype(ml_dtypes.bfloat16)
    table = jnp.asarray(stage)
    upright = jnp.asarray(np.ascontiguousarray(stage.transpose(0, 2, 1)))
    unit = jnp.asarray(np.eye(outputs).astype(ml_dtypes.bfloat16))
    assert table.shape == (CLASSES, outputs, 2 * LANES) and outputs == LANES

    away = pl.BlockSpec(memory_space=pl.ANY)
    near = pl.BlockSpec(memory_space=pltpu.VMEM)

    def scratch(count, shape):
        return [
            pltpu.VMEM(voltages.shape, BF16),
            pltpu.VMEM(taper.shape, F32),
            pltpu.VMEM(shape, BF16),
            pltpu.VMEM((RADIX, count, HALF, LANES), F32),
            pltpu.VMEM((8, 8, HALF, LANES), F32),
            pltpu.VMEM((CLASSES, count * in_dev, 2 * LANES), BF16),
            pltpu.SemaphoreType.DMA((2 * CHUNKS + 2,)),
        ]

    wide = [pltpu.VMEM((RADIX, RADIX, times * in_dev), BF16)]
    carried = pl.pallas_call(
        carried_kernel,
        in_specs=[away] * 3,
        out_specs=away,
        out_shape=jax.ShapeDtypeStruct((CLASSES, early * in_dev, outputs), BF16),
        scratch_shapes=scratch(early, upright.shape)
        + [
            pltpu.VMEM((CLASSES, early * in_dev, outputs), BF16),
            pltpu.SemaphoreType.DMA((CHUNKS,)),
        ],
        compiler_params=params(),
        cost_estimate=cost(1e10, 2e7),
        name="carried",
    )(voltages, taper, upright)
    carried, later_taper = lax.optimization_barrier((carried, taper))
    carried = lax.ppermute(carried, "chan", [(i, i + 1) for i in range(n_chan - 1)])

    send_shape = jax.ShapeDtypeStruct((groups, sets, 2 * channels, LANES), BF16)
    late_send = pl.pallas_call(
        lambda *refs: spectra_kernel(times, False, *refs),
        in_specs=[away] * 3,
        out_specs=near,
        out_shape=send_shape,
        scratch_shapes=scratch(times, table.shape) + wide,
        compiler_params=params(),
        cost_estimate=cost(5e10, 4e7),
        name="late",
    )(voltages, later_taper, table)

    def exchange(value):
        value = lax.all_to_all(value, ("inp", "chan"), split_axis=0, concat_axis=0, tiled=True)
        return value.reshape(n_inp, n_chan, sets, 2 * channels, LANES)

    late_got = exchange(late_send)

    keep = (lax.axis_index("chan") == 0).astype(F32).reshape(1)
    early_send = pl.pallas_call(
        lambda *refs: spectra_kernel(0, True, *refs),
        in_specs=[pl.BlockSpec(memory_space=pltpu.SMEM), near, near, near] + [away] * 3,
        out_specs=near,
        out_shape=send_shape,
        scratch_shapes=scratch(times, table.shape) + wide,
        compiler_params=params(),
        cost_estimate=cost(2e11, 4e7),
        name="early",
    )(keep, jnp.transpose(history, (1, 0, 2)), carried, unit, voltages, taper, table)
    early_got = exchange(early_send)

    late_rows = pl.pallas_call(
        order_kernel,
        in_specs=[near],
        out_specs=near,
        out_shape=jax.ShapeDtypeStruct((2 * channels, span, total), BF16),
        compiler_params=params(),
        cost_estimate=cost(1e4, 1e4),
        name="order",
    )(late_got)

    held = pltpu.VMEM((2 * channels, span, total), BF16)
    return pl.pallas_call(
        lambda *refs: finish_kernel(1.0 / (n_chan * s_dev), *refs),
        in_specs=[away, away],
        out_specs=away,
        out_shape=jax.ShapeDtypeStruct((2, channels, total, total), BF16),
        scratch_shapes=[
            pltpu.VMEM(early_got.shape, BF16),
            held,
            held,
            pltpu.VMEM((2, channels, total, total), BF16),
            pltpu.SemaphoreType.DMA((channels // HALF + 2,)),
        ],
        compiler_params=params(),
        cost_estimate=cost(1e10, 1e7),
        name="finish",
    )(early_got, late_rows)


def solution(mesh):
    in_specs = (P("inp", "chan", None), P("inp", None, None), P())
    out_specs = P(None, ("inp", "chan"), None, None)
    return jax.shard_map(
        on_device, mesh=mesh, in_specs=in_specs, out_specs=out_specs, check_vma=False
    )
```

```python
import math

import jax
import jax.numpy as jnp
import ml_dtypes
import numpy as np
from jax import lax
from jax.experimental import pallas as pl
from jax.experimental.pallas import tpu as pltpu
from jax.sharding import PartitionSpec as P

BAND = 2048
LOW = 1024
LANES = 128
RADIX = 64
HALF = 16
PAIR = 2
BLOCK = 8
CLASSES = RADIX // 2
ROOT = math.sqrt(0.5)
F32 = jnp.float32
BF16 = jnp.bfloat16
VMEM = 63 * 1024 * 1024


def stage_table(frame):
    high = BAND // RADIX
    lane = np.arange(LANES)
    table = np.zeros((CLASSES, 2, high, 2, 2, LANES))
    for q in range(CLASSES):
        for half in range(2):
            low = q if half == 0 else (RADIX - q if q else RADIX // 2)
            k = low + RADIX * (LOW // RADIX + np.arange(high))
            angle = 2.0 * np.pi * (np.outer(k, lane) % frame) / frame
            cos, sin = np.cos(angle), np.sin(angle)
            if q == 0:
                table[q, half, :, 0, half] = cos
                table[q, half, :, 1, half] = -sin
            elif half == 0:
                table[q, half, :, 0, 0] = cos
                table[q, half, :, 0, 1] = sin
                table[q, half, :, 1, 0] = -sin
                table[q, half, :, 1, 1] = cos
            else:
                table[q, half, :, 0, 0] = cos
                table[q, half, :, 0, 1] = -sin
                table[q, half, :, 1, 0] = -sin
                table[q, half, :, 1, 1] = -cos
    table = table / math.sqrt(frame)
    return table.reshape(CLASSES, 2 * high * 2, 2 * LANES)


def real_dft8(x):
    s = [x[j] + x[j + 4] for j in range(4)]
    d = [x[j] - x[j + 4] for j in range(4)]
    e0, e1 = s[0] + s[2], s[0] - s[2]
    o0, o1 = s[1] + s[3], s[3] - s[1]
    u, v = (d[1] - d[3]) * ROOT, (d[1] + d[3]) * ROOT
    return [
        (e0 + o0, None),
        (d[0] + u, -(d[2] + v)),
        (e1, o1),
        (d[0] - u, d[2] - v),
        (e0 - o0, None),
    ]


def complex_dft8(x):
    def add(a, b):
        return (a[0] + b[0], a[1] + b[1])

    def sub(a, b):
        return (a[0] - b[0], a[1] - b[1])

    def add_i(a, b):
        return (a[0] - b[1], a[1] + b[0])

    def sub_i(a, b):
        return (a[0] + b[1], a[1] - b[0])

    s = [add(x[j], x[j + 4]) for j in range(4)]
    d = [sub(x[j], x[j + 4]) for j in range(4)]
    e0, e1 = add(s[0], s[2]), sub(s[0], s[2])
    o0, o1 = add(s[1], s[3]), sub(s[1], s[3])
    p, m = sub(d[1], d[3]), add(d[1], d[3])
    b = ((p[0] + m[1]) * ROOT, (p[1] - m[0]) * ROOT)
    c = ((m[1] - p[0]) * ROOT, (-p[1] - m[0]) * ROOT)
    f, g = sub_i(d[0], d[2]), add_i(d[0], d[2])
    return [
        add(e0, o0),
        add(f, b),
        sub_i(e1, o1),
        add(g, c),
        sub(e0, o0),
        sub(f, b),
        add_i(e1, o1),
        sub(g, c),
    ]


def turned(value, step):
    angle = 2.0 * math.pi * (step % RADIX) / RADIX
    cos, sin = math.cos(angle), math.sin(angle)
    real, imag = value
    if imag is None:
        return (real * cos, real * -sin)
    if step % RADIX == 0:
        return value
    return (real * cos + imag * sin, imag * cos - real * sin)


def unrolled(count, copies, body):
    def step(i, carry):
        for copy in range(copies):
            body(i * copies + copy, copy)
        return carry

    lax.fori_loop(0, count // copies, step, 0)


def transform_rows(fir, mid, zed, half):
    halves = zed.shape[1] // (fir.shape[1] * HALF)

    def one(s, carry):
        for low in range(8):
            parts = real_dft8([fir[8 * high + low, s] for high in range(8)])
            mid[0, low] = parts[0][0]
            mid[7, low] = parts[4][0]
            for k in (1, 2, 3):
                value = turned(parts[k], low * k)
                mid[2 * k - 1, low] = value[0]
                mid[2 * k, low] = value[1]
        rows = pl.ds(pl.multiple_of((s * halves + half) * HALF, HALF), HALF)

        def put(q, half, value):
            zed[q, rows, half * LANES : (half + 1) * LANES] = value.astype(BF16)

        parts = real_dft8([mid[0, low] for low in range(8)])
        put(0, 0, parts[0][0])
        put(0, 1, parts[4][0])
        for m in (1, 2, 3):
            put(8 * m, 0, parts[m][0])
            put(8 * m, 1, parts[m][1])
        for k in (1, 2, 3):
            parts = complex_dft8([(mid[2 * k - 1, low], mid[2 * k, low]) for low in range(8)])
            for m in range(8):
                index = k + 8 * m
                if index < CLASSES:
                    put(index, 0, parts[m][0])
                    put(index, 1, parts[m][1])
                else:
                    put(RADIX - index, 0, parts[m][0])
                    put(RADIX - index, 1, -parts[m][1])
        parts = complex_dft8([turned((mid[7, low], None), 4 * low) for low in range(8)])
        for m in range(4):
            put(4 + 8 * m, 0, parts[m][0])
            put(4 + 8 * m, 1, parts[m][1])
        return carry

    lax.fori_loop(0, fir.shape[1], one, 0)


CHUNKS = 4
CONTRACT = (((1,), (1,)), ((), ()))


def fill(first, hist, keep, volt_in, taper_in, table_in, volt, taper, held, fir, mid, zed, sems):
    taps = taper.shape[0]
    in_dev, s_dev, frame = volt.shape
    halves = in_dev // HALF
    count = fir.shape[1]
    part = frame // CHUNKS
    wanted = [f for f in range(first - taps + 1, first + count) if f < s_dev]

    def volt_copy(h, j):
        where = (pl.ds(h * HALF, HALF), slice(None), pl.ds(pl.multiple_of(j * part, part), part))
        return pltpu.make_async_copy(volt_in.at[where], volt.at[where], sems.at[h * CHUNKS + j])

    taper_copy = pltpu.make_async_copy(taper_in, taper, sems.at[halves * CHUNKS])
    table_copy = pltpu.make_async_copy(table_in, held, sems.at[halves * CHUNKS + 1])
    taper_copy.start()
    for h in range(halves):
        for j in range(CHUNKS):
            volt_copy(h, j).start()
    table_copy.start()
    taper_copy.wait()

    def one_half(h, carry):
        inputs = pl.ds(pl.multiple_of(h * HALF, HALF), HALF)

        def one_chunk(j, carry):
            volt_copy(h, j).wait()

            def one(i, copy):
                a = j * (part // LANES) + i
                lanes = pl.ds(pl.multiple_of(a * LANES, LANES), LANES)
                by_time = jnp.swapaxes(volt[inputs, :, lanes], 0, 1)
                frames = {}
                for f in wanted:
                    if f >= 0:
                        frames[f] = by_time[f].astype(F32)
                    elif hist is not None:
                        frames[f] = hist[taps - 1 + f, inputs, lanes].astype(F32) * keep
                weights = [taper[t : t + 1, lanes] for t in range(taps)]
                for row in range(count):
                    total = None
                    for t in range(taps):
                        f = first + row + t - taps + 1
                        if f in frames:
                            term = weights[t] * frames[f]
                            total = term if total is None else total + term
                    fir[a, row] = total

            unrolled(part // LANES, 8, one)
            return carry

        lax.fori_loop(0, CHUNKS, one_chunk, 0)
        transform_rows(fir, mid, zed, h)
        return carry

    lax.fori_loop(0, halves, one_half, 0)
    table_copy.wait()


def carried_kernel(volt_in, taper_in, table_in, out_ref, *scratch):
    *scratch, out, out_sems = scratch
    volt, taper, held, fir, mid, zed, sems = scratch
    fill(
        volt.shape[1], None, None,
        volt_in, taper_in, table_in, volt, taper, held, fir, mid, zed, sems,
    )
    block = CLASSES // CHUNKS

    def out_copy(j):
        where = pl.ds(j * block, block)
        return pltpu.make_async_copy(out.at[where], out_ref.at[where], out_sems.at[j])

    def some(j, carry):
        for i in range(block):
            q = j * block + i
            out[q] = jnp.dot(zed[q], held[q], preferred_element_type=F32).astype(BF16)
        out_copy(j).start()
        return carry

    lax.fori_loop(0, CHUNKS, some, 0)

    def finish(j, carry):
        out_copy(j).wait()
        return carry

    lax.fori_loop(0, CHUNKS, finish, 0)


def spectra_kernel(first, boundary, *refs):
    if boundary:
        keep, place, hist, carried, unit, *refs = refs
        keep = keep[0]
        here = place[0] * place[1] + place[2]
    else:
        keep, hist, here = None, None, None
    volt_in, taper_in, table_in, out, volt, taper, held, fir, mid, zed, sems, wide = refs
    fill(
        first, hist, keep,
        volt_in, taper_in, table_in, volt, taper, held, fir, mid, zed, sems,
    )
    step = RADIX

    def one(q, copy):
        value = lax.dot_general(held[q], zed[q], CONTRACT, preferred_element_type=F32)
        if boundary:
            part = carried[q]
            short = zed.shape[1] - part.shape[0]
            part = jnp.concatenate([part, jnp.zeros((short, LANES), BF16)], axis=0)
            value = value + lax.dot_general(
                unit[...], part, CONTRACT, preferred_element_type=F32
            )
        wide[q] = value[:step].astype(BF16)
        wide[jnp.where(q == 0, CLASSES, RADIX - q)] = value[step:].astype(BF16)

    unrolled(CLASSES, 4, one)
    channels = out.shape[2] // 2
    split = RADIX // channels
    high = HALF // 2

    def two(b, copy):
        rows = pl.ds(pl.multiple_of(b * HALF, HALF), HALF)
        for tile in range(out.shape[1]):
            lanes = slice(tile * LANES, (tile + 1) * LANES)
            for first_k in range(0, RADIX, HALF):
                value = jnp.swapaxes(wide[first_k : first_k + HALF, rows, lanes], 0, 1)
                u, k = divmod(first_k, channels)
                for j in range(HALF):
                    start = j % 2 * channels + k
                    group = (b * high + j // 2) * split + u
                    if here is not None:
                        group = group ^ here
                    out[group, tile, start : start + HALF, :] = value[j]

    unrolled(step // HALF, 1, two)


def reorder(read, shape, first, put):
    n_inp, sets, rows = shape
    blocks = HALF // (sets * PAIR)
    width = LANES // blocks
    block = lax.broadcasted_iota(jnp.int32, (HALF, LANES), 1) // width
    masks = {d: (block & d) == 0 for d in (1, 2)}
    assert blocks == 4

    def one(b, copy):
        here = pl.ds(pl.multiple_of(b * HALF, HALF), HALF)
        for tile in range(n_inp // blocks):
            pieces = []
            for c in range(PAIR):
                for part in range(sets):
                    x = [read(tile * blocks + p, first + c, part, here) for p in range(blocks)]
                    for d in (1, 2):
                        for p in range(blocks):
                            if p & d == 0:
                                low, up = x[p], x[p | d]
                                x[p] = jnp.where(masks[d], low, pltpu.roll(up, width * d, 1))
                                x[p | d] = jnp.where(
                                    masks[d], pltpu.roll(low, LANES - width * d, 1), up
                                )
                    pieces += x
            value = jnp.swapaxes(jnp.stack(pieces), 0, 1)
            for j in range(HALF):
                put(b * HALF + j, tile, value[j])

    unrolled(rows // HALF, 2, one)


def order_pair(read, shape, j, out):
    def put(r, tile, value):
        times = pl.ds(pl.multiple_of(j * HALF, HALF), HALF)
        out[r, times, tile * LANES : (tile + 1) * LANES] = value

    reorder(read, shape, j * PAIR, put)


def order_kernel(got, out):
    n_inp, n_chan, sets, rows, _ = got.shape

    def step(j, carry):
        order_pair(lambda a, c, part, here: got[a, c, part, here, :], (n_inp, sets, rows), j, out)
        return carry

    lax.fori_loop(0, n_chan // PAIR, step, 0)


def finish_kernel(scale, place, late_in, *refs):
    *got_in, out_ref, got, late, early, out, sems, got_sems = refs
    n_chan, n_inp, sets, rows, _ = got.shape
    channels, width = out.shape[1], out.shape[-1]
    count = channels // BLOCK
    inp = place[0]

    def out_copy(j):
        where = (slice(None), pl.ds(j * BLOCK, BLOCK))
        return pltpu.make_async_copy(out.at[where], out_ref.at[where], sems.at[j])

    copies = [
        pltpu.make_async_copy(got_in[c], got.at[c], got_sems.at[c]) for c in range(n_chan)
    ]
    late_copy = pltpu.make_async_copy(late_in, late, sems.at[count])
    for copy in copies:
        copy.start()
    late_copy.start()
    for copy in copies:
        copy.wait()

    def order(j, carry):
        order_pair(
            lambda a, c, part, here: got[c, a ^ inp, part, here, :], (n_inp, sets, rows), j, early
        )
        return carry

    lax.fori_loop(0, n_chan // PAIR, order, 0)
    late_copy.wait()

    def gram(j, carry):
        for i in range(BLOCK):
            k = j * BLOCK + i
            real = jnp.concatenate([late[k], early[k]], axis=0)
            imag = jnp.concatenate([late[channels + k], early[channels + k]], axis=0)
            left = jnp.concatenate([real, imag], axis=0)
            right = jnp.concatenate([-imag, real], axis=0)
            value = lax.dot_general(
                left,
                jnp.concatenate([left, right], axis=1),
                (((0,), (0,)), ((), ())),
                preferred_element_type=F32,
            )
            value = value * scale
            out[0, k] = value[:, :width].astype(BF16)
            out[1, k] = value[:, width:].astype(BF16)
        out_copy(j).start()
        return carry

    lax.fori_loop(0, count, gram, 0)

    def finish(j, carry):
        out_copy(j).wait()
        return carry

    lax.fori_loop(0, count, finish, 0)


def params():
    return pltpu.CompilerParams(vmem_limit_bytes=VMEM)


def cost(flops, moved):
    return pl.CostEstimate(flops=int(flops), bytes_accessed=int(moved), transcendentals=0)


def on_device(voltages, history, taper):
    in_dev, s_dev, frame = voltages.shape
    taps = taper.shape[0]
    n_inp = lax.axis_size("inp")
    n_chan = lax.axis_size("chan")
    groups = n_inp * n_chan
    channels = BAND // groups
    total = n_inp * in_dev
    times = s_dev // 2
    early = taps - 1
    blocks = LANES // in_dev
    sets = times // blocks
    span = n_chan * times
    assert frame == RADIX * LANES and in_dev == 2 * HALF and PAIR * times == HALF
    assert early == times - 1 and RADIX % channels == 0 and n_inp % blocks == 0
    assert n_chan & (n_chan - 1) == 0 and n_inp & (n_inp - 1) == 0
    assert n_chan % PAIR == 0 and channels % BLOCK == 0

    outputs = 2 * BAND // CLASSES
    stage = stage_table(frame).astype(np.float32).astype(ml_dtypes.bfloat16)
    table = jnp.asarray(stage)
    upright = jnp.asarray(np.ascontiguousarray(stage.transpose(0, 2, 1)))
    unit = jnp.asarray(np.eye(outputs).astype(ml_dtypes.bfloat16))
    assert table.shape == (CLASSES, outputs, 2 * LANES) and outputs == LANES

    away = pl.BlockSpec(memory_space=pl.ANY)
    near = pl.BlockSpec(memory_space=pltpu.VMEM)

    def scratch(count, shape):
        return [
            pltpu.VMEM(voltages.shape, BF16),
            pltpu.VMEM(taper.shape, F32),
            pltpu.VMEM(shape, BF16),
            pltpu.VMEM((RADIX, count, HALF, LANES), F32),
            pltpu.VMEM((8, 8, HALF, LANES), F32),
            pltpu.VMEM((CLASSES, count * in_dev, 2 * LANES), BF16),
            pltpu.SemaphoreType.DMA((2 * CHUNKS + 2,)),
        ]

    wide = [pltpu.VMEM((RADIX, RADIX, times * in_dev), BF16)]
    carried = pl.pallas_call(
        carried_kernel,
        in_specs=[away] * 3,
        out_specs=away,
        out_shape=jax.ShapeDtypeStruct((CLASSES, early * in_dev, outputs), BF16),
        scratch_shapes=scratch(early, upright.shape)
        + [
            pltpu.VMEM((CLASSES, early * in_dev, outputs), BF16),
            pltpu.SemaphoreType.DMA((CHUNKS,)),
        ],
        compiler_params=params(),
        cost_estimate=cost(1e10, 2e7),
        name="carried",
    )(voltages, taper, upright)
    carried, later_taper = lax.optimization_barrier((carried, taper))
    carried = lax.ppermute(carried, "chan", [(i, i + 1) for i in range(n_chan - 1)])

    send_shape = jax.ShapeDtypeStruct((groups, sets, 2 * channels, LANES), BF16)
    late_send = pl.pallas_call(
        lambda *refs: spectra_kernel(times, False, *refs),
        in_specs=[away] * 3,
        out_specs=near,
        out_shape=send_shape,
        scratch_shapes=scratch(times, table.shape) + wide,
        compiler_params=params(),
        cost_estimate=cost(5e10, 4e7),
        name="late",
    )(voltages, later_taper, table)

    late_send, early_taper = lax.optimization_barrier((late_send, later_taper))
    late_got = lax.all_to_all(late_send, ("inp", "chan"), split_axis=0, concat_axis=0, tiled=True)
    late_got = late_got.reshape(n_inp, n_chan, sets, 2 * channels, LANES)

    inp, chan = lax.axis_index("inp"), lax.axis_index("chan")
    place = jnp.stack([inp, jnp.full_like(inp, n_chan), chan]).astype(jnp.int32)
    keep = (chan == 0).astype(F32).reshape(1)
    scalars = pl.BlockSpec(memory_space=pltpu.SMEM)
    early_send = pl.pallas_call(
        lambda *refs: spectra_kernel(0, True, *refs),
        in_specs=[scalars, scalars, near, near, near] + [away] * 3,
        out_specs=near,
        out_shape=send_shape,
        scratch_shapes=scratch(times, table.shape) + wide,
        compiler_params=params(),
        cost_estimate=cost(2e11, 4e7),
        name="early",
    )(keep, place, jnp.transpose(history, (1, 0, 2)), carried, unit, voltages, early_taper, table)

    early_send = early_send.reshape(n_inp, n_chan, sets, 2 * channels, LANES)
    level = [early_send[0]] + [
        lax.ppermute(early_send[x], "inp", [(i, i ^ x) for i in range(n_inp)])
        for x in range(1, n_inp)
    ]
    pieces = [jnp.stack([value[k] for value in level]) for k in range(n_chan)]
    early_got = [None] * n_chan
    early_got[0] = pieces[0]
    for k in reversed(range(1, n_chan)):
        early_got[k] = lax.ppermute(pieces[k], "chan", [(i, i ^ k) for i in range(n_chan)])

    late_rows = pl.pallas_call(
        order_kernel,
        in_specs=[near],
        out_specs=near,
        out_shape=jax.ShapeDtypeStruct((2 * channels, span, total), BF16),
        compiler_params=params(),
        cost_estimate=cost(1e4, 1e4),
        name="order",
    )(late_got)

    held = pltpu.VMEM((2 * channels, span, total), BF16)
    return pl.pallas_call(
        lambda *refs: finish_kernel(1.0 / (n_chan * s_dev), *refs),
        in_specs=[scalars, away] + [away] * n_chan,
        out_specs=away,
        out_shape=jax.ShapeDtypeStruct((2, channels, total, total), BF16),
        scratch_shapes=[
            pltpu.VMEM((n_chan, n_inp, sets, 2 * channels, LANES), BF16),
            held,
            held,
            pltpu.VMEM((2, channels, total, total), BF16),
            pltpu.SemaphoreType.DMA((channels // BLOCK + 1,)),
            pltpu.SemaphoreType.DMA((n_chan,)),
        ],
        compiler_params=params(),
        cost_estimate=cost(1e10, 1e7),
        name="finish",
    )(place, late_rows, *early_got)


def solution(mesh):
    in_specs = (P("inp", "chan", None), P("inp", None, None), P())
    out_specs = P(None, ("inp", "chan"), None, None)
    return jax.shard_map(
        on_device, mesh=mesh, in_specs=in_specs, out_specs=out_specs, check_vma=False
    )
```

```python
import math

import jax
import jax.numpy as jnp
import ml_dtypes
import numpy as np
from jax import lax
from jax.experimental import pallas as pl
from jax.experimental.pallas import tpu as pltpu
from jax.sharding import PartitionSpec as P

BAND = 2048
LOW = 1024
LANES = 128
RADIX = 64
HALF = 16
PAIR = 2
BLOCK = 8
CLASSES = RADIX // 2
ROOT = math.sqrt(0.5)
F32 = jnp.float32
BF16 = jnp.bfloat16
VMEM = 63 * 1024 * 1024


def stage_table(frame):
    high = BAND // RADIX
    lane = np.arange(LANES)
    table = np.zeros((CLASSES, 2, high, 2, 2, LANES))
    for q in range(CLASSES):
        for half in range(2):
            low = q if half == 0 else (RADIX - q if q else RADIX // 2)
            k = low + RADIX * (LOW // RADIX + np.arange(high))
            angle = 2.0 * np.pi * (np.outer(k, lane) % frame) / frame
            cos, sin = np.cos(angle), np.sin(angle)
            if q == 0:
                table[q, half, :, 0, half] = cos
                table[q, half, :, 1, half] = -sin
            elif half == 0:
                table[q, half, :, 0, 0] = cos
                table[q, half, :, 0, 1] = sin
                table[q, half, :, 1, 0] = -sin
                table[q, half, :, 1, 1] = cos
            else:
                table[q, half, :, 0, 0] = cos
                table[q, half, :, 0, 1] = -sin
                table[q, half, :, 1, 0] = -sin
                table[q, half, :, 1, 1] = -cos
    table = table / math.sqrt(frame)
    return table.reshape(CLASSES, 2 * high * 2, 2 * LANES)


def real_dft8(x):
    s = [x[j] + x[j + 4] for j in range(4)]
    d = [x[j] - x[j + 4] for j in range(4)]
    e0, e1 = s[0] + s[2], s[0] - s[2]
    o0, o1 = s[1] + s[3], s[3] - s[1]
    u, v = (d[1] - d[3]) * ROOT, (d[1] + d[3]) * ROOT
    return [
        (e0 + o0, None),
        (d[0] + u, -(d[2] + v)),
        (e1, o1),
        (d[0] - u, d[2] - v),
        (e0 - o0, None),
    ]


def complex_dft8(x):
    def add(a, b):
        return (a[0] + b[0], a[1] + b[1])

    def sub(a, b):
        return (a[0] - b[0], a[1] - b[1])

    def add_i(a, b):
        return (a[0] - b[1], a[1] + b[0])

    def sub_i(a, b):
        return (a[0] + b[1], a[1] - b[0])

    s = [add(x[j], x[j + 4]) for j in range(4)]
    d = [sub(x[j], x[j + 4]) for j in range(4)]
    e0, e1 = add(s[0], s[2]), sub(s[0], s[2])
    o0, o1 = add(s[1], s[3]), sub(s[1], s[3])
    p, m = sub(d[1], d[3]), add(d[1], d[3])
    b = ((p[0] + m[1]) * ROOT, (p[1] - m[0]) * ROOT)
    c = ((m[1] - p[0]) * ROOT, (-p[1] - m[0]) * ROOT)
    f, g = sub_i(d[0], d[2]), add_i(d[0], d[2])
    return [
        add(e0, o0),
        add(f, b),
        sub_i(e1, o1),
        add(g, c),
        sub(e0, o0),
        sub(f, b),
        add_i(e1, o1),
        sub(g, c),
    ]


def turned(value, step):
    angle = 2.0 * math.pi * (step % RADIX) / RADIX
    cos, sin = math.cos(angle), math.sin(angle)
    real, imag = value
    if imag is None:
        return (real * cos, real * -sin)
    if step % RADIX == 0:
        return value
    return (real * cos + imag * sin, imag * cos - real * sin)


def unrolled(count, copies, body):
    def step(i, carry):
        for copy in range(copies):
            body(i * copies + copy, copy)
        return carry

    lax.fori_loop(0, count // copies, step, 0)


def transform_rows(fir, mids, zed, half):
    halves = zed.shape[1] // (fir.shape[1] * HALF)

    def one(s, copy):
        mid = mids.at[copy]
        for low in range(8):
            parts = real_dft8([fir[8 * high + low, s] for high in range(8)])
            mid[0, low] = parts[0][0]
            mid[7, low] = parts[4][0]
            for k in (1, 2, 3):
                value = turned(parts[k], low * k)
                mid[2 * k - 1, low] = value[0]
                mid[2 * k, low] = value[1]
        rows = pl.ds(pl.multiple_of((s * halves + half) * HALF, HALF), HALF)

        def put(q, half, value):
            zed[q, rows, half * LANES : (half + 1) * LANES] = value.astype(BF16)

        parts = real_dft8([mid[0, low] for low in range(8)])
        put(0, 0, parts[0][0])
        put(0, 1, parts[4][0])
        for m in (1, 2, 3):
            put(8 * m, 0, parts[m][0])
            put(8 * m, 1, parts[m][1])
        for k in (1, 2, 3):
            parts = complex_dft8([(mid[2 * k - 1, low], mid[2 * k, low]) for low in range(8)])
            for m in range(8):
                index = k + 8 * m
                if index < CLASSES:
                    put(index, 0, parts[m][0])
                    put(index, 1, parts[m][1])
                else:
                    put(RADIX - index, 0, parts[m][0])
                    put(RADIX - index, 1, -parts[m][1])
        parts = complex_dft8([turned((mid[7, low], None), 4 * low) for low in range(8)])
        for m in range(4):
            put(4 + 8 * m, 0, parts[m][0])
            put(4 + 8 * m, 1, parts[m][1])

    unrolled(fir.shape[1], 2 - fir.shape[1] % 2, one)


CHUNKS = 4
CONTRACT = (((1,), (1,)), ((), ()))


def fill(first, hist, keep, volt_in, taper_in, table_in, volt, taper, held, fir, mid, zed, sems):
    taps = taper.shape[0]
    in_dev, s_dev, frame = volt.shape
    halves = in_dev // HALF
    count = fir.shape[1]
    part = frame // CHUNKS
    wanted = [f for f in range(first - taps + 1, first + count) if f < s_dev]

    def volt_copy(h, j):
        where = (pl.ds(h * HALF, HALF), slice(None), pl.ds(pl.multiple_of(j * part, part), part))
        return pltpu.make_async_copy(volt_in.at[where], volt.at[where], sems.at[h * CHUNKS + j])

    taper_copy = pltpu.make_async_copy(taper_in, taper, sems.at[halves * CHUNKS])
    table_copy = pltpu.make_async_copy(table_in, held, sems.at[halves * CHUNKS + 1])
    taper_copy.start()
    for h in range(halves):
        for j in range(CHUNKS):
            volt_copy(h, j).start()
    table_copy.start()
    taper_copy.wait()

    def one_half(h, carry):
        inputs = pl.ds(pl.multiple_of(h * HALF, HALF), HALF)

        def one_chunk(j, carry):
            volt_copy(h, j).wait()

            def one(i, copy):
                a = j * (part // LANES) + i
                lanes = pl.ds(pl.multiple_of(a * LANES, LANES), LANES)
                by_time = jnp.swapaxes(volt[inputs, :, lanes], 0, 1)
                frames = {}
                for f in wanted:
                    if f >= 0:
                        frames[f] = by_time[f].astype(F32)
                    elif hist is not None:
                        frames[f] = hist[taps - 1 + f, inputs, lanes].astype(F32) * keep
                weights = [taper[t : t + 1, lanes] for t in range(taps)]
                for row in range(count):
                    total = None
                    for t in range(taps):
                        f = first + row + t - taps + 1
                        if f in frames:
                            term = weights[t] * frames[f]
                            total = term if total is None else total + term
                    fir[a, row] = total

            unrolled(part // LANES, 8, one)
            return carry

        lax.fori_loop(0, CHUNKS, one_chunk, 0)
        transform_rows(fir, mid, zed, h)
        return carry

    lax.fori_loop(0, halves, one_half, 0)
    table_copy.wait()


def carried_kernel(volt_in, taper_in, table_in, out_ref, *scratch):
    *scratch, out, out_sems = scratch
    volt, taper, held, fir, mid, zed, sems = scratch
    fill(
        volt.shape[1], None, None,
        volt_in, taper_in, table_in, volt, taper, held, fir, mid, zed, sems,
    )
    block = CLASSES // CHUNKS

    def out_copy(j):
        where = pl.ds(j * block, block)
        return pltpu.make_async_copy(out.at[where], out_ref.at[where], out_sems.at[j])

    def some(j, carry):
        for i in range(block):
            q = j * block + i
            out[q] = jnp.dot(zed[q], held[q], preferred_element_type=F32).astype(BF16)
        out_copy(j).start()
        return carry

    lax.fori_loop(0, CHUNKS, some, 0)

    def finish(j, carry):
        out_copy(j).wait()
        return carry

    lax.fori_loop(0, CHUNKS, finish, 0)


def spectra_kernel(first, boundary, *refs):
    if boundary:
        keep, hist, carried, unit, *refs = refs
        keep = keep[0]
    else:
        keep, hist = None, None
    volt_in, taper_in, table_in, out_ref, volt, taper, held, fir, mid, zed, sems, wide, out = refs
    fill(
        first, hist, keep,
        volt_in, taper_in, table_in, volt, taper, held, fir, mid, zed, sems,
    )
    step = RADIX

    def one(q, copy):
        value = lax.dot_general(held[q], zed[q], CONTRACT, preferred_element_type=F32)
        if boundary:
            part = carried[q]
            short = zed.shape[1] - part.shape[0]
            part = jnp.concatenate([part, jnp.zeros((short, LANES), BF16)], axis=0)
            value = value + lax.dot_general(
                unit[...], part, CONTRACT, preferred_element_type=F32
            )
        wide[q] = value[:step].astype(BF16)
        wide[jnp.where(q == 0, CLASSES, RADIX - q)] = value[step:].astype(BF16)

    unrolled(CLASSES, 4, one)
    channels = out.shape[2] // 2
    split = RADIX // channels
    high = HALF // 2

    def two(b, copy):
        here = pl.ds(pl.multiple_of(b * HALF, HALF), HALF)
        for tile in range(out.shape[1]):
            lanes = slice(tile * LANES, (tile + 1) * LANES)
            for first_k in range(0, RADIX, HALF):
                value = jnp.swapaxes(wide[first_k : first_k + HALF, here, lanes], 0, 1)
                u, k = divmod(first_k, channels)
                for j in range(HALF):
                    start = j % 2 * channels + k
                    out[(b * high + j // 2) * split + u, tile, start : start + HALF, :] = value[j]

        out_copy(b).start()

    def out_copy(b):
        where = pl.ds(b * high * split, high * split)
        return pltpu.make_async_copy(out.at[where], out_ref.at[where], sems.at[b])

    unrolled(step // HALF, 1, two)

    def finish(b, carry):
        out_copy(b).wait()
        return carry

    lax.fori_loop(0, step // HALF, finish, 0)


def reorder(got, first, put):
    n_inp, _, sets, rows, _ = got.shape
    blocks = HALF // (sets * PAIR)
    width = LANES // blocks
    block = lax.broadcasted_iota(jnp.int32, (HALF, LANES), 1) // width
    masks = {d: (block & d) == 0 for d in (1, 2)}
    assert blocks == 4

    def one(b, copy):
        here = pl.ds(pl.multiple_of(b * HALF, HALF), HALF)
        for tile in range(n_inp // blocks):
            pieces = []
            for c in range(PAIR):
                for part in range(sets):
                    x = [got[tile * blocks + p, first + c, part, here, :] for p in range(blocks)]
                    for d in (1, 2):
                        for p in range(blocks):
                            if p & d == 0:
                                low, up = x[p], x[p | d]
                                x[p] = jnp.where(masks[d], low, pltpu.roll(up, width * d, 1))
                                x[p | d] = jnp.where(
                                    masks[d], pltpu.roll(low, LANES - width * d, 1), up
                                )
                    pieces += x
            value = jnp.swapaxes(jnp.stack(pieces), 0, 1)
            for j in range(HALF):
                put(b * HALF + j, tile, value[j])

    unrolled(rows // HALF, min(4, rows // HALF), one)


def order_pair(got, j, out):
    def put(r, tile, value):
        times = pl.ds(pl.multiple_of(j * HALF, HALF), HALF)
        out[r, times, tile * LANES : (tile + 1) * LANES] = value

    reorder(got, j * PAIR, put)


def gram(rows, k):
    real, imag = rows[k], rows[rows.shape[0] // 2 + k]
    left = jnp.concatenate([real, imag], axis=0)
    right = jnp.concatenate([-imag, real], axis=0)
    return lax.dot_general(
        left,
        jnp.concatenate([left, right], axis=1),
        (((0,), (0,)), ((), ())),
        preferred_element_type=F32,
    )


def prior_kernel(got, out, rows):
    def step(j, carry):
        order_pair(got, j, rows)
        return carry

    lax.fori_loop(0, got.shape[1] // PAIR, step, 0)

    def one(k, copy):
        out[k] = gram(rows, k)

    unrolled(out.shape[0], BLOCK, one)


def finish_kernel(scale, got_in, prior_in, out_ref, got, prior, rows, out, sems):
    steps = got.shape[1] // PAIR
    channels, width = out.shape[1], out.shape[-1]
    count = channels // BLOCK

    def got_copy(j):
        where = (slice(None), pl.ds(j * PAIR, PAIR))
        return pltpu.make_async_copy(got_in.at[where], got.at[where], sems.at[count + j])

    def out_copy(j):
        where = (slice(None), pl.ds(j * BLOCK, BLOCK))
        return pltpu.make_async_copy(out.at[where], out_ref.at[where], sems.at[j])

    for j in range(steps):
        got_copy(j).start()
    prior_copy = pltpu.make_async_copy(prior_in, prior, sems.at[count + steps])
    prior_copy.start()

    def order(j, carry):
        got_copy(j).wait()
        order_pair(got, j, rows)
        return carry

    lax.fori_loop(0, steps, order, 0)
    prior_copy.wait()

    def some(j, carry):
        for i in range(BLOCK):
            k = j * BLOCK + i
            value = (gram(rows, k) + prior[k]) * scale
            out[0, k] = value[:, :width].astype(BF16)
            out[1, k] = value[:, width:].astype(BF16)
        out_copy(j).start()
        return carry

    lax.fori_loop(0, count, some, 0)

    def finish(j, carry):
        out_copy(j).wait()
        return carry

    lax.fori_loop(0, count, finish, 0)


def params():
    return pltpu.CompilerParams(vmem_limit_bytes=VMEM)


def cost(flops, moved):
    return pl.CostEstimate(flops=int(flops), bytes_accessed=int(moved), transcendentals=0)


def on_device(voltages, history, taper):
    in_dev, s_dev, frame = voltages.shape
    taps = taper.shape[0]
    n_inp = lax.axis_size("inp")
    n_chan = lax.axis_size("chan")
    groups = n_inp * n_chan
    channels = BAND // groups
    total = n_inp * in_dev
    times = s_dev // 2
    early = taps - 1
    blocks = LANES // in_dev
    sets = times // blocks
    span = n_chan * times
    assert frame == RADIX * LANES and in_dev == 2 * HALF and PAIR * times == HALF
    assert early == times - 1 and RADIX % channels == 0 and n_inp % blocks == 0
    assert n_chan % PAIR == 0 and channels % BLOCK == 0

    outputs = 2 * BAND // CLASSES
    stage = stage_table(frame).astype(np.float32).astype(ml_dtypes.bfloat16)
    table = jnp.asarray(stage)
    upright = jnp.asarray(np.ascontiguousarray(stage.transpose(0, 2, 1)))
    unit = jnp.asarray(np.eye(outputs).astype(ml_dtypes.bfloat16))
    assert table.shape == (CLASSES, outputs, 2 * LANES) and outputs == LANES

    away = pl.BlockSpec(memory_space=pl.ANY)
    near = pl.BlockSpec(memory_space=pltpu.VMEM)

    def scratch(count, shape):
        return [
            pltpu.VMEM(voltages.shape, BF16),
            pltpu.VMEM(taper.shape, F32),
            pltpu.VMEM(shape, BF16),
            pltpu.VMEM((RADIX, count, HALF, LANES), F32),
            pltpu.VMEM((2, 8, 8, HALF, LANES), F32),
            pltpu.VMEM((CLASSES, count * in_dev, 2 * LANES), BF16),
            pltpu.SemaphoreType.DMA((2 * CHUNKS + 2,)),
        ]

    send_shape = jax.ShapeDtypeStruct((groups, sets, 2 * channels, LANES), BF16)
    wide = [pltpu.VMEM((RADIX, RADIX, times * in_dev), BF16), pltpu.VMEM(send_shape.shape, BF16)]
    carried = pl.pallas_call(
        carried_kernel,
        in_specs=[away] * 3,
        out_specs=away,
        out_shape=jax.ShapeDtypeStruct((CLASSES, early * in_dev, outputs), BF16),
        scratch_shapes=scratch(early, upright.shape)
        + [
            pltpu.VMEM((CLASSES, early * in_dev, outputs), BF16),
            pltpu.SemaphoreType.DMA((CHUNKS,)),
        ],
        compiler_params=params(),
        cost_estimate=cost(1e10, 2e7),
        name="carried",
    )(voltages, taper, upright)
    carried, later_taper = lax.optimization_barrier((carried, taper))
    carried = lax.ppermute(carried, "chan", [(i, i + 1) for i in range(n_chan - 1)])

    late_send = pl.pallas_call(
        lambda *refs: spectra_kernel(times, False, *refs),
        in_specs=[away] * 3,
        out_specs=away,
        out_shape=send_shape,
        scratch_shapes=scratch(times, table.shape) + wide,
        compiler_params=params(),
        cost_estimate=cost(5e10, 4e7),
        name="late",
    )(voltages, later_taper, table)

    def exchange(value):
        value = lax.all_to_all(value, ("inp", "chan"), split_axis=0, concat_axis=0, tiled=True)
        return value.reshape(n_inp, n_chan, sets, 2 * channels, LANES)

    late_got = exchange(late_send)

    keep = (lax.axis_index("chan") == 0).astype(F32).reshape(1)
    early_send = pl.pallas_call(
        lambda *refs: spectra_kernel(0, True, *refs),
        in_specs=[pl.BlockSpec(memory_space=pltpu.SMEM), near, near, near] + [away] * 3,
        out_specs=away,
        out_shape=send_shape,
        scratch_shapes=scratch(times, table.shape) + wide,
        compiler_params=params(),
        cost_estimate=cost(2e11, 4e7),
        name="early",
    )(keep, jnp.transpose(history, (1, 0, 2)), carried, unit, voltages, taper, table)
    early_got = exchange(early_send)

    rows = pltpu.VMEM((2 * channels, span, total), BF16)
    prior_shape = (channels, total, 2 * total)
    prior = pl.pallas_call(
        prior_kernel,
        in_specs=[near],
        out_specs=near,
        out_shape=jax.ShapeDtypeStruct(prior_shape, F32),
        scratch_shapes=[rows],
        compiler_params=params(),
        cost_estimate=cost(1e4, 1e4),
        name="prior",
    )(late_got)
    return pl.pallas_call(
        lambda *refs: finish_kernel(1.0 / (n_chan * s_dev), *refs),
        in_specs=[away, away],
        out_specs=away,
        out_shape=jax.ShapeDtypeStruct((2, channels, total, total), BF16),
        scratch_shapes=[
            pltpu.VMEM(early_got.shape, BF16),
            pltpu.VMEM(prior_shape, F32),
            rows,
            pltpu.VMEM((2, channels, total, total), BF16),
            pltpu.SemaphoreType.DMA((channels // BLOCK + n_chan // PAIR + 1,)),
        ],
        compiler_params=params(),
        cost_estimate=cost(1e10, 1e7),
        name="finish",
    )(early_got, prior)


def solution(mesh):
    in_specs = (P("inp", "chan", None), P("inp", None, None), P())
    out_specs = P(None, ("inp", "chan"), None, None)
    return jax.shard_map(
        on_device, mesh=mesh, in_specs=in_specs, out_specs=out_specs, check_vma=False
    )
```

```python
import math

import jax
import jax.numpy as jnp
import ml_dtypes
import numpy as np
from jax import lax
from jax.experimental import pallas as pl
from jax.experimental.pallas import tpu as pltpu
from jax.sharding import PartitionSpec as P

BAND = 2048
LOW = 1024
LANES = 128
RADIX = 64
HALF = 16
PAIR = 2
BLOCK = 8
CLASSES = RADIX // 2
ROOT = math.sqrt(0.5)
F32 = jnp.float32
BF16 = jnp.bfloat16
VMEM = 63 * 1024 * 1024


def stage_table(frame):
    high = BAND // RADIX
    lane = np.arange(LANES)
    table = np.zeros((CLASSES, 2, high, 2, 2, LANES))
    for q in range(CLASSES):
        for half in range(2):
            low = q if half == 0 else (RADIX - q if q else RADIX // 2)
            k = low + RADIX * (LOW // RADIX + np.arange(high))
            angle = 2.0 * np.pi * (np.outer(k, lane) % frame) / frame
            cos, sin = np.cos(angle), np.sin(angle)
            if q == 0:
                table[q, half, :, 0, half] = cos
                table[q, half, :, 1, half] = -sin
            elif half == 0:
                table[q, half, :, 0, 0] = cos
                table[q, half, :, 0, 1] = sin
                table[q, half, :, 1, 0] = -sin
                table[q, half, :, 1, 1] = cos
            else:
                table[q, half, :, 0, 0] = cos
                table[q, half, :, 0, 1] = -sin
                table[q, half, :, 1, 0] = -sin
                table[q, half, :, 1, 1] = -cos
    table = table / math.sqrt(frame)
    return table.reshape(CLASSES, 2 * high * 2, 2 * LANES)


def real_dft8(x):
    s = [x[j] + x[j + 4] for j in range(4)]
    d = [x[j] - x[j + 4] for j in range(4)]
    e0, e1 = s[0] + s[2], s[0] - s[2]
    o0, o1 = s[1] + s[3], s[3] - s[1]
    u, v = (d[1] - d[3]) * ROOT, (d[1] + d[3]) * ROOT
    return [
        (e0 + o0, None),
        (d[0] + u, -(d[2] + v)),
        (e1, o1),
        (d[0] - u, d[2] - v),
        (e0 - o0, None),
    ]


def complex_dft8(x):
    def add(a, b):
        return (a[0] + b[0], a[1] + b[1])

    def sub(a, b):
        return (a[0] - b[0], a[1] - b[1])

    def add_i(a, b):
        return (a[0] - b[1], a[1] + b[0])

    def sub_i(a, b):
        return (a[0] + b[1], a[1] - b[0])

    s = [add(x[j], x[j + 4]) for j in range(4)]
    d = [sub(x[j], x[j + 4]) for j in range(4)]
    e0, e1 = add(s[0], s[2]), sub(s[0], s[2])
    o0, o1 = add(s[1], s[3]), sub(s[1], s[3])
    p, m = sub(d[1], d[3]), add(d[1], d[3])
    b = ((p[0] + m[1]) * ROOT, (p[1] - m[0]) * ROOT)
    c = ((m[1] - p[0]) * ROOT, (-p[1] - m[0]) * ROOT)
    f, g = sub_i(d[0], d[2]), add_i(d[0], d[2])
    return [
        add(e0, o0),
        add(f, b),
        sub_i(e1, o1),
        add(g, c),
        sub(e0, o0),
        sub(f, b),
        add_i(e1, o1),
        sub(g, c),
    ]


def turned(value, step):
    angle = 2.0 * math.pi * (step % RADIX) / RADIX
    cos, sin = math.cos(angle), math.sin(angle)
    real, imag = value
    if imag is None:
        return (real * cos, real * -sin)
    if step % RADIX == 0:
        return value
    return (real * cos + imag * sin, imag * cos - real * sin)


def unrolled(count, copies, body):
    def step(i, carry):
        for copy in range(copies):
            body(i * copies + copy, copy)
        return carry

    lax.fori_loop(0, count // copies, step, 0)


def transform_rows(fir, mids, zed, half):
    halves = zed.shape[1] // (fir.shape[1] * HALF)

    def one(s, copy):
        mid = mids.at[copy]
        for low in range(8):
            parts = real_dft8([fir[8 * high + low, s] for high in range(8)])
            mid[0, low] = parts[0][0]
            mid[7, low] = parts[4][0]
            for k in (1, 2, 3):
                value = turned(parts[k], low * k)
                mid[2 * k - 1, low] = value[0]
                mid[2 * k, low] = value[1]
        rows = pl.ds(pl.multiple_of((s * halves + half) * HALF, HALF), HALF)

        def put(q, half, value):
            zed[q, rows, half * LANES : (half + 1) * LANES] = value.astype(BF16)

        parts = real_dft8([mid[0, low] for low in range(8)])
        put(0, 0, parts[0][0])
        put(0, 1, parts[4][0])
        for m in (1, 2, 3):
            put(8 * m, 0, parts[m][0])
            put(8 * m, 1, parts[m][1])
        for k in (1, 2, 3):
            parts = complex_dft8([(mid[2 * k - 1, low], mid[2 * k, low]) for low in range(8)])
            for m in range(8):
                index = k + 8 * m
                if index < CLASSES:
                    put(index, 0, parts[m][0])
                    put(index, 1, parts[m][1])
                else:
                    put(RADIX - index, 0, parts[m][0])
                    put(RADIX - index, 1, -parts[m][1])
        parts = complex_dft8([turned((mid[7, low], None), 4 * low) for low in range(8)])
        for m in range(4):
            put(4 + 8 * m, 0, parts[m][0])
            put(4 + 8 * m, 1, parts[m][1])

    count = fir.shape[1]
    unrolled(count // 2 * 2, 2, one)
    for s in range(count // 2 * 2, count):
        one(s, 0)


CHUNKS = 8
CONTRACT = (((1,), (1,)), ((), ()))


def fill(first, hist, keep, volt_in, taper_in, table_in, volt, taper, held, fir, mid, zed, sems):
    taps = taper.shape[0]
    in_dev, s_dev, frame = volt.shape
    halves = in_dev // HALF
    count = fir.shape[1]
    part = frame // CHUNKS
    wanted = [f for f in range(first - taps + 1, first + count) if f < s_dev]

    def volt_copy(h, j):
        where = (pl.ds(h * HALF, HALF), slice(None), pl.ds(pl.multiple_of(j * part, part), part))
        return pltpu.make_async_copy(volt_in.at[where], volt.at[where], sems.at[h * CHUNKS + j])

    taper_copy = pltpu.make_async_copy(taper_in, taper, sems.at[halves * CHUNKS])
    table_copy = pltpu.make_async_copy(table_in, held, sems.at[halves * CHUNKS + 1])
    taper_copy.start()
    for h in range(halves):
        for j in range(CHUNKS):
            volt_copy(h, j).start()
    table_copy.start()
    taper_copy.wait()

    def one_half(h, carry):
        inputs = pl.ds(pl.multiple_of(h * HALF, HALF), HALF)

        def one_chunk(j, carry):
            volt_copy(h, j).wait()

            def one(i, copy):
                a = j * (part // LANES) + i
                lanes = pl.ds(pl.multiple_of(a * LANES, LANES), LANES)
                by_time = jnp.swapaxes(volt[inputs, :, lanes], 0, 1)
                frames = {}
                for f in wanted:
                    if f >= 0:
                        frames[f] = by_time[f].astype(F32)
                    elif hist is not None:
                        frames[f] = hist[taps - 1 + f, inputs, lanes].astype(F32) * keep
                weights = [taper[t : t + 1, lanes] for t in range(taps)]
                for row in range(count):
                    total = None
                    for t in range(taps):
                        f = first + row + t - taps + 1
                        if f in frames:
                            term = weights[t] * frames[f]
                            total = term if total is None else total + term
                    fir[a, row] = total

            unrolled(part // LANES, 8, one)
            return carry

        lax.fori_loop(0, CHUNKS, one_chunk, 0)
        transform_rows(fir, mid, zed, h)
        return carry

    lax.fori_loop(0, halves, one_half, 0)
    table_copy.wait()


def carried_kernel(volt_in, taper_in, table_in, out_ref, *scratch):
    *scratch, out, out_sems = scratch
    volt, taper, held, fir, mid, zed, sems = scratch
    fill(
        volt.shape[1], None, None,
        volt_in, taper_in, table_in, volt, taper, held, fir, mid, zed, sems,
    )
    block = CLASSES // CHUNKS

    def out_copy(j):
        where = pl.ds(j * block, block)
        return pltpu.make_async_copy(out.at[where], out_ref.at[where], out_sems.at[j])

    def some(j, carry):
        for i in range(block):
            q = j * block + i
            out[q] = jnp.dot(zed[q], held[q], preferred_element_type=F32).astype(BF16)
        out_copy(j).start()
        return carry

    lax.fori_loop(0, CHUNKS, some, 0)

    def finish(j, carry):
        out_copy(j).wait()
        return carry

    lax.fori_loop(0, CHUNKS, finish, 0)


def spectra_kernel(first, boundary, *refs):
    if boundary:
        keep, hist, carried, unit, *refs = refs
        keep = keep[0]
    else:
        keep, hist = None, None
    volt_in, taper_in, table_in, out_ref, volt, taper, held, fir, mid, zed, sems, wide, out = refs
    fill(
        first, hist, keep,
        volt_in, taper_in, table_in, volt, taper, held, fir, mid, zed, sems,
    )
    step = RADIX

    def one(q, copy):
        value = lax.dot_general(held[q], zed[q], CONTRACT, preferred_element_type=F32)
        if boundary:
            part = carried[q]
            short = zed.shape[1] - part.shape[0]
            part = jnp.concatenate([part, jnp.zeros((short, LANES), BF16)], axis=0)
            value = value + lax.dot_general(
                unit[...], part, CONTRACT, preferred_element_type=F32
            )
        wide[q] = value[:step].astype(BF16)
        wide[jnp.where(q == 0, CLASSES, RADIX - q)] = value[step:].astype(BF16)

    unrolled(CLASSES, 4, one)
    channels = out.shape[2] // 2
    split = RADIX // channels
    high = HALF // 2

    def two(b, copy):
        here = pl.ds(pl.multiple_of(b * HALF, HALF), HALF)
        for tile in range(out.shape[1]):
            lanes = slice(tile * LANES, (tile + 1) * LANES)
            for first_k in range(0, RADIX, HALF):
                value = jnp.swapaxes(wide[first_k : first_k + HALF, here, lanes], 0, 1)
                u, k = divmod(first_k, channels)
                for j in range(HALF):
                    start = j % 2 * channels + k
                    out[(b * high + j // 2) * split + u, tile, start : start + HALF, :] = value[j]

        out_copy(b).start()

    def out_copy(b):
        where = pl.ds(b * high * split, high * split)
        return pltpu.make_async_copy(out.at[where], out_ref.at[where], sems.at[b])

    unrolled(step // HALF, 1, two)

    def finish(b, carry):
        out_copy(b).wait()
        return carry

    lax.fori_loop(0, step // HALF, finish, 0)


def reorder(got, row, first, put):
    n_inp, _, sets, rows, _ = got.shape
    blocks = HALF // (sets * PAIR)
    width = LANES // blocks
    block = lax.broadcasted_iota(jnp.int32, (HALF, LANES), 1) // width
    masks = {d: (block & d) == 0 for d in (1, 2)}
    assert blocks == 4

    here = pl.ds(pl.multiple_of(row, HALF), HALF)
    for tile in range(n_inp // blocks):
        pieces = []
        for c in range(PAIR):
            for part in range(sets):
                x = [got[tile * blocks + p, first + c, part, here, :] for p in range(blocks)]
                for d in (1, 2):
                    for p in range(blocks):
                        if p & d == 0:
                            low, up = x[p], x[p | d]
                            x[p] = jnp.where(masks[d], low, pltpu.roll(up, width * d, 1))
                            x[p | d] = jnp.where(
                                masks[d], pltpu.roll(low, LANES - width * d, 1), up
                            )
                pieces += x
        value = jnp.swapaxes(jnp.stack(pieces), 0, 1)
        for j in range(HALF):
            put(j, tile, value[j])


def order_unit(got, row, j, out, base):
    def put(r, tile, value):
        times = pl.ds(pl.multiple_of(j * HALF, HALF), HALF)
        out[base + r, times, tile * LANES : (tile + 1) * LANES] = value

    reorder(got, row, j * PAIR, put)


def gram(rows, k):
    real, imag = rows[k], rows[rows.shape[0] // 2 + k]
    left = jnp.concatenate([real, imag], axis=0)
    right = jnp.concatenate([-imag, real], axis=0)
    return lax.dot_general(
        left,
        jnp.concatenate([left, right], axis=1),
        (((0,), (0,)), ((), ())),
        preferred_element_type=F32,
    )


def prior_kernel(got, out, rows):
    def step(j, carry):
        def unit(b, copy):
            order_unit(got, b * HALF, j, rows, b * HALF)

        unrolled(rows.shape[0] // HALF, 2, unit)
        return carry

    lax.fori_loop(0, got.shape[1] // PAIR, step, 0)

    def one(k, copy):
        out[k] = gram(rows, k)

    unrolled(out.shape[0], BLOCK, one)


def finish_kernel(scale, got_in, prior_in, out_ref, got, prior, even, odd, out, sems):
    steps = got.shape[1] // PAIR
    units = 2 * steps
    channels, width = out.shape[1], out.shape[-1]
    count = channels // HALF
    each = HALF // units

    def got_copy(b, part):
        where = (slice(None),) * 3 + (pl.ds(part * channels + b * HALF, HALF),)
        return pltpu.make_async_copy(
            got_in.at[where], got.at[where], sems.at[count + 2 * b + part]
        )

    def out_copy(b):
        where = (slice(None), pl.ds(b * HALF, HALF))
        return pltpu.make_async_copy(out.at[where], out_ref.at[where], sems.at[b])

    prior_copy = pltpu.make_async_copy(prior_in, prior, sems.at[3 * count])
    for b in range(count):
        for part in range(2):
            got_copy(b, part).start()
    prior_copy.start()

    for b in range(count + 1):
        now, before = (even, odd) if b % 2 == 0 else (odd, even)
        if b < count:
            for part in range(2):
                got_copy(b, part).wait()
        if b == 1:
            prior_copy.wait()

        def unit(u, copy):
            if b > 0:
                for i in range(each):
                    index = u * each + i
                    k = (b - 1) * HALF + index
                    value = (gram(before, index) + prior[k]) * scale
                    out[0, k] = value[:, :width].astype(BF16)
                    out[1, k] = value[:, width:].astype(BF16)
            if b < count:
                part, pair = lax.div(u, steps), lax.rem(u, steps)
                order_unit(got, part * channels + b * HALF, pair, now, part * HALF)

        unrolled(units, min(4, units), unit)
        if b > 0:
            out_copy(b - 1).start()

    for b in range(count):
        out_copy(b).wait()


def params():
    return pltpu.CompilerParams(vmem_limit_bytes=VMEM)


def cost(flops, moved):
    return pl.CostEstimate(flops=int(flops), bytes_accessed=int(moved), transcendentals=0)


def on_device(voltages, history, taper):
    in_dev, s_dev, frame = voltages.shape
    taps = taper.shape[0]
    n_inp = lax.axis_size("inp")
    n_chan = lax.axis_size("chan")
    groups = n_inp * n_chan
    channels = BAND // groups
    total = n_inp * in_dev
    times = s_dev // 2
    early = taps - 1
    blocks = LANES // in_dev
    sets = times // blocks
    span = n_chan * times
    assert frame == RADIX * LANES and in_dev == 2 * HALF and PAIR * times == HALF
    assert early == times - 1 and RADIX % channels == 0 and n_inp % blocks == 0
    assert n_chan % PAIR == 0 and channels % HALF == 0 and n_chan <= HALF

    outputs = 2 * BAND // CLASSES
    stage = stage_table(frame).astype(np.float32).astype(ml_dtypes.bfloat16)
    table = jnp.asarray(stage)
    upright = jnp.asarray(np.ascontiguousarray(stage.transpose(0, 2, 1)))
    unit = jnp.asarray(np.eye(outputs).astype(ml_dtypes.bfloat16))
    assert table.shape == (CLASSES, outputs, 2 * LANES) and outputs == LANES

    away = pl.BlockSpec(memory_space=pl.ANY)
    near = pl.BlockSpec(memory_space=pltpu.VMEM)

    def scratch(count, shape):
        return [
            pltpu.VMEM(voltages.shape, BF16),
            pltpu.VMEM(taper.shape, F32),
            pltpu.VMEM(shape, BF16),
            pltpu.VMEM((RADIX, count, HALF, LANES), F32),
            pltpu.VMEM((2, 8, 8, HALF, LANES), F32),
            pltpu.VMEM((CLASSES, count * in_dev, 2 * LANES), BF16),
            pltpu.SemaphoreType.DMA((2 * CHUNKS + 2,)),
        ]

    send_shape = jax.ShapeDtypeStruct((groups, sets, 2 * channels, LANES), BF16)
    wide = [pltpu.VMEM((RADIX, RADIX, times * in_dev), BF16), pltpu.VMEM(send_shape.shape, BF16)]
    carried = pl.pallas_call(
        carried_kernel,
        in_specs=[away] * 3,
        out_specs=away,
        out_shape=jax.ShapeDtypeStruct((CLASSES, early * in_dev, outputs), BF16),
        scratch_shapes=scratch(early, upright.shape)
        + [
            pltpu.VMEM((CLASSES, early * in_dev, outputs), BF16),
            pltpu.SemaphoreType.DMA((CHUNKS,)),
        ],
        compiler_params=params(),
        cost_estimate=cost(1e10, 2e7),
        name="carried",
    )(voltages, taper, upright)
    carried, later_taper = lax.optimization_barrier((carried, taper))
    carried = lax.ppermute(carried, "chan", [(i, i + 1) for i in range(n_chan - 1)])

    late_send = pl.pallas_call(
        lambda *refs: spectra_kernel(times, False, *refs),
        in_specs=[away] * 3,
        out_specs=away,
        out_shape=send_shape,
        scratch_shapes=scratch(times, table.shape) + wide,
        compiler_params=params(),
        cost_estimate=cost(5e10, 4e7),
        name="late",
    )(voltages, later_taper, table)

    def exchange(value):
        value = lax.all_to_all(value, ("inp", "chan"), split_axis=0, concat_axis=0, tiled=True)
        return value.reshape(n_inp, n_chan, sets, 2 * channels, LANES)

    late_got = exchange(late_send)

    keep = (lax.axis_index("chan") == 0).astype(F32).reshape(1)
    early_send = pl.pallas_call(
        lambda *refs: spectra_kernel(0, True, *refs),
        in_specs=[pl.BlockSpec(memory_space=pltpu.SMEM), near, near, near] + [away] * 3,
        out_specs=away,
        out_shape=send_shape,
        scratch_shapes=scratch(times, table.shape) + wide,
        compiler_params=params(),
        cost_estimate=cost(2e11, 4e7),
        name="early",
    )(keep, jnp.transpose(history, (1, 0, 2)), carried, unit, voltages, taper, table)
    early_got = exchange(early_send)

    rows = pltpu.VMEM((2 * channels, span, total), BF16)
    prior_shape = (channels, total, 2 * total)
    prior = pl.pallas_call(
        prior_kernel,
        in_specs=[near],
        out_specs=near,
        out_shape=jax.ShapeDtypeStruct(prior_shape, F32),
        scratch_shapes=[rows],
        compiler_params=params(),
        cost_estimate=cost(1e4, 1e4),
        name="prior",
    )(late_got)
    return pl.pallas_call(
        lambda *refs: finish_kernel(1.0 / (n_chan * s_dev), *refs),
        in_specs=[away, away],
        out_specs=away,
        out_shape=jax.ShapeDtypeStruct((2, channels, total, total), BF16),
        scratch_shapes=[
            pltpu.VMEM(early_got.shape, BF16),
            pltpu.VMEM(prior_shape, F32),
            pltpu.VMEM((2 * HALF, span, total), BF16),
            pltpu.VMEM((2 * HALF, span, total), BF16),
            pltpu.VMEM((2, channels, total, total), BF16),
            pltpu.SemaphoreType.DMA((3 * channels // HALF + 1,)),
        ],
        compiler_params=params(),
        cost_estimate=cost(1e10, 1e7),
        name="finish",
    )(early_got, prior)


def solution(mesh):
    in_specs = (P("inp", "chan", None), P("inp", None, None), P())
    out_specs = P(None, ("inp", "chan"), None, None)
    return jax.shard_map(
        on_device, mesh=mesh, in_specs=in_specs, out_specs=out_specs, check_vma=False
    )
```

```python
import math

import jax
import jax.numpy as jnp
import ml_dtypes
import numpy as np
from jax import lax
from jax.experimental import pallas as pl
from jax.experimental.pallas import tpu as pltpu
from jax.sharding import PartitionSpec as P

BAND = 2048
LOW = 1024
LANES = 128
RADIX = 64
HALF = 16
PAIR = 2
BLOCK = 8
CLASSES = RADIX // 2
ROOT = math.sqrt(0.5)
F32 = jnp.float32
BF16 = jnp.bfloat16
VMEM = 63 * 1024 * 1024


def stage_table(frame):
    high = BAND // RADIX
    lane = np.arange(LANES)
    table = np.zeros((CLASSES, 2, high, 2, 2, LANES))
    for q in range(CLASSES):
        for half in range(2):
            low = q if half == 0 else (RADIX - q if q else RADIX // 2)
            k = low + RADIX * (LOW // RADIX + np.arange(high))
            angle = 2.0 * np.pi * (np.outer(k, lane) % frame) / frame
            cos, sin = np.cos(angle), np.sin(angle)
            if q == 0:
                table[q, half, :, 0, half] = cos
                table[q, half, :, 1, half] = -sin
            elif half == 0:
                table[q, half, :, 0, 0] = cos
                table[q, half, :, 0, 1] = sin
                table[q, half, :, 1, 0] = -sin
                table[q, half, :, 1, 1] = cos
            else:
                table[q, half, :, 0, 0] = cos
                table[q, half, :, 0, 1] = -sin
                table[q, half, :, 1, 0] = -sin
                table[q, half, :, 1, 1] = -cos
    table = table / math.sqrt(frame)
    return table.reshape(CLASSES, 2 * high * 2, 2 * LANES)


def real_dft8(x):
    s = [x[j] + x[j + 4] for j in range(4)]
    d = [x[j] - x[j + 4] for j in range(4)]
    e0, e1 = s[0] + s[2], s[0] - s[2]
    o0, o1 = s[1] + s[3], s[3] - s[1]
    u, v = (d[1] - d[3]) * ROOT, (d[1] + d[3]) * ROOT
    return [
        (e0 + o0, None),
        (d[0] + u, -(d[2] + v)),
        (e1, o1),
        (d[0] - u, d[2] - v),
        (e0 - o0, None),
    ]


def complex_dft8(x):
    def add(a, b):
        return (a[0] + b[0], a[1] + b[1])

    def sub(a, b):
        return (a[0] - b[0], a[1] - b[1])

    def add_i(a, b):
        return (a[0] - b[1], a[1] + b[0])

    def sub_i(a, b):
        return (a[0] + b[1], a[1] - b[0])

    s = [add(x[j], x[j + 4]) for j in range(4)]
    d = [sub(x[j], x[j + 4]) for j in range(4)]
    e0, e1 = add(s[0], s[2]), sub(s[0], s[2])
    o0, o1 = add(s[1], s[3]), sub(s[1], s[3])
    p, m = sub(d[1], d[3]), add(d[1], d[3])
    b = ((p[0] + m[1]) * ROOT, (p[1] - m[0]) * ROOT)
    c = ((m[1] - p[0]) * ROOT, (-p[1] - m[0]) * ROOT)
    f, g = sub_i(d[0], d[2]), add_i(d[0], d[2])
    return [
        add(e0, o0),
        add(f, b),
        sub_i(e1, o1),
        add(g, c),
        sub(e0, o0),
        sub(f, b),
        add_i(e1, o1),
        sub(g, c),
    ]


def turned(value, step):
    angle = 2.0 * math.pi * (step % RADIX) / RADIX
    cos, sin = math.cos(angle), math.sin(angle)
    real, imag = value
    if imag is None:
        return (real * cos, real * -sin)
    if step % RADIX == 0:
        return value
    return (real * cos + imag * sin, imag * cos - real * sin)


def unrolled(count, copies, body):
    def step(i, carry):
        for copy in range(copies):
            body(i * copies + copy, copy)
        return carry

    lax.fori_loop(0, count // copies, step, 0)


def transform_rows(fir, mids, zed, half, copies):
    halves = zed.shape[1] // (fir.shape[1] * HALF)

    def one(s, copy):
        mid = mids.at[copy]
        for low in range(8):
            parts = real_dft8([fir[8 * high + low, s] for high in range(8)])
            mid[0, low] = parts[0][0]
            mid[7, low] = parts[4][0]
            for k in (1, 2, 3):
                value = turned(parts[k], low * k)
                mid[2 * k - 1, low] = value[0]
                mid[2 * k, low] = value[1]
        rows = pl.ds(pl.multiple_of((s * halves + half) * HALF, HALF), HALF)

        def put(q, half, value):
            zed[q, rows, half * LANES : (half + 1) * LANES] = value.astype(BF16)

        parts = real_dft8([mid[0, low] for low in range(8)])
        put(0, 0, parts[0][0])
        put(0, 1, parts[4][0])
        for m in (1, 2, 3):
            put(8 * m, 0, parts[m][0])
            put(8 * m, 1, parts[m][1])
        for k in (1, 2, 3):
            parts = complex_dft8([(mid[2 * k - 1, low], mid[2 * k, low]) for low in range(8)])
            for m in range(8):
                index = k + 8 * m
                if index < CLASSES:
                    put(index, 0, parts[m][0])
                    put(index, 1, parts[m][1])
                else:
                    put(RADIX - index, 0, parts[m][0])
                    put(RADIX - index, 1, -parts[m][1])
        parts = complex_dft8([turned((mid[7, low], None), 4 * low) for low in range(8)])
        for m in range(4):
            put(4 + 8 * m, 0, parts[m][0])
            put(4 + 8 * m, 1, parts[m][1])

    unrolled(fir.shape[1], copies, one)


CHUNKS = 4
CONTRACT = (((1,), (1,)), ((), ()))


def fill(first, copies, hist, keep, volt_in, taper_in, table_in, volt, taper, held, fir, mid, zed, sems):
    taps = taper.shape[0]
    in_dev, s_dev, frame = volt.shape
    halves = in_dev // HALF
    count = fir.shape[1]
    part = frame // CHUNKS
    wanted = [f for f in range(first - taps + 1, first + count) if f < s_dev]

    def volt_copy(h, j):
        where = (pl.ds(h * HALF, HALF), slice(None), pl.ds(pl.multiple_of(j * part, part), part))
        return pltpu.make_async_copy(volt_in.at[where], volt.at[where], sems.at[h * CHUNKS + j])

    taper_copy = pltpu.make_async_copy(taper_in, taper, sems.at[halves * CHUNKS])
    table_copy = pltpu.make_async_copy(table_in, held, sems.at[halves * CHUNKS + 1])
    taper_copy.start()
    for h in range(halves):
        for j in range(CHUNKS):
            volt_copy(h, j).start()
    table_copy.start()
    taper_copy.wait()

    def one_half(h, carry):
        inputs = pl.ds(pl.multiple_of(h * HALF, HALF), HALF)

        def one_chunk(j, carry):
            volt_copy(h, j).wait()

            def one(i, copy):
                a = j * (part // LANES) + i
                lanes = pl.ds(pl.multiple_of(a * LANES, LANES), LANES)
                by_time = jnp.swapaxes(volt[inputs, :, lanes], 0, 1)
                frames = {}
                for f in wanted:
                    if f >= 0:
                        frames[f] = by_time[f].astype(F32)
                    elif hist is not None:
                        frames[f] = hist[taps - 1 + f, inputs, lanes].astype(F32) * keep
                weights = [taper[t : t + 1, lanes] for t in range(taps)]
                for row in range(count):
                    total = None
                    for t in range(taps):
                        f = first + row + t - taps + 1
                        if f in frames:
                            term = weights[t] * frames[f]
                            total = term if total is None else total + term
                    fir[a, row] = total

            unrolled(part // LANES, copies[0], one)
            return carry

        lax.fori_loop(0, CHUNKS, one_chunk, 0)
        transform_rows(fir, mid, zed, h, copies[1])
        return carry

    lax.fori_loop(0, halves, one_half, 0)
    table_copy.wait()


def carried_kernel(volt_in, taper_in, table_in, out_ref, *scratch):
    *scratch, out, out_sems = scratch
    volt, taper, held, fir, mid, zed, sems = scratch
    fill(
        volt.shape[1], (4, 1), None, None,
        volt_in, taper_in, table_in, volt, taper, held, fir, mid, zed, sems,
    )
    block = CLASSES // CHUNKS

    def out_copy(j):
        where = pl.ds(j * block, block)
        return pltpu.make_async_copy(out.at[where], out_ref.at[where], out_sems.at[j])

    def some(j, carry):
        for i in range(block):
            q = j * block + i
            out[q] = jnp.dot(zed[q], held[q], preferred_element_type=F32).astype(BF16)
        out_copy(j).start()
        return carry

    lax.fori_loop(0, CHUNKS, some, 0)

    def finish(j, carry):
        out_copy(j).wait()
        return carry

    lax.fori_loop(0, CHUNKS, finish, 0)


def spectra_kernel(first, boundary, *refs):
    if boundary:
        keep, hist, carried, unit, *refs = refs
        keep = keep[0]
    else:
        keep, hist = None, None
    volt_in, taper_in, table_in, out_ref, volt, taper, held, fir, mid, zed, sems, wide, out = refs
    fill(
        first, (4, 2) if boundary else (8, 1), hist, keep,
        volt_in, taper_in, table_in, volt, taper, held, fir, mid, zed, sems,
    )
    step = RADIX

    def one(q, copy):
        value = lax.dot_general(held[q], zed[q], CONTRACT, preferred_element_type=F32)
        if boundary:
            part = carried[q]
            short = zed.shape[1] - part.shape[0]
            part = jnp.concatenate([part, jnp.zeros((short, LANES), BF16)], axis=0)
            value = value + lax.dot_general(
                unit[...], part, CONTRACT, preferred_element_type=F32
            )
        wide[q] = value[:step].astype(BF16)
        wide[jnp.where(q == 0, CLASSES, RADIX - q)] = value[step:].astype(BF16)

    unrolled(CLASSES, 4, one)
    channels = out.shape[2] // 2
    split = RADIX // channels
    high = HALF // 2

    def two(b, copy):
        here = pl.ds(pl.multiple_of(b * HALF, HALF), HALF)
        for tile in range(out.shape[1]):
            lanes = slice(tile * LANES, (tile + 1) * LANES)
            for first_k in range(0, RADIX, HALF):
                value = jnp.swapaxes(wide[first_k : first_k + HALF, here, lanes], 0, 1)
                u, k = divmod(first_k, channels)
                for j in range(HALF):
                    start = j % 2 * channels + k
                    out[(b * high + j // 2) * split + u, tile, start : start + HALF, :] = value[j]

        out_copy(b).start()

    def out_copy(b):
        where = pl.ds(b * high * split, high * split)
        return pltpu.make_async_copy(out.at[where], out_ref.at[where], sems.at[b])

    unrolled(step // HALF, 1, two)

    def finish(b, carry):
        out_copy(b).wait()
        return carry

    lax.fori_loop(0, step // HALF, finish, 0)


def reorder(got, first, copies, put):
    n_inp, _, sets, rows, _ = got.shape
    blocks = HALF // (sets * PAIR)
    width = LANES // blocks
    block = lax.broadcasted_iota(jnp.int32, (HALF, LANES), 1) // width
    masks = {d: (block & d) == 0 for d in (1, 2)}
    assert blocks == 4

    def one(b, copy):
        here = pl.ds(pl.multiple_of(b * HALF, HALF), HALF)
        for tile in range(n_inp // blocks):
            pieces = []
            for c in range(PAIR):
                for part in range(sets):
                    x = [got[tile * blocks + p, first + c, part, here, :] for p in range(blocks)]
                    for d in (1, 2):
                        for p in range(blocks):
                            if p & d == 0:
                                low, up = x[p], x[p | d]
                                x[p] = jnp.where(masks[d], low, pltpu.roll(up, width * d, 1))
                                x[p | d] = jnp.where(
                                    masks[d], pltpu.roll(low, LANES - width * d, 1), up
                                )
                    pieces += x
            value = jnp.swapaxes(jnp.stack(pieces), 0, 1)
            for j in range(HALF):
                put(b * HALF + j, tile, value[j])

    unrolled(rows // HALF, copies, one)


def order_pair(got, j, copies, out):
    def put(r, tile, value):
        times = pl.ds(pl.multiple_of(j * HALF, HALF), HALF)
        out[r, times, tile * LANES : (tile + 1) * LANES] = value

    reorder(got, j * PAIR, copies, put)


def gram(rows, k):
    real, imag = rows[k], rows[rows.shape[0] // 2 + k]
    left = jnp.concatenate([real, imag], axis=0)
    right = jnp.concatenate([-imag, real], axis=0)
    return lax.dot_general(
        left,
        jnp.concatenate([left, right], axis=1),
        (((0,), (0,)), ((), ())),
        preferred_element_type=F32,
    )


def prior_kernel(got, out, rows):
    def step(j, carry):
        order_pair(got, j, 1, rows)
        return carry

    lax.fori_loop(0, got.shape[1] // PAIR, step, 0)

    def one(k, copy):
        out[k] = gram(rows, k)

    unrolled(out.shape[0], BLOCK, one)


def finish_kernel(scale, got_in, prior_in, out_ref, got, prior, rows, out, sems):
    steps = got.shape[1] // PAIR
    channels, width = out.shape[1], out.shape[-1]
    count = channels // BLOCK

    def got_copy(j):
        where = (slice(None), pl.ds(j * PAIR, PAIR))
        return pltpu.make_async_copy(got_in.at[where], got.at[where], sems.at[count + j])

    def out_copy(j):
        where = (slice(None), pl.ds(j * BLOCK, BLOCK))
        return pltpu.make_async_copy(out.at[where], out_ref.at[where], sems.at[j])

    for j in range(steps):
        got_copy(j).start()
    prior_copy = pltpu.make_async_copy(prior_in, prior, sems.at[count + steps])
    prior_copy.start()

    def order(j, carry):
        got_copy(j).wait()
        order_pair(got, j, 2, rows)
        return carry

    lax.fori_loop(0, steps, order, 0)
    prior_copy.wait()

    def some(j, carry):
        def one(i, copy):
            k = j * BLOCK + i
            value = (gram(rows, k) + prior[k]) * scale
            out[0, k] = value[:, :width].astype(BF16)
            out[1, k] = value[:, width:].astype(BF16)

        unrolled(BLOCK, 4, one)
        out_copy(j).start()
        return carry

    lax.fori_loop(0, count, some, 0)

    def finish(j, carry):
        out_copy(j).wait()
        return carry

    lax.fori_loop(0, count, finish, 0)


def params():
    return pltpu.CompilerParams(vmem_limit_bytes=VMEM)


def cost(flops, moved):
    return pl.CostEstimate(flops=int(flops), bytes_accessed=int(moved), transcendentals=0)


def on_device(voltages, history, taper):
    in_dev, s_dev, frame = voltages.shape
    taps = taper.shape[0]
    n_inp = lax.axis_size("inp")
    n_chan = lax.axis_size("chan")
    groups = n_inp * n_chan
    channels = BAND // groups
    total = n_inp * in_dev
    times = s_dev // 2
    early = taps - 1
    blocks = LANES // in_dev
    sets = times // blocks
    span = n_chan * times
    assert frame == RADIX * LANES and in_dev == 2 * HALF and PAIR * times == HALF
    assert early == times - 1 and RADIX % channels == 0 and n_inp % blocks == 0
    assert n_chan % PAIR == 0 and channels % BLOCK == 0

    outputs = 2 * BAND // CLASSES
    stage = stage_table(frame).astype(np.float32).astype(ml_dtypes.bfloat16)
    table = jnp.asarray(stage)
    upright = jnp.asarray(np.ascontiguousarray(stage.transpose(0, 2, 1)))
    unit = jnp.asarray(np.eye(outputs).astype(ml_dtypes.bfloat16))
    assert table.shape == (CLASSES, outputs, 2 * LANES) and outputs == LANES

    away = pl.BlockSpec(memory_space=pl.ANY)
    near = pl.BlockSpec(memory_space=pltpu.VMEM)

    def scratch(count, shape):
        return [
            pltpu.VMEM(voltages.shape, BF16),
            pltpu.VMEM(taper.shape, F32),
            pltpu.VMEM(shape, BF16),
            pltpu.VMEM((RADIX, count, HALF, LANES), F32),
            pltpu.VMEM((2, 8, 8, HALF, LANES), F32),
            pltpu.VMEM((CLASSES, count * in_dev, 2 * LANES), BF16),
            pltpu.SemaphoreType.DMA((2 * CHUNKS + 2,)),
        ]

    send_shape = jax.ShapeDtypeStruct((groups, sets, 2 * channels, LANES), BF16)
    wide = [pltpu.VMEM((RADIX, RADIX, times * in_dev), BF16), pltpu.VMEM(send_shape.shape, BF16)]
    carried = pl.pallas_call(
        carried_kernel,
        in_specs=[away] * 3,
        out_specs=away,
        out_shape=jax.ShapeDtypeStruct((CLASSES, early * in_dev, outputs), BF16),
        scratch_shapes=scratch(early, upright.shape)
        + [
            pltpu.VMEM((CLASSES, early * in_dev, outputs), BF16),
            pltpu.SemaphoreType.DMA((CHUNKS,)),
        ],
        compiler_params=params(),
        cost_estimate=cost(1e10, 2e7),
        name="carried",
    )(voltages, taper, upright)
    carried, later_taper = lax.optimization_barrier((carried, taper))
    carried = lax.ppermute(carried, "chan", [(i, i + 1) for i in range(n_chan - 1)])

    late_send = pl.pallas_call(
        lambda *refs: spectra_kernel(times, False, *refs),
        in_specs=[away] * 3,
        out_specs=away,
        out_shape=send_shape,
        scratch_shapes=scratch(times, table.shape) + wide,
        compiler_params=params(),
        cost_estimate=cost(5e10, 4e7),
        name="late",
    )(voltages, later_taper, table)

    def exchange(value):
        value = lax.all_to_all(value, ("inp", "chan"), split_axis=0, concat_axis=0, tiled=True)
        return value.reshape(n_inp, n_chan, sets, 2 * channels, LANES)

    late_got = exchange(late_send)

    keep = (lax.axis_index("chan") == 0).astype(F32).reshape(1)
    early_send = pl.pallas_call(
        lambda *refs: spectra_kernel(0, True, *refs),
        in_specs=[pl.BlockSpec(memory_space=pltpu.SMEM), near, near, near] + [away] * 3,
        out_specs=away,
        out_shape=send_shape,
        scratch_shapes=scratch(times, table.shape) + wide,
        compiler_params=params(),
        cost_estimate=cost(2e11, 4e7),
        name="early",
    )(keep, jnp.transpose(history, (1, 0, 2)), carried, unit, voltages, taper, table)
    early_got = exchange(early_send)

    rows = pltpu.VMEM((2 * channels, span, total), BF16)
    prior_shape = (channels, total, 2 * total)
    prior = pl.pallas_call(
        prior_kernel,
        in_specs=[near],
        out_specs=near,
        out_shape=jax.ShapeDtypeStruct(prior_shape, F32),
        scratch_shapes=[rows],
        compiler_params=params(),
        cost_estimate=cost(1e4, 1e4),
        name="prior",
    )(late_got)
    return pl.pallas_call(
        lambda *refs: finish_kernel(1.0 / (n_chan * s_dev), *refs),
        in_specs=[away, away],
        out_specs=away,
        out_shape=jax.ShapeDtypeStruct((2, channels, total, total), BF16),
        scratch_shapes=[
            pltpu.VMEM(early_got.shape, BF16),
            pltpu.VMEM(prior_shape, F32),
            rows,
            pltpu.VMEM((2, channels, total, total), BF16),
            pltpu.SemaphoreType.DMA((channels // BLOCK + n_chan // PAIR + 1,)),
        ],
        compiler_params=params(),
        cost_estimate=cost(1e10, 1e7),
        name="finish",
    )(early_got, prior)


def solution(mesh):
    in_specs = (P("inp", "chan", None), P("inp", None, None), P())
    out_specs = P(None, ("inp", "chan"), None, None)
    return jax.shard_map(
        on_device, mesh=mesh, in_specs=in_specs, out_specs=out_specs, check_vma=False
    )
```

```python
import math

import jax
import jax.numpy as jnp
import ml_dtypes
import numpy as np
from jax import lax
from jax.experimental import pallas as pl
from jax.experimental.pallas import tpu as pltpu
from jax.sharding import PartitionSpec as P

BAND = 2048
LOW = 1024
LANES = 128
RADIX = 64
HALF = 16
PAIR = 2
BLOCK = 8
CLASSES = RADIX // 2
ROOT = math.sqrt(0.5)
F32 = jnp.float32
BF16 = jnp.bfloat16
VMEM = 63 * 1024 * 1024


def stage_table(frame):
    high = BAND // RADIX
    lane = np.arange(LANES)
    table = np.zeros((CLASSES, 2, high, 2, 2, LANES))
    for q in range(CLASSES):
        for half in range(2):
            low = q if half == 0 else (RADIX - q if q else RADIX // 2)
            k = low + RADIX * (LOW // RADIX + np.arange(high))
            angle = 2.0 * np.pi * (np.outer(k, lane) % frame) / frame
            cos, sin = np.cos(angle), np.sin(angle)
            if q == 0:
                table[q, half, :, 0, half] = cos
                table[q, half, :, 1, half] = -sin
            elif half == 0:
                table[q, half, :, 0, 0] = cos
                table[q, half, :, 0, 1] = sin
                table[q, half, :, 1, 0] = -sin
                table[q, half, :, 1, 1] = cos
            else:
                table[q, half, :, 0, 0] = cos
                table[q, half, :, 0, 1] = -sin
                table[q, half, :, 1, 0] = -sin
                table[q, half, :, 1, 1] = -cos
    table = table / math.sqrt(frame)
    return table.reshape(CLASSES, 2 * high * 2, 2 * LANES)


def real_dft8(x):
    s = [x[j] + x[j + 4] for j in range(4)]
    d = [x[j] - x[j + 4] for j in range(4)]
    e0, e1 = s[0] + s[2], s[0] - s[2]
    o0, o1 = s[1] + s[3], s[3] - s[1]
    u, v = (d[1] - d[3]) * ROOT, (d[1] + d[3]) * ROOT
    return [
        (e0 + o0, None),
        (d[0] + u, -(d[2] + v)),
        (e1, o1),
        (d[0] - u, d[2] - v),
        (e0 - o0, None),
    ]


def complex_dft8(x):
    def add(a, b):
        return (a[0] + b[0], a[1] + b[1])

    def sub(a, b):
        return (a[0] - b[0], a[1] - b[1])

    def add_i(a, b):
        return (a[0] - b[1], a[1] + b[0])

    def sub_i(a, b):
        return (a[0] + b[1], a[1] - b[0])

    s = [add(x[j], x[j + 4]) for j in range(4)]
    d = [sub(x[j], x[j + 4]) for j in range(4)]
    e0, e1 = add(s[0], s[2]), sub(s[0], s[2])
    o0, o1 = add(s[1], s[3]), sub(s[1], s[3])
    p, m = sub(d[1], d[3]), add(d[1], d[3])
    b = ((p[0] + m[1]) * ROOT, (p[1] - m[0]) * ROOT)
    c = ((m[1] - p[0]) * ROOT, (-p[1] - m[0]) * ROOT)
    f, g = sub_i(d[0], d[2]), add_i(d[0], d[2])
    return [
        add(e0, o0),
        add(f, b),
        sub_i(e1, o1),
        add(g, c),
        sub(e0, o0),
        sub(f, b),
        add_i(e1, o1),
        sub(g, c),
    ]


def turned(value, step):
    angle = 2.0 * math.pi * (step % RADIX) / RADIX
    cos, sin = math.cos(angle), math.sin(angle)
    real, imag = value
    if imag is None:
        return (real * cos, real * -sin)
    if step % RADIX == 0:
        return value
    return (real * cos + imag * sin, imag * cos - real * sin)


def unrolled(count, copies, body):
    def step(i, carry):
        for copy in range(copies):
            body(i * copies + copy, copy)
        return carry

    lax.fori_loop(0, count // copies, step, 0)


def transform_rows(fir, mids, zed, half, copies):
    halves = zed.shape[1] // (fir.shape[1] * HALF)

    def one(s, copy):
        mid = mids.at[copy]
        for low in range(8):
            parts = real_dft8([fir[8 * high + low, s] for high in range(8)])
            mid[0, low] = parts[0][0]
            mid[7, low] = parts[4][0]
            for k in (1, 2, 3):
                value = turned(parts[k], low * k)
                mid[2 * k - 1, low] = value[0]
                mid[2 * k, low] = value[1]
        rows = pl.ds(pl.multiple_of((s * halves + half) * HALF, HALF), HALF)

        def put(q, half, value):
            zed[q, rows, half * LANES : (half + 1) * LANES] = value.astype(BF16)

        parts = real_dft8([mid[0, low] for low in range(8)])
        put(0, 0, parts[0][0])
        put(0, 1, parts[4][0])
        for m in (1, 2, 3):
            put(8 * m, 0, parts[m][0])
            put(8 * m, 1, parts[m][1])
        for k in (1, 2, 3):
            parts = complex_dft8([(mid[2 * k - 1, low], mid[2 * k, low]) for low in range(8)])
            for m in range(8):
                index = k + 8 * m
                if index < CLASSES:
                    put(index, 0, parts[m][0])
                    put(index, 1, parts[m][1])
                else:
                    put(RADIX - index, 0, parts[m][0])
                    put(RADIX - index, 1, -parts[m][1])
        parts = complex_dft8([turned((mid[7, low], None), 4 * low) for low in range(8)])
        for m in range(4):
            put(4 + 8 * m, 0, parts[m][0])
            put(4 + 8 * m, 1, parts[m][1])

    unrolled(fir.shape[1], copies, one)


CHUNKS = 4
CONTRACT = (((1,), (1,)), ((), ()))


def fill(first, copies, hist, keep, volt_in, taper_in, table_in, volt, taper, held, fir, mid, zed, sems):
    taps = taper.shape[0]
    in_dev, s_dev, frame = volt.shape
    halves = in_dev // HALF
    count = fir.shape[1]
    part = frame // CHUNKS
    wanted = [f for f in range(first - taps + 1, first + count) if f < s_dev]

    def volt_copy(h, j):
        where = (pl.ds(h * HALF, HALF), slice(None), pl.ds(pl.multiple_of(j * part, part), part))
        return pltpu.make_async_copy(volt_in.at[where], volt.at[where], sems.at[h * CHUNKS + j])

    taper_copy = pltpu.make_async_copy(taper_in, taper, sems.at[halves * CHUNKS])
    table_copy = pltpu.make_async_copy(table_in, held, sems.at[halves * CHUNKS + 1])
    taper_copy.start()
    for h in range(halves):
        for j in range(CHUNKS):
            volt_copy(h, j).start()
    table_copy.start()
    taper_copy.wait()

    def one_half(h, carry):
        inputs = pl.ds(pl.multiple_of(h * HALF, HALF), HALF)

        def one_chunk(j, carry):
            volt_copy(h, j).wait()

            def one(i, copy):
                a = j * (part // LANES) + i
                lanes = pl.ds(pl.multiple_of(a * LANES, LANES), LANES)
                by_time = jnp.swapaxes(volt[inputs, :, lanes], 0, 1)
                frames = {}
                for f in wanted:
                    if f >= 0:
                        frames[f] = by_time[f].astype(F32)
                    elif hist is not None:
                        frames[f] = hist[taps - 1 + f, inputs, lanes].astype(F32) * keep
                weights = [taper[t : t + 1, lanes] for t in range(taps)]
                for row in range(count):
                    total = None
                    for t in range(taps):
                        f = first + row + t - taps + 1
                        if f in frames:
                            term = weights[t] * frames[f]
                            total = term if total is None else total + term
                    fir[a, row] = total

            unrolled(part // LANES, copies[0], one)
            return carry

        lax.fori_loop(0, CHUNKS, one_chunk, 0)
        transform_rows(fir, mid, zed, h, copies[1])
        return carry

    lax.fori_loop(0, halves, one_half, 0)
    table_copy.wait()


def carried_kernel(volt_in, taper_in, table_in, out_ref, *scratch):
    *scratch, out, out_sems = scratch
    volt, taper, held, fir, mid, zed, sems = scratch
    fill(
        volt.shape[1], (16, 1), None, None,
        volt_in, taper_in, table_in, volt, taper, held, fir, mid, zed, sems,
    )
    block = CLASSES // CHUNKS

    def out_copy(j):
        where = pl.ds(j * block, block)
        return pltpu.make_async_copy(out.at[where], out_ref.at[where], out_sems.at[j])

    def some(j, carry):
        for i in range(block):
            q = j * block + i
            out[q] = jnp.dot(zed[q], held[q], preferred_element_type=F32).astype(BF16)
        out_copy(j).start()
        return carry

    lax.fori_loop(0, CHUNKS, some, 0)

    def finish(j, carry):
        out_copy(j).wait()
        return carry

    lax.fori_loop(0, CHUNKS, finish, 0)


def spectra_kernel(first, boundary, *refs):
    if boundary:
        keep, hist, carried, unit, *refs = refs
        keep = keep[0]
    else:
        keep, hist = None, None
    volt_in, taper_in, table_in, out_ref, volt, taper, held, fir, mid, zed, sems, wide, out = refs
    fill(
        first, (16, 4) if boundary else (8, 2), hist, keep,
        volt_in, taper_in, table_in, volt, taper, held, fir, mid, zed, sems,
    )
    step = RADIX

    def one(q, copy):
        value = lax.dot_general(held[q], zed[q], CONTRACT, preferred_element_type=F32)
        if boundary:
            part = carried[q]
            short = zed.shape[1] - part.shape[0]
            part = jnp.concatenate([part, jnp.zeros((short, LANES), BF16)], axis=0)
            value = value + lax.dot_general(
                unit[...], part, CONTRACT, preferred_element_type=F32
            )
        wide[q] = value[:step].astype(BF16)
        wide[jnp.where(q == 0, CLASSES, RADIX - q)] = value[step:].astype(BF16)

    unrolled(CLASSES, 4 if boundary else 8, one)
    channels = out.shape[2] // 2
    split = RADIX // channels
    high = HALF // 2

    def two(b, copy):
        here = pl.ds(pl.multiple_of(b * HALF, HALF), HALF)
        for tile in range(out.shape[1]):
            lanes = slice(tile * LANES, (tile + 1) * LANES)
            for first_k in range(0, RADIX, HALF):
                value = jnp.swapaxes(wide[first_k : first_k + HALF, here, lanes], 0, 1)
                u, k = divmod(first_k, channels)
                for j in range(HALF):
                    start = j % 2 * channels + k
                    out[(b * high + j // 2) * split + u, tile, start : start + HALF, :] = value[j]

        out_copy(b).start()

    def out_copy(b):
        where = pl.ds(b * high * split, high * split)
        return pltpu.make_async_copy(out.at[where], out_ref.at[where], sems.at[b])

    unrolled(step // HALF, 1 if boundary else 2, two)

    def finish(b, carry):
        out_copy(b).wait()
        return carry

    lax.fori_loop(0, step // HALF, finish, 0)


def reorder(got, first, copies, put):
    n_inp, _, sets, rows, _ = got.shape
    blocks = HALF // (sets * PAIR)
    width = LANES // blocks
    block = lax.broadcasted_iota(jnp.int32, (HALF, LANES), 1) // width
    masks = {d: (block & d) == 0 for d in (1, 2)}
    assert blocks == 4

    def one(b, copy):
        here = pl.ds(pl.multiple_of(b * HALF, HALF), HALF)
        for tile in range(n_inp // blocks):
            pieces = []
            for c in range(PAIR):
                for part in range(sets):
                    x = [got[tile * blocks + p, first + c, part, here, :] for p in range(blocks)]
                    for d in (1, 2):
                        for p in range(blocks):
                            if p & d == 0:
                                low, up = x[p], x[p | d]
                                x[p] = jnp.where(masks[d], low, pltpu.roll(up, width * d, 1))
                                x[p | d] = jnp.where(
                                    masks[d], pltpu.roll(low, LANES - width * d, 1), up
                                )
                    pieces += x
            value = jnp.swapaxes(jnp.stack(pieces), 0, 1)
            for j in range(HALF):
                put(b * HALF + j, tile, value[j])

    unrolled(rows // HALF, min(copies, rows // HALF), one)


def order_pair(got, j, copies, out):
    def put(r, tile, value):
        times = pl.ds(pl.multiple_of(j * HALF, HALF), HALF)
        out[r, times, tile * LANES : (tile + 1) * LANES] = value

    reorder(got, j * PAIR, copies, put)


def gram(rows, k):
    real, imag = rows[k], rows[rows.shape[0] // 2 + k]
    left = jnp.concatenate([real, imag], axis=0)
    right = jnp.concatenate([-imag, real], axis=0)
    return lax.dot_general(
        left,
        jnp.concatenate([left, right], axis=1),
        (((0,), (0,)), ((), ())),
        preferred_element_type=F32,
    )


def prior_kernel(got, out, rows):
    def step(j, carry):
        order_pair(got, j, 8, rows)
        return carry

    lax.fori_loop(0, got.shape[1] // PAIR, step, 0)

    def one(k, copy):
        out[k] = gram(rows, k)

    unrolled(out.shape[0], BLOCK, one)


def finish_kernel(scale, got_in, prior_in, out_ref, got, prior, rows, out, sems):
    steps = got.shape[1] // PAIR
    channels, width = out.shape[1], out.shape[-1]
    count = channels // BLOCK

    def got_copy(j):
        where = (slice(None), pl.ds(j * PAIR, PAIR))
        return pltpu.make_async_copy(got_in.at[where], got.at[where], sems.at[count + j])

    def out_copy(j):
        where = (slice(None), pl.ds(j * BLOCK, BLOCK))
        return pltpu.make_async_copy(out.at[where], out_ref.at[where], sems.at[j])

    for j in range(steps):
        got_copy(j).start()
    prior_copy = pltpu.make_async_copy(prior_in, prior, sems.at[count + steps])
    prior_copy.start()

    def order(j, carry):
        got_copy(j).wait()
        order_pair(got, j, 8, rows)
        return carry

    lax.fori_loop(0, steps, order, 0)
    prior_copy.wait()

    def some(j, carry):
        def one(i, copy):
            k = j * BLOCK + i
            value = (gram(rows, k) + prior[k]) * scale
            out[0, k] = value[:, :width].astype(BF16)
            out[1, k] = value[:, width:].astype(BF16)

        unrolled(BLOCK, BLOCK, one)
        out_copy(j).start()
        return carry

    lax.fori_loop(0, count, some, 0)

    def finish(j, carry):
        out_copy(j).wait()
        return carry

    lax.fori_loop(0, count, finish, 0)


def params():
    return pltpu.CompilerParams(vmem_limit_bytes=VMEM)


def cost(flops, moved):
    return pl.CostEstimate(flops=int(flops), bytes_accessed=int(moved), transcendentals=0)


def on_device(voltages, history, taper):
    in_dev, s_dev, frame = voltages.shape
    taps = taper.shape[0]
    n_inp = lax.axis_size("inp")
    n_chan = lax.axis_size("chan")
    groups = n_inp * n_chan
    channels = BAND // groups
    total = n_inp * in_dev
    times = s_dev // 2
    early = taps - 1
    blocks = LANES // in_dev
    sets = times // blocks
    span = n_chan * times
    assert frame == RADIX * LANES and in_dev == 2 * HALF and PAIR * times == HALF
    assert early == times - 1 and RADIX % channels == 0 and n_inp % blocks == 0
    assert n_chan % PAIR == 0 and channels % BLOCK == 0

    outputs = 2 * BAND // CLASSES
    stage = stage_table(frame).astype(np.float32).astype(ml_dtypes.bfloat16)
    table = jnp.asarray(stage)
    upright = jnp.asarray(np.ascontiguousarray(stage.transpose(0, 2, 1)))
    unit = jnp.asarray(np.eye(outputs).astype(ml_dtypes.bfloat16))
    assert table.shape == (CLASSES, outputs, 2 * LANES) and outputs == LANES

    away = pl.BlockSpec(memory_space=pl.ANY)
    near = pl.BlockSpec(memory_space=pltpu.VMEM)

    def scratch(count, shape):
        return [
            pltpu.VMEM(voltages.shape, BF16),
            pltpu.VMEM(taper.shape, F32),
            pltpu.VMEM(shape, BF16),
            pltpu.VMEM((RADIX, count, HALF, LANES), F32),
            pltpu.VMEM((4, 8, 8, HALF, LANES), F32),
            pltpu.VMEM((CLASSES, count * in_dev, 2 * LANES), BF16),
            pltpu.SemaphoreType.DMA((2 * CHUNKS + 2,)),
        ]

    send_shape = jax.ShapeDtypeStruct((groups, sets, 2 * channels, LANES), BF16)
    wide = [pltpu.VMEM((RADIX, RADIX, times * in_dev), BF16), pltpu.VMEM(send_shape.shape, BF16)]
    carried = pl.pallas_call(
        carried_kernel,
        in_specs=[away] * 3,
        out_specs=away,
        out_shape=jax.ShapeDtypeStruct((CLASSES, early * in_dev, outputs), BF16),
        scratch_shapes=scratch(early, upright.shape)
        + [
            pltpu.VMEM((CLASSES, early * in_dev, outputs), BF16),
            pltpu.SemaphoreType.DMA((CHUNKS,)),
        ],
        compiler_params=params(),
        cost_estimate=cost(1e10, 2e7),
        name="carried",
    )(voltages, taper, upright)
    carried, later_taper = lax.optimization_barrier((carried, taper))
    carried = lax.ppermute(carried, "chan", [(i, i + 1) for i in range(n_chan - 1)])

    late_send = pl.pallas_call(
        lambda *refs: spectra_kernel(times, False, *refs),
        in_specs=[away] * 3,
        out_specs=away,
        out_shape=send_shape,
        scratch_shapes=scratch(times, table.shape) + wide,
        compiler_params=params(),
        cost_estimate=cost(5e10, 4e7),
        name="late",
    )(voltages, later_taper, table)

    def exchange(value):
        value = lax.all_to_all(value, ("inp", "chan"), split_axis=0, concat_axis=0, tiled=True)
        return value.reshape(n_inp, n_chan, sets, 2 * channels, LANES)

    late_got = exchange(late_send)

    keep = (lax.axis_index("chan") == 0).astype(F32).reshape(1)
    early_send = pl.pallas_call(
        lambda *refs: spectra_kernel(0, True, *refs),
        in_specs=[pl.BlockSpec(memory_space=pltpu.SMEM), near, near, near] + [away] * 3,
        out_specs=away,
        out_shape=send_shape,
        scratch_shapes=scratch(times, table.shape) + wide,
        compiler_params=params(),
        cost_estimate=cost(2e11, 4e7),
        name="early",
    )(keep, jnp.transpose(history, (1, 0, 2)), carried, unit, voltages, taper, table)
    early_got = exchange(early_send)

    rows = pltpu.VMEM((2 * channels, span, total), BF16)
    prior_shape = (channels, total, 2 * total)
    prior = pl.pallas_call(
        prior_kernel,
        in_specs=[near],
        out_specs=near,
        out_shape=jax.ShapeDtypeStruct(prior_shape, F32),
        scratch_shapes=[rows],
        compiler_params=params(),
        cost_estimate=cost(1e4, 1e4),
        name="prior",
    )(late_got)
    return pl.pallas_call(
        lambda *refs: finish_kernel(1.0 / (n_chan * s_dev), *refs),
        in_specs=[away, away],
        out_specs=away,
        out_shape=jax.ShapeDtypeStruct((2, channels, total, total), BF16),
        scratch_shapes=[
            pltpu.VMEM(early_got.shape, BF16),
            pltpu.VMEM(prior_shape, F32),
            rows,
            pltpu.VMEM((2, channels, total, total), BF16),
            pltpu.SemaphoreType.DMA((channels // BLOCK + n_chan // PAIR + 1,)),
        ],
        compiler_params=params(),
        cost_estimate=cost(1e10, 1e7),
        name="finish",
    )(early_got, prior)


def solution(mesh):
    in_specs = (P("inp", "chan", None), P("inp", None, None), P())
    out_specs = P(None, ("inp", "chan"), None, None)
    return jax.shard_map(
        on_device, mesh=mesh, in_specs=in_specs, out_specs=out_specs, check_vma=False
    )
```

```python
import math

import jax
import jax.numpy as jnp
import ml_dtypes
import numpy as np
from jax import lax
from jax.experimental import pallas as pl
from jax.experimental.pallas import tpu as pltpu
from jax.sharding import PartitionSpec as P

BAND = 2048
LOW = 1024
LANES = 128
RADIX = 64
HALF = 16
PAIR = 2
BLOCK = 8
CLASSES = RADIX // 2
ROOT = math.sqrt(0.5)
F32 = jnp.float32
BF16 = jnp.bfloat16
VMEM = 63 * 1024 * 1024


def stage_table(frame):
    high = BAND // RADIX
    lane = np.arange(LANES)
    table = np.zeros((CLASSES, 2, high, 2, 2, LANES))
    for q in range(CLASSES):
        for half in range(2):
            low = q if half == 0 else (RADIX - q if q else RADIX // 2)
            k = low + RADIX * (LOW // RADIX + np.arange(high))
            angle = 2.0 * np.pi * (np.outer(k, lane) % frame) / frame
            cos, sin = np.cos(angle), np.sin(angle)
            if q == 0:
                table[q, half, :, 0, half] = cos
                table[q, half, :, 1, half] = -sin
            elif half == 0:
                table[q, half, :, 0, 0] = cos
                table[q, half, :, 0, 1] = sin
                table[q, half, :, 1, 0] = -sin
                table[q, half, :, 1, 1] = cos
            else:
                table[q, half, :, 0, 0] = cos
                table[q, half, :, 0, 1] = -sin
                table[q, half, :, 1, 0] = -sin
                table[q, half, :, 1, 1] = -cos
    table = table / math.sqrt(frame)
    return table.swapaxes(2, 3).reshape(CLASSES, 2 * high * 2, 2 * LANES)


def real_dft8(x):
    s = [x[j] + x[j + 4] for j in range(4)]
    d = [x[j] - x[j + 4] for j in range(4)]
    e0, e1 = s[0] + s[2], s[0] - s[2]
    o0, o1 = s[1] + s[3], s[3] - s[1]
    u, v = (d[1] - d[3]) * ROOT, (d[1] + d[3]) * ROOT
    return [
        (e0 + o0, None),
        (d[0] + u, -(d[2] + v)),
        (e1, o1),
        (d[0] - u, d[2] - v),
        (e0 - o0, None),
    ]


def complex_dft8(x):
    def add(a, b):
        return (a[0] + b[0], a[1] + b[1])

    def sub(a, b):
        return (a[0] - b[0], a[1] - b[1])

    def add_i(a, b):
        return (a[0] - b[1], a[1] + b[0])

    def sub_i(a, b):
        return (a[0] + b[1], a[1] - b[0])

    s = [add(x[j], x[j + 4]) for j in range(4)]
    d = [sub(x[j], x[j + 4]) for j in range(4)]
    e0, e1 = add(s[0], s[2]), sub(s[0], s[2])
    o0, o1 = add(s[1], s[3]), sub(s[1], s[3])
    p, m = sub(d[1], d[3]), add(d[1], d[3])
    b = ((p[0] + m[1]) * ROOT, (p[1] - m[0]) * ROOT)
    c = ((m[1] - p[0]) * ROOT, (-p[1] - m[0]) * ROOT)
    f, g = sub_i(d[0], d[2]), add_i(d[0], d[2])
    return [
        add(e0, o0),
        add(f, b),
        sub_i(e1, o1),
        add(g, c),
        sub(e0, o0),
        sub(f, b),
        add_i(e1, o1),
        sub(g, c),
    ]


def turned(value, step):
    angle = 2.0 * math.pi * (step % RADIX) / RADIX
    cos, sin = math.cos(angle), math.sin(angle)
    real, imag = value
    if imag is None:
        return (real * cos, real * -sin)
    if step % RADIX == 0:
        return value
    return (real * cos + imag * sin, imag * cos - real * sin)


def unrolled(count, copies, body):
    def step(i, carry):
        for copy in range(copies):
            body(i * copies + copy, copy)
        return carry

    lax.fori_loop(0, count // copies, step, 0)


def transform_rows(fir, mids, zed, half, copies):
    halves = zed.shape[1] // (fir.shape[1] * HALF)

    def one(s, copy):
        mid = mids.at[copy]
        for low in range(8):
            parts = real_dft8([fir[8 * high + low, s] for high in range(8)])
            mid[0, low] = parts[0][0]
            mid[7, low] = parts[4][0]
            for k in (1, 2, 3):
                value = turned(parts[k], low * k)
                mid[2 * k - 1, low] = value[0]
                mid[2 * k, low] = value[1]
        rows = pl.ds(pl.multiple_of((s * halves + half) * HALF, HALF), HALF)

        def put(q, half, value):
            zed[q, rows, half * LANES : (half + 1) * LANES] = value.astype(BF16)

        parts = real_dft8([mid[0, low] for low in range(8)])
        put(0, 0, parts[0][0])
        put(0, 1, parts[4][0])
        for m in (1, 2, 3):
            put(8 * m, 0, parts[m][0])
            put(8 * m, 1, parts[m][1])
        for k in (1, 2, 3):
            parts = complex_dft8([(mid[2 * k - 1, low], mid[2 * k, low]) for low in range(8)])
            for m in range(8):
                index = k + 8 * m
                if index < CLASSES:
                    put(index, 0, parts[m][0])
                    put(index, 1, parts[m][1])
                else:
                    put(RADIX - index, 0, parts[m][0])
                    put(RADIX - index, 1, -parts[m][1])
        parts = complex_dft8([turned((mid[7, low], None), 4 * low) for low in range(8)])
        for m in range(4):
            put(4 + 8 * m, 0, parts[m][0])
            put(4 + 8 * m, 1, parts[m][1])

    unrolled(fir.shape[1], copies, one)


CHUNKS = 4
CONTRACT = (((1,), (1,)), ((), ()))


def fill(first, copies, hist, keep, volt_in, taper_in, table_in, volt, taper, held, fir, mid, zed, sems):
    taps = taper.shape[0]
    in_dev, s_dev, frame = volt.shape
    halves = in_dev // HALF
    count = fir.shape[1]
    part = frame // CHUNKS
    wanted = [f for f in range(first - taps + 1, first + count) if f < s_dev]

    def volt_copy(h, j):
        where = (pl.ds(h * HALF, HALF), slice(None), pl.ds(pl.multiple_of(j * part, part), part))
        return pltpu.make_async_copy(volt_in.at[where], volt.at[where], sems.at[h * CHUNKS + j])

    taper_copy = pltpu.make_async_copy(taper_in, taper, sems.at[halves * CHUNKS])
    table_copy = pltpu.make_async_copy(table_in, held, sems.at[halves * CHUNKS + 1])
    taper_copy.start()
    for h in range(halves):
        for j in range(CHUNKS):
            volt_copy(h, j).start()
    table_copy.start()
    taper_copy.wait()

    def one_half(h, carry):
        inputs = pl.ds(pl.multiple_of(h * HALF, HALF), HALF)

        def one_chunk(j, carry):
            volt_copy(h, j).wait()

            def one(i, copy):
                a = j * (part // LANES) + i
                lanes = pl.ds(pl.multiple_of(a * LANES, LANES), LANES)
                by_time = jnp.swapaxes(volt[inputs, :, lanes], 0, 1)
                frames = {}
                for f in wanted:
                    if f >= 0:
                        frames[f] = by_time[f].astype(F32)
                    elif hist is not None:
                        frames[f] = hist[taps - 1 + f, inputs, lanes].astype(F32) * keep
                weights = [taper[t : t + 1, lanes] for t in range(taps)]
                for row in range(count):
                    total = None
                    for t in range(taps):
                        f = first + row + t - taps + 1
                        if f in frames:
                            term = weights[t] * frames[f]
                            total = term if total is None else total + term
                    fir[a, row] = total

            unrolled(part // LANES, copies[0], one)
            return carry

        lax.fori_loop(0, CHUNKS, one_chunk, 0)
        transform_rows(fir, mid, zed, h, copies[1])
        return carry

    lax.fori_loop(0, halves, one_half, 0)
    table_copy.wait()


def carried_kernel(volt_in, taper_in, table_in, out_ref, *scratch):
    *scratch, out, out_sems = scratch
    volt, taper, held, fir, mid, zed, sems = scratch
    fill(
        volt.shape[1], (16, 1), None, None,
        volt_in, taper_in, table_in, volt, taper, held, fir, mid, zed, sems,
    )
    block = CLASSES // CHUNKS

    def out_copy(j):
        where = pl.ds(j * block, block)
        return pltpu.make_async_copy(out.at[where], out_ref.at[where], out_sems.at[j])

    def some(j, carry):
        for i in range(block):
            q = j * block + i
            out[q] = jnp.dot(zed[q], held[q], preferred_element_type=F32).astype(BF16)
        out_copy(j).start()
        return carry

    lax.fori_loop(0, CHUNKS, some, 0)

    def finish(j, carry):
        out_copy(j).wait()
        return carry

    lax.fori_loop(0, CHUNKS, finish, 0)


def lane_swap(x):
    width = LANES // 4
    block = lax.broadcasted_iota(jnp.int32, (HALF, LANES), 1) // width
    x = list(x)
    for d in (1, 2):
        mask = (block & d) == 0
        for p in range(4):
            if p & d == 0:
                low, up = x[p], x[p | d]
                x[p] = jnp.where(mask, low, pltpu.roll(up, width * d, 1))
                x[p | d] = jnp.where(mask, pltpu.roll(low, LANES - width * d, 1), up)
    return x


def spectra_kernel(first, boundary, *refs):
    if boundary:
        keep, hist, carried, unit, *refs = refs
        keep = keep[0]
    else:
        keep, hist = None, None
    volt_in, taper_in, table_in, out_ref, volt, taper, held, fir, mid, zed, sems, wide, out = refs
    fill(
        first, (16, 4) if boundary else (8, 2), hist, keep,
        volt_in, taper_in, table_in, volt, taper, held, fir, mid, zed, sems,
    )
    step = RADIX
    high = step // 2
    sides = wide.shape[2] // LANES
    split = out.shape[0] // high
    channels = RADIX // split

    def one(q, copy):
        value = lax.dot_general(held[q], zed[q], CONTRACT, preferred_element_type=F32)
        if boundary:
            part = carried[q]
            short = zed.shape[1] - part.shape[0]
            part = jnp.concatenate([part, jnp.zeros((short, LANES), BF16)], axis=0)
            value = value + lax.dot_general(
                unit[...], part, CONTRACT, preferred_element_type=F32
            )
        wide[q] = value[:step].astype(BF16)
        wide[jnp.where(q == 0, CLASSES, RADIX - q)] = value[step:].astype(BF16)

    unrolled(CLASSES, 4 if boundary else 8, one)

    def out_copy(b):
        where = pl.ds(b * HALF * split, HALF * split)
        return pltpu.make_async_copy(out.at[where], out_ref.at[where], sems.at[b])

    def rows_of(b, part):
        return pl.ds(pl.multiple_of(part * high + b * HALF, HALF), HALF)

    def late_block(b, copy):
        for part in range(2):
            for side in range(sides):
                lanes = slice(side * LANES, (side + 1) * LANES)
                for first_k in range(0, RADIX, HALF):
                    value = jnp.swapaxes(
                        wide[first_k : first_k + HALF, rows_of(b, part), lanes], 0, 1
                    )
                    u, k = divmod(first_k, channels)
                    start = part * channels + k
                    for j in range(HALF):
                        group = (b * HALF + j) * split + u
                        out[group, side, start : start + HALF, :] = value[j]
        out_copy(b).start()

    def early_block(b, copy):
        def quad(k, copy):
            tiles = []
            for part in range(2):
                for side in range(sides):
                    lanes = slice(side * LANES, (side + 1) * LANES)
                    tiles += lane_swap([wide[4 * k + p, rows_of(b, part), lanes] for p in range(4)])
            value = jnp.swapaxes(jnp.stack(tiles), 0, 1)
            u, inside = lax.div(k, channels // 4), lax.rem(k, channels // 4)
            for j in range(HALF):
                out[(b * HALF + j) * split + u, inside] = value[j]

        unrolled(RADIX // 4, 4, quad)
        out_copy(b).start()

    unrolled(high // HALF, 1, early_block if boundary else late_block)

    def finish(b, carry):
        out_copy(b).wait()
        return carry

    lax.fori_loop(0, high // HALF, finish, 0)


def reorder(got, first, copies, put):
    n_inp, _, sets, rows, _ = got.shape
    assert HALF // (sets * PAIR) == 4

    def one(b, copy):
        here = pl.ds(pl.multiple_of(b * HALF, HALF), HALF)
        for tile in range(n_inp // 4):
            pieces = []
            for c in range(PAIR):
                for part in range(sets):
                    pieces += lane_swap(
                        [got[tile * 4 + p, first + c, part, here, :] for p in range(4)]
                    )
            value = jnp.swapaxes(jnp.stack(pieces), 0, 1)
            for j in range(HALF):
                put(b * HALF + j, tile, value[j])

    unrolled(rows // HALF, min(copies, rows // HALF), one)


def order_pair(got, j, copies, out):
    def put(r, tile, value):
        times = pl.ds(pl.multiple_of(j * HALF, HALF), HALF)
        out[r, times, tile * LANES : (tile + 1) * LANES] = value

    reorder(got, j * PAIR, copies, put)


def gram(left, right):
    return lax.dot_general(
        left,
        jnp.concatenate([left, right], axis=1),
        (((0,), (0,)), ((), ())),
        preferred_element_type=F32,
    )


def prior_kernel(got, out, rows):
    channels = out.shape[0]

    def step(j, carry):
        order_pair(got, j, 4, rows)
        return carry

    lax.fori_loop(0, got.shape[1] // PAIR, step, 0)

    def one(k, copy):
        real, imag = rows[k], rows[channels + k]
        left = jnp.concatenate([real, imag], axis=0)
        out[k] = gram(left, jnp.concatenate([-imag, real], axis=0))

    unrolled(channels, BLOCK, one)


def finish_kernel(scale, got_in, prior_in, out_ref, got, prior, rows, out, sems):
    n_inp, n_chan, quads, _, _ = got.shape
    steps = n_chan // PAIR
    channels, width = out.shape[1], out.shape[-1]
    count = channels // BLOCK

    def got_copy(j):
        where = (slice(None), pl.ds(j * PAIR, PAIR))
        return pltpu.make_async_copy(got_in.at[where], got.at[where], sems.at[count + j])

    def out_copy(j):
        where = (slice(None), pl.ds(j * BLOCK, BLOCK))
        return pltpu.make_async_copy(out.at[where], out_ref.at[where], sems.at[j])

    for j in range(steps):
        got_copy(j).start()
    prior_copy = pltpu.make_async_copy(prior_in, prior, sems.at[count + steps])
    prior_copy.start()

    def order(j, carry):
        got_copy(j).wait()

        def quad(k, copy):
            for c in range(PAIR):
                times = pl.ds(pl.multiple_of((j * PAIR + c) * HALF, HALF), HALF)
                for tile in range(n_inp // 4):
                    x = lane_swap([got[tile * 4 + p, j * PAIR + c, k] for p in range(4)])
                    for p in range(4):
                        rows[4 * k + p, times, tile * LANES : (tile + 1) * LANES] = x[p]

        unrolled(quads, 4, quad)
        return carry

    lax.fori_loop(0, steps, order, 0)
    prior_copy.wait()

    def some(j, carry):
        for i in range(BLOCK):
            k = j * BLOCK + i
            left = rows[k]
            parts = left.astype(F32).reshape(n_chan, 2, HALF // 2, width)
            right = jnp.stack([-parts[:, 1], parts[:, 0]], axis=1).reshape(left.shape)
            value = (gram(left, right.astype(BF16)) + prior[k]) * scale
            out[0, k] = value[:, :width].astype(BF16)
            out[1, k] = value[:, width:].astype(BF16)
        out_copy(j).start()
        return carry

    lax.fori_loop(0, count, some, 0)

    def finish(j, carry):
        out_copy(j).wait()
        return carry

    lax.fori_loop(0, count, finish, 0)


def params():
    return pltpu.CompilerParams(vmem_limit_bytes=VMEM)


def cost(flops, moved):
    return pl.CostEstimate(flops=int(flops), bytes_accessed=int(moved), transcendentals=0)


def on_device(voltages, history, taper):
    in_dev, s_dev, frame = voltages.shape
    taps = taper.shape[0]
    n_inp = lax.axis_size("inp")
    n_chan = lax.axis_size("chan")
    groups = n_inp * n_chan
    channels = BAND // groups
    total = n_inp * in_dev
    times = s_dev // 2
    early = taps - 1
    blocks = LANES // in_dev
    sets = times // blocks
    span = n_chan * times
    assert frame == RADIX * LANES and in_dev == 2 * HALF and PAIR * times == HALF
    assert early == times - 1 and RADIX % channels == 0 and n_inp % blocks == 0
    assert n_chan % PAIR == 0 and channels % BLOCK == 0

    outputs = 2 * BAND // CLASSES
    stage = stage_table(frame).astype(np.float32).astype(ml_dtypes.bfloat16)
    table = jnp.asarray(stage)
    upright = jnp.asarray(np.ascontiguousarray(stage.transpose(0, 2, 1)))
    unit = jnp.asarray(np.eye(outputs).astype(ml_dtypes.bfloat16))
    assert table.shape == (CLASSES, outputs, 2 * LANES) and outputs == LANES

    away = pl.BlockSpec(memory_space=pl.ANY)
    near = pl.BlockSpec(memory_space=pltpu.VMEM)

    def scratch(count, shape):
        return [
            pltpu.VMEM(voltages.shape, BF16),
            pltpu.VMEM(taper.shape, F32),
            pltpu.VMEM(shape, BF16),
            pltpu.VMEM((RADIX, count, HALF, LANES), F32),
            pltpu.VMEM((4, 8, 8, HALF, LANES), F32),
            pltpu.VMEM((CLASSES, count * in_dev, 2 * LANES), BF16),
            pltpu.SemaphoreType.DMA((2 * CHUNKS + 2,)),
        ]

    late_shape = (sets, 2 * channels, LANES)
    early_shape = (channels // 4, HALF, LANES)

    def sent(shape):
        return jax.ShapeDtypeStruct((groups,) + shape, BF16)

    def wide(shape):
        return [
            pltpu.VMEM((RADIX, RADIX, times * in_dev), BF16),
            pltpu.VMEM((groups,) + shape, BF16),
        ]

    carried = pl.pallas_call(
        carried_kernel,
        in_specs=[away] * 3,
        out_specs=away,
        out_shape=jax.ShapeDtypeStruct((CLASSES, early * in_dev, outputs), BF16),
        scratch_shapes=scratch(early, upright.shape)
        + [
            pltpu.VMEM((CLASSES, early * in_dev, outputs), BF16),
            pltpu.SemaphoreType.DMA((CHUNKS,)),
        ],
        compiler_params=params(),
        cost_estimate=cost(1e10, 2e7),
        name="carried",
    )(voltages, taper, upright)
    carried, later_taper = lax.optimization_barrier((carried, taper))
    carried = lax.ppermute(carried, "chan", [(i, i + 1) for i in range(n_chan - 1)])

    late_send = pl.pallas_call(
        lambda *refs: spectra_kernel(times, False, *refs),
        in_specs=[away] * 3,
        out_specs=away,
        out_shape=sent(late_shape),
        scratch_shapes=scratch(times, table.shape) + wide(late_shape),
        compiler_params=params(),
        cost_estimate=cost(5e10, 4e7),
        name="late",
    )(voltages, later_taper, table)

    def exchange(value, shape):
        value = lax.all_to_all(value, ("inp", "chan"), split_axis=0, concat_axis=0, tiled=True)
        return value.reshape((n_inp, n_chan) + shape)

    late_got = exchange(late_send, late_shape)

    keep = (lax.axis_index("chan") == 0).astype(F32).reshape(1)
    early_send = pl.pallas_call(
        lambda *refs: spectra_kernel(0, True, *refs),
        in_specs=[pl.BlockSpec(memory_space=pltpu.SMEM), near, near, near] + [away] * 3,
        out_specs=away,
        out_shape=sent(early_shape),
        scratch_shapes=scratch(times, table.shape) + wide(early_shape),
        compiler_params=params(),
        cost_estimate=cost(2e11, 4e7),
        name="early",
    )(keep, jnp.transpose(history, (1, 0, 2)), carried, unit, voltages, taper, table)
    early_got = exchange(early_send, early_shape)

    rows = pltpu.VMEM((2 * channels, span, total), BF16)
    prior_shape = (channels, total, 2 * total)
    prior = pl.pallas_call(
        prior_kernel,
        in_specs=[near],
        out_specs=near,
        out_shape=jax.ShapeDtypeStruct(prior_shape, F32),
        scratch_shapes=[rows],
        compiler_params=params(),
        cost_estimate=cost(1e4, 1e4),
        name="prior",
    )(late_got)
    return pl.pallas_call(
        lambda *refs: finish_kernel(1.0 / (n_chan * s_dev), *refs),
        in_specs=[away, away],
        out_specs=away,
        out_shape=jax.ShapeDtypeStruct((2, channels, total, total), BF16),
        scratch_shapes=[
            pltpu.VMEM(early_got.shape, BF16),
            pltpu.VMEM(prior_shape, F32),
            pltpu.VMEM((channels, n_chan * HALF, total), BF16),
            pltpu.VMEM((2, channels, total, total), BF16),
            pltpu.SemaphoreType.DMA((channels // BLOCK + n_chan // PAIR + 1,)),
        ],
        compiler_params=params(),
        cost_estimate=cost(1e10, 1e7),
        name="finish",
    )(early_got, prior)


def solution(mesh):
    in_specs = (P("inp", "chan", None), P("inp", None, None), P())
    out_specs = P(None, ("inp", "chan"), None, None)
    return jax.shard_map(
        on_device, mesh=mesh, in_specs=in_specs, out_specs=out_specs, check_vma=False
    )
```

```python
import math

import jax
import jax.numpy as jnp
import ml_dtypes
import numpy as np
from jax import lax
from jax.experimental import pallas as pl
from jax.experimental.pallas import tpu as pltpu
from jax.sharding import PartitionSpec as P

BAND = 2048
LOW = 1024
LANES = 128
RADIX = 64
HALF = 16
PAIR = 2
BLOCK = 8
CLASSES = RADIX // 2
ROOT = math.sqrt(0.5)
F32 = jnp.float32
BF16 = jnp.bfloat16
VMEM = 63 * 1024 * 1024


def stage_table(frame):
    high = BAND // RADIX
    lane = np.arange(LANES)
    table = np.zeros((CLASSES, 2, high, 2, 2, LANES))
    for q in range(CLASSES):
        for half in range(2):
            low = q if half == 0 else (RADIX - q if q else RADIX // 2)
            k = low + RADIX * (LOW // RADIX + np.arange(high))
            angle = 2.0 * np.pi * (np.outer(k, lane) % frame) / frame
            cos, sin = np.cos(angle), np.sin(angle)
            if q == 0:
                table[q, half, :, 0, half] = cos
                table[q, half, :, 1, half] = -sin
            elif half == 0:
                table[q, half, :, 0, 0] = cos
                table[q, half, :, 0, 1] = sin
                table[q, half, :, 1, 0] = -sin
                table[q, half, :, 1, 1] = cos
            else:
                table[q, half, :, 0, 0] = cos
                table[q, half, :, 0, 1] = -sin
                table[q, half, :, 1, 0] = -sin
                table[q, half, :, 1, 1] = -cos
    table = table / math.sqrt(frame)
    return table.swapaxes(2, 3).reshape(CLASSES, 2 * high * 2, 2 * LANES)


def real_dft8(x):
    s = [x[j] + x[j + 4] for j in range(4)]
    d = [x[j] - x[j + 4] for j in range(4)]
    e0, e1 = s[0] + s[2], s[0] - s[2]
    o0, o1 = s[1] + s[3], s[3] - s[1]
    u, v = (d[1] - d[3]) * ROOT, (d[1] + d[3]) * ROOT
    return [
        (e0 + o0, None),
        (d[0] + u, -(d[2] + v)),
        (e1, o1),
        (d[0] - u, d[2] - v),
        (e0 - o0, None),
    ]


def complex_dft8(x):
    def add(a, b):
        return (a[0] + b[0], a[1] + b[1])

    def sub(a, b):
        return (a[0] - b[0], a[1] - b[1])

    def add_i(a, b):
        return (a[0] - b[1], a[1] + b[0])

    def sub_i(a, b):
        return (a[0] + b[1], a[1] - b[0])

    s = [add(x[j], x[j + 4]) for j in range(4)]
    d = [sub(x[j], x[j + 4]) for j in range(4)]
    e0, e1 = add(s[0], s[2]), sub(s[0], s[2])
    o0, o1 = add(s[1], s[3]), sub(s[1], s[3])
    p, m = sub(d[1], d[3]), add(d[1], d[3])
    b = ((p[0] + m[1]) * ROOT, (p[1] - m[0]) * ROOT)
    c = ((m[1] - p[0]) * ROOT, (-p[1] - m[0]) * ROOT)
    f, g = sub_i(d[0], d[2]), add_i(d[0], d[2])
    return [
        add(e0, o0),
        add(f, b),
        sub_i(e1, o1),
        add(g, c),
        sub(e0, o0),
        sub(f, b),
        add_i(e1, o1),
        sub(g, c),
    ]


def turned(value, step):
    angle = 2.0 * math.pi * (step % RADIX) / RADIX
    cos, sin = math.cos(angle), math.sin(angle)
    real, imag = value
    if imag is None:
        return (real * cos, real * -sin)
    if step % RADIX == 0:
        return value
    return (real * cos + imag * sin, imag * cos - real * sin)


def unrolled(count, copies, body):
    def step(i, carry):
        for copy in range(copies):
            body(i * copies + copy, copy)
        return carry

    lax.fori_loop(0, count // copies, step, 0)


def transform_rows(fir, mids, zed, half, copies):
    halves = zed.shape[1] // (fir.shape[1] * HALF)

    def one(s, copy):
        mid = mids.at[copy]
        for low in range(8):
            parts = real_dft8([fir[8 * high + low, s] for high in range(8)])
            mid[0, low] = parts[0][0]
            mid[7, low] = parts[4][0]
            for k in (1, 2, 3):
                value = turned(parts[k], low * k)
                mid[2 * k - 1, low] = value[0]
                mid[2 * k, low] = value[1]
        rows = pl.ds(pl.multiple_of((s * halves + half) * HALF, HALF), HALF)

        def put(q, half, value):
            zed[q, rows, half * LANES : (half + 1) * LANES] = value.astype(BF16)

        parts = real_dft8([mid[0, low] for low in range(8)])
        put(0, 0, parts[0][0])
        put(0, 1, parts[4][0])
        for m in (1, 2, 3):
            put(8 * m, 0, parts[m][0])
            put(8 * m, 1, parts[m][1])
        for k in (1, 2, 3):
            parts = complex_dft8([(mid[2 * k - 1, low], mid[2 * k, low]) for low in range(8)])
            for m in range(8):
                index = k + 8 * m
                if index < CLASSES:
                    put(index, 0, parts[m][0])
                    put(index, 1, parts[m][1])
                else:
                    put(RADIX - index, 0, parts[m][0])
                    put(RADIX - index, 1, -parts[m][1])
        parts = complex_dft8([turned((mid[7, low], None), 4 * low) for low in range(8)])
        for m in range(4):
            put(4 + 8 * m, 0, parts[m][0])
            put(4 + 8 * m, 1, parts[m][1])

    unrolled(fir.shape[1], copies, one)


CHUNKS = 4
CONTRACT = (((1,), (1,)), ((), ()))


def fill(first, copies, hist, keep, volt_in, taper_in, table_in, volt, taper, held, fir, mid, zed, sems):
    taps = taper.shape[0]
    in_dev, s_dev, frame = volt.shape
    halves = in_dev // HALF
    count = fir.shape[1]
    part = frame // CHUNKS
    wanted = [f for f in range(first - taps + 1, first + count) if f < s_dev]

    def volt_copy(h, j):
        where = (pl.ds(h * HALF, HALF), slice(None), pl.ds(pl.multiple_of(j * part, part), part))
        return pltpu.make_async_copy(volt_in.at[where], volt.at[where], sems.at[h * CHUNKS + j])

    taper_copy = pltpu.make_async_copy(taper_in, taper, sems.at[halves * CHUNKS])
    table_copy = pltpu.make_async_copy(table_in, held, sems.at[halves * CHUNKS + 1])
    taper_copy.start()
    for h in range(halves):
        for j in range(CHUNKS):
            volt_copy(h, j).start()
    table_copy.start()
    taper_copy.wait()

    def one_half(h, carry):
        inputs = pl.ds(pl.multiple_of(h * HALF, HALF), HALF)

        def one_chunk(j, carry):
            volt_copy(h, j).wait()

            def one(i, copy):
                a = j * (part // LANES) + i
                lanes = pl.ds(pl.multiple_of(a * LANES, LANES), LANES)
                by_time = jnp.swapaxes(volt[inputs, :, lanes], 0, 1)
                frames = {}
                for f in wanted:
                    if f >= 0:
                        frames[f] = by_time[f].astype(F32)
                    elif hist is not None:
                        frames[f] = hist[taps - 1 + f, inputs, lanes].astype(F32) * keep
                weights = [taper[t : t + 1, lanes] for t in range(taps)]
                for row in range(count):
                    total = None
                    for t in range(taps):
                        f = first + row + t - taps + 1
                        if f in frames:
                            term = weights[t] * frames[f]
                            total = term if total is None else total + term
                    fir[a, row] = total

            unrolled(part // LANES, copies[0], one)
            return carry

        lax.fori_loop(0, CHUNKS, one_chunk, 0)
        transform_rows(fir, mid, zed, h, copies[1])
        return carry

    lax.fori_loop(0, halves, one_half, 0)
    table_copy.wait()


def carried_kernel(volt_in, taper_in, table_in, out_ref, *scratch):
    *scratch, out, out_sems = scratch
    volt, taper, held, fir, mid, zed, sems = scratch
    fill(
        volt.shape[1], (16, 1), None, None,
        volt_in, taper_in, table_in, volt, taper, held, fir, mid, zed, sems,
    )
    block = CLASSES // CHUNKS

    def out_copy(j):
        where = pl.ds(j * block, block)
        return pltpu.make_async_copy(out.at[where], out_ref.at[where], out_sems.at[j])

    def some(j, carry):
        for i in range(block):
            q = j * block + i
            out[q] = jnp.dot(zed[q], held[q], preferred_element_type=F32).astype(BF16)
        out_copy(j).start()
        return carry

    lax.fori_loop(0, CHUNKS, some, 0)

    def finish(j, carry):
        out_copy(j).wait()
        return carry

    lax.fori_loop(0, CHUNKS, finish, 0)


def lane_swap(x):
    width = LANES // 4
    block = lax.broadcasted_iota(jnp.int32, (HALF, LANES), 1) // width
    x = list(x)
    for d in (1, 2):
        mask = (block & d) == 0
        for p in range(4):
            if p & d == 0:
                low, up = x[p], x[p | d]
                x[p] = jnp.where(mask, low, pltpu.roll(up, width * d, 1))
                x[p | d] = jnp.where(mask, pltpu.roll(low, LANES - width * d, 1), up)
    return x


def spectra_kernel(first, boundary, *refs):
    if boundary:
        keep, hist, carried, unit, *refs = refs
        keep = keep[0]
    else:
        keep, hist = None, None
    volt_in, taper_in, table_in, out_ref, volt, taper, held, fir, mid, zed, sems, wide, out = refs
    fill(
        first, (16, 4) if boundary else (8, 2), hist, keep,
        volt_in, taper_in, table_in, volt, taper, held, fir, mid, zed, sems,
    )
    step = RADIX
    high = step // 2
    sides = wide.shape[2] // LANES
    split = out.shape[0] // high
    channels = RADIX // split

    def one(q, copy):
        value = lax.dot_general(held[q], zed[q], CONTRACT, preferred_element_type=F32)
        if boundary:
            part = carried[q]
            short = zed.shape[1] - part.shape[0]
            part = jnp.concatenate([part, jnp.zeros((short, LANES), BF16)], axis=0)
            value = value + lax.dot_general(
                unit[...], part, CONTRACT, preferred_element_type=F32
            )
        wide[q] = value[:step].astype(BF16)
        wide[jnp.where(q == 0, CLASSES, RADIX - q)] = value[step:].astype(BF16)

    unrolled(CLASSES, 4 if boundary else 8, one)

    def out_copy(b):
        where = pl.ds(b * HALF * split, HALF * split)
        return pltpu.make_async_copy(out.at[where], out_ref.at[where], sems.at[b])

    def rows_of(b, part):
        return pl.ds(pl.multiple_of(part * high + b * HALF, HALF), HALF)

    def late_block(b, copy):
        for part in range(2):
            for side in range(sides):
                lanes = slice(side * LANES, (side + 1) * LANES)
                for first_k in range(0, RADIX, HALF):
                    value = jnp.swapaxes(
                        wide[first_k : first_k + HALF, rows_of(b, part), lanes], 0, 1
                    )
                    u, k = divmod(first_k, channels)
                    start = part * channels + k
                    for j in range(HALF):
                        group = (b * HALF + j) * split + u
                        out[group, side, start : start + HALF, :] = value[j]
        out_copy(b).start()

    def early_block(b, copy):
        def quad(k, copy):
            tiles = []
            for part in range(2):
                for side in range(sides):
                    lanes = slice(side * LANES, (side + 1) * LANES)
                    tiles += lane_swap([wide[4 * k + p, rows_of(b, part), lanes] for p in range(4)])
            value = jnp.swapaxes(jnp.stack(tiles), 0, 1)
            u, inside = lax.div(k, channels // 4), lax.rem(k, channels // 4)
            for j in range(HALF):
                out[(b * HALF + j) * split + u, inside] = value[j]

        unrolled(RADIX // 4, 4, quad)
        out_copy(b).start()

    unrolled(high // HALF, 1, early_block if boundary else late_block)

    def finish(b, carry):
        out_copy(b).wait()
        return carry

    lax.fori_loop(0, high // HALF, finish, 0)


def reorder(got, first, copies, put):
    n_inp, _, sets, rows, _ = got.shape
    assert HALF // (sets * PAIR) == 4

    def one(b, copy):
        here = pl.ds(pl.multiple_of(b * HALF, HALF), HALF)
        for tile in range(n_inp // 4):
            pieces = []
            for c in range(PAIR):
                for part in range(sets):
                    pieces += lane_swap(
                        [got[tile * 4 + p, first + c, part, here, :] for p in range(4)]
                    )
            value = jnp.swapaxes(jnp.stack(pieces), 0, 1)
            for j in range(HALF):
                put(b * HALF + j, tile, value[j])

    unrolled(rows // HALF, min(copies, rows // HALF), one)


def order_pair(got, j, copies, out):
    def put(r, tile, value):
        times = pl.ds(pl.multiple_of(j * HALF, HALF), HALF)
        out[r, times, tile * LANES : (tile + 1) * LANES] = value

    reorder(got, j * PAIR, copies, put)


def gram(left, right):
    return lax.dot_general(
        left,
        jnp.concatenate([left, right], axis=1),
        (((0,), (0,)), ((), ())),
        preferred_element_type=F32,
    )


def order_kernel(got, out):
    def step(j, carry):
        order_pair(got, j, 4, out)
        return carry

    lax.fori_loop(0, got.shape[1] // PAIR, step, 0)


def finish_kernel(scale, got_in, late_in, out_ref, got, late, rows, out, sems):
    n_inp, n_chan, quads, _, _ = got.shape
    steps = n_chan // PAIR
    channels, width = out.shape[1], out.shape[-1]
    count = channels // BLOCK

    def got_copy(j):
        where = (slice(None), pl.ds(j * PAIR, PAIR))
        return pltpu.make_async_copy(got_in.at[where], got.at[where], sems.at[count + j])

    def out_copy(j):
        where = (slice(None), pl.ds(j * BLOCK, BLOCK))
        return pltpu.make_async_copy(out.at[where], out_ref.at[where], sems.at[j])

    for j in range(steps):
        got_copy(j).start()
    late_copy = pltpu.make_async_copy(late_in, late, sems.at[count + steps])
    late_copy.start()

    def order(j, carry):
        got_copy(j).wait()

        def quad(k, copy):
            for c in range(PAIR):
                times = pl.ds(pl.multiple_of((j * PAIR + c) * HALF, HALF), HALF)
                for tile in range(n_inp // 4):
                    x = lane_swap([got[tile * 4 + p, j * PAIR + c, k] for p in range(4)])
                    for p in range(4):
                        rows[4 * k + p, times, tile * LANES : (tile + 1) * LANES] = x[p]

        unrolled(quads, 4, quad)
        return carry

    lax.fori_loop(0, steps, order, 0)
    late_copy.wait()

    def some(j, carry):
        for i in range(BLOCK):
            k = j * BLOCK + i
            real, imag, both = late[k], late[channels + k], rows[k]
            parts = both.astype(F32).reshape(n_chan, 2, HALF // 2, width)
            turned_rows = jnp.stack([-parts[:, 1], parts[:, 0]], axis=1).reshape(both.shape)
            value = gram(
                jnp.concatenate([real, imag, both], axis=0),
                jnp.concatenate([-imag, real, turned_rows.astype(BF16)], axis=0),
            )
            value = value * scale
            out[0, k] = value[:, :width].astype(BF16)
            out[1, k] = value[:, width:].astype(BF16)
        out_copy(j).start()
        return carry

    lax.fori_loop(0, count, some, 0)

    def finish(j, carry):
        out_copy(j).wait()
        return carry

    lax.fori_loop(0, count, finish, 0)


def params():
    return pltpu.CompilerParams(vmem_limit_bytes=VMEM)


def cost(flops, moved):
    return pl.CostEstimate(flops=int(flops), bytes_accessed=int(moved), transcendentals=0)


def on_device(voltages, history, taper):
    in_dev, s_dev, frame = voltages.shape
    taps = taper.shape[0]
    n_inp = lax.axis_size("inp")
    n_chan = lax.axis_size("chan")
    groups = n_inp * n_chan
    channels = BAND // groups
    total = n_inp * in_dev
    times = s_dev // 2
    early = taps - 1
    blocks = LANES // in_dev
    sets = times // blocks
    span = n_chan * times
    assert frame == RADIX * LANES and in_dev == 2 * HALF and PAIR * times == HALF
    assert early == times - 1 and RADIX % channels == 0 and n_inp % blocks == 0
    assert n_chan % PAIR == 0 and channels % BLOCK == 0

    outputs = 2 * BAND // CLASSES
    stage = stage_table(frame).astype(np.float32).astype(ml_dtypes.bfloat16)
    table = jnp.asarray(stage)
    upright = jnp.asarray(np.ascontiguousarray(stage.transpose(0, 2, 1)))
    unit = jnp.asarray(np.eye(outputs).astype(ml_dtypes.bfloat16))
    assert table.shape == (CLASSES, outputs, 2 * LANES) and outputs == LANES

    away = pl.BlockSpec(memory_space=pl.ANY)
    near = pl.BlockSpec(memory_space=pltpu.VMEM)

    def scratch(count, shape):
        return [
            pltpu.VMEM(voltages.shape, BF16),
            pltpu.VMEM(taper.shape, F32),
            pltpu.VMEM(shape, BF16),
            pltpu.VMEM((RADIX, count, HALF, LANES), F32),
            pltpu.VMEM((4, 8, 8, HALF, LANES), F32),
            pltpu.VMEM((CLASSES, count * in_dev, 2 * LANES), BF16),
            pltpu.SemaphoreType.DMA((2 * CHUNKS + 2,)),
        ]

    late_shape = (sets, 2 * channels, LANES)
    early_shape = (channels // 4, HALF, LANES)

    def sent(shape):
        return jax.ShapeDtypeStruct((groups,) + shape, BF16)

    def wide(shape):
        return [
            pltpu.VMEM((RADIX, RADIX, times * in_dev), BF16),
            pltpu.VMEM((groups,) + shape, BF16),
        ]

    carried = pl.pallas_call(
        carried_kernel,
        in_specs=[away] * 3,
        out_specs=away,
        out_shape=jax.ShapeDtypeStruct((CLASSES, early * in_dev, outputs), BF16),
        scratch_shapes=scratch(early, upright.shape)
        + [
            pltpu.VMEM((CLASSES, early * in_dev, outputs), BF16),
            pltpu.SemaphoreType.DMA((CHUNKS,)),
        ],
        compiler_params=params(),
        cost_estimate=cost(1e10, 2e7),
        name="carried",
    )(voltages, taper, upright)
    carried, later_taper = lax.optimization_barrier((carried, taper))
    carried = lax.ppermute(carried, "chan", [(i, i + 1) for i in range(n_chan - 1)])

    late_send = pl.pallas_call(
        lambda *refs: spectra_kernel(times, False, *refs),
        in_specs=[away] * 3,
        out_specs=away,
        out_shape=sent(late_shape),
        scratch_shapes=scratch(times, table.shape) + wide(late_shape),
        compiler_params=params(),
        cost_estimate=cost(5e10, 4e7),
        name="late",
    )(voltages, later_taper, table)

    def exchange(value, shape):
        value = lax.all_to_all(value, ("inp", "chan"), split_axis=0, concat_axis=0, tiled=True)
        return value.reshape((n_inp, n_chan) + shape)

    late_got = exchange(late_send, late_shape)

    keep = (lax.axis_index("chan") == 0).astype(F32).reshape(1)
    early_send = pl.pallas_call(
        lambda *refs: spectra_kernel(0, True, *refs),
        in_specs=[pl.BlockSpec(memory_space=pltpu.SMEM), near, near, near] + [away] * 3,
        out_specs=away,
        out_shape=sent(early_shape),
        scratch_shapes=scratch(times, table.shape) + wide(early_shape),
        compiler_params=params(),
        cost_estimate=cost(2e11, 4e7),
        name="early",
    )(keep, jnp.transpose(history, (1, 0, 2)), carried, unit, voltages, taper, table)
    early_got = exchange(early_send, early_shape)

    late_rows = pl.pallas_call(
        order_kernel,
        in_specs=[near],
        out_specs=near,
        out_shape=jax.ShapeDtypeStruct((2 * channels, span, total), BF16),
        compiler_params=params(),
        cost_estimate=cost(1e4, 1e4),
        name="order",
    )(late_got)
    return pl.pallas_call(
        lambda *refs: finish_kernel(1.0 / (n_chan * s_dev), *refs),
        in_specs=[away, away],
        out_specs=away,
        out_shape=jax.ShapeDtypeStruct((2, channels, total, total), BF16),
        scratch_shapes=[
            pltpu.VMEM(early_got.shape, BF16),
            pltpu.VMEM(late_rows.shape, BF16),
            pltpu.VMEM((channels, n_chan * HALF, total), BF16),
            pltpu.VMEM((2, channels, total, total), BF16),
            pltpu.SemaphoreType.DMA((channels // BLOCK + n_chan // PAIR + 1,)),
        ],
        compiler_params=params(),
        cost_estimate=cost(1e10, 1e7),
        name="finish",
    )(early_got, late_rows)


def solution(mesh):
    in_specs = (P("inp", "chan", None), P("inp", None, None), P())
    out_specs = P(None, ("inp", "chan"), None, None)
    return jax.shard_map(
        on_device, mesh=mesh, in_specs=in_specs, out_specs=out_specs, check_vma=False
    )
```

```python
import math

import jax
import jax.numpy as jnp
import ml_dtypes
import numpy as np
from jax import lax
from jax.experimental import pallas as pl
from jax.experimental.pallas import tpu as pltpu
from jax.sharding import PartitionSpec as P

BAND = 2048
LOW = 1024
LANES = 128
RADIX = 64
HALF = 16
PAIR = 2
BLOCK = 8
CLASSES = RADIX // 2
ROOT = math.sqrt(0.5)
F32 = jnp.float32
BF16 = jnp.bfloat16
VMEM = 63 * 1024 * 1024


def stage_table(frame):
    high = BAND // RADIX
    lane = np.arange(LANES)
    table = np.zeros((CLASSES, 2, high, 2, 2, LANES))
    for q in range(CLASSES):
        for half in range(2):
            low = q if half == 0 else (RADIX - q if q else RADIX // 2)
            k = low + RADIX * (LOW // RADIX + np.arange(high))
            angle = 2.0 * np.pi * (np.outer(k, lane) % frame) / frame
            cos, sin = np.cos(angle), np.sin(angle)
            if q == 0:
                table[q, half, :, 0, half] = cos
                table[q, half, :, 1, half] = -sin
            elif half == 0:
                table[q, half, :, 0, 0] = cos
                table[q, half, :, 0, 1] = sin
                table[q, half, :, 1, 0] = -sin
                table[q, half, :, 1, 1] = cos
            else:
                table[q, half, :, 0, 0] = cos
                table[q, half, :, 0, 1] = -sin
                table[q, half, :, 1, 0] = -sin
                table[q, half, :, 1, 1] = -cos
    table = table / math.sqrt(frame)
    return table.swapaxes(2, 3).reshape(CLASSES, 2 * high * 2, 2 * LANES)


def real_dft8(x):
    s = [x[j] + x[j + 4] for j in range(4)]
    d = [x[j] - x[j + 4] for j in range(4)]
    e0, e1 = s[0] + s[2], s[0] - s[2]
    o0, o1 = s[1] + s[3], s[3] - s[1]
    u, v = (d[1] - d[3]) * ROOT, (d[1] + d[3]) * ROOT
    return [
        (e0 + o0, None),
        (d[0] + u, -(d[2] + v)),
        (e1, o1),
        (d[0] - u, d[2] - v),
        (e0 - o0, None),
    ]


def complex_dft8(x):
    def add(a, b):
        return (a[0] + b[0], a[1] + b[1])

    def sub(a, b):
        return (a[0] - b[0], a[1] - b[1])

    def add_i(a, b):
        return (a[0] - b[1], a[1] + b[0])

    def sub_i(a, b):
        return (a[0] + b[1], a[1] - b[0])

    s = [add(x[j], x[j + 4]) for j in range(4)]
    d = [sub(x[j], x[j + 4]) for j in range(4)]
    e0, e1 = add(s[0], s[2]), sub(s[0], s[2])
    o0, o1 = add(s[1], s[3]), sub(s[1], s[3])
    p, m = sub(d[1], d[3]), add(d[1], d[3])
    b = ((p[0] + m[1]) * ROOT, (p[1] - m[0]) * ROOT)
    c = ((m[1] - p[0]) * ROOT, (-p[1] - m[0]) * ROOT)
    f, g = sub_i(d[0], d[2]), add_i(d[0], d[2])
    return [
        add(e0, o0),
        add(f, b),
        sub_i(e1, o1),
        add(g, c),
        sub(e0, o0),
        sub(f, b),
        add_i(e1, o1),
        sub(g, c),
    ]


def turned(value, step):
    angle = 2.0 * math.pi * (step % RADIX) / RADIX
    cos, sin = math.cos(angle), math.sin(angle)
    real, imag = value
    if imag is None:
        return (real * cos, real * -sin)
    if step % RADIX == 0:
        return value
    return (real * cos + imag * sin, imag * cos - real * sin)


def unrolled(count, copies, body):
    def step(i, carry):
        for copy in range(copies):
            body(i * copies + copy, copy)
        return carry

    lax.fori_loop(0, count // copies, step, 0)


def transform_rows(fir, mids, zed, half, copies):
    halves = zed.shape[1] // (fir.shape[1] * HALF)

    def one(s, copy):
        mid = mids.at[copy]
        for low in range(8):
            parts = real_dft8([fir[8 * high + low, s] for high in range(8)])
            mid[0, low] = parts[0][0]
            mid[7, low] = parts[4][0]
            for k in (1, 2, 3):
                value = turned(parts[k], low * k)
                mid[2 * k - 1, low] = value[0]
                mid[2 * k, low] = value[1]
        rows = pl.ds(pl.multiple_of((s * halves + half) * HALF, HALF), HALF)

        def put(q, half, value):
            zed[q, rows, half * LANES : (half + 1) * LANES] = value.astype(BF16)

        parts = real_dft8([mid[0, low] for low in range(8)])
        put(0, 0, parts[0][0])
        put(0, 1, parts[4][0])
        for m in (1, 2, 3):
            put(8 * m, 0, parts[m][0])
            put(8 * m, 1, parts[m][1])
        for k in (1, 2, 3):
            parts = complex_dft8([(mid[2 * k - 1, low], mid[2 * k, low]) for low in range(8)])
            for m in range(8):
                index = k + 8 * m
                if index < CLASSES:
                    put(index, 0, parts[m][0])
                    put(index, 1, parts[m][1])
                else:
                    put(RADIX - index, 0, parts[m][0])
                    put(RADIX - index, 1, -parts[m][1])
        parts = complex_dft8([turned((mid[7, low], None), 4 * low) for low in range(8)])
        for m in range(4):
            put(4 + 8 * m, 0, parts[m][0])
            put(4 + 8 * m, 1, parts[m][1])

    unrolled(fir.shape[1], copies, one)


CHUNKS = 4
CONTRACT = (((1,), (1,)), ((), ()))


def fill(first, copies, hist, keep, volt_in, taper_in, table_in, volt, taper, held, fir, mid, zed, sems):
    taps = taper.shape[0]
    in_dev, s_dev, frame = volt.shape
    halves = in_dev // HALF
    count = fir.shape[1]
    part = frame // CHUNKS
    wanted = [f for f in range(first - taps + 1, first + count) if f < s_dev]

    def volt_copy(h, j):
        where = (pl.ds(h * HALF, HALF), slice(None), pl.ds(pl.multiple_of(j * part, part), part))
        return pltpu.make_async_copy(volt_in.at[where], volt.at[where], sems.at[h * CHUNKS + j])

    taper_copy = pltpu.make_async_copy(taper_in, taper, sems.at[halves * CHUNKS])
    table_copy = pltpu.make_async_copy(table_in, held, sems.at[halves * CHUNKS + 1])
    taper_copy.start()
    for h in range(halves):
        for j in range(CHUNKS):
            volt_copy(h, j).start()
    table_copy.start()
    taper_copy.wait()

    def one_half(h, carry):
        inputs = pl.ds(pl.multiple_of(h * HALF, HALF), HALF)

        def one_chunk(j, carry):
            volt_copy(h, j).wait()

            def one(i, copy):
                a = j * (part // LANES) + i
                lanes = pl.ds(pl.multiple_of(a * LANES, LANES), LANES)
                by_time = jnp.swapaxes(volt[inputs, :, lanes], 0, 1)
                frames = {}
                for f in wanted:
                    if f >= 0:
                        frames[f] = by_time[f].astype(F32)
                    elif hist is not None:
                        frames[f] = hist[taps - 1 + f, inputs, lanes].astype(F32) * keep
                weights = [taper[t : t + 1, lanes] for t in range(taps)]
                for row in range(count):
                    total = None
                    for t in range(taps):
                        f = first + row + t - taps + 1
                        if f in frames:
                            term = weights[t] * frames[f]
                            total = term if total is None else total + term
                    fir[a, row] = total

            unrolled(part // LANES, copies[0], one)
            return carry

        lax.fori_loop(0, CHUNKS, one_chunk, 0)
        transform_rows(fir, mid, zed, h, copies[1])
        return carry

    lax.fori_loop(0, halves, one_half, 0)
    table_copy.wait()


def carried_kernel(volt_in, taper_in, table_in, out_ref, *scratch):
    *scratch, out, out_sems = scratch
    volt, taper, held, fir, mid, zed, sems = scratch
    fill(
        volt.shape[1], (16, 1), None, None,
        volt_in, taper_in, table_in, volt, taper, held, fir, mid, zed, sems,
    )
    block = CLASSES // CHUNKS

    def out_copy(j):
        where = pl.ds(j * block, block)
        return pltpu.make_async_copy(out.at[where], out_ref.at[where], out_sems.at[j])

    def some(j, carry):
        for i in range(block):
            q = j * block + i
            out[q] = jnp.dot(zed[q], held[q], preferred_element_type=F32).astype(BF16)
        out_copy(j).start()
        return carry

    lax.fori_loop(0, CHUNKS, some, 0)

    def finish(j, carry):
        out_copy(j).wait()
        return carry

    lax.fori_loop(0, CHUNKS, finish, 0)


def lane_swap(x):
    width = LANES // 4
    block = lax.broadcasted_iota(jnp.int32, (HALF, LANES), 1) // width
    x = list(x)
    for d in (1, 2):
        mask = (block & d) == 0
        for p in range(4):
            if p & d == 0:
                low, up = x[p], x[p | d]
                x[p] = jnp.where(mask, low, pltpu.roll(up, width * d, 1))
                x[p | d] = jnp.where(mask, pltpu.roll(low, LANES - width * d, 1), up)
    return x


def spectra_kernel(first, boundary, *refs):
    if boundary:
        keep, hist, carried, unit, *refs = refs
        keep = keep[0]
    else:
        keep, hist = None, None
    volt_in, taper_in, table_in, out_ref, volt, taper, held, fir, mid, zed, sems, wide, out = refs
    fill(
        first, (16, 4) if boundary else (8, 2), hist, keep,
        volt_in, taper_in, table_in, volt, taper, held, fir, mid, zed, sems,
    )
    step = RADIX
    high = step // 2
    sides = wide.shape[2] // LANES
    split = out.shape[0] // high
    channels = RADIX // split

    def one(q, copy):
        value = lax.dot_general(held[q], zed[q], CONTRACT, preferred_element_type=F32)
        if boundary:
            part = carried[q]
            short = zed.shape[1] - part.shape[0]
            part = jnp.concatenate([part, jnp.zeros((short, LANES), BF16)], axis=0)
            value = value + lax.dot_general(
                unit[...], part, CONTRACT, preferred_element_type=F32
            )
        wide[q] = value[:step].astype(BF16)
        wide[jnp.where(q == 0, CLASSES, RADIX - q)] = value[step:].astype(BF16)

    unrolled(CLASSES, 4 if boundary else 8, one)

    def out_copy(b):
        where = pl.ds(b * HALF * split, HALF * split)
        return pltpu.make_async_copy(out.at[where], out_ref.at[where], sems.at[b])

    def rows_of(b, part):
        return pl.ds(pl.multiple_of(part * high + b * HALF, HALF), HALF)

    def late_block(b, copy):
        for part in range(2):
            for side in range(sides):
                lanes = slice(side * LANES, (side + 1) * LANES)
                for first_k in range(0, RADIX, HALF):
                    value = jnp.swapaxes(
                        wide[first_k : first_k + HALF, rows_of(b, part), lanes], 0, 1
                    )
                    u, k = divmod(first_k, channels)
                    start = part * channels + k
                    for j in range(HALF):
                        group = (b * HALF + j) * split + u
                        out[group, side, start : start + HALF, :] = value[j]
        out_copy(b).start()

    def early_block(b, copy):
        def quad(k, copy):
            tiles = []
            for part in range(2):
                for side in range(sides):
                    lanes = slice(side * LANES, (side + 1) * LANES)
                    tiles += lane_swap([wide[4 * k + p, rows_of(b, part), lanes] for p in range(4)])
            value = jnp.swapaxes(jnp.stack(tiles), 0, 1)
            u, inside = lax.div(k, channels // 4), lax.rem(k, channels // 4)
            for j in range(HALF):
                out[(b * HALF + j) * split + u, inside] = value[j]

        unrolled(RADIX // 4, 4, quad)
        out_copy(b).start()

    unrolled(high // HALF, 1, early_block if boundary else late_block)

    def finish(b, carry):
        out_copy(b).wait()
        return carry

    lax.fori_loop(0, high // HALF, finish, 0)


def reorder(got, first, copies, put):
    n_inp, _, sets, rows, _ = got.shape
    assert HALF // (sets * PAIR) == 4

    def one(b, copy):
        here = pl.ds(pl.multiple_of(b * HALF, HALF), HALF)
        for tile in range(n_inp // 4):
            pieces = []
            for c in range(PAIR):
                for part in range(sets):
                    pieces += lane_swap(
                        [got[tile * 4 + p, first + c, part, here, :] for p in range(4)]
                    )
            value = jnp.swapaxes(jnp.stack(pieces), 0, 1)
            for j in range(HALF):
                put(b * HALF + j, tile, value[j])

    unrolled(rows // HALF, min(copies, rows // HALF), one)


def order_pair(got, j, copies, out):
    def put(r, tile, value):
        times = pl.ds(pl.multiple_of(j * HALF, HALF), HALF)
        out[r, times, tile * LANES : (tile + 1) * LANES] = value

    reorder(got, j * PAIR, copies, put)


def gram(left, right):
    return lax.dot_general(
        left,
        jnp.concatenate([left, right], axis=1),
        (((0,), (0,)), ((), ())),
        preferred_element_type=F32,
    )


def prior_kernel(got, out, rows):
    channels = out.shape[0]

    def step(j, carry):
        order_pair(got, j, 4, rows)
        return carry

    lax.fori_loop(0, got.shape[1] // PAIR, step, 0)

    def one(k, copy):
        real, imag = rows[k], rows[channels + k]
        left = jnp.concatenate([real, imag], axis=0)
        out[k] = gram(left, jnp.concatenate([-imag, real], axis=0))

    unrolled(channels, BLOCK, one)


def finish_kernel(scale, got_in, prior_in, out_ref, got, prior, rows, out, sems):
    n_inp, n_chan, quads, _, _ = got.shape
    steps = n_chan // PAIR
    channels, width = out.shape[1], out.shape[-1]
    count = channels // BLOCK

    def got_copy(j):
        where = (slice(None), pl.ds(j * PAIR, PAIR))
        return pltpu.make_async_copy(got_in.at[where], got.at[where], sems.at[count + j])

    def out_copy(j):
        where = (slice(None), pl.ds(j * BLOCK, BLOCK))
        return pltpu.make_async_copy(out.at[where], out_ref.at[where], sems.at[j])

    for j in range(steps):
        got_copy(j).start()
    def prior_copy(j):
        where = pl.ds(j * BLOCK, BLOCK)
        return pltpu.make_async_copy(
            prior_in.at[where], prior.at[where], sems.at[count + steps + j]
        )

    for j in range(count):
        prior_copy(j).start()

    def order(j, carry):
        got_copy(j).wait()

        def quad(k, copy):
            for c in range(PAIR):
                times = pl.ds(pl.multiple_of((j * PAIR + c) * HALF, HALF), HALF)
                for tile in range(n_inp // 4):
                    x = lane_swap([got[tile * 4 + p, j * PAIR + c, k] for p in range(4)])
                    for p in range(4):
                        rows[4 * k + p, times, tile * LANES : (tile + 1) * LANES] = x[p]

        unrolled(quads, 4, quad)
        return carry

    lax.fori_loop(0, steps, order, 0)

    def some(j, carry):
        prior_copy(j).wait()
        for i in range(BLOCK):
            k = j * BLOCK + i
            left = rows[k]
            parts = left.astype(F32).reshape(n_chan, 2, HALF // 2, width)
            right = jnp.stack([-parts[:, 1], parts[:, 0]], axis=1).reshape(left.shape)
            value = (gram(left, right.astype(BF16)) + prior[k]) * scale
            out[0, k] = value[:, :width].astype(BF16)
            out[1, k] = value[:, width:].astype(BF16)
        out_copy(j).start()
        return carry

    lax.fori_loop(0, count, some, 0)

    def finish(j, carry):
        out_copy(j).wait()
        return carry

    lax.fori_loop(0, count, finish, 0)


def params():
    return pltpu.CompilerParams(vmem_limit_bytes=VMEM)


def cost(flops, moved):
    return pl.CostEstimate(flops=int(flops), bytes_accessed=int(moved), transcendentals=0)


def on_device(voltages, history, taper):
    in_dev, s_dev, frame = voltages.shape
    taps = taper.shape[0]
    n_inp = lax.axis_size("inp")
    n_chan = lax.axis_size("chan")
    groups = n_inp * n_chan
    channels = BAND // groups
    total = n_inp * in_dev
    times = s_dev // 2
    early = taps - 1
    blocks = LANES // in_dev
    sets = times // blocks
    span = n_chan * times
    assert frame == RADIX * LANES and in_dev == 2 * HALF and PAIR * times == HALF
    assert early == times - 1 and RADIX % channels == 0 and n_inp % blocks == 0
    assert n_chan % PAIR == 0 and channels % BLOCK == 0

    outputs = 2 * BAND // CLASSES
    stage = stage_table(frame).astype(np.float32).astype(ml_dtypes.bfloat16)
    table = jnp.asarray(stage)
    upright = jnp.asarray(np.ascontiguousarray(stage.transpose(0, 2, 1)))
    unit = jnp.asarray(np.eye(outputs).astype(ml_dtypes.bfloat16))
    assert table.shape == (CLASSES, outputs, 2 * LANES) and outputs == LANES

    away = pl.BlockSpec(memory_space=pl.ANY)
    near = pl.BlockSpec(memory_space=pltpu.VMEM)

    def scratch(count, shape):
        return [
            pltpu.VMEM(voltages.shape, BF16),
            pltpu.VMEM(taper.shape, F32),
            pltpu.VMEM(shape, BF16),
            pltpu.VMEM((RADIX, count, HALF, LANES), F32),
            pltpu.VMEM((4, 8, 8, HALF, LANES), F32),
            pltpu.VMEM((CLASSES, count * in_dev, 2 * LANES), BF16),
            pltpu.SemaphoreType.DMA((2 * CHUNKS + 2,)),
        ]

    late_shape = (sets, 2 * channels, LANES)
    early_shape = (channels // 4, HALF, LANES)

    def sent(shape):
        return jax.ShapeDtypeStruct((groups,) + shape, BF16)

    def wide(shape):
        return [
            pltpu.VMEM((RADIX, RADIX, times * in_dev), BF16),
            pltpu.VMEM((groups,) + shape, BF16),
        ]

    carried = pl.pallas_call(
        carried_kernel,
        in_specs=[away] * 3,
        out_specs=away,
        out_shape=jax.ShapeDtypeStruct((CLASSES, early * in_dev, outputs), BF16),
        scratch_shapes=scratch(early, upright.shape)
        + [
            pltpu.VMEM((CLASSES, early * in_dev, outputs), BF16),
            pltpu.SemaphoreType.DMA((CHUNKS,)),
        ],
        compiler_params=params(),
        cost_estimate=cost(1e10, 2e7),
        name="carried",
    )(voltages, taper, upright)
    carried, later_taper = lax.optimization_barrier((carried, taper))
    carried = lax.ppermute(carried, "chan", [(i, i + 1) for i in range(n_chan - 1)])

    late_send = pl.pallas_call(
        lambda *refs: spectra_kernel(times, False, *refs),
        in_specs=[away] * 3,
        out_specs=away,
        out_shape=sent(late_shape),
        scratch_shapes=scratch(times, table.shape) + wide(late_shape),
        compiler_params=params(),
        cost_estimate=cost(5e10, 4e7),
        name="late",
    )(voltages, later_taper, table)

    def exchange(value, shape):
        value = lax.all_to_all(value, ("inp", "chan"), split_axis=0, concat_axis=0, tiled=True)
        return value.reshape((n_inp, n_chan) + shape)

    late_got = exchange(late_send, late_shape)

    keep = (lax.axis_index("chan") == 0).astype(F32).reshape(1)
    early_send = pl.pallas_call(
        lambda *refs: spectra_kernel(0, True, *refs),
        in_specs=[pl.BlockSpec(memory_space=pltpu.SMEM), near, near, near] + [away] * 3,
        out_specs=away,
        out_shape=sent(early_shape),
        scratch_shapes=scratch(times, table.shape) + wide(early_shape),
        compiler_params=params(),
        cost_estimate=cost(2e11, 4e7),
        name="early",
    )(keep, jnp.transpose(history, (1, 0, 2)), carried, unit, voltages, taper, table)
    early_got = exchange(early_send, early_shape)

    rows = pltpu.VMEM((2 * channels, span, total), BF16)
    prior_shape = (channels, total, 2 * total)
    prior = pl.pallas_call(
        prior_kernel,
        in_specs=[near],
        out_specs=near,
        out_shape=jax.ShapeDtypeStruct(prior_shape, F32),
        scratch_shapes=[rows],
        compiler_params=params(),
        cost_estimate=cost(1e4, 1e4),
        name="prior",
    )(late_got)
    return pl.pallas_call(
        lambda *refs: finish_kernel(1.0 / (n_chan * s_dev), *refs),
        in_specs=[away, away],
        out_specs=away,
        out_shape=jax.ShapeDtypeStruct((2, channels, total, total), BF16),
        scratch_shapes=[
            pltpu.VMEM(early_got.shape, BF16),
            pltpu.VMEM(prior_shape, F32),
            pltpu.VMEM((channels, n_chan * HALF, total), BF16),
            pltpu.VMEM((2, channels, total, total), BF16),
            pltpu.SemaphoreType.DMA((2 * (channels // BLOCK) + n_chan // PAIR,)),
        ],
        compiler_params=params(),
        cost_estimate=cost(1e10, 1e7),
        name="finish",
    )(early_got, prior)


def solution(mesh):
    in_specs = (P("inp", "chan", None), P("inp", None, None), P())
    out_specs = P(None, ("inp", "chan"), None, None)
    return jax.shard_map(
        on_device, mesh=mesh, in_specs=in_specs, out_specs=out_specs, check_vma=False
    )
```

```python
import math

import jax
import jax.numpy as jnp
import ml_dtypes
import numpy as np
from jax import lax
from jax.experimental import pallas as pl
from jax.experimental.pallas import tpu as pltpu
from jax.sharding import PartitionSpec as P

BAND = 2048
LOW = 1024
LANES = 128
RADIX = 64
HALF = 16
PAIR = 2
BLOCK = 16
CLASSES = RADIX // 2
ROOT = math.sqrt(0.5)
F32 = jnp.float32
BF16 = jnp.bfloat16
VMEM = 63 * 1024 * 1024


def stage_table(frame):
    high = BAND // RADIX
    lane = np.arange(LANES)
    table = np.zeros((CLASSES, 2, high, 2, 2, LANES))
    for q in range(CLASSES):
        for half in range(2):
            low = q if half == 0 else (RADIX - q if q else RADIX // 2)
            k = low + RADIX * (LOW // RADIX + np.arange(high))
            angle = 2.0 * np.pi * (np.outer(k, lane) % frame) / frame
            cos, sin = np.cos(angle), np.sin(angle)
            if q == 0:
                table[q, half, :, 0, half] = cos
                table[q, half, :, 1, half] = -sin
            elif half == 0:
                table[q, half, :, 0, 0] = cos
                table[q, half, :, 0, 1] = sin
                table[q, half, :, 1, 0] = -sin
                table[q, half, :, 1, 1] = cos
            else:
                table[q, half, :, 0, 0] = cos
                table[q, half, :, 0, 1] = -sin
                table[q, half, :, 1, 0] = -sin
                table[q, half, :, 1, 1] = -cos
    table = table / math.sqrt(frame)
    return table.swapaxes(2, 3).reshape(CLASSES, 2 * high * 2, 2 * LANES)


def real_dft8(x):
    s = [x[j] + x[j + 4] for j in range(4)]
    d = [x[j] - x[j + 4] for j in range(4)]
    e0, e1 = s[0] + s[2], s[0] - s[2]
    o0, o1 = s[1] + s[3], s[3] - s[1]
    u, v = (d[1] - d[3]) * ROOT, (d[1] + d[3]) * ROOT
    return [
        (e0 + o0, None),
        (d[0] + u, -(d[2] + v)),
        (e1, o1),
        (d[0] - u, d[2] - v),
        (e0 - o0, None),
    ]


def complex_dft8(x):
    def add(a, b):
        return (a[0] + b[0], a[1] + b[1])

    def sub(a, b):
        return (a[0] - b[0], a[1] - b[1])

    def add_i(a, b):
        return (a[0] - b[1], a[1] + b[0])

    def sub_i(a, b):
        return (a[0] + b[1], a[1] - b[0])

    s = [add(x[j], x[j + 4]) for j in range(4)]
    d = [sub(x[j], x[j + 4]) for j in range(4)]
    e0, e1 = add(s[0], s[2]), sub(s[0], s[2])
    o0, o1 = add(s[1], s[3]), sub(s[1], s[3])
    p, m = sub(d[1], d[3]), add(d[1], d[3])
    b = ((p[0] + m[1]) * ROOT, (p[1] - m[0]) * ROOT)
    c = ((m[1] - p[0]) * ROOT, (-p[1] - m[0]) * ROOT)
    f, g = sub_i(d[0], d[2]), add_i(d[0], d[2])
    return [
        add(e0, o0),
        add(f, b),
        sub_i(e1, o1),
        add(g, c),
        sub(e0, o0),
        sub(f, b),
        add_i(e1, o1),
        sub(g, c),
    ]


def turned(value, step):
    angle = 2.0 * math.pi * (step % RADIX) / RADIX
    cos, sin = math.cos(angle), math.sin(angle)
    real, imag = value
    if imag is None:
        return (real * cos, real * -sin)
    if step % RADIX == 0:
        return value
    return (real * cos + imag * sin, imag * cos - real * sin)


def unrolled(count, copies, body):
    def step(i, carry):
        for copy in range(copies):
            body(i * copies + copy, copy)
        return carry

    lax.fori_loop(0, count // copies, step, 0)


def transform_rows(fir, mids, zed, half, copies):
    halves = zed.shape[1] // (fir.shape[1] * HALF)

    def one(s, copy):
        mid = mids.at[copy]
        for low in range(8):
            parts = real_dft8([fir[8 * high + low, s] for high in range(8)])
            mid[0, low] = parts[0][0]
            mid[7, low] = parts[4][0]
            for k in (1, 2, 3):
                value = turned(parts[k], low * k)
                mid[2 * k - 1, low] = value[0]
                mid[2 * k, low] = value[1]
        rows = pl.ds(pl.multiple_of((s * halves + half) * HALF, HALF), HALF)

        def put(q, half, value):
            zed[q, rows, half * LANES : (half + 1) * LANES] = value.astype(BF16)

        parts = real_dft8([mid[0, low] for low in range(8)])
        put(0, 0, parts[0][0])
        put(0, 1, parts[4][0])
        for m in (1, 2, 3):
            put(8 * m, 0, parts[m][0])
            put(8 * m, 1, parts[m][1])
        for k in (1, 2, 3):
            parts = complex_dft8([(mid[2 * k - 1, low], mid[2 * k, low]) for low in range(8)])
            for m in range(8):
                index = k + 8 * m
                if index < CLASSES:
                    put(index, 0, parts[m][0])
                    put(index, 1, parts[m][1])
                else:
                    put(RADIX - index, 0, parts[m][0])
                    put(RADIX - index, 1, -parts[m][1])
        parts = complex_dft8([turned((mid[7, low], None), 4 * low) for low in range(8)])
        for m in range(4):
            put(4 + 8 * m, 0, parts[m][0])
            put(4 + 8 * m, 1, parts[m][1])

    unrolled(fir.shape[1], copies, one)


CHUNKS = 4
CONTRACT = (((1,), (1,)), ((), ()))


def fill(first, copies, hist, keep, volt_in, taper_in, table_in, volt, taper, held, fir, mid, zed, sems):
    taps = taper.shape[0]
    in_dev, s_dev, frame = volt.shape
    halves = in_dev // HALF
    count = fir.shape[1]
    part = frame // CHUNKS
    wanted = [f for f in range(first - taps + 1, first + count) if f < s_dev]

    def volt_copy(h, j):
        where = (pl.ds(h * HALF, HALF), slice(None), pl.ds(pl.multiple_of(j * part, part), part))
        return pltpu.make_async_copy(volt_in.at[where], volt.at[where], sems.at[h * CHUNKS + j])

    taper_copy = pltpu.make_async_copy(taper_in, taper, sems.at[halves * CHUNKS])
    table_copy = pltpu.make_async_copy(table_in, held, sems.at[halves * CHUNKS + 1])
    taper_copy.start()
    for h in range(halves):
        for j in range(CHUNKS):
            volt_copy(h, j).start()
    table_copy.start()
    taper_copy.wait()

    def one_half(h, carry):
        inputs = pl.ds(pl.multiple_of(h * HALF, HALF), HALF)

        def one_chunk(j, carry):
            volt_copy(h, j).wait()

            def one(i, copy):
                a = j * (part // LANES) + i
                lanes = pl.ds(pl.multiple_of(a * LANES, LANES), LANES)
                by_time = jnp.swapaxes(volt[inputs, :, lanes], 0, 1)
                frames = {}
                for f in wanted:
                    if f >= 0:
                        frames[f] = by_time[f].astype(F32)
                    elif hist is not None:
                        frames[f] = hist[taps - 1 + f, inputs, lanes].astype(F32) * keep
                weights = [taper[t : t + 1, lanes] for t in range(taps)]
                for row in range(count):
                    total = None
                    for t in range(taps):
                        f = first + row + t - taps + 1
                        if f in frames:
                            term = weights[t] * frames[f]
                            total = term if total is None else total + term
                    fir[a, row] = total

            unrolled(part // LANES, copies[0], one)
            return carry

        lax.fori_loop(0, CHUNKS, one_chunk, 0)
        transform_rows(fir, mid, zed, h, copies[1])
        return carry

    lax.fori_loop(0, halves, one_half, 0)
    table_copy.wait()


def carried_kernel(volt_in, taper_in, table_in, out_ref, *scratch):
    *scratch, out, out_sems = scratch
    volt, taper, held, fir, mid, zed, sems = scratch
    fill(
        volt.shape[1], (16, 1), None, None,
        volt_in, taper_in, table_in, volt, taper, held, fir, mid, zed, sems,
    )
    block = CLASSES // CHUNKS

    def out_copy(j):
        where = pl.ds(j * block, block)
        return pltpu.make_async_copy(out.at[where], out_ref.at[where], out_sems.at[j])

    def some(j, carry):
        for i in range(block):
            q = j * block + i
            out[q] = jnp.dot(zed[q], held[q], preferred_element_type=F32).astype(BF16)
        out_copy(j).start()
        return carry

    lax.fori_loop(0, CHUNKS, some, 0)

    def finish(j, carry):
        out_copy(j).wait()
        return carry

    lax.fori_loop(0, CHUNKS, finish, 0)


def lane_swap(x):
    width = LANES // 4
    block = lax.broadcasted_iota(jnp.int32, (HALF, LANES), 1) // width
    x = list(x)
    for d in (1, 2):
        mask = (block & d) == 0
        for p in range(4):
            if p & d == 0:
                low, up = x[p], x[p | d]
                x[p] = jnp.where(mask, low, pltpu.roll(up, width * d, 1))
                x[p | d] = jnp.where(mask, pltpu.roll(low, LANES - width * d, 1), up)
    return x


def spectra_kernel(first, boundary, *refs):
    if boundary:
        keep, hist, carried, unit, *refs = refs
        keep = keep[0]
    else:
        keep, hist = None, None
    volt_in, taper_in, table_in, out_ref, volt, taper, held, fir, mid, zed, sems, wide, out = refs
    fill(
        first, (16, 4) if boundary else (8, 2), hist, keep,
        volt_in, taper_in, table_in, volt, taper, held, fir, mid, zed, sems,
    )
    step = RADIX
    high = step // 2
    sides = wide.shape[2] // LANES
    split = out.shape[0] // high
    channels = RADIX // split

    def one(q, copy):
        value = lax.dot_general(held[q], zed[q], CONTRACT, preferred_element_type=F32)
        if boundary:
            part = carried[q]
            short = zed.shape[1] - part.shape[0]
            part = jnp.concatenate([part, jnp.zeros((short, LANES), BF16)], axis=0)
            value = value + lax.dot_general(
                unit[...], part, CONTRACT, preferred_element_type=F32
            )
        wide[q] = value[:step].astype(BF16)
        wide[jnp.where(q == 0, CLASSES, RADIX - q)] = value[step:].astype(BF16)

    unrolled(CLASSES, 4 if boundary else 16, one)

    def out_copy(b):
        where = pl.ds(b * HALF * split, HALF * split)
        return pltpu.make_async_copy(out.at[where], out_ref.at[where], sems.at[b])

    def rows_of(b, part):
        return pl.ds(pl.multiple_of(part * high + b * HALF, HALF), HALF)

    def late_block(b, copy):
        for part in range(2):
            for side in range(sides):
                lanes = slice(side * LANES, (side + 1) * LANES)
                for first_k in range(0, RADIX, HALF):
                    value = jnp.swapaxes(
                        wide[first_k : first_k + HALF, rows_of(b, part), lanes], 0, 1
                    )
                    u, k = divmod(first_k, channels)
                    start = part * channels + k
                    for j in range(HALF):
                        group = (b * HALF + j) * split + u
                        out[group, side, start : start + HALF, :] = value[j]
        out_copy(b).start()

    def early_block(b, copy):
        def quad(k, copy):
            tiles = []
            for part in range(2):
                for side in range(sides):
                    lanes = slice(side * LANES, (side + 1) * LANES)
                    tiles += lane_swap([wide[4 * k + p, rows_of(b, part), lanes] for p in range(4)])
            value = jnp.swapaxes(jnp.stack(tiles), 0, 1)
            u, inside = lax.div(k, channels // 4), lax.rem(k, channels // 4)
            for j in range(HALF):
                out[(b * HALF + j) * split + u, inside] = value[j]

        unrolled(RADIX // 4, 4, quad)
        out_copy(b).start()

    unrolled(high // HALF, 1, early_block if boundary else late_block)

    def finish(b, carry):
        out_copy(b).wait()
        return carry

    lax.fori_loop(0, high // HALF, finish, 0)


def reorder(got, first, copies, put):
    n_inp, _, sets, rows, _ = got.shape
    assert HALF // (sets * PAIR) == 4

    def one(b, copy):
        here = pl.ds(pl.multiple_of(b * HALF, HALF), HALF)
        for tile in range(n_inp // 4):
            pieces = []
            for c in range(PAIR):
                for part in range(sets):
                    pieces += lane_swap(
                        [got[tile * 4 + p, first + c, part, here, :] for p in range(4)]
                    )
            value = jnp.swapaxes(jnp.stack(pieces), 0, 1)
            for j in range(HALF):
                put(b * HALF + j, tile, value[j])

    unrolled(rows // HALF, min(copies, rows // HALF), one)


def order_pair(got, j, copies, out):
    def put(r, tile, value):
        times = pl.ds(pl.multiple_of(j * HALF, HALF), HALF)
        out[r, times, tile * LANES : (tile + 1) * LANES] = value

    reorder(got, j * PAIR, copies, put)


def gram(left, right):
    return lax.dot_general(
        left,
        jnp.concatenate([left, right], axis=1),
        (((0,), (0,)), ((), ())),
        preferred_element_type=F32,
    )


def prior_kernel(got, out, rows):
    channels = out.shape[0]

    def step(j, carry):
        order_pair(got, j, 4, rows)
        return carry

    lax.fori_loop(0, got.shape[1] // PAIR, step, 0)

    def one(k, copy):
        real, imag = rows[k], rows[channels + k]
        left = jnp.concatenate([real, imag], axis=0)
        out[k] = gram(left, jnp.concatenate([-imag, real], axis=0))

    unrolled(channels, 8, one)


def finish_kernel(scale, got_in, prior_in, out_ref, got, prior, rows, out, sems):
    n_inp, n_chan, quads, _, _ = got.shape
    steps = n_chan // PAIR
    channels, width = out.shape[1], out.shape[-1]
    count = channels // BLOCK

    def got_copy(j):
        where = (slice(None), pl.ds(j * PAIR, PAIR))
        return pltpu.make_async_copy(got_in.at[where], got.at[where], sems.at[count + j])

    def out_copy(j):
        where = (slice(None), pl.ds(j * BLOCK, BLOCK))
        return pltpu.make_async_copy(out.at[where], out_ref.at[where], sems.at[j])

    for j in range(steps):
        got_copy(j).start()
    def prior_copy(j):
        where = pl.ds(j * BLOCK, BLOCK)
        return pltpu.make_async_copy(
            prior_in.at[where], prior.at[where], sems.at[count + steps + j]
        )

    for j in range(count):
        prior_copy(j).start()

    def order(j, carry):
        got_copy(j).wait()

        def quad(k, copy):
            for c in range(PAIR):
                times = pl.ds(pl.multiple_of((j * PAIR + c) * HALF, HALF), HALF)
                for tile in range(n_inp // 4):
                    x = lane_swap([got[tile * 4 + p, j * PAIR + c, k] for p in range(4)])
                    for p in range(4):
                        rows[4 * k + p, times, tile * LANES : (tile + 1) * LANES] = x[p]

        unrolled(quads, min(8, quads), quad)
        return carry

    lax.fori_loop(0, steps, order, 0)

    def some(j, carry):
        prior_copy(j).wait()
        for i in range(BLOCK):
            k = j * BLOCK + i
            left = rows[k]
            parts = left.astype(F32).reshape(n_chan, 2, HALF // 2, width)
            right = jnp.stack([-parts[:, 1], parts[:, 0]], axis=1).reshape(left.shape)
            value = (gram(left, right.astype(BF16)) + prior[k]) * scale
            out[0, k] = value[:, :width].astype(BF16)
            out[1, k] = value[:, width:].astype(BF16)
        out_copy(j).start()
        return carry

    lax.fori_loop(0, count, some, 0)

    def finish(j, carry):
        out_copy(j).wait()
        return carry

    lax.fori_loop(0, count, finish, 0)


def params():
    return pltpu.CompilerParams(vmem_limit_bytes=VMEM)


def cost(flops, moved):
    return pl.CostEstimate(flops=int(flops), bytes_accessed=int(moved), transcendentals=0)


def on_device(voltages, history, taper):
    in_dev, s_dev, frame = voltages.shape
    taps = taper.shape[0]
    n_inp = lax.axis_size("inp")
    n_chan = lax.axis_size("chan")
    groups = n_inp * n_chan
    channels = BAND // groups
    total = n_inp * in_dev
    times = s_dev // 2
    early = taps - 1
    blocks = LANES // in_dev
    sets = times // blocks
    span = n_chan * times
    assert frame == RADIX * LANES and in_dev == 2 * HALF and PAIR * times == HALF
    assert early == times - 1 and RADIX % channels == 0 and n_inp % blocks == 0
    assert n_chan % PAIR == 0 and channels % BLOCK == 0

    outputs = 2 * BAND // CLASSES
    stage = stage_table(frame).astype(np.float32).astype(ml_dtypes.bfloat16)
    table = jnp.asarray(stage)
    upright = jnp.asarray(np.ascontiguousarray(stage.transpose(0, 2, 1)))
    unit = jnp.asarray(np.eye(outputs).astype(ml_dtypes.bfloat16))
    assert table.shape == (CLASSES, outputs, 2 * LANES) and outputs == LANES

    away = pl.BlockSpec(memory_space=pl.ANY)
    near = pl.BlockSpec(memory_space=pltpu.VMEM)

    def scratch(count, shape):
        return [
            pltpu.VMEM(voltages.shape, BF16),
            pltpu.VMEM(taper.shape, F32),
            pltpu.VMEM(shape, BF16),
            pltpu.VMEM((RADIX, count, HALF, LANES), F32),
            pltpu.VMEM((4, 8, 8, HALF, LANES), F32),
            pltpu.VMEM((CLASSES, count * in_dev, 2 * LANES), BF16),
            pltpu.SemaphoreType.DMA((2 * CHUNKS + 2,)),
        ]

    late_shape = (sets, 2 * channels, LANES)
    early_shape = (channels // 4, HALF, LANES)

    def sent(shape):
        return jax.ShapeDtypeStruct((groups,) + shape, BF16)

    def wide(shape):
        return [
            pltpu.VMEM((RADIX, RADIX, times * in_dev), BF16),
            pltpu.VMEM((groups,) + shape, BF16),
        ]

    carried = pl.pallas_call(
        carried_kernel,
        in_specs=[away] * 3,
        out_specs=away,
        out_shape=jax.ShapeDtypeStruct((CLASSES, early * in_dev, outputs), BF16),
        scratch_shapes=scratch(early, upright.shape)
        + [
            pltpu.VMEM((CLASSES, early * in_dev, outputs), BF16),
            pltpu.SemaphoreType.DMA((CHUNKS,)),
        ],
        compiler_params=params(),
        cost_estimate=cost(1e10, 2e7),
        name="carried",
    )(voltages, taper, upright)
    carried, later_taper = lax.optimization_barrier((carried, taper))
    carried = lax.ppermute(carried, "chan", [(i, i + 1) for i in range(n_chan - 1)])

    late_send = pl.pallas_call(
        lambda *refs: spectra_kernel(times, False, *refs),
        in_specs=[away] * 3,
        out_specs=away,
        out_shape=sent(late_shape),
        scratch_shapes=scratch(times, table.shape) + wide(late_shape),
        compiler_params=params(),
        cost_estimate=cost(5e10, 4e7),
        name="late",
    )(voltages, later_taper, table)

    def exchange(value, shape):
        value = lax.all_to_all(value, ("inp", "chan"), split_axis=0, concat_axis=0, tiled=True)
        return value.reshape((n_inp, n_chan) + shape)

    late_got = exchange(late_send, late_shape)

    keep = (lax.axis_index("chan") == 0).astype(F32).reshape(1)
    early_send = pl.pallas_call(
        lambda *refs: spectra_kernel(0, True, *refs),
        in_specs=[pl.BlockSpec(memory_space=pltpu.SMEM), near, near, near] + [away] * 3,
        out_specs=away,
        out_shape=sent(early_shape),
        scratch_shapes=scratch(times, table.shape) + wide(early_shape),
        compiler_params=params(),
        cost_estimate=cost(2e11, 4e7),
        name="early",
    )(keep, jnp.transpose(history, (1, 0, 2)), carried, unit, voltages, taper, table)
    early_got = exchange(early_send, early_shape)

    rows = pltpu.VMEM((2 * channels, span, total), BF16)
    prior_shape = (channels, total, 2 * total)
    prior = pl.pallas_call(
        prior_kernel,
        in_specs=[near],
        out_specs=near,
        out_shape=jax.ShapeDtypeStruct(prior_shape, F32),
        scratch_shapes=[rows],
        compiler_params=params(),
        cost_estimate=cost(1e4, 1e4),
        name="prior",
    )(late_got)
    return pl.pallas_call(
        lambda *refs: finish_kernel(1.0 / (n_chan * s_dev), *refs),
        in_specs=[away, away],
        out_specs=away,
        out_shape=jax.ShapeDtypeStruct((2, channels, total, total), BF16),
        scratch_shapes=[
            pltpu.VMEM(early_got.shape, BF16),
            pltpu.VMEM(prior_shape, F32),
            pltpu.VMEM((channels, n_chan * HALF, total), BF16),
            pltpu.VMEM((2, channels, total, total), BF16),
            pltpu.SemaphoreType.DMA((2 * (channels // BLOCK) + n_chan // PAIR,)),
        ],
        compiler_params=params(),
        cost_estimate=cost(1e10, 1e7),
        name="finish",
    )(early_got, prior)


def solution(mesh):
    in_specs = (P("inp", "chan", None), P("inp", None, None), P())
    out_specs = P(None, ("inp", "chan"), None, None)
    return jax.shard_map(
        on_device, mesh=mesh, in_specs=in_specs, out_specs=out_specs, check_vma=False
    )
```

```python
import math

import jax
import jax.numpy as jnp
import ml_dtypes
import numpy as np
from jax import lax
from jax.experimental import pallas as pl
from jax.experimental.pallas import tpu as pltpu
from jax.sharding import PartitionSpec as P

BAND = 2048
LOW = 1024
LANES = 128
RADIX = 64
HALF = 16
PAIR = 2
BLOCK = 32
CLASSES = RADIX // 2
ROOT = math.sqrt(0.5)
F32 = jnp.float32
BF16 = jnp.bfloat16
VMEM = 63 * 1024 * 1024


def stage_table(frame):
    high = BAND // RADIX
    lane = np.arange(LANES)
    table = np.zeros((CLASSES, 2, high, 2, 2, LANES))
    for q in range(CLASSES):
        for half in range(2):
            low = q if half == 0 else (RADIX - q if q else RADIX // 2)
            k = low + RADIX * (LOW // RADIX + np.arange(high))
            angle = 2.0 * np.pi * (np.outer(k, lane) % frame) / frame
            cos, sin = np.cos(angle), np.sin(angle)
            if q == 0:
                table[q, half, :, 0, half] = cos
                table[q, half, :, 1, half] = -sin
            elif half == 0:
                table[q, half, :, 0, 0] = cos
                table[q, half, :, 0, 1] = sin
                table[q, half, :, 1, 0] = -sin
                table[q, half, :, 1, 1] = cos
            else:
                table[q, half, :, 0, 0] = cos
                table[q, half, :, 0, 1] = -sin
                table[q, half, :, 1, 0] = -sin
                table[q, half, :, 1, 1] = -cos
    table = table / math.sqrt(frame)
    return table.swapaxes(2, 3).reshape(CLASSES, 2 * high * 2, 2 * LANES)


def real_dft8(x):
    s = [x[j] + x[j + 4] for j in range(4)]
    d = [x[j] - x[j + 4] for j in range(4)]
    e0, e1 = s[0] + s[2], s[0] - s[2]
    o0, o1 = s[1] + s[3], s[3] - s[1]
    u, v = (d[1] - d[3]) * ROOT, (d[1] + d[3]) * ROOT
    return [
        (e0 + o0, None),
        (d[0] + u, -(d[2] + v)),
        (e1, o1),
        (d[0] - u, d[2] - v),
        (e0 - o0, None),
    ]


def complex_dft8(x):
    def add(a, b):
        return (a[0] + b[0], a[1] + b[1])

    def sub(a, b):
        return (a[0] - b[0], a[1] - b[1])

    def add_i(a, b):
        return (a[0] - b[1], a[1] + b[0])

    def sub_i(a, b):
        return (a[0] + b[1], a[1] - b[0])

    s = [add(x[j], x[j + 4]) for j in range(4)]
    d = [sub(x[j], x[j + 4]) for j in range(4)]
    e0, e1 = add(s[0], s[2]), sub(s[0], s[2])
    o0, o1 = add(s[1], s[3]), sub(s[1], s[3])
    p, m = sub(d[1], d[3]), add(d[1], d[3])
    b = ((p[0] + m[1]) * ROOT, (p[1] - m[0]) * ROOT)
    c = ((m[1] - p[0]) * ROOT, (-p[1] - m[0]) * ROOT)
    f, g = sub_i(d[0], d[2]), add_i(d[0], d[2])
    return [
        add(e0, o0),
        add(f, b),
        sub_i(e1, o1),
        add(g, c),
        sub(e0, o0),
        sub(f, b),
        add_i(e1, o1),
        sub(g, c),
    ]


def turned(value, step):
    angle = 2.0 * math.pi * (step % RADIX) / RADIX
    cos, sin = math.cos(angle), math.sin(angle)
    real, imag = value
    if imag is None:
        return (real * cos, real * -sin)
    if step % RADIX == 0:
        return value
    return (real * cos + imag * sin, imag * cos - real * sin)


def unrolled(count, copies, body):
    def step(i, carry):
        for copy in range(copies):
            body(i * copies + copy, copy)
        return carry

    lax.fori_loop(0, count // copies, step, 0)


def transform_rows(fir, mids, zed, half, copies):
    halves = zed.shape[1] // (fir.shape[1] * HALF)

    def one(s, copy):
        mid = mids.at[copy]
        for low in range(8):
            parts = real_dft8([fir[8 * high + low, s] for high in range(8)])
            mid[0, low] = parts[0][0]
            mid[7, low] = parts[4][0]
            for k in (1, 2, 3):
                value = turned(parts[k], low * k)
                mid[2 * k - 1, low] = value[0]
                mid[2 * k, low] = value[1]
        rows = pl.ds(pl.multiple_of((s * halves + half) * HALF, HALF), HALF)

        def put(q, half, value):
            zed[q, rows, half * LANES : (half + 1) * LANES] = value.astype(BF16)

        parts = real_dft8([mid[0, low] for low in range(8)])
        put(0, 0, parts[0][0])
        put(0, 1, parts[4][0])
        for m in (1, 2, 3):
            put(8 * m, 0, parts[m][0])
            put(8 * m, 1, parts[m][1])
        for k in (1, 2, 3):
            parts = complex_dft8([(mid[2 * k - 1, low], mid[2 * k, low]) for low in range(8)])
            for m in range(8):
                index = k + 8 * m
                if index < CLASSES:
                    put(index, 0, parts[m][0])
                    put(index, 1, parts[m][1])
                else:
                    put(RADIX - index, 0, parts[m][0])
                    put(RADIX - index, 1, -parts[m][1])
        parts = complex_dft8([turned((mid[7, low], None), 4 * low) for low in range(8)])
        for m in range(4):
            put(4 + 8 * m, 0, parts[m][0])
            put(4 + 8 * m, 1, parts[m][1])

    unrolled(fir.shape[1], copies, one)


CHUNKS = 4
CONTRACT = (((1,), (1,)), ((), ()))


def fill(first, copies, hist, keep, volt_in, taper_in, table_in, volt, taper, held, fir, mid, zed, sems):
    taps = taper.shape[0]
    in_dev, s_dev, frame = volt.shape
    halves = in_dev // HALF
    count = fir.shape[1]
    part = frame // CHUNKS
    wanted = [f for f in range(first - taps + 1, first + count) if f < s_dev]

    def volt_copy(h, j):
        where = (pl.ds(h * HALF, HALF), slice(None), pl.ds(pl.multiple_of(j * part, part), part))
        return pltpu.make_async_copy(volt_in.at[where], volt.at[where], sems.at[h * CHUNKS + j])

    taper_copy = pltpu.make_async_copy(taper_in, taper, sems.at[halves * CHUNKS])
    table_copy = pltpu.make_async_copy(table_in, held, sems.at[halves * CHUNKS + 1])
    taper_copy.start()
    for h in range(halves):
        for j in range(CHUNKS):
            volt_copy(h, j).start()
    table_copy.start()
    taper_copy.wait()

    def one_half(h, carry):
        inputs = pl.ds(pl.multiple_of(h * HALF, HALF), HALF)

        def one_chunk(j, carry):
            volt_copy(h, j).wait()

            def one(i, copy):
                a = j * (part // LANES) + i
                lanes = pl.ds(pl.multiple_of(a * LANES, LANES), LANES)
                by_time = jnp.swapaxes(volt[inputs, :, lanes], 0, 1)
                frames = {}
                for f in wanted:
                    if f >= 0:
                        frames[f] = by_time[f].astype(F32)
                    elif hist is not None:
                        frames[f] = hist[taps - 1 + f, inputs, lanes].astype(F32) * keep
                weights = [taper[t : t + 1, lanes] for t in range(taps)]
                for row in range(count):
                    total = None
                    for t in range(taps):
                        f = first + row + t - taps + 1
                        if f in frames:
                            term = weights[t] * frames[f]
                            total = term if total is None else total + term
                    fir[a, row] = total

            unrolled(part // LANES, copies[0], one)
            return carry

        lax.fori_loop(0, CHUNKS, one_chunk, 0)
        transform_rows(fir, mid, zed, h, copies[1])
        return carry

    lax.fori_loop(0, halves, one_half, 0)
    table_copy.wait()


def carried_kernel(volt_in, taper_in, table_in, out_ref, *scratch):
    *scratch, out, out_sems = scratch
    volt, taper, held, fir, mid, zed, sems = scratch
    fill(
        volt.shape[1], (16, 1), None, None,
        volt_in, taper_in, table_in, volt, taper, held, fir, mid, zed, sems,
    )
    block = CLASSES // 2

    def out_copy(j):
        where = pl.ds(j * block, block)
        return pltpu.make_async_copy(out.at[where], out_ref.at[where], out_sems.at[j])

    def some(j, carry):
        for i in range(block):
            q = j * block + i
            out[q] = jnp.dot(zed[q], held[q], preferred_element_type=F32).astype(BF16)
        out_copy(j).start()
        return carry

    lax.fori_loop(0, 2, some, 0)

    def finish(j, carry):
        out_copy(j).wait()
        return carry

    lax.fori_loop(0, 2, finish, 0)


def lane_swap(x):
    width = LANES // 4
    block = lax.broadcasted_iota(jnp.int32, (HALF, LANES), 1) // width
    x = list(x)
    for d in (1, 2):
        mask = (block & d) == 0
        for p in range(4):
            if p & d == 0:
                low, up = x[p], x[p | d]
                x[p] = jnp.where(mask, low, pltpu.roll(up, width * d, 1))
                x[p | d] = jnp.where(mask, pltpu.roll(low, LANES - width * d, 1), up)
    return x


def spectra_kernel(first, boundary, *refs):
    if boundary:
        keep, hist, carried, unit, *refs = refs
        keep = keep[0]
    else:
        keep, hist = None, None
    volt_in, taper_in, table_in, out_ref, volt, taper, held, fir, mid, zed, sems, wide, out = refs
    fill(
        first, (16, 4) if boundary else (16, 2), hist, keep,
        volt_in, taper_in, table_in, volt, taper, held, fir, mid, zed, sems,
    )
    step = RADIX
    high = step // 2
    sides = wide.shape[2] // LANES
    split = out.shape[0] // high
    channels = RADIX // split

    def one(q, copy):
        value = lax.dot_general(held[q], zed[q], CONTRACT, preferred_element_type=F32)
        if boundary:
            part = carried[q]
            short = zed.shape[1] - part.shape[0]
            part = jnp.concatenate([part, jnp.zeros((short, LANES), BF16)], axis=0)
            value = value + lax.dot_general(
                unit[...], part, CONTRACT, preferred_element_type=F32
            )
        wide[q] = value[:step].astype(BF16)
        wide[jnp.where(q == 0, CLASSES, RADIX - q)] = value[step:].astype(BF16)

    unrolled(CLASSES, 4 if boundary else 16, one)

    def out_copy(b):
        where = pl.ds(b * HALF * split, HALF * split)
        return pltpu.make_async_copy(out.at[where], out_ref.at[where], sems.at[b])

    def rows_of(b, part):
        return pl.ds(pl.multiple_of(part * high + b * HALF, HALF), HALF)

    def late_block(b, copy):
        for part in range(2):
            for side in range(sides):
                lanes = slice(side * LANES, (side + 1) * LANES)
                for first_k in range(0, RADIX, HALF):
                    value = jnp.swapaxes(
                        wide[first_k : first_k + HALF, rows_of(b, part), lanes], 0, 1
                    )
                    u, k = divmod(first_k, channels)
                    start = part * channels + k
                    for j in range(HALF):
                        group = (b * HALF + j) * split + u
                        out[group, side, start : start + HALF, :] = value[j]
        out_copy(b).start()

    def early_block(b, copy):
        def quad(k, copy):
            tiles = []
            for part in range(2):
                for side in range(sides):
                    lanes = slice(side * LANES, (side + 1) * LANES)
                    tiles += lane_swap([wide[4 * k + p, rows_of(b, part), lanes] for p in range(4)])
            value = jnp.swapaxes(jnp.stack(tiles), 0, 1)
            u, inside = lax.div(k, channels // 4), lax.rem(k, channels // 4)
            for j in range(HALF):
                out[(b * HALF + j) * split + u, inside] = value[j]

        unrolled(RADIX // 4, 4, quad)
        out_copy(b).start()

    unrolled(high // HALF, 1, early_block if boundary else late_block)

    def finish(b, carry):
        out_copy(b).wait()
        return carry

    lax.fori_loop(0, high // HALF, finish, 0)


def reorder(got, first, copies, put):
    n_inp, _, sets, rows, _ = got.shape
    assert HALF // (sets * PAIR) == 4

    def one(b, copy):
        here = pl.ds(pl.multiple_of(b * HALF, HALF), HALF)
        for tile in range(n_inp // 4):
            pieces = []
            for c in range(PAIR):
                for part in range(sets):
                    pieces += lane_swap(
                        [got[tile * 4 + p, first + c, part, here, :] for p in range(4)]
                    )
            value = jnp.swapaxes(jnp.stack(pieces), 0, 1)
            for j in range(HALF):
                put(b * HALF + j, tile, value[j])

    unrolled(rows // HALF, min(copies, rows // HALF), one)


def order_pair(got, j, copies, out):
    def put(r, tile, value):
        times = pl.ds(pl.multiple_of(j * HALF, HALF), HALF)
        out[r, times, tile * LANES : (tile + 1) * LANES] = value

    reorder(got, j * PAIR, copies, put)


def gram(left, right):
    return lax.dot_general(
        left,
        jnp.concatenate([left, right], axis=1),
        (((0,), (0,)), ((), ())),
        preferred_element_type=F32,
    )


def prior_kernel(got, out, rows):
    channels = out.shape[0]

    def step(j, carry):
        order_pair(got, j, 4, rows)
        return carry

    lax.fori_loop(0, got.shape[1] // PAIR, step, 0)

    def one(k, copy):
        real, imag = rows[k], rows[channels + k]
        left = jnp.concatenate([real, imag], axis=0)
        out[k] = gram(left, jnp.concatenate([-imag, real], axis=0))

    unrolled(channels, 8, one)


def finish_kernel(scale, got_in, prior_in, out_ref, got, prior, rows, out, sems):
    n_inp, n_chan, quads, _, _ = got.shape
    steps = n_chan // PAIR
    channels, width = out.shape[1], out.shape[-1]
    each = min(BLOCK, channels)
    count = channels // each

    def got_copy(j):
        where = (slice(None), pl.ds(j * PAIR, PAIR))
        return pltpu.make_async_copy(got_in.at[where], got.at[where], sems.at[count + j])

    def out_copy(j):
        where = (slice(None), pl.ds(j * each, each))
        return pltpu.make_async_copy(out.at[where], out_ref.at[where], sems.at[j])

    for j in range(steps):
        got_copy(j).start()
    def prior_copy(j):
        where = pl.ds(j * each, each)
        return pltpu.make_async_copy(
            prior_in.at[where], prior.at[where], sems.at[count + steps + j]
        )

    for j in range(count):
        prior_copy(j).start()

    def order(j, carry):
        got_copy(j).wait()

        def quad(k, copy):
            for c in range(PAIR):
                times = pl.ds(pl.multiple_of((j * PAIR + c) * HALF, HALF), HALF)
                for tile in range(n_inp // 4):
                    x = lane_swap([got[tile * 4 + p, j * PAIR + c, k] for p in range(4)])
                    for p in range(4):
                        rows[4 * k + p, times, tile * LANES : (tile + 1) * LANES] = x[p]

        unrolled(quads, quads, quad)
        return carry

    lax.fori_loop(0, steps, order, 0)

    def some(j, carry):
        prior_copy(j).wait()
        for i in range(each):
            k = j * each + i
            left = rows[k]
            parts = left.astype(F32).reshape(n_chan, 2, HALF // 2, width)
            right = jnp.stack([-parts[:, 1], parts[:, 0]], axis=1).reshape(left.shape)
            value = (gram(left, right.astype(BF16)) + prior[k]) * scale
            out[0, k] = value[:, :width].astype(BF16)
            out[1, k] = value[:, width:].astype(BF16)
        out_copy(j).start()
        return carry

    lax.fori_loop(0, count, some, 0)

    def finish(j, carry):
        out_copy(j).wait()
        return carry

    lax.fori_loop(0, count, finish, 0)


def params():
    return pltpu.CompilerParams(vmem_limit_bytes=VMEM)


def cost(flops, moved):
    return pl.CostEstimate(flops=int(flops), bytes_accessed=int(moved), transcendentals=0)


def on_device(voltages, history, taper):
    in_dev, s_dev, frame = voltages.shape
    taps = taper.shape[0]
    n_inp = lax.axis_size("inp")
    n_chan = lax.axis_size("chan")
    groups = n_inp * n_chan
    channels = BAND // groups
    total = n_inp * in_dev
    times = s_dev // 2
    early = taps - 1
    blocks = LANES // in_dev
    sets = times // blocks
    span = n_chan * times
    assert frame == RADIX * LANES and in_dev == 2 * HALF and PAIR * times == HALF
    assert early == times - 1 and RADIX % channels == 0 and n_inp % blocks == 0
    assert n_chan % PAIR == 0

    outputs = 2 * BAND // CLASSES
    stage = stage_table(frame).astype(np.float32).astype(ml_dtypes.bfloat16)
    table = jnp.asarray(stage)
    upright = jnp.asarray(np.ascontiguousarray(stage.transpose(0, 2, 1)))
    unit = jnp.asarray(np.eye(outputs).astype(ml_dtypes.bfloat16))
    assert table.shape == (CLASSES, outputs, 2 * LANES) and outputs == LANES

    away = pl.BlockSpec(memory_space=pl.ANY)
    near = pl.BlockSpec(memory_space=pltpu.VMEM)

    def scratch(count, shape):
        return [
            pltpu.VMEM(voltages.shape, BF16),
            pltpu.VMEM(taper.shape, F32),
            pltpu.VMEM(shape, BF16),
            pltpu.VMEM((RADIX, count, HALF, LANES), F32),
            pltpu.VMEM((4, 8, 8, HALF, LANES), F32),
            pltpu.VMEM((CLASSES, count * in_dev, 2 * LANES), BF16),
            pltpu.SemaphoreType.DMA((2 * CHUNKS + 2,)),
        ]

    late_shape = (sets, 2 * channels, LANES)
    early_shape = (channels // 4, HALF, LANES)

    def sent(shape):
        return jax.ShapeDtypeStruct((groups,) + shape, BF16)

    def wide(shape):
        return [
            pltpu.VMEM((RADIX, RADIX, times * in_dev), BF16),
            pltpu.VMEM((groups,) + shape, BF16),
        ]

    carried = pl.pallas_call(
        carried_kernel,
        in_specs=[away] * 3,
        out_specs=away,
        out_shape=jax.ShapeDtypeStruct((CLASSES, early * in_dev, outputs), BF16),
        scratch_shapes=scratch(early, upright.shape)
        + [
            pltpu.VMEM((CLASSES, early * in_dev, outputs), BF16),
            pltpu.SemaphoreType.DMA((CHUNKS,)),
        ],
        compiler_params=params(),
        cost_estimate=cost(1e10, 2e7),
        name="carried",
    )(voltages, taper, upright)
    carried, later_taper = lax.optimization_barrier((carried, taper))
    carried = lax.ppermute(carried, "chan", [(i, i + 1) for i in range(n_chan - 1)])

    late_send = pl.pallas_call(
        lambda *refs: spectra_kernel(times, False, *refs),
        in_specs=[away] * 3,
        out_specs=away,
        out_shape=sent(late_shape),
        scratch_shapes=scratch(times, table.shape) + wide(late_shape),
        compiler_params=params(),
        cost_estimate=cost(5e10, 4e7),
        name="late",
    )(voltages, later_taper, table)

    def exchange(value, shape):
        value = lax.all_to_all(value, ("inp", "chan"), split_axis=0, concat_axis=0, tiled=True)
        return value.reshape((n_inp, n_chan) + shape)

    late_got = exchange(late_send, late_shape)

    keep = (lax.axis_index("chan") == 0).astype(F32).reshape(1)
    early_send = pl.pallas_call(
        lambda *refs: spectra_kernel(0, True, *refs),
        in_specs=[pl.BlockSpec(memory_space=pltpu.SMEM), near, near, near] + [away] * 3,
        out_specs=away,
        out_shape=sent(early_shape),
        scratch_shapes=scratch(times, table.shape) + wide(early_shape),
        compiler_params=params(),
        cost_estimate=cost(2e11, 4e7),
        name="early",
    )(keep, jnp.transpose(history, (1, 0, 2)), carried, unit, voltages, taper, table)
    early_got = exchange(early_send, early_shape)

    rows = pltpu.VMEM((2 * channels, span, total), BF16)
    prior_shape = (channels, total, 2 * total)
    prior = pl.pallas_call(
        prior_kernel,
        in_specs=[near],
        out_specs=near,
        out_shape=jax.ShapeDtypeStruct(prior_shape, F32),
        scratch_shapes=[rows],
        compiler_params=params(),
        cost_estimate=cost(1e4, 1e4),
        name="prior",
    )(late_got)
    return pl.pallas_call(
        lambda *refs: finish_kernel(1.0 / (n_chan * s_dev), *refs),
        in_specs=[away, away],
        out_specs=away,
        out_shape=jax.ShapeDtypeStruct((2, channels, total, total), BF16),
        scratch_shapes=[
            pltpu.VMEM(early_got.shape, BF16),
            pltpu.VMEM(prior_shape, F32),
            pltpu.VMEM((channels, n_chan * HALF, total), BF16),
            pltpu.VMEM((2, channels, total, total), BF16),
            pltpu.SemaphoreType.DMA((2 * channels // min(BLOCK, channels) + n_chan // PAIR,)),
        ],
        compiler_params=params(),
        cost_estimate=cost(1e10, 1e7),
        name="finish",
    )(early_got, prior)


def solution(mesh):
    in_specs = (P("inp", "chan", None), P("inp", None, None), P())
    out_specs = P(None, ("inp", "chan"), None, None)
    return jax.shard_map(
        on_device, mesh=mesh, in_specs=in_specs, out_specs=out_specs, check_vma=False
    )
```

```python
import math

import jax
import jax.numpy as jnp
import ml_dtypes
import numpy as np
from jax import lax
from jax.experimental import pallas as pl
from jax.experimental.pallas import tpu as pltpu
from jax.sharding import PartitionSpec as P

BAND = 2048
LOW = 1024
LANES = 128
RADIX = 64
HALF = 16
PAIR = 2
BLOCK = 16
CLASSES = RADIX // 2
ROOT = math.sqrt(0.5)
F32 = jnp.float32
BF16 = jnp.bfloat16
VMEM = 63 * 1024 * 1024


def stage_table(frame):
    high = BAND // RADIX
    lane = np.arange(LANES)
    table = np.zeros((CLASSES, 2, high, 2, 2, LANES))
    for q in range(CLASSES):
        for half in range(2):
            low = q if half == 0 else (RADIX - q if q else RADIX // 2)
            k = low + RADIX * (LOW // RADIX + np.arange(high))
            angle = 2.0 * np.pi * (np.outer(k, lane) % frame) / frame
            cos, sin = np.cos(angle), np.sin(angle)
            if q == 0:
                table[q, half, :, 0, half] = cos
                table[q, half, :, 1, half] = -sin
            elif half == 0:
                table[q, half, :, 0, 0] = cos
                table[q, half, :, 0, 1] = sin
                table[q, half, :, 1, 0] = -sin
                table[q, half, :, 1, 1] = cos
            else:
                table[q, half, :, 0, 0] = cos
                table[q, half, :, 0, 1] = -sin
                table[q, half, :, 1, 0] = -sin
                table[q, half, :, 1, 1] = -cos
    table = table / math.sqrt(frame)
    return table.swapaxes(2, 3).reshape(CLASSES, 2 * high * 2, 2 * LANES)


def real_dft8(x):
    s = [x[j] + x[j + 4] for j in range(4)]
    d = [x[j] - x[j + 4] for j in range(4)]
    e0, e1 = s[0] + s[2], s[0] - s[2]
    o0, o1 = s[1] + s[3], s[3] - s[1]
    u, v = (d[1] - d[3]) * ROOT, (d[1] + d[3]) * ROOT
    return [
        (e0 + o0, None),
        (d[0] + u, -(d[2] + v)),
        (e1, o1),
        (d[0] - u, d[2] - v),
        (e0 - o0, None),
    ]


def complex_dft8(x):
    def add(a, b):
        return (a[0] + b[0], a[1] + b[1])

    def sub(a, b):
        return (a[0] - b[0], a[1] - b[1])

    def add_i(a, b):
        return (a[0] - b[1], a[1] + b[0])

    def sub_i(a, b):
        return (a[0] + b[1], a[1] - b[0])

    s = [add(x[j], x[j + 4]) for j in range(4)]
    d = [sub(x[j], x[j + 4]) for j in range(4)]
    e0, e1 = add(s[0], s[2]), sub(s[0], s[2])
    o0, o1 = add(s[1], s[3]), sub(s[1], s[3])
    p, m = sub(d[1], d[3]), add(d[1], d[3])
    b = ((p[0] + m[1]) * ROOT, (p[1] - m[0]) * ROOT)
    c = ((m[1] - p[0]) * ROOT, (-p[1] - m[0]) * ROOT)
    f, g = sub_i(d[0], d[2]), add_i(d[0], d[2])
    return [
        add(e0, o0),
        add(f, b),
        sub_i(e1, o1),
        add(g, c),
        sub(e0, o0),
        sub(f, b),
        add_i(e1, o1),
        sub(g, c),
    ]


def turned(value, step):
    angle = 2.0 * math.pi * (step % RADIX) / RADIX
    cos, sin = math.cos(angle), math.sin(angle)
    real, imag = value
    if imag is None:
        return (real * cos, real * -sin)
    if step % RADIX == 0:
        return value
    return (real * cos + imag * sin, imag * cos - real * sin)


def unrolled(count, copies, body):
    def step(i, carry):
        for copy in range(copies):
            body(i * copies + copy, copy)
        return carry

    lax.fori_loop(0, count // copies, step, 0)


def transform_rows(fir, mids, zed, half, copies):
    halves = zed.shape[1] // (fir.shape[1] * HALF)

    def one(s, copy):
        mid = mids.at[copy]
        for low in range(8):
            parts = real_dft8([fir[8 * high + low, s] for high in range(8)])
            mid[0, low] = parts[0][0]
            mid[7, low] = parts[4][0]
            for k in (1, 2, 3):
                value = turned(parts[k], low * k)
                mid[2 * k - 1, low] = value[0]
                mid[2 * k, low] = value[1]
        rows = pl.ds(pl.multiple_of((s * halves + half) * HALF, HALF), HALF)

        def put(q, half, value):
            zed[q, rows, half * LANES : (half + 1) * LANES] = value.astype(BF16)

        parts = real_dft8([mid[0, low] for low in range(8)])
        put(0, 0, parts[0][0])
        put(0, 1, parts[4][0])
        for m in (1, 2, 3):
            put(8 * m, 0, parts[m][0])
            put(8 * m, 1, parts[m][1])
        for k in (1, 2, 3):
            parts = complex_dft8([(mid[2 * k - 1, low], mid[2 * k, low]) for low in range(8)])
            for m in range(8):
                index = k + 8 * m
                if index < CLASSES:
                    put(index, 0, parts[m][0])
                    put(index, 1, parts[m][1])
                else:
                    put(RADIX - index, 0, parts[m][0])
                    put(RADIX - index, 1, -parts[m][1])
        parts = complex_dft8([turned((mid[7, low], None), 4 * low) for low in range(8)])
        for m in range(4):
            put(4 + 8 * m, 0, parts[m][0])
            put(4 + 8 * m, 1, parts[m][1])

    unrolled(fir.shape[1], copies, one)


CHUNKS = 4
CONTRACT = (((1,), (1,)), ((), ()))


def fill(first, copies, hist, keep, volt_in, taper_in, table_in, volt, taper, held, fir, mid, zed, sems):
    taps = taper.shape[0]
    in_dev, s_dev, frame = volt.shape
    halves = in_dev // HALF
    count = fir.shape[1]
    part = frame // CHUNKS
    wanted = [f for f in range(first - taps + 1, first + count) if f < s_dev]

    def volt_copy(h, j):
        where = (pl.ds(h * HALF, HALF), slice(None), pl.ds(pl.multiple_of(j * part, part), part))
        return pltpu.make_async_copy(volt_in.at[where], volt.at[where], sems.at[h * CHUNKS + j])

    taper_copy = pltpu.make_async_copy(taper_in, taper, sems.at[halves * CHUNKS])
    table_copy = pltpu.make_async_copy(table_in, held, sems.at[halves * CHUNKS + 1])
    taper_copy.start()
    for h in range(halves):
        for j in range(CHUNKS):
            volt_copy(h, j).start()
    table_copy.start()
    taper_copy.wait()

    def one_half(h, carry):
        inputs = pl.ds(pl.multiple_of(h * HALF, HALF), HALF)

        def one_chunk(j, carry):
            volt_copy(h, j).wait()

            def one(i, copy):
                a = j * (part // LANES) + i
                lanes = pl.ds(pl.multiple_of(a * LANES, LANES), LANES)
                by_time = jnp.swapaxes(volt[inputs, :, lanes], 0, 1)
                frames = {}
                for f in wanted:
                    if f >= 0:
                        frames[f] = by_time[f].astype(F32)
                    elif hist is not None:
                        frames[f] = hist[taps - 1 + f, inputs, lanes].astype(F32) * keep
                weights = [taper[t : t + 1, lanes] for t in range(taps)]
                for row in range(count):
                    total = None
                    for t in range(taps):
                        f = first + row + t - taps + 1
                        if f in frames:
                            term = weights[t] * frames[f]
                            total = term if total is None else total + term
                    fir[a, row] = total

            unrolled(part // LANES, copies[0], one)
            return carry

        lax.fori_loop(0, CHUNKS, one_chunk, 0)
        transform_rows(fir, mid, zed, h, copies[1])
        return carry

    lax.fori_loop(0, halves, one_half, 0)
    table_copy.wait()


def carried_kernel(volt_in, taper_in, table_in, out_ref, *scratch):
    *scratch, out, out_sems = scratch
    volt, taper, held, fir, mid, zed, sems = scratch
    fill(
        volt.shape[1], (16, 1), None, None,
        volt_in, taper_in, table_in, volt, taper, held, fir, mid, zed, sems,
    )
    block = CLASSES // 2

    def out_copy(j):
        where = pl.ds(j * block, block)
        return pltpu.make_async_copy(out.at[where], out_ref.at[where], out_sems.at[j])

    def some(j, carry):
        for i in range(block):
            q = j * block + i
            out[q] = jnp.dot(zed[q], held[q], preferred_element_type=F32).astype(BF16)
        out_copy(j).start()
        return carry

    lax.fori_loop(0, 2, some, 0)

    def finish(j, carry):
        out_copy(j).wait()
        return carry

    lax.fori_loop(0, 2, finish, 0)


def lane_swap(x):
    width = LANES // 4
    block = lax.broadcasted_iota(jnp.int32, (HALF, LANES), 1) // width
    x = list(x)
    mask = (block & 1) == 0
    for p in (0, 2):
        low, up = x[p], x[p + 1]
        x[p] = jnp.where(mask, low, pltpu.roll(up, width, 1))
        x[p + 1] = jnp.where(mask, pltpu.roll(low, LANES - width, 1), up)
    mask = (block & 2) == 0
    for p in (0, 1):
        low, up = x[p], x[p + 2]
        moved = pltpu.roll(jnp.where(mask, up, low), 2 * width, 1)
        x[p] = jnp.where(mask, low, moved)
        x[p + 2] = jnp.where(mask, moved, up)
    return x


def spectra_kernel(first, boundary, *refs):
    if boundary:
        keep, hist, carried, unit, *refs = refs
        keep = keep[0]
    else:
        keep, hist = None, None
    volt_in, taper_in, table_in, out_ref, volt, taper, held, fir, mid, zed, sems, wide, out = refs
    fill(
        first, (16, 4) if boundary else (8, 2), hist, keep,
        volt_in, taper_in, table_in, volt, taper, held, fir, mid, zed, sems,
    )
    step = RADIX
    high = step // 2
    sides = wide.shape[2] // LANES
    split = out.shape[0] // high
    channels = RADIX // split

    def one(q, copy):
        value = lax.dot_general(held[q], zed[q], CONTRACT, preferred_element_type=F32)
        if boundary:
            part = carried[q]
            short = zed.shape[1] - part.shape[0]
            part = jnp.concatenate([part, jnp.zeros((short, LANES), BF16)], axis=0)
            value = value + lax.dot_general(
                unit[...], part, CONTRACT, preferred_element_type=F32
            )
        wide[q] = value[:step].astype(BF16)
        wide[jnp.where(q == 0, CLASSES, RADIX - q)] = value[step:].astype(BF16)

    unrolled(CLASSES, 4 if boundary else 16, one)

    def out_copy(b):
        where = pl.ds(b * HALF * split, HALF * split)
        return pltpu.make_async_copy(out.at[where], out_ref.at[where], sems.at[b])

    def rows_of(b, part):
        return pl.ds(pl.multiple_of(part * high + b * HALF, HALF), HALF)

    def late_block(b, copy):
        for part in range(2):
            for side in range(sides):
                lanes = slice(side * LANES, (side + 1) * LANES)
                for first_k in range(0, RADIX, HALF):
                    value = jnp.swapaxes(
                        wide[first_k : first_k + HALF, rows_of(b, part), lanes], 0, 1
                    )
                    u, k = divmod(first_k, channels)
                    start = part * channels + k
                    for j in range(HALF):
                        group = (b * HALF + j) * split + u
                        out[group, side, start : start + HALF, :] = value[j]
        out_copy(b).start()

    def early_block(b, copy):
        def quad(k, copy):
            tiles = []
            for part in range(2):
                for side in range(sides):
                    lanes = slice(side * LANES, (side + 1) * LANES)
                    tiles += lane_swap([wide[4 * k + p, rows_of(b, part), lanes] for p in range(4)])
            value = jnp.swapaxes(jnp.stack(tiles), 0, 1)
            u, inside = lax.div(k, channels // 4), lax.rem(k, channels // 4)
            for j in range(HALF):
                out[(b * HALF + j) * split + u, inside] = value[j]

        unrolled(RADIX // 4, 4, quad)
        out_copy(b).start()

    unrolled(high // HALF, 1, early_block if boundary else late_block)

    def finish(b, carry):
        out_copy(b).wait()
        return carry

    lax.fori_loop(0, high // HALF, finish, 0)


def reorder(got, first, copies, put):
    n_inp, _, sets, rows, _ = got.shape
    assert HALF // (sets * PAIR) == 4

    def one(b, copy):
        here = pl.ds(pl.multiple_of(b * HALF, HALF), HALF)
        for tile in range(n_inp // 4):
            pieces = []
            for c in range(PAIR):
                for part in range(sets):
                    pieces += lane_swap(
                        [got[tile * 4 + p, first + c, part, here, :] for p in range(4)]
                    )
            value = jnp.swapaxes(jnp.stack(pieces), 0, 1)
            for j in range(HALF):
                put(b * HALF + j, tile, value[j])

    unrolled(rows // HALF, min(copies, rows // HALF), one)


def order_pair(got, j, copies, out):
    def put(r, tile, value):
        times = pl.ds(pl.multiple_of(j * HALF, HALF), HALF)
        out[r, times, tile * LANES : (tile + 1) * LANES] = value

    reorder(got, j * PAIR, copies, put)


def gram(left, right):
    return lax.dot_general(
        left,
        jnp.concatenate([left, right], axis=1),
        (((0,), (0,)), ((), ())),
        preferred_element_type=F32,
    )


def prior_kernel(got, out, rows):
    channels = out.shape[0]

    def step(j, carry):
        order_pair(got, j, 4, rows)
        return carry

    lax.fori_loop(0, got.shape[1] // PAIR, step, 0)

    def one(k, copy):
        real, imag = rows[k], rows[channels + k]
        left = jnp.concatenate([real, imag], axis=0)
        out[k] = gram(left, jnp.concatenate([-imag, real], axis=0))

    unrolled(channels, 8, one)


def finish_kernel(scale, got_in, prior_in, out_ref, got, prior, rows, out, sems):
    n_inp, n_chan, quads, _, _ = got.shape
    steps = n_chan // PAIR
    channels, width = out.shape[1], out.shape[-1]
    count = channels // BLOCK

    def got_copy(j):
        where = (slice(None), pl.ds(j * PAIR, PAIR))
        return pltpu.make_async_copy(got_in.at[where], got.at[where], sems.at[count + j])

    def out_copy(j):
        where = (slice(None), pl.ds(j * BLOCK, BLOCK))
        return pltpu.make_async_copy(out.at[where], out_ref.at[where], sems.at[j])

    for j in range(steps):
        got_copy(j).start()
    def prior_copy(j):
        where = pl.ds(j * BLOCK, BLOCK)
        return pltpu.make_async_copy(
            prior_in.at[where], prior.at[where], sems.at[count + steps + j]
        )

    for j in range(count):
        prior_copy(j).start()

    def order(j, carry):
        got_copy(j).wait()

        def quad(k, copy):
            for c in range(PAIR):
                times = pl.ds(pl.multiple_of((j * PAIR + c) * HALF, HALF), HALF)
                for tile in range(n_inp // 4):
                    x = lane_swap([got[tile * 4 + p, j * PAIR + c, k] for p in range(4)])
                    for p in range(4):
                        rows[4 * k + p, times, tile * LANES : (tile + 1) * LANES] = x[p]

        unrolled(quads, min(8, quads), quad)
        return carry

    lax.fori_loop(0, steps, order, 0)

    def some(j, carry):
        prior_copy(j).wait()
        for i in range(BLOCK):
            k = j * BLOCK + i
            left = rows[k]
            parts = left.astype(F32).reshape(n_chan, 2, HALF // 2, width)
            right = jnp.stack([-parts[:, 1], parts[:, 0]], axis=1).reshape(left.shape)
            value = (gram(left, right.astype(BF16)) + prior[k]) * scale
            out[0, k] = value[:, :width].astype(BF16)
            out[1, k] = value[:, width:].astype(BF16)
        out_copy(j).start()
        return carry

    lax.fori_loop(0, count, some, 0)

    def finish(j, carry):
        out_copy(j).wait()
        return carry

    lax.fori_loop(0, count, finish, 0)


def params():
    return pltpu.CompilerParams(vmem_limit_bytes=VMEM)


def cost(flops, moved):
    return pl.CostEstimate(flops=int(flops), bytes_accessed=int(moved), transcendentals=0)


def on_device(voltages, history, taper):
    in_dev, s_dev, frame = voltages.shape
    taps = taper.shape[0]
    n_inp = lax.axis_size("inp")
    n_chan = lax.axis_size("chan")
    groups = n_inp * n_chan
    channels = BAND // groups
    total = n_inp * in_dev
    times = s_dev // 2
    early = taps - 1
    blocks = LANES // in_dev
    sets = times // blocks
    span = n_chan * times
    assert frame == RADIX * LANES and in_dev == 2 * HALF and PAIR * times == HALF
    assert early == times - 1 and RADIX % channels == 0 and n_inp % blocks == 0
    assert n_chan % PAIR == 0 and channels % BLOCK == 0

    outputs = 2 * BAND // CLASSES
    stage = stage_table(frame).astype(np.float32).astype(ml_dtypes.bfloat16)
    table = jnp.asarray(stage)
    upright = jnp.asarray(np.ascontiguousarray(stage.transpose(0, 2, 1)))
    unit = jnp.asarray(np.eye(outputs).astype(ml_dtypes.bfloat16))
    assert table.shape == (CLASSES, outputs, 2 * LANES) and outputs == LANES

    away = pl.BlockSpec(memory_space=pl.ANY)
    near = pl.BlockSpec(memory_space=pltpu.VMEM)

    def scratch(count, shape):
        return [
            pltpu.VMEM(voltages.shape, BF16),
            pltpu.VMEM(taper.shape, F32),
            pltpu.VMEM(shape, BF16),
            pltpu.VMEM((RADIX, count, HALF, LANES), F32),
            pltpu.VMEM((4, 8, 8, HALF, LANES), F32),
            pltpu.VMEM((CLASSES, count * in_dev, 2 * LANES), BF16),
            pltpu.SemaphoreType.DMA((2 * CHUNKS + 2,)),
        ]

    late_shape = (sets, 2 * channels, LANES)
    early_shape = (channels // 4, HALF, LANES)

    def sent(shape):
        return jax.ShapeDtypeStruct((groups,) + shape, BF16)

    def wide(shape):
        return [
            pltpu.VMEM((RADIX, RADIX, times * in_dev), BF16),
            pltpu.VMEM((groups,) + shape, BF16),
        ]

    carried = pl.pallas_call(
        carried_kernel,
        in_specs=[away] * 3,
        out_specs=away,
        out_shape=jax.ShapeDtypeStruct((CLASSES, early * in_dev, outputs), BF16),
        scratch_shapes=scratch(early, upright.shape)
        + [
            pltpu.VMEM((CLASSES, early * in_dev, outputs), BF16),
            pltpu.SemaphoreType.DMA((CHUNKS,)),
        ],
        compiler_params=params(),
        cost_estimate=cost(1e10, 2e7),
        name="carried",
    )(voltages, taper, upright)
    carried, later_taper = lax.optimization_barrier((carried, taper))
    carried = lax.ppermute(carried, "chan", [(i, i + 1) for i in range(n_chan - 1)])

    late_send = pl.pallas_call(
        lambda *refs: spectra_kernel(times, False, *refs),
        in_specs=[away] * 3,
        out_specs=away,
        out_shape=sent(late_shape),
        scratch_shapes=scratch(times, table.shape) + wide(late_shape),
        compiler_params=params(),
        cost_estimate=cost(5e10, 4e7),
        name="late",
    )(voltages, later_taper, table)

    def exchange(value, shape):
        value = lax.all_to_all(value, ("inp", "chan"), split_axis=0, concat_axis=0, tiled=True)
        return value.reshape((n_inp, n_chan) + shape)

    late_got = exchange(late_send, late_shape)

    keep = (lax.axis_index("chan") == 0).astype(F32).reshape(1)
    early_send = pl.pallas_call(
        lambda *refs: spectra_kernel(0, True, *refs),
        in_specs=[pl.BlockSpec(memory_space=pltpu.SMEM), near, near, near] + [away] * 3,
        out_specs=away,
        out_shape=sent(early_shape),
        scratch_shapes=scratch(times, table.shape) + wide(early_shape),
        compiler_params=params(),
        cost_estimate=cost(2e11, 4e7),
        name="early",
    )(keep, jnp.transpose(history, (1, 0, 2)), carried, unit, voltages, taper, table)
    early_got = exchange(early_send, early_shape)

    rows = pltpu.VMEM((2 * channels, span, total), BF16)
    prior_shape = (channels, total, 2 * total)
    prior = pl.pallas_call(
        prior_kernel,
        in_specs=[near],
        out_specs=near,
        out_shape=jax.ShapeDtypeStruct(prior_shape, F32),
        scratch_shapes=[rows],
        compiler_params=params(),
        cost_estimate=cost(1e4, 1e4),
        name="prior",
    )(late_got)
    return pl.pallas_call(
        lambda *refs: finish_kernel(1.0 / (n_chan * s_dev), *refs),
        in_specs=[away, away],
        out_specs=away,
        out_shape=jax.ShapeDtypeStruct((2, channels, total, total), BF16),
        scratch_shapes=[
            pltpu.VMEM(early_got.shape, BF16),
            pltpu.VMEM(prior_shape, F32),
            pltpu.VMEM((channels, n_chan * HALF, total), BF16),
            pltpu.VMEM((2, channels, total, total), BF16),
            pltpu.SemaphoreType.DMA((2 * (channels // BLOCK) + n_chan // PAIR,)),
        ],
        compiler_params=params(),
        cost_estimate=cost(1e10, 1e7),
        name="finish",
    )(early_got, prior)


def solution(mesh):
    in_specs = (P("inp", "chan", None), P("inp", None, None), P())
    out_specs = P(None, ("inp", "chan"), None, None)
    return jax.shard_map(
        on_device, mesh=mesh, in_specs=in_specs, out_specs=out_specs, check_vma=False
    )
```

```python
import math

import jax
import jax.numpy as jnp
import ml_dtypes
import numpy as np
from jax import lax
from jax.experimental import pallas as pl
from jax.experimental.pallas import tpu as pltpu
from jax.sharding import PartitionSpec as P

BAND = 2048
LOW = 1024
LANES = 128
RADIX = 64
HALF = 16
PAIR = 2
BLOCK = 16
CLASSES = RADIX // 2
ROOT = math.sqrt(0.5)
F32 = jnp.float32
BF16 = jnp.bfloat16
VMEM = 63 * 1024 * 1024


def stage_table(frame):
    high = BAND // RADIX
    lane = np.arange(LANES)
    table = np.zeros((CLASSES, 2, high, 2, 2, LANES))
    for q in range(CLASSES):
        for half in range(2):
            low = q if half == 0 else (RADIX - q if q else RADIX // 2)
            k = low + RADIX * (LOW // RADIX + np.arange(high))
            angle = 2.0 * np.pi * (np.outer(k, lane) % frame) / frame
            cos, sin = np.cos(angle), np.sin(angle)
            if q == 0:
                table[q, half, :, 0, half] = cos
                table[q, half, :, 1, half] = -sin
            elif half == 0:
                table[q, half, :, 0, 0] = cos
                table[q, half, :, 0, 1] = sin
                table[q, half, :, 1, 0] = -sin
                table[q, half, :, 1, 1] = cos
            else:
                table[q, half, :, 0, 0] = cos
                table[q, half, :, 0, 1] = -sin
                table[q, half, :, 1, 0] = -sin
                table[q, half, :, 1, 1] = -cos
    table = table / math.sqrt(frame)
    return table.swapaxes(2, 3).reshape(CLASSES, 2 * high * 2, 2 * LANES)


def real_dft8(x):
    s = [x[j] + x[j + 4] for j in range(4)]
    d = [x[j] - x[j + 4] for j in range(4)]
    e0, e1 = s[0] + s[2], s[0] - s[2]
    o0, o1 = s[1] + s[3], s[3] - s[1]
    u, v = (d[1] - d[3]) * ROOT, (d[1] + d[3]) * ROOT
    return [
        (e0 + o0, None),
        (d[0] + u, -(d[2] + v)),
        (e1, o1),
        (d[0] - u, d[2] - v),
        (e0 - o0, None),
    ]


def complex_dft8(x):
    def add(a, b):
        return (a[0] + b[0], a[1] + b[1])

    def sub(a, b):
        return (a[0] - b[0], a[1] - b[1])

    def add_i(a, b):
        return (a[0] - b[1], a[1] + b[0])

    def sub_i(a, b):
        return (a[0] + b[1], a[1] - b[0])

    s = [add(x[j], x[j + 4]) for j in range(4)]
    d = [sub(x[j], x[j + 4]) for j in range(4)]
    e0, e1 = add(s[0], s[2]), sub(s[0], s[2])
    o0, o1 = add(s[1], s[3]), sub(s[1], s[3])
    p, m = sub(d[1], d[3]), add(d[1], d[3])
    b = ((p[0] + m[1]) * ROOT, (p[1] - m[0]) * ROOT)
    c = ((m[1] - p[0]) * ROOT, (-p[1] - m[0]) * ROOT)
    f, g = sub_i(d[0], d[2]), add_i(d[0], d[2])
    return [
        add(e0, o0),
        add(f, b),
        sub_i(e1, o1),
        add(g, c),
        sub(e0, o0),
        sub(f, b),
        add_i(e1, o1),
        sub(g, c),
    ]


def turned(value, step):
    angle = 2.0 * math.pi * (step % RADIX) / RADIX
    cos, sin = math.cos(angle), math.sin(angle)
    real, imag = value
    if imag is None:
        return (real * cos, real * -sin)
    if step % RADIX == 0:
        return value
    return (real * cos + imag * sin, imag * cos - real * sin)


def unrolled(count, copies, body):
    def step(i, carry):
        for copy in range(copies):
            body(i * copies + copy, copy)
        return carry

    lax.fori_loop(0, count // copies, step, 0)


def transform_rows(fir, mids, zed, copies):
    def one(s, copy):
        mid = mids.at[copy]
        for low in range(8):
            parts = real_dft8([fir[8 * high + low, s] for high in range(8)])
            mid[0, low] = parts[0][0]
            mid[7, low] = parts[4][0]
            for k in (1, 2, 3):
                value = turned(parts[k], low * k)
                mid[2 * k - 1, low] = value[0]
                mid[2 * k, low] = value[1]
        rows = pl.ds(pl.multiple_of(s * HALF, HALF), HALF)

        def put(q, half, value):
            zed[q, rows, half * LANES : (half + 1) * LANES] = value.astype(BF16)

        parts = real_dft8([mid[0, low] for low in range(8)])
        put(0, 0, parts[0][0])
        put(0, 1, parts[4][0])
        for m in (1, 2, 3):
            put(8 * m, 0, parts[m][0])
            put(8 * m, 1, parts[m][1])
        for k in (1, 2, 3):
            parts = complex_dft8([(mid[2 * k - 1, low], mid[2 * k, low]) for low in range(8)])
            for m in range(8):
                index = k + 8 * m
                if index < CLASSES:
                    put(index, 0, parts[m][0])
                    put(index, 1, parts[m][1])
                else:
                    put(RADIX - index, 0, parts[m][0])
                    put(RADIX - index, 1, -parts[m][1])
        parts = complex_dft8([turned((mid[7, low], None), 4 * low) for low in range(8)])
        for m in range(4):
            put(4 + 8 * m, 0, parts[m][0])
            put(4 + 8 * m, 1, parts[m][1])

    unrolled(fir.shape[1], copies, one)


CHUNKS = 8
CONTRACT = (((1,), (1,)), ((), ()))


def fill(first, copies, hist, keep, volt_in, taper_in, table_in, volt, taper, held, fir, mid, zed, sems):
    taps = taper.shape[0]
    in_dev, s_dev, frame = volt.shape
    halves = in_dev // HALF
    count = fir.shape[1] // halves
    part = frame // CHUNKS
    wanted = [f for f in range(first - taps + 1, first + count) if f < s_dev]

    def volt_copy(j):
        where = (slice(None), slice(None), pl.ds(pl.multiple_of(j * part, part), part))
        return pltpu.make_async_copy(volt_in.at[where], volt.at[where], sems.at[j])

    taper_copy = pltpu.make_async_copy(taper_in, taper, sems.at[CHUNKS])
    table_copy = pltpu.make_async_copy(table_in, held, sems.at[CHUNKS + 1])
    taper_copy.start()
    for j in range(CHUNKS):
        volt_copy(j).start()
    table_copy.start()
    taper_copy.wait()

    def one_chunk(j, carry):
        volt_copy(j).wait()

        def one(i, copy):
            a = j * (part // LANES) + i
            lanes = pl.ds(pl.multiple_of(a * LANES, LANES), LANES)
            weights = [taper[t : t + 1, lanes] for t in range(taps)]
            for h in range(halves):
                inputs = slice(h * HALF, (h + 1) * HALF)
                by_time = jnp.swapaxes(volt[inputs, :, lanes], 0, 1)
                frames = {}
                for f in wanted:
                    if f >= 0:
                        frames[f] = by_time[f].astype(F32)
                    elif hist is not None:
                        frames[f] = hist[taps - 1 + f, inputs, lanes].astype(F32) * keep
                for row in range(count):
                    total = None
                    for t in range(taps):
                        f = first + row + t - taps + 1
                        if f in frames:
                            term = weights[t] * frames[f]
                            total = term if total is None else total + term
                    fir[a, row * halves + h] = total

        unrolled(part // LANES, copies[0], one)
        return carry

    lax.fori_loop(0, CHUNKS, one_chunk, 0)
    transform_rows(fir, mid, zed, copies[1])
    table_copy.wait()


def carried_kernel(volt_in, taper_in, table_in, out_ref, *scratch):
    *scratch, out, out_sems = scratch
    volt, taper, held, fir, mid, zed, sems = scratch
    fill(
        volt.shape[1], (4, 2), None, None,
        volt_in, taper_in, table_in, volt, taper, held, fir, mid, zed, sems,
    )
    block = CLASSES // 2

    def out_copy(j):
        where = pl.ds(j * block, block)
        return pltpu.make_async_copy(out.at[where], out_ref.at[where], out_sems.at[j])

    def some(j, carry):
        for i in range(block):
            q = j * block + i
            out[q] = jnp.dot(zed[q], held[q], preferred_element_type=F32).astype(BF16)
        out_copy(j).start()
        return carry

    lax.fori_loop(0, 2, some, 0)

    def finish(j, carry):
        out_copy(j).wait()
        return carry

    lax.fori_loop(0, 2, finish, 0)


def lane_swap(x):
    width = LANES // 4
    block = lax.broadcasted_iota(jnp.int32, (HALF, LANES), 1) // width
    x = list(x)
    mask = (block & 1) == 0
    for p in (0, 2):
        low, up = x[p], x[p + 1]
        x[p] = jnp.where(mask, low, pltpu.roll(up, width, 1))
        x[p + 1] = jnp.where(mask, pltpu.roll(low, LANES - width, 1), up)
    mask = (block & 2) == 0
    for p in (0, 1):
        low, up = x[p], x[p + 2]
        moved = pltpu.roll(jnp.where(mask, up, low), 2 * width, 1)
        x[p] = jnp.where(mask, low, moved)
        x[p + 2] = jnp.where(mask, moved, up)
    return x


def spectra_kernel(first, boundary, *refs):
    if boundary:
        keep, hist, carried, unit, *refs = refs
        keep = keep[0]
    else:
        keep, hist = None, None
    volt_in, taper_in, table_in, out_ref, volt, taper, held, fir, mid, zed, sems, wide, out = refs
    fill(
        first, (4, 2), hist, keep,
        volt_in, taper_in, table_in, volt, taper, held, fir, mid, zed, sems,
    )
    step = RADIX
    high = step // 2
    sides = wide.shape[2] // LANES
    split = out.shape[0] // high
    channels = RADIX // split

    def one(q, copy):
        value = lax.dot_general(held[q], zed[q], CONTRACT, preferred_element_type=F32)
        if boundary:
            part = carried[q]
            short = zed.shape[1] - part.shape[0]
            part = jnp.concatenate([part, jnp.zeros((short, LANES), BF16)], axis=0)
            value = value + lax.dot_general(
                unit[...], part, CONTRACT, preferred_element_type=F32
            )
        wide[q] = value[:step].astype(BF16)
        wide[jnp.where(q == 0, CLASSES, RADIX - q)] = value[step:].astype(BF16)

    unrolled(CLASSES, 4 if boundary else 16, one)

    def out_copy(b):
        where = pl.ds(b * HALF * split, HALF * split)
        return pltpu.make_async_copy(out.at[where], out_ref.at[where], sems.at[b])

    def rows_of(b, part):
        return pl.ds(pl.multiple_of(part * high + b * HALF, HALF), HALF)

    def late_block(b, copy):
        for part in range(2):
            for side in range(sides):
                lanes = slice(side * LANES, (side + 1) * LANES)
                for first_k in range(0, RADIX, HALF):
                    value = jnp.swapaxes(
                        wide[first_k : first_k + HALF, rows_of(b, part), lanes], 0, 1
                    )
                    u, k = divmod(first_k, channels)
                    start = part * channels + k
                    for j in range(HALF):
                        group = (b * HALF + j) * split + u
                        out[group, side, start : start + HALF, :] = value[j]
        out_copy(b).start()

    def early_block(b, copy):
        def quad(k, copy):
            tiles = []
            for part in range(2):
                for side in range(sides):
                    lanes = slice(side * LANES, (side + 1) * LANES)
                    tiles += lane_swap([wide[4 * k + p, rows_of(b, part), lanes] for p in range(4)])
            value = jnp.swapaxes(jnp.stack(tiles), 0, 1)
            u, inside = lax.div(k, channels // 4), lax.rem(k, channels // 4)
            for j in range(HALF):
                out[(b * HALF + j) * split + u, inside] = value[j]

        unrolled(RADIX // 4, 4, quad)
        out_copy(b).start()

    unrolled(high // HALF, 1, early_block if boundary else late_block)

    def finish(b, carry):
        out_copy(b).wait()
        return carry

    lax.fori_loop(0, high // HALF, finish, 0)


def reorder(got, first, copies, put):
    n_inp, _, sets, rows, _ = got.shape
    assert HALF // (sets * PAIR) == 4

    def one(b, copy):
        here = pl.ds(pl.multiple_of(b * HALF, HALF), HALF)
        for tile in range(n_inp // 4):
            pieces = []
            for c in range(PAIR):
                for part in range(sets):
                    pieces += lane_swap(
                        [got[tile * 4 + p, first + c, part, here, :] for p in range(4)]
                    )
            value = jnp.swapaxes(jnp.stack(pieces), 0, 1)
            for j in range(HALF):
                put(b * HALF + j, tile, value[j])

    unrolled(rows // HALF, min(copies, rows // HALF), one)


def order_pair(got, j, copies, out):
    def put(r, tile, value):
        times = pl.ds(pl.multiple_of(j * HALF, HALF), HALF)
        out[r, times, tile * LANES : (tile + 1) * LANES] = value

    reorder(got, j * PAIR, copies, put)


def gram(left, right):
    return lax.dot_general(
        left,
        jnp.concatenate([left, right], axis=1),
        (((0,), (0,)), ((), ())),
        preferred_element_type=F32,
    )


def prior_kernel(got, out, rows):
    channels = out.shape[0]

    def step(j, carry):
        order_pair(got, j, 4, rows)
        return carry

    lax.fori_loop(0, got.shape[1] // PAIR, step, 0)

    def one(k, copy):
        real, imag = rows[k], rows[channels + k]
        left = jnp.concatenate([real, imag], axis=0)
        out[k] = gram(left, jnp.concatenate([-imag, real], axis=0))

    unrolled(channels, 8, one)


def finish_kernel(scale, got_in, prior_in, out_ref, got, prior, rows, out, sems):
    n_inp, n_chan, quads, _, _ = got.shape
    steps = n_chan // PAIR
    channels, width = out.shape[1], out.shape[-1]
    count = channels // BLOCK

    def got_copy(j):
        where = (slice(None), pl.ds(j * PAIR, PAIR))
        return pltpu.make_async_copy(got_in.at[where], got.at[where], sems.at[count + j])

    def out_copy(j):
        where = (slice(None), pl.ds(j * BLOCK, BLOCK))
        return pltpu.make_async_copy(out.at[where], out_ref.at[where], sems.at[j])

    for j in range(steps):
        got_copy(j).start()
    def prior_copy(j):
        where = pl.ds(j * BLOCK, BLOCK)
        return pltpu.make_async_copy(
            prior_in.at[where], prior.at[where], sems.at[count + steps + j]
        )

    for j in range(count):
        prior_copy(j).start()

    def order(j, carry):
        got_copy(j).wait()

        def quad(k, copy):
            for c in range(PAIR):
                times = pl.ds(pl.multiple_of((j * PAIR + c) * HALF, HALF), HALF)
                for tile in range(n_inp // 4):
                    x = lane_swap([got[tile * 4 + p, j * PAIR + c, k] for p in range(4)])
                    for p in range(4):
                        rows[4 * k + p, times, tile * LANES : (tile + 1) * LANES] = x[p]

        unrolled(quads, min(8, quads), quad)
        return carry

    lax.fori_loop(0, steps, order, 0)

    def some(j, carry):
        prior_copy(j).wait()
        for i in range(BLOCK):
            k = j * BLOCK + i
            left = rows[k]
            parts = left.astype(F32).reshape(n_chan, 2, HALF // 2, width)
            right = jnp.stack([-parts[:, 1], parts[:, 0]], axis=1).reshape(left.shape)
            value = (gram(left, right.astype(BF16)) + prior[k]) * scale
            out[0, k] = value[:, :width].astype(BF16)
            out[1, k] = value[:, width:].astype(BF16)
        out_copy(j).start()
        return carry

    lax.fori_loop(0, count, some, 0)

    def finish(j, carry):
        out_copy(j).wait()
        return carry

    lax.fori_loop(0, count, finish, 0)


def params():
    return pltpu.CompilerParams(vmem_limit_bytes=VMEM)


def cost(flops, moved):
    return pl.CostEstimate(flops=int(flops), bytes_accessed=int(moved), transcendentals=0)


def on_device(voltages, history, taper):
    in_dev, s_dev, frame = voltages.shape
    taps = taper.shape[0]
    n_inp = lax.axis_size("inp")
    n_chan = lax.axis_size("chan")
    groups = n_inp * n_chan
    channels = BAND // groups
    total = n_inp * in_dev
    times = s_dev // 2
    early = taps - 1
    blocks = LANES // in_dev
    sets = times // blocks
    span = n_chan * times
    assert frame == RADIX * LANES and in_dev == 2 * HALF and PAIR * times == HALF
    assert early == times - 1 and RADIX % channels == 0 and n_inp % blocks == 0
    assert n_chan % PAIR == 0 and channels % BLOCK == 0

    outputs = 2 * BAND // CLASSES
    stage = stage_table(frame).astype(np.float32).astype(ml_dtypes.bfloat16)
    table = jnp.asarray(stage)
    upright = jnp.asarray(np.ascontiguousarray(stage.transpose(0, 2, 1)))
    unit = jnp.asarray(np.eye(outputs).astype(ml_dtypes.bfloat16))
    assert table.shape == (CLASSES, outputs, 2 * LANES) and outputs == LANES

    away = pl.BlockSpec(memory_space=pl.ANY)
    near = pl.BlockSpec(memory_space=pltpu.VMEM)

    def scratch(count, shape):
        return [
            pltpu.VMEM(voltages.shape, BF16),
            pltpu.VMEM(taper.shape, F32),
            pltpu.VMEM(shape, BF16),
            pltpu.VMEM((RADIX, 2 * count, HALF, LANES), F32),
            pltpu.VMEM((2, 8, 8, HALF, LANES), F32),
            pltpu.VMEM((CLASSES, count * in_dev, 2 * LANES), BF16),
            pltpu.SemaphoreType.DMA((CHUNKS + 2,)),
        ]

    late_shape = (sets, 2 * channels, LANES)
    early_shape = (channels // 4, HALF, LANES)

    def sent(shape):
        return jax.ShapeDtypeStruct((groups,) + shape, BF16)

    def wide(shape):
        return [
            pltpu.VMEM((RADIX, RADIX, times * in_dev), BF16),
            pltpu.VMEM((groups,) + shape, BF16),
        ]

    carried = pl.pallas_call(
        carried_kernel,
        in_specs=[away] * 3,
        out_specs=away,
        out_shape=jax.ShapeDtypeStruct((CLASSES, early * in_dev, outputs), BF16),
        scratch_shapes=scratch(early, upright.shape)
        + [
            pltpu.VMEM((CLASSES, early * in_dev, outputs), BF16),
            pltpu.SemaphoreType.DMA((2,)),
        ],
        compiler_params=params(),
        cost_estimate=cost(1e10, 2e7),
        name="carried",
    )(voltages, taper, upright)
    carried, later_taper = lax.optimization_barrier((carried, taper))
    carried = lax.ppermute(carried, "chan", [(i, i + 1) for i in range(n_chan - 1)])

    late_send = pl.pallas_call(
        lambda *refs: spectra_kernel(times, False, *refs),
        in_specs=[away] * 3,
        out_specs=away,
        out_shape=sent(late_shape),
        scratch_shapes=scratch(times, table.shape) + wide(late_shape),
        compiler_params=params(),
        cost_estimate=cost(5e10, 4e7),
        name="late",
    )(voltages, later_taper, table)

    def exchange(value, shape):
        value = lax.all_to_all(value, ("inp", "chan"), split_axis=0, concat_axis=0, tiled=True)
        return value.reshape((n_inp, n_chan) + shape)

    late_got = exchange(late_send, late_shape)

    keep = (lax.axis_index("chan") == 0).astype(F32).reshape(1)
    early_send = pl.pallas_call(
        lambda *refs: spectra_kernel(0, True, *refs),
        in_specs=[pl.BlockSpec(memory_space=pltpu.SMEM), near, near, near] + [away] * 3,
        out_specs=away,
        out_shape=sent(early_shape),
        scratch_shapes=scratch(times, table.shape) + wide(early_shape),
        compiler_params=params(),
        cost_estimate=cost(2e11, 4e7),
        name="early",
    )(keep, jnp.transpose(history, (1, 0, 2)), carried, unit, voltages, taper, table)
    early_got = exchange(early_send, early_shape)

    rows = pltpu.VMEM((2 * channels, span, total), BF16)
    prior_shape = (channels, total, 2 * total)
    prior = pl.pallas_call(
        prior_kernel,
        in_specs=[near],
        out_specs=near,
        out_shape=jax.ShapeDtypeStruct(prior_shape, F32),
        scratch_shapes=[rows],
        compiler_params=params(),
        cost_estimate=cost(1e4, 1e4),
        name="prior",
    )(late_got)
    return pl.pallas_call(
        lambda *refs: finish_kernel(1.0 / (n_chan * s_dev), *refs),
        in_specs=[away, away],
        out_specs=away,
        out_shape=jax.ShapeDtypeStruct((2, channels, total, total), BF16),
        scratch_shapes=[
            pltpu.VMEM(early_got.shape, BF16),
            pltpu.VMEM(prior_shape, F32),
            pltpu.VMEM((channels, n_chan * HALF, total), BF16),
            pltpu.VMEM((2, channels, total, total), BF16),
            pltpu.SemaphoreType.DMA((2 * (channels // BLOCK) + n_chan // PAIR,)),
        ],
        compiler_params=params(),
        cost_estimate=cost(1e10, 1e7),
        name="finish",
    )(early_got, prior)


def solution(mesh):
    in_specs = (P("inp", "chan", None), P("inp", None, None), P())
    out_specs = P(None, ("inp", "chan"), None, None)
    return jax.shard_map(
        on_device, mesh=mesh, in_specs=in_specs, out_specs=out_specs, check_vma=False
    )
```

```python
import math

import jax
import jax.numpy as jnp
import ml_dtypes
import numpy as np
from jax import lax
from jax.experimental import pallas as pl
from jax.experimental.pallas import tpu as pltpu
from jax.sharding import PartitionSpec as P

BAND = 2048
LOW = 1024
LANES = 128
RADIX = 64
HALF = 16
PAIR = 2
BLOCK = 16
CLASSES = RADIX // 2
ROOT = math.sqrt(0.5)
F32 = jnp.float32
BF16 = jnp.bfloat16
VMEM = 63 * 1024 * 1024


def stage_table(frame):
    high = BAND // RADIX
    lane = np.arange(LANES)
    table = np.zeros((CLASSES, 2, high, 2, 2, LANES))
    for q in range(CLASSES):
        for half in range(2):
            low = q if half == 0 else (RADIX - q if q else RADIX // 2)
            k = low + RADIX * (LOW // RADIX + np.arange(high))
            angle = 2.0 * np.pi * (np.outer(k, lane) % frame) / frame
            cos, sin = np.cos(angle), np.sin(angle)
            if q == 0:
                table[q, half, :, 0, half] = cos
                table[q, half, :, 1, half] = -sin
            elif half == 0:
                table[q, half, :, 0, 0] = cos
                table[q, half, :, 0, 1] = sin
                table[q, half, :, 1, 0] = -sin
                table[q, half, :, 1, 1] = cos
            else:
                table[q, half, :, 0, 0] = cos
                table[q, half, :, 0, 1] = -sin
                table[q, half, :, 1, 0] = -sin
                table[q, half, :, 1, 1] = -cos
    table = table / math.sqrt(frame)
    return table.swapaxes(2, 3).reshape(CLASSES, 2 * high * 2, 2 * LANES)


def real_dft8(x):
    s = [x[j] + x[j + 4] for j in range(4)]
    d = [x[j] - x[j + 4] for j in range(4)]
    e0, e1 = s[0] + s[2], s[0] - s[2]
    o0, o1 = s[1] + s[3], s[3] - s[1]
    u, v = (d[1] - d[3]) * ROOT, (d[1] + d[3]) * ROOT
    return [
        (e0 + o0, None),
        (d[0] + u, -(d[2] + v)),
        (e1, o1),
        (d[0] - u, d[2] - v),
        (e0 - o0, None),
    ]


def complex_dft8(x):
    def add(a, b):
        return (a[0] + b[0], a[1] + b[1])

    def sub(a, b):
        return (a[0] - b[0], a[1] - b[1])

    def add_i(a, b):
        return (a[0] - b[1], a[1] + b[0])

    def sub_i(a, b):
        return (a[0] + b[1], a[1] - b[0])

    s = [add(x[j], x[j + 4]) for j in range(4)]
    d = [sub(x[j], x[j + 4]) for j in range(4)]
    e0, e1 = add(s[0], s[2]), sub(s[0], s[2])
    o0, o1 = add(s[1], s[3]), sub(s[1], s[3])
    p, m = sub(d[1], d[3]), add(d[1], d[3])
    b = ((p[0] + m[1]) * ROOT, (p[1] - m[0]) * ROOT)
    c = ((m[1] - p[0]) * ROOT, (-p[1] - m[0]) * ROOT)
    f, g = sub_i(d[0], d[2]), add_i(d[0], d[2])
    return [
        add(e0, o0),
        add(f, b),
        sub_i(e1, o1),
        add(g, c),
        sub(e0, o0),
        sub(f, b),
        add_i(e1, o1),
        sub(g, c),
    ]


def turned(value, step):
    angle = 2.0 * math.pi * (step % RADIX) / RADIX
    cos, sin = math.cos(angle), math.sin(angle)
    real, imag = value
    if imag is None:
        return (real * cos, real * -sin)
    if step % RADIX == 0:
        return value
    return (real * cos + imag * sin, imag * cos - real * sin)


def unrolled(count, copies, body):
    def step(i, carry):
        for copy in range(copies):
            body(i * copies + copy, copy)
        return carry

    lax.fori_loop(0, count // copies, step, 0)


def transform_rows(fir, mids, zed, copies):
    def one(s, copy):
        mid = mids.at[copy]
        for low in range(8):
            parts = real_dft8([fir[8 * high + low, s] for high in range(8)])
            mid[0, low] = parts[0][0]
            mid[7, low] = parts[4][0]
            for k in (1, 2, 3):
                value = turned(parts[k], low * k)
                mid[2 * k - 1, low] = value[0]
                mid[2 * k, low] = value[1]
        rows = pl.ds(pl.multiple_of(s * HALF, HALF), HALF)

        def put(q, half, value):
            zed[q, rows, half * LANES : (half + 1) * LANES] = value.astype(BF16)

        parts = real_dft8([mid[0, low] for low in range(8)])
        put(0, 0, parts[0][0])
        put(0, 1, parts[4][0])
        for m in (1, 2, 3):
            put(8 * m, 0, parts[m][0])
            put(8 * m, 1, parts[m][1])
        for k in (1, 2, 3):
            parts = complex_dft8([(mid[2 * k - 1, low], mid[2 * k, low]) for low in range(8)])
            for m in range(8):
                index = k + 8 * m
                if index < CLASSES:
                    put(index, 0, parts[m][0])
                    put(index, 1, parts[m][1])
                else:
                    put(RADIX - index, 0, parts[m][0])
                    put(RADIX - index, 1, -parts[m][1])
        parts = complex_dft8([turned((mid[7, low], None), 4 * low) for low in range(8)])
        for m in range(4):
            put(4 + 8 * m, 0, parts[m][0])
            put(4 + 8 * m, 1, parts[m][1])

    unrolled(fir.shape[1], copies, one)


CHUNKS = 8
CONTRACT = (((1,), (1,)), ((), ()))


def fill(first, copies, hist, keep, volt_in, taper_in, table_in, volt, taper, held, fir, mid, zed, sems):
    taps = taper.shape[0]
    in_dev, s_dev, frame = volt.shape
    halves = in_dev // HALF
    count = fir.shape[1] // halves
    part = frame // CHUNKS
    wanted = [f for f in range(first - taps + 1, first + count) if f < s_dev]

    def volt_copy(j):
        where = (slice(None), slice(None), pl.ds(pl.multiple_of(j * part, part), part))
        return pltpu.make_async_copy(volt_in.at[where], volt.at[where], sems.at[j])

    taper_copy = pltpu.make_async_copy(taper_in, taper, sems.at[CHUNKS])
    table_copy = pltpu.make_async_copy(table_in, held, sems.at[CHUNKS + 1])
    taper_copy.start()
    for j in range(CHUNKS):
        volt_copy(j).start()
    table_copy.start()
    taper_copy.wait()

    def one_chunk(j, carry):
        volt_copy(j).wait()

        def one(i, copy):
            a = j * (part // LANES) + i
            lanes = pl.ds(pl.multiple_of(a * LANES, LANES), LANES)
            weights = [taper[t : t + 1, lanes] for t in range(taps)]
            for h in range(halves):
                inputs = slice(h * HALF, (h + 1) * HALF)
                by_time = jnp.swapaxes(volt[inputs, :, lanes], 0, 1)
                frames = {}
                for f in wanted:
                    if f >= 0:
                        frames[f] = by_time[f].astype(F32)
                    elif hist is not None:
                        frames[f] = hist[taps - 1 + f, inputs, lanes].astype(F32) * keep
                for row in range(count):
                    total = None
                    for t in range(taps):
                        f = first + row + t - taps + 1
                        if f in frames:
                            term = weights[t] * frames[f]
                            total = term if total is None else total + term
                    fir[a, row * halves + h] = total

        unrolled(part // LANES, copies[0], one)
        return carry

    lax.fori_loop(0, CHUNKS, one_chunk, 0)
    transform_rows(fir, mid, zed, copies[1])
    table_copy.wait()


def carried_kernel(volt_in, taper_in, table_in, out_ref, *scratch):
    *scratch, out, out_sems = scratch
    volt, taper, held, fir, mid, zed, sems = scratch
    fill(
        volt.shape[1], (4, 2), None, None,
        volt_in, taper_in, table_in, volt, taper, held, fir, mid, zed, sems,
    )
    block = CLASSES // 2

    def out_copy(j):
        where = pl.ds(j * block, block)
        return pltpu.make_async_copy(out.at[where], out_ref.at[where], out_sems.at[j])

    def some(j, carry):
        for i in range(block):
            q = j * block + i
            out[q] = jnp.dot(zed[q], held[q], preferred_element_type=F32).astype(BF16)
        out_copy(j).start()
        return carry

    lax.fori_loop(0, 2, some, 0)

    def finish(j, carry):
        out_copy(j).wait()
        return carry

    lax.fori_loop(0, 2, finish, 0)


def lane_swap(x):
    width = LANES // 4
    block = lax.broadcasted_iota(jnp.int32, (HALF, LANES), 1) // width
    x = list(x)
    mask = (block & 1) == 0
    for p in (0, 2):
        low, up = x[p], x[p + 1]
        x[p] = jnp.where(mask, low, pltpu.roll(up, width, 1))
        x[p + 1] = jnp.where(mask, pltpu.roll(low, LANES - width, 1), up)
    mask = (block & 2) == 0
    for p in (0, 1):
        low, up = x[p], x[p + 2]
        moved = pltpu.roll(jnp.where(mask, up, low), 2 * width, 1)
        x[p] = jnp.where(mask, low, moved)
        x[p + 2] = jnp.where(mask, moved, up)
    return x


def spectra_kernel(first, boundary, *refs):
    if boundary:
        keep, hist, carried, unit, *refs = refs
        keep = keep[0]
    else:
        keep, hist = None, None
    volt_in, taper_in, table_in, out_ref, volt, taper, held, fir, mid, zed, sems, wide, out = refs
    fill(
        first, (4, 2), hist, keep,
        volt_in, taper_in, table_in, volt, taper, held, fir, mid, zed, sems,
    )
    step = RADIX
    high = step // 2
    sides = wide.shape[2] // LANES
    split = out.shape[0] // high
    channels = RADIX // split

    def one(q, copy):
        value = lax.dot_general(held[q], zed[q], CONTRACT, preferred_element_type=F32)
        if boundary:
            part = carried[q]
            short = zed.shape[1] - part.shape[0]
            part = jnp.concatenate([part, jnp.zeros((short, LANES), BF16)], axis=0)
            value = value + lax.dot_general(
                unit[...], part, CONTRACT, preferred_element_type=F32
            )
        wide[q] = value[:step].astype(BF16)
        wide[jnp.where(q == 0, CLASSES, RADIX - q)] = value[step:].astype(BF16)

    unrolled(CLASSES, 4 if boundary else 16, one)

    def out_copy(b):
        where = pl.ds(b * HALF * split, HALF * split)
        return pltpu.make_async_copy(out.at[where], out_ref.at[where], sems.at[b])

    def rows_of(b, part):
        return pl.ds(pl.multiple_of(part * high + b * HALF, HALF), HALF)

    def late_block(b, copy):
        for part in range(2):
            for side in range(sides):
                lanes = slice(side * LANES, (side + 1) * LANES)
                for first_k in range(0, RADIX, HALF):
                    value = jnp.swapaxes(
                        wide[first_k : first_k + HALF, rows_of(b, part), lanes], 0, 1
                    )
                    u, k = divmod(first_k, channels)
                    start = part * channels + k
                    for j in range(HALF):
                        group = (b * HALF + j) * split + u
                        out[group, side, start : start + HALF, :] = value[j]
        out_copy(b).start()

    def early_block(b, copy):
        def quad(k, copy):
            tiles = []
            for part in range(2):
                for side in range(sides):
                    lanes = slice(side * LANES, (side + 1) * LANES)
                    tiles += lane_swap([wide[4 * k + p, rows_of(b, part), lanes] for p in range(4)])
            value = jnp.swapaxes(jnp.stack(tiles), 0, 1)
            u, inside = lax.div(k, channels // 4), lax.rem(k, channels // 4)
            for j in range(HALF):
                out[(b * HALF + j) * split + u, inside] = value[j]

        unrolled(RADIX // 4, 4, quad)
        out_copy(b).start()

    unrolled(high // HALF, 1, early_block if boundary else late_block)

    def finish(b, carry):
        out_copy(b).wait()
        return carry

    lax.fori_loop(0, high // HALF, finish, 0)


def reorder(got, first, copies, put):
    n_inp, _, sets, rows, _ = got.shape
    assert HALF // (sets * PAIR) == 4

    def one(b, copy):
        here = pl.ds(pl.multiple_of(b * HALF, HALF), HALF)
        for tile in range(n_inp // 4):
            pieces = []
            for c in range(PAIR):
                for part in range(sets):
                    pieces += lane_swap(
                        [got[tile * 4 + p, first + c, part, here, :] for p in range(4)]
                    )
            value = jnp.swapaxes(jnp.stack(pieces), 0, 1)
            for j in range(HALF):
                put(b * HALF + j, tile, value[j])

    unrolled(rows // HALF, min(copies, rows // HALF), one)


def order_pair(got, j, copies, out):
    def put(r, tile, value):
        times = pl.ds(pl.multiple_of(j * HALF, HALF), HALF)
        out[r, times, tile * LANES : (tile + 1) * LANES] = value

    reorder(got, j * PAIR, copies, put)


def gram(left, right):
    return lax.dot_general(
        left,
        jnp.concatenate([left, right], axis=1),
        (((0,), (0,)), ((), ())),
        preferred_element_type=F32,
    )


def prior_kernel(got, out, rows):
    channels = out.shape[0]

    def step(j, carry):
        order_pair(got, j, 4, rows)
        return carry

    lax.fori_loop(0, got.shape[1] // PAIR, step, 0)

    def one(k, copy):
        real, imag = rows[k], rows[channels + k]
        left = jnp.concatenate([real, imag], axis=0)
        out[k] = gram(left, jnp.concatenate([-imag, real], axis=0))

    unrolled(channels, 8, one)


def finish_kernel(scale, got_in, prior_in, out_ref, got, prior, rows, out, sems):
    n_inp, n_chan, quads, _, _ = got.shape
    steps = n_chan // PAIR
    channels, width = out.shape[1], out.shape[-1]
    count = channels // BLOCK

    def got_copy(j):
        where = (slice(None), pl.ds(j * PAIR, PAIR))
        return pltpu.make_async_copy(got_in.at[where], got.at[where], sems.at[count + j])

    def out_copy(j):
        where = (slice(None), pl.ds(j * BLOCK, BLOCK))
        return pltpu.make_async_copy(out.at[where], out_ref.at[where], sems.at[j])

    for j in range(steps):
        got_copy(j).start()
    def prior_copy(j):
        where = pl.ds(j * BLOCK, BLOCK)
        return pltpu.make_async_copy(
            prior_in.at[where], prior.at[where], sems.at[count + steps + j]
        )

    for j in range(count):
        prior_copy(j).start()

    def order(j, carry):
        got_copy(j).wait()

        def quad(k, copy):
            for c in range(PAIR):
                times = pl.ds(pl.multiple_of((j * PAIR + c) * HALF, HALF), HALF)
                for tile in range(n_inp // 4):
                    x = lane_swap([got[tile * 4 + p, j * PAIR + c, k] for p in range(4)])
                    for p in range(4):
                        rows[4 * k + p, times, tile * LANES : (tile + 1) * LANES] = x[p]

        unrolled(quads, min(8, quads), quad)
        return carry

    lax.fori_loop(0, steps, order, 0)

    row = lax.broadcasted_iota(jnp.int32, (HALF, width), 0)
    sign = jnp.where(row < HALF // 2, -1.0, 1.0).astype(BF16)

    def some(j, carry):
        prior_copy(j).wait()
        for i in range(BLOCK):
            k = j * BLOCK + i
            left = rows[k]
            right = jnp.concatenate(
                [
                    pltpu.roll(left[c * HALF : (c + 1) * HALF], HALF // 2, 0) * sign
                    for c in range(n_chan)
                ],
                axis=0,
            )
            value = (gram(left, right) + prior[k]) * scale
            out[0, k] = value[:, :width].astype(BF16)
            out[1, k] = value[:, width:].astype(BF16)
        out_copy(j).start()
        return carry

    lax.fori_loop(0, count, some, 0)

    def finish(j, carry):
        out_copy(j).wait()
        return carry

    lax.fori_loop(0, count, finish, 0)


def params():
    return pltpu.CompilerParams(vmem_limit_bytes=VMEM)


def cost(flops, moved):
    return pl.CostEstimate(flops=int(flops), bytes_accessed=int(moved), transcendentals=0)


def on_device(voltages, history, taper):
    in_dev, s_dev, frame = voltages.shape
    taps = taper.shape[0]
    n_inp = lax.axis_size("inp")
    n_chan = lax.axis_size("chan")
    groups = n_inp * n_chan
    channels = BAND // groups
    total = n_inp * in_dev
    times = s_dev // 2
    early = taps - 1
    blocks = LANES // in_dev
    sets = times // blocks
    span = n_chan * times
    assert frame == RADIX * LANES and in_dev == 2 * HALF and PAIR * times == HALF
    assert early == times - 1 and RADIX % channels == 0 and n_inp % blocks == 0
    assert n_chan % PAIR == 0 and channels % BLOCK == 0

    outputs = 2 * BAND // CLASSES
    stage = stage_table(frame).astype(np.float32).astype(ml_dtypes.bfloat16)
    table = jnp.asarray(stage)
    upright = jnp.asarray(np.ascontiguousarray(stage.transpose(0, 2, 1)))
    unit = jnp.asarray(np.eye(outputs).astype(ml_dtypes.bfloat16))
    assert table.shape == (CLASSES, outputs, 2 * LANES) and outputs == LANES

    away = pl.BlockSpec(memory_space=pl.ANY)
    near = pl.BlockSpec(memory_space=pltpu.VMEM)

    def scratch(count, shape):
        return [
            pltpu.VMEM(voltages.shape, BF16),
            pltpu.VMEM(taper.shape, F32),
            pltpu.VMEM(shape, BF16),
            pltpu.VMEM((RADIX, 2 * count, HALF, LANES), F32),
            pltpu.VMEM((2, 8, 8, HALF, LANES), F32),
            pltpu.VMEM((CLASSES, count * in_dev, 2 * LANES), BF16),
            pltpu.SemaphoreType.DMA((CHUNKS + 2,)),
        ]

    late_shape = (sets, 2 * channels, LANES)
    early_shape = (channels // 4, HALF, LANES)

    def sent(shape):
        return jax.ShapeDtypeStruct((groups,) + shape, BF16)

    def wide(shape):
        return [
            pltpu.VMEM((RADIX, RADIX, times * in_dev), BF16),
            pltpu.VMEM((groups,) + shape, BF16),
        ]

    carried = pl.pallas_call(
        carried_kernel,
        in_specs=[away] * 3,
        out_specs=away,
        out_shape=jax.ShapeDtypeStruct((CLASSES, early * in_dev, outputs), BF16),
        scratch_shapes=scratch(early, upright.shape)
        + [
            pltpu.VMEM((CLASSES, early * in_dev, outputs), BF16),
            pltpu.SemaphoreType.DMA((2,)),
        ],
        compiler_params=params(),
        cost_estimate=cost(1e10, 2e7),
        name="carried",
    )(voltages, taper, upright)
    carried, later_taper = lax.optimization_barrier((carried, taper))
    carried = lax.ppermute(carried, "chan", [(i, i + 1) for i in range(n_chan - 1)])

    late_send = pl.pallas_call(
        lambda *refs: spectra_kernel(times, False, *refs),
        in_specs=[away] * 3,
        out_specs=away,
        out_shape=sent(late_shape),
        scratch_shapes=scratch(times, table.shape) + wide(late_shape),
        compiler_params=params(),
        cost_estimate=cost(5e10, 4e7),
        name="late",
    )(voltages, later_taper, table)

    def exchange(value, shape):
        value = lax.all_to_all(value, ("inp", "chan"), split_axis=0, concat_axis=0, tiled=True)
        return value.reshape((n_inp, n_chan) + shape)

    late_got = exchange(late_send, late_shape)

    keep = (lax.axis_index("chan") == 0).astype(F32).reshape(1)
    early_send = pl.pallas_call(
        lambda *refs: spectra_kernel(0, True, *refs),
        in_specs=[pl.BlockSpec(memory_space=pltpu.SMEM), near, near, near] + [away] * 3,
        out_specs=away,
        out_shape=sent(early_shape),
        scratch_shapes=scratch(times, table.shape) + wide(early_shape),
        compiler_params=params(),
        cost_estimate=cost(2e11, 4e7),
        name="early",
    )(keep, jnp.transpose(history, (1, 0, 2)), carried, unit, voltages, taper, table)
    early_got = exchange(early_send, early_shape)

    rows = pltpu.VMEM((2 * channels, span, total), BF16)
    prior_shape = (channels, total, 2 * total)
    prior = pl.pallas_call(
        prior_kernel,
        in_specs=[near],
        out_specs=near,
        out_shape=jax.ShapeDtypeStruct(prior_shape, F32),
        scratch_shapes=[rows],
        compiler_params=params(),
        cost_estimate=cost(1e4, 1e4),
        name="prior",
    )(late_got)
    return pl.pallas_call(
        lambda *refs: finish_kernel(1.0 / (n_chan * s_dev), *refs),
        in_specs=[away, away],
        out_specs=away,
        out_shape=jax.ShapeDtypeStruct((2, channels, total, total), BF16),
        scratch_shapes=[
            pltpu.VMEM(early_got.shape, BF16),
            pltpu.VMEM(prior_shape, F32),
            pltpu.VMEM((channels, n_chan * HALF, total), BF16),
            pltpu.VMEM((2, channels, total, total), BF16),
            pltpu.SemaphoreType.DMA((2 * (channels // BLOCK) + n_chan // PAIR,)),
        ],
        compiler_params=params(),
        cost_estimate=cost(1e10, 1e7),
        name="finish",
    )(early_got, prior)


def solution(mesh):
    in_specs = (P("inp", "chan", None), P("inp", None, None), P())
    out_specs = P(None, ("inp", "chan"), None, None)
    return jax.shard_map(
        on_device, mesh=mesh, in_specs=in_specs, out_specs=out_specs, check_vma=False
    )
```

```python
import math

import jax
import jax.numpy as jnp
import ml_dtypes
import numpy as np
from jax import lax
from jax.experimental import pallas as pl
from jax.experimental.pallas import tpu as pltpu
from jax.sharding import PartitionSpec as P

BAND = 2048
LOW = 1024
LANES = 128
RADIX = 64
HALF = 16
PAIR = 2
BLOCK = 16
CLASSES = RADIX // 2
ROOT = math.sqrt(0.5)
F32 = jnp.float32
BF16 = jnp.bfloat16
VMEM = 63 * 1024 * 1024


def stage_table(frame):
    high = BAND // RADIX
    lane = np.arange(LANES)
    table = np.zeros((CLASSES, 2, high, 2, 2, LANES))
    for q in range(CLASSES):
        for half in range(2):
            low = q if half == 0 else (RADIX - q if q else RADIX // 2)
            k = low + RADIX * (LOW // RADIX + np.arange(high))
            angle = 2.0 * np.pi * (np.outer(k, lane) % frame) / frame
            cos, sin = np.cos(angle), np.sin(angle)
            if q == 0:
                table[q, half, :, 0, half] = cos
                table[q, half, :, 1, half] = -sin
            elif half == 0:
                table[q, half, :, 0, 0] = cos
                table[q, half, :, 0, 1] = sin
                table[q, half, :, 1, 0] = -sin
                table[q, half, :, 1, 1] = cos
            else:
                table[q, half, :, 0, 0] = cos
                table[q, half, :, 0, 1] = -sin
                table[q, half, :, 1, 0] = -sin
                table[q, half, :, 1, 1] = -cos
    table = table / math.sqrt(frame)
    return table.swapaxes(2, 3).reshape(CLASSES, 2 * high * 2, 2 * LANES)


def real_dft8(x):
    s = [x[j] + x[j + 4] for j in range(4)]
    d = [x[j] - x[j + 4] for j in range(4)]
    e0, e1 = s[0] + s[2], s[0] - s[2]
    o0, o1 = s[1] + s[3], s[3] - s[1]
    u, v = (d[1] - d[3]) * ROOT, (d[1] + d[3]) * ROOT
    return [
        (e0 + o0, None),
        (d[0] + u, -(d[2] + v)),
        (e1, o1),
        (d[0] - u, d[2] - v),
        (e0 - o0, None),
    ]


def complex_dft8(x):
    def add(a, b):
        return (a[0] + b[0], a[1] + b[1])

    def sub(a, b):
        return (a[0] - b[0], a[1] - b[1])

    def add_i(a, b):
        return (a[0] - b[1], a[1] + b[0])

    def sub_i(a, b):
        return (a[0] + b[1], a[1] - b[0])

    s = [add(x[j], x[j + 4]) for j in range(4)]
    d = [sub(x[j], x[j + 4]) for j in range(4)]
    e0, e1 = add(s[0], s[2]), sub(s[0], s[2])
    o0, o1 = add(s[1], s[3]), sub(s[1], s[3])
    p, m = sub(d[1], d[3]), add(d[1], d[3])
    b = ((p[0] + m[1]) * ROOT, (p[1] - m[0]) * ROOT)
    c = ((m[1] - p[0]) * ROOT, (-p[1] - m[0]) * ROOT)
    f, g = sub_i(d[0], d[2]), add_i(d[0], d[2])
    return [
        add(e0, o0),
        add(f, b),
        sub_i(e1, o1),
        add(g, c),
        sub(e0, o0),
        sub(f, b),
        add_i(e1, o1),
        sub(g, c),
    ]


def turned(value, step):
    angle = 2.0 * math.pi * (step % RADIX) / RADIX
    cos, sin = math.cos(angle), math.sin(angle)
    real, imag = value
    if imag is None:
        return (real * cos, real * -sin)
    if step % RADIX == 0:
        return value
    return (real * cos + imag * sin, imag * cos - real * sin)


def unrolled(count, copies, body):
    def step(i, carry):
        for copy in range(copies):
            body(i * copies + copy, copy)
        return carry

    lax.fori_loop(0, count // copies, step, 0)


def transform_rows(fir, mids, zed, copies):
    def one(s, copy):
        mid = mids.at[copy]
        for low in range(8):
            parts = real_dft8([fir[8 * high + low, s] for high in range(8)])
            mid[0, low] = parts[0][0]
            mid[7, low] = parts[4][0]
            for k in (1, 2, 3):
                value = turned(parts[k], low * k)
                mid[2 * k - 1, low] = value[0]
                mid[2 * k, low] = value[1]
        rows = pl.ds(pl.multiple_of(s * HALF, HALF), HALF)

        def put(q, half, value):
            zed[q, rows, half * LANES : (half + 1) * LANES] = value.astype(BF16)

        parts = real_dft8([mid[0, low] for low in range(8)])
        put(0, 0, parts[0][0])
        put(0, 1, parts[4][0])
        for m in (1, 2, 3):
            put(8 * m, 0, parts[m][0])
            put(8 * m, 1, parts[m][1])
        for k in (1, 2, 3):
            parts = complex_dft8([(mid[2 * k - 1, low], mid[2 * k, low]) for low in range(8)])
            for m in range(8):
                index = k + 8 * m
                if index < CLASSES:
                    put(index, 0, parts[m][0])
                    put(index, 1, parts[m][1])
                else:
                    put(RADIX - index, 0, parts[m][0])
                    put(RADIX - index, 1, -parts[m][1])
        parts = complex_dft8([turned((mid[7, low], None), 4 * low) for low in range(8)])
        for m in range(4):
            put(4 + 8 * m, 0, parts[m][0])
            put(4 + 8 * m, 1, parts[m][1])

    unrolled(fir.shape[1], copies, one)


CHUNKS = 8
CONTRACT = (((1,), (1,)), ((), ()))


def fill(first, copies, hist, keep, volt_in, taper_in, table_in, volt, taper, held, fir, mid, zed, sems):
    taps = taper.shape[0]
    in_dev, s_dev, frame = volt.shape
    halves = in_dev // HALF
    count = fir.shape[1] // halves
    part = frame // CHUNKS
    wanted = [f for f in range(first - taps + 1, first + count) if f < s_dev]

    def volt_copy(j):
        where = (slice(None), slice(None), pl.ds(pl.multiple_of(j * part, part), part))
        return pltpu.make_async_copy(volt_in.at[where], volt.at[where], sems.at[j])

    taper_copy = pltpu.make_async_copy(taper_in, taper, sems.at[CHUNKS])
    table_copy = pltpu.make_async_copy(table_in, held, sems.at[CHUNKS + 1])
    taper_copy.start()
    for j in range(CHUNKS):
        volt_copy(j).start()
    table_copy.start()
    taper_copy.wait()

    def one_chunk(j, carry):
        volt_copy(j).wait()

        def one(i, copy):
            a = j * (part // LANES) + i
            lanes = pl.ds(pl.multiple_of(a * LANES, LANES), LANES)
            weights = [taper[t : t + 1, lanes] for t in range(taps)]
            for h in range(halves):
                inputs = slice(h * HALF, (h + 1) * HALF)
                by_time = jnp.swapaxes(volt[inputs, :, lanes], 0, 1)
                frames = {}
                for f in wanted:
                    if f >= 0:
                        frames[f] = by_time[f].astype(F32)
                    elif hist is not None:
                        frames[f] = hist[taps - 1 + f, inputs, lanes].astype(F32) * keep
                for row in range(count):
                    total = None
                    for t in range(taps):
                        f = first + row + t - taps + 1
                        if f in frames:
                            term = weights[t] * frames[f]
                            total = term if total is None else total + term
                    fir[a, row * halves + h] = total

        unrolled(part // LANES, copies[0], one)
        return carry

    lax.fori_loop(0, CHUNKS, one_chunk, 0)
    transform_rows(fir, mid, zed, copies[1])
    table_copy.wait()


def carried_kernel(volt_in, taper_in, table_in, out_ref, *scratch):
    *scratch, out, out_sems = scratch
    volt, taper, held, fir, mid, zed, sems = scratch
    fill(
        volt.shape[1], (4, 2), None, None,
        volt_in, taper_in, table_in, volt, taper, held, fir, mid, zed, sems,
    )
    block = CLASSES // 2

    def out_copy(j):
        where = pl.ds(j * block, block)
        return pltpu.make_async_copy(out.at[where], out_ref.at[where], out_sems.at[j])

    def some(j, carry):
        for i in range(block):
            q = j * block + i
            out[q] = jnp.dot(zed[q], held[q], preferred_element_type=F32).astype(BF16)
        out_copy(j).start()
        return carry

    lax.fori_loop(0, 2, some, 0)

    def finish(j, carry):
        out_copy(j).wait()
        return carry

    lax.fori_loop(0, 2, finish, 0)


def lane_swap(x):
    width = LANES // 4
    block = lax.broadcasted_iota(jnp.int32, (HALF, LANES), 1) // width
    x = list(x)
    even, left, outer = (block & 1) == 0, block < 2, (block == 0) | (block == 3)
    for p in (0, 2):
        low, up = x[p], x[p + 1]
        moved = pltpu.roll(jnp.where(even, up, low), width, 1)
        x[p] = jnp.where(even, low, moved)
        x[p + 1] = jnp.where(even, moved, up)
    low, up = x[0], x[2]
    moved = pltpu.roll(jnp.where(left, up, low), 2 * width, 1)
    x[0], x[2] = jnp.where(left, low, moved), jnp.where(left, moved, up)
    low, up = x[1], x[3]
    moved = pltpu.roll(jnp.where(left, up, low), 2 * width, 1)
    stay = jnp.where(left, low, up)
    x[1], x[3] = jnp.where(outer, moved, stay), jnp.where(outer, stay, moved)
    return x


def spectra_kernel(first, boundary, *refs):
    if boundary:
        keep, hist, carried, unit, *refs = refs
        keep = keep[0]
    else:
        keep, hist = None, None
    volt_in, taper_in, table_in, out_ref, volt, taper, held, fir, mid, zed, sems, wide, out = refs
    fill(
        first, (4, 2), hist, keep,
        volt_in, taper_in, table_in, volt, taper, held, fir, mid, zed, sems,
    )
    step = RADIX
    high = step // 2
    sides = wide.shape[2] // LANES
    split = out.shape[0] // high
    channels = RADIX // split

    def one(q, copy):
        value = lax.dot_general(held[q], zed[q], CONTRACT, preferred_element_type=F32)
        if boundary:
            part = carried[q]
            short = zed.shape[1] - part.shape[0]
            part = jnp.concatenate([part, jnp.zeros((short, LANES), BF16)], axis=0)
            value = value + lax.dot_general(
                unit[...], part, CONTRACT, preferred_element_type=F32
            )
        wide[q] = value[:step].astype(BF16)
        wide[jnp.where(q == 0, CLASSES, RADIX - q)] = value[step:].astype(BF16)

    unrolled(CLASSES, 4 if boundary else 16, one)

    def out_copy(b):
        where = pl.ds(b * HALF * split, HALF * split)
        return pltpu.make_async_copy(out.at[where], out_ref.at[where], sems.at[b])

    def rows_of(b, part):
        return pl.ds(pl.multiple_of(part * high + b * HALF, HALF), HALF)

    def late_block(b, copy):
        for part in range(2):
            for side in range(sides):
                lanes = slice(side * LANES, (side + 1) * LANES)
                for first_k in range(0, RADIX, HALF):
                    value = jnp.swapaxes(
                        wide[first_k : first_k + HALF, rows_of(b, part), lanes], 0, 1
                    )
                    u, k = divmod(first_k, channels)
                    start = part * channels + k
                    for j in range(HALF):
                        group = (b * HALF + j) * split + u
                        out[group, side, start : start + HALF, :] = value[j]
        out_copy(b).start()

    def early_block(b, copy):
        def quad(k, copy):
            tiles = []
            for part in range(2):
                for side in range(sides):
                    lanes = slice(side * LANES, (side + 1) * LANES)
                    tiles += lane_swap([wide[4 * k + p, rows_of(b, part), lanes] for p in range(4)])
            value = jnp.swapaxes(jnp.stack(tiles), 0, 1)
            u, inside = lax.div(k, channels // 4), lax.rem(k, channels // 4)
            for j in range(HALF):
                out[(b * HALF + j) * split + u, inside] = value[j]

        unrolled(RADIX // 4, 4, quad)
        out_copy(b).start()

    unrolled(high // HALF, 1, early_block if boundary else late_block)

    def finish(b, carry):
        out_copy(b).wait()
        return carry

    lax.fori_loop(0, high // HALF, finish, 0)


def reorder(got, first, copies, put):
    n_inp, _, sets, rows, _ = got.shape
    assert HALF // (sets * PAIR) == 4

    def one(b, copy):
        here = pl.ds(pl.multiple_of(b * HALF, HALF), HALF)
        for tile in range(n_inp // 4):
            pieces = []
            for c in range(PAIR):
                for part in range(sets):
                    pieces += lane_swap(
                        [got[tile * 4 + p, first + c, part, here, :] for p in range(4)]
                    )
            value = jnp.swapaxes(jnp.stack(pieces), 0, 1)
            for j in range(HALF):
                put(b * HALF + j, tile, value[j])

    unrolled(rows // HALF, min(copies, rows // HALF), one)


def order_pair(got, j, copies, out):
    def put(r, tile, value):
        times = pl.ds(pl.multiple_of(j * HALF, HALF), HALF)
        out[r, times, tile * LANES : (tile + 1) * LANES] = value

    reorder(got, j * PAIR, copies, put)


def gram(left, right):
    return lax.dot_general(
        left,
        jnp.concatenate([left, right], axis=1),
        (((0,), (0,)), ((), ())),
        preferred_element_type=F32,
    )


def prior_kernel(got, out, rows):
    channels = out.shape[0]

    def step(j, carry):
        order_pair(got, j, 4, rows)
        return carry

    lax.fori_loop(0, got.shape[1] // PAIR, step, 0)

    def one(k, copy):
        real, imag = rows[k], rows[channels + k]
        left = jnp.concatenate([real, imag], axis=0)
        out[k] = gram(left, jnp.concatenate([-imag, real], axis=0))

    unrolled(channels, 8, one)


def finish_kernel(scale, got_in, prior_in, out_ref, got, prior, rows, out, sems):
    n_inp, n_chan, quads, _, _ = got.shape
    steps = n_chan // PAIR
    channels, width = out.shape[1], out.shape[-1]
    count = channels // BLOCK

    def got_copy(j):
        where = (slice(None), pl.ds(j * PAIR, PAIR))
        return pltpu.make_async_copy(got_in.at[where], got.at[where], sems.at[count + j])

    def out_copy(j):
        where = (slice(None), pl.ds(j * BLOCK, BLOCK))
        return pltpu.make_async_copy(out.at[where], out_ref.at[where], sems.at[j])

    for j in range(steps):
        got_copy(j).start()
    def prior_copy(j):
        where = pl.ds(j * BLOCK, BLOCK)
        return pltpu.make_async_copy(
            prior_in.at[where], prior.at[where], sems.at[count + steps + j]
        )

    for j in range(count):
        prior_copy(j).start()

    def order(j, carry):
        got_copy(j).wait()

        def quad(k, copy):
            for c in range(PAIR):
                times = pl.ds(pl.multiple_of((j * PAIR + c) * HALF, HALF), HALF)
                for tile in range(n_inp // 4):
                    x = lane_swap([got[tile * 4 + p, j * PAIR + c, k] for p in range(4)])
                    for p in range(4):
                        rows[4 * k + p, times, tile * LANES : (tile + 1) * LANES] = x[p]

        unrolled(quads, min(8, quads), quad)
        return carry

    lax.fori_loop(0, steps, order, 0)

    def some(j, carry):
        prior_copy(j).wait()
        for i in range(BLOCK):
            k = j * BLOCK + i
            left = rows[k]
            parts = left.astype(F32).reshape(n_chan, 2, HALF // 2, width)
            right = jnp.stack([-parts[:, 1], parts[:, 0]], axis=1).reshape(left.shape)
            value = (gram(left, right.astype(BF16)) + prior[k]) * scale
            out[0, k] = value[:, :width].astype(BF16)
            out[1, k] = value[:, width:].astype(BF16)
        out_copy(j).start()
        return carry

    lax.fori_loop(0, count, some, 0)

    def finish(j, carry):
        out_copy(j).wait()
        return carry

    lax.fori_loop(0, count, finish, 0)


def params():
    return pltpu.CompilerParams(vmem_limit_bytes=VMEM)


def cost(flops, moved):
    return pl.CostEstimate(flops=int(flops), bytes_accessed=int(moved), transcendentals=0)


def on_device(voltages, history, taper):
    in_dev, s_dev, frame = voltages.shape
    taps = taper.shape[0]
    n_inp = lax.axis_size("inp")
    n_chan = lax.axis_size("chan")
    groups = n_inp * n_chan
    channels = BAND // groups
    total = n_inp * in_dev
    times = s_dev // 2
    early = taps - 1
    blocks = LANES // in_dev
    sets = times // blocks
    span = n_chan * times
    assert frame == RADIX * LANES and in_dev == 2 * HALF and PAIR * times == HALF
    assert early == times - 1 and RADIX % channels == 0 and n_inp % blocks == 0
    assert n_chan % PAIR == 0 and channels % BLOCK == 0

    outputs = 2 * BAND // CLASSES
    stage = stage_table(frame).astype(np.float32).astype(ml_dtypes.bfloat16)
    table = jnp.asarray(stage)
    upright = jnp.asarray(np.ascontiguousarray(stage.transpose(0, 2, 1)))
    unit = jnp.asarray(np.eye(outputs).astype(ml_dtypes.bfloat16))
    assert table.shape == (CLASSES, outputs, 2 * LANES) and outputs == LANES

    away = pl.BlockSpec(memory_space=pl.ANY)
    near = pl.BlockSpec(memory_space=pltpu.VMEM)

    def scratch(count, shape):
        return [
            pltpu.VMEM(voltages.shape, BF16),
            pltpu.VMEM(taper.shape, F32),
            pltpu.VMEM(shape, BF16),
            pltpu.VMEM((RADIX, 2 * count, HALF, LANES), F32),
            pltpu.VMEM((2, 8, 8, HALF, LANES), F32),
            pltpu.VMEM((CLASSES, count * in_dev, 2 * LANES), BF16),
            pltpu.SemaphoreType.DMA((CHUNKS + 2,)),
        ]

    late_shape = (sets, 2 * channels, LANES)
    early_shape = (channels // 4, HALF, LANES)

    def sent(shape):
        return jax.ShapeDtypeStruct((groups,) + shape, BF16)

    def wide(shape):
        return [
            pltpu.VMEM((RADIX, RADIX, times * in_dev), BF16),
            pltpu.VMEM((groups,) + shape, BF16),
        ]

    carried = pl.pallas_call(
        carried_kernel,
        in_specs=[away] * 3,
        out_specs=away,
        out_shape=jax.ShapeDtypeStruct((CLASSES, early * in_dev, outputs), BF16),
        scratch_shapes=scratch(early, upright.shape)
        + [
            pltpu.VMEM((CLASSES, early * in_dev, outputs), BF16),
            pltpu.SemaphoreType.DMA((2,)),
        ],
        compiler_params=params(),
        cost_estimate=cost(1e10, 2e7),
        name="carried",
    )(voltages, taper, upright)
    carried, later_taper = lax.optimization_barrier((carried, taper))
    carried = lax.ppermute(carried, "chan", [(i, i + 1) for i in range(n_chan - 1)])

    late_send = pl.pallas_call(
        lambda *refs: spectra_kernel(times, False, *refs),
        in_specs=[away] * 3,
        out_specs=away,
        out_shape=sent(late_shape),
        scratch_shapes=scratch(times, table.shape) + wide(late_shape),
        compiler_params=params(),
        cost_estimate=cost(5e10, 4e7),
        name="late",
    )(voltages, later_taper, table)

    def exchange(value, shape):
        value = lax.all_to_all(value, ("inp", "chan"), split_axis=0, concat_axis=0, tiled=True)
        return value.reshape((n_inp, n_chan) + shape)

    late_got = exchange(late_send, late_shape)

    keep = (lax.axis_index("chan") == 0).astype(F32).reshape(1)
    early_send = pl.pallas_call(
        lambda *refs: spectra_kernel(0, True, *refs),
        in_specs=[pl.BlockSpec(memory_space=pltpu.SMEM), near, near, near] + [away] * 3,
        out_specs=away,
        out_shape=sent(early_shape),
        scratch_shapes=scratch(times, table.shape) + wide(early_shape),
        compiler_params=params(),
        cost_estimate=cost(2e11, 4e7),
        name="early",
    )(keep, jnp.transpose(history, (1, 0, 2)), carried, unit, voltages, taper, table)
    early_got = exchange(early_send, early_shape)

    rows = pltpu.VMEM((2 * channels, span, total), BF16)
    prior_shape = (channels, total, 2 * total)
    prior = pl.pallas_call(
        prior_kernel,
        in_specs=[near],
        out_specs=near,
        out_shape=jax.ShapeDtypeStruct(prior_shape, F32),
        scratch_shapes=[rows],
        compiler_params=params(),
        cost_estimate=cost(1e4, 1e4),
        name="prior",
    )(late_got)
    return pl.pallas_call(
        lambda *refs: finish_kernel(1.0 / (n_chan * s_dev), *refs),
        in_specs=[away, away],
        out_specs=away,
        out_shape=jax.ShapeDtypeStruct((2, channels, total, total), BF16),
        scratch_shapes=[
            pltpu.VMEM(early_got.shape, BF16),
            pltpu.VMEM(prior_shape, F32),
            pltpu.VMEM((channels, n_chan * HALF, total), BF16),
            pltpu.VMEM((2, channels, total, total), BF16),
            pltpu.SemaphoreType.DMA((2 * (channels // BLOCK) + n_chan // PAIR,)),
        ],
        compiler_params=params(),
        cost_estimate=cost(1e10, 1e7),
        name="finish",
    )(early_got, prior)


def solution(mesh):
    in_specs = (P("inp", "chan", None), P("inp", None, None), P())
    out_specs = P(None, ("inp", "chan"), None, None)
    return jax.shard_map(
        on_device, mesh=mesh, in_specs=in_specs, out_specs=out_specs, check_vma=False
    )
```
